32 devices in a mesh: branch: 2 (over core), gi: 8 (over z, y), gj: 2 (over x).
Axes of the slice: x: 2, y: 2, z: 4, core: 2. Of those that a mesh axis runs over, the one named last changes fastest.
Arguments:
- homolog_embedding: float32 [32, 128, 256], P(('branch', 'gj'), 'gi'), may hold values from -6 to 6
- pair_input_tensor: float32 [128, 128, 128], P('gi', ('branch', 'gj')), may hold values from -6 to 6
- layernorm_scales: float32 [4, 256], replicated, may hold values from 0.5 to 1.5
- pair_norm_gains: float32 [3, 128], replicated, may hold values from 0.5 to 1.5
- pair_bias_matrix: float32 [128, 8], replicated
- horizontal_qkvg_kernel: float32 [256, 1024], replicated, may hold values from -0.375 to 0.375
- horizontal_final_kernel: float32 [256, 256], replicated, may hold values from -0.375 to 0.375
- vertical_qkvg_kernel: float32 [256, 1024], replicated, may hold values from -0.375 to 0.375
- vertical_final_kernel: float32 [256, 256], replicated, may hold values from -0.375 to 0.375
- feedforward_expand_kernel: float32 [256, 1024], replicated, may hold values from -0.375 to 0.375
- feedforward_shrink_kernel: float32 [1024, 256], replicated, may hold values from -0.1875 to 0.1875
- dyadic_sides_kernel: float32 [256, 64], replicated, may hold values from -0.375 to 0.375
- outer_output_matrix: float32 [1024, 128], replicated, may hold values from -1 to 1
- triangle_input_matrix: float32 [128, 640], replicated, may hold values from -0.5 to 0.5
- triangle_output_matrix: float32 [128, 128], replicated, may hold values from -0.5 to 0.5
Outputs:
- alignment_output: float32 [32, 128, 256], P(('branch', 'gj'), 'gi')
- pair_output_tensor: float32 [128, 128, 128], P('gi', ('branch', 'gj'))
The draws below stay inside these ranges and needn't reach their ends.
All inputs are finite; a program needn't handle non-finite values.
Results may differ from the reference program's by a relative error of at most 0.0003.
Values sent between devices are 32-bit elements; how exact they have to be, the bound alone decides.
No kernel may reach another device: no remote copies, remote signals or barrier semaphores. Data moves between devices by JAX's collectives and lax.ppermute only.
A program may use at most 64 MiB of HBM per device.

```python
import math
import jax
import jax.numpy as jnp
from jax import lax

EMBED_DIM = 256
CZ = 128
H = 8
HS = 32
PRODUCT_DIM = 32
HEADS_BY_SIZE = 256
HIDDEN_UNITS = 1024
HOMOLOG_NUMBER = 32
CHAIN_LENGTH = 128


def draw_pair_bias_matrix(key, part):
    base = jax.random.normal(key, (CZ, H), jnp.float32)
    return base * (2.0 / math.sqrt(CZ))


def levels(own_key, shape, shards, smallest, top_value):
    gain, own = 1.0, jax.random.fold_in(own_key, 6)
    for dim, shards_of in shards:
        steps = jnp.exp(jax.random.uniform(jax.random.fold_in(own, dim), (shards_of,), jnp.float32, smallest / len(shards), top_value / len(shards)))
        gain = gain * jnp.repeat(steps, shape[dim] // shards_of).reshape([-1 if axis == dim else 1 for axis in range(len(shape))])
    return gain


def scatter_about(own_key, dims, spread, most, pieces=(), kind=jnp.bfloat16):
    result = spread * jax.random.normal(own_key, dims, jnp.float32)
    if pieces:
        result = result * levels(own_key, dims, pieces, -0.22, 0.18)
    return jnp.clip(result, -most, most).astype(kind)


def setup_inputs(seed: int = 0) -> dict:
    key_list = jax.random.split(jax.random.key(seed), 16)
    homolog_embedding = scatter_about(key_list[0], (HOMOLOG_NUMBER, CHAIN_LENGTH, EMBED_DIM), 1.0, 6.0, ((0, 4), (1, 8)), jnp.float32)
    pair_input_tensor = scatter_about(key_list[1], (CHAIN_LENGTH, CHAIN_LENGTH, CZ), 1.0, 6.0, ((0, 8), (1, 4)), jnp.float32)
    layernorm_scales = jnp.clip(1.0 + 0.1 * jax.random.normal(key_list[2], (4, EMBED_DIM), jnp.float32), 0.5, 1.5)
    pair_norm_gains = jnp.clip(1.0 + 0.1 * jax.random.normal(key_list[3], (3, CZ), jnp.float32), 0.5, 1.5)
    pair_bias_matrix = draw_pair_bias_matrix(jax.random.fold_in(key_list[15], 71), 0)
    horizontal_qkvg_kernel = scatter_about(key_list[5], (EMBED_DIM, 4 * HEADS_BY_SIZE), EMBED_DIM ** -0.5, 0.375, (), jnp.float32)
    horizontal_final_kernel = scatter_about(key_list[6], (HEADS_BY_SIZE, EMBED_DIM), HEADS_BY_SIZE ** -0.5, 0.375, (), jnp.float32)
    vertical_qkvg_kernel = scatter_about(key_list[7], (EMBED_DIM, 4 * HEADS_BY_SIZE), EMBED_DIM ** -0.5, 0.375, (), jnp.float32)
    vertical_final_kernel = scatter_about(key_list[8], (HEADS_BY_SIZE, EMBED_DIM), HEADS_BY_SIZE ** -0.5, 0.375, (), jnp.float32)
    feedforward_expand_kernel = scatter_about(key_list[9], (EMBED_DIM, HIDDEN_UNITS), EMBED_DIM ** -0.5, 0.375, (), jnp.float32)
    feedforward_shrink_kernel = scatter_about(key_list[10], (HIDDEN_UNITS, EMBED_DIM), HIDDEN_UNITS ** -0.5, 0.1875, (), jnp.float32)
    dyadic_sides_kernel = scatter_about(key_list[11], (EMBED_DIM, 2 * PRODUCT_DIM), EMBED_DIM ** -0.5, 0.375, (), jnp.float32)
    outer_output_matrix = scatter_about(key_list[12], (PRODUCT_DIM * PRODUCT_DIM, CZ), PRODUCT_DIM ** -0.5, 1.0, (), jnp.float32)
    triangle_input_matrix = scatter_about(key_list[13], (CZ, 5 * CZ), CZ ** -0.5, 0.5, (), jnp.float32)
    triangle_output_matrix = scatter_about(key_list[14], (CZ, CZ), CZ ** -0.5, 0.5, (), jnp.float32)
    return {"homolog_embedding": homolog_embedding, "pair_input_tensor": pair_input_tensor, "layernorm_scales": layernorm_scales, "pair_norm_gains": pair_norm_gains, "pair_bias_matrix": pair_bias_matrix, "horizontal_qkvg_kernel": horizontal_qkvg_kernel, "horizontal_final_kernel": horizontal_final_kernel, "vertical_qkvg_kernel": vertical_qkvg_kernel, "vertical_final_kernel": vertical_final_kernel, "feedforward_expand_kernel": feedforward_expand_kernel, "feedforward_shrink_kernel": feedforward_shrink_kernel, "dyadic_sides_kernel": dyadic_sides_kernel, "outer_output_matrix": outer_output_matrix, "triangle_input_matrix": triangle_input_matrix, "triangle_output_matrix": triangle_output_matrix}


epsilon = 1e-05
highest = lax.Precision.HIGHEST

def layer_normalise(values, norm_gain):
    average = lax.optimization_barrier(jnp.mean(values, axis=-1, keepdims=True))
    centred = values - average
    variance = lax.optimization_barrier(jnp.mean(centred * centred, axis=-1, keepdims=True))
    return centred * lax.rsqrt(variance + epsilon) * norm_gain

def apply_projection(values, weight):
    return jnp.einsum('...c,cd->...d', values, weight, precision=highest)

def transition_update(values, norm_gain, feedforward_expand_kernel, feedforward_shrink_kernel):
    expanded = jax.nn.relu(apply_projection(layer_normalise(values, norm_gain), feedforward_expand_kernel))
    return values + apply_projection(expanded, feedforward_shrink_kernel)

def reference(homolog_embedding, pair_input_tensor, layernorm_scales, pair_norm_gains, pair_bias_matrix, horizontal_qkvg_kernel, horizontal_final_kernel, vertical_qkvg_kernel, vertical_final_kernel, feedforward_expand_kernel, feedforward_shrink_kernel, dyadic_sides_kernel, outer_output_matrix, triangle_input_matrix, triangle_output_matrix):
    bias_heads = jnp.transpose(apply_projection(layer_normalise(pair_input_tensor, pair_norm_gains[0]), pair_bias_matrix), (2, 0, 1))
    projected_values = apply_projection(layer_normalise(homolog_embedding, layernorm_scales[0]), horizontal_qkvg_kernel)
    queries = projected_values[..., :HEADS_BY_SIZE].reshape(HOMOLOG_NUMBER, CHAIN_LENGTH, H, HS)
    key_rows = projected_values[..., HEADS_BY_SIZE:2 * HEADS_BY_SIZE].reshape(HOMOLOG_NUMBER, CHAIN_LENGTH, H, HS)
    value_rows = projected_values[..., 2 * HEADS_BY_SIZE:3 * HEADS_BY_SIZE].reshape(HOMOLOG_NUMBER, CHAIN_LENGTH, H, HS)
    gate_row_values = projected_values[..., 3 * HEADS_BY_SIZE:]

    def row_single(inputs):
        query_row, key_row, value_row = inputs
        scores = jnp.einsum('ihd,jhd->hij', query_row, key_row, precision=highest) / math.sqrt(HS) + bias_heads
        weights = jax.nn.softmax(scores, axis=-1)
        return jnp.einsum('hij,jhd->ihd', weights, value_row, precision=highest)
    attention_result = lax.map(row_single, (queries, key_rows, value_rows)).reshape(HOMOLOG_NUMBER, CHAIN_LENGTH, HEADS_BY_SIZE)
    alignment_after_rows = homolog_embedding + apply_projection(jax.nn.sigmoid(gate_row_values) * attention_result, horizontal_final_kernel)
    projected_values = apply_projection(layer_normalise(alignment_after_rows, layernorm_scales[1]), vertical_qkvg_kernel)
    queries = jnp.transpose(projected_values[..., :HEADS_BY_SIZE].reshape(HOMOLOG_NUMBER, CHAIN_LENGTH, H, HS), (1, 0, 2, 3))
    key_rows = jnp.transpose(projected_values[..., HEADS_BY_SIZE:2 * HEADS_BY_SIZE].reshape(HOMOLOG_NUMBER, CHAIN_LENGTH, H, HS), (1, 0, 2, 3))
    value_rows = jnp.transpose(projected_values[..., 2 * HEADS_BY_SIZE:3 * HEADS_BY_SIZE].reshape(HOMOLOG_NUMBER, CHAIN_LENGTH, H, HS), (1, 0, 2, 3))
    gate_row_values = projected_values[..., 3 * HEADS_BY_SIZE:]

    def column_single(inputs):
        query_col, key_col, value_col = inputs
        scores = jnp.einsum('shd,thd->hst', query_col, key_col, precision=highest) / math.sqrt(HS)
        weights = jax.nn.softmax(scores, axis=-1)
        return jnp.einsum('hst,thd->shd', weights, value_col, precision=highest)
    attention_result = jnp.transpose(lax.map(column_single, (queries, key_rows, value_rows)), (1, 0, 2, 3)).reshape(HOMOLOG_NUMBER, CHAIN_LENGTH, HEADS_BY_SIZE)
    alignment_after_columns = alignment_after_rows + apply_projection(jax.nn.sigmoid(gate_row_values) * attention_result, vertical_final_kernel)
    alignment_output = transition_update(alignment_after_columns, layernorm_scales[2], feedforward_expand_kernel, feedforward_shrink_kernel)
    factor_pair = apply_projection(layer_normalise(alignment_output, layernorm_scales[3]), dyadic_sides_kernel)
    left_side = jnp.transpose(factor_pair[..., :PRODUCT_DIM], (1, 0, 2))
    right_side = jnp.transpose(factor_pair[..., PRODUCT_DIM:], (1, 0, 2))

    def outer_single(left_row):
        outer = jnp.einsum('sc,jsd->jcd', left_row, right_side, precision=highest) / HOMOLOG_NUMBER
        return apply_projection(outer.reshape(CHAIN_LENGTH, PRODUCT_DIM * PRODUCT_DIM), outer_output_matrix)
    pair_first = pair_input_tensor + lax.map(outer_single, left_side)
    projected_values = apply_projection(layer_normalise(pair_first, pair_norm_gains[1]), triangle_input_matrix)
    left_tri = jax.nn.sigmoid(projected_values[..., CZ:2 * CZ]) * projected_values[..., :CZ]
    right_tri = jax.nn.sigmoid(projected_values[..., 3 * CZ:4 * CZ]) * projected_values[..., 2 * CZ:3 * CZ]
    out_gate = projected_values[..., 4 * CZ:]
    product = jnp.einsum('ikc,jkc->ijc', left_tri, right_tri, precision=highest)
    pair_output_tensor = pair_first + jax.nn.sigmoid(out_gate) * apply_projection(layer_normalise(product, pair_norm_gains[2]), triangle_output_matrix)
    return (alignment_output, pair_output_tensor)
```

```python
import math

import jax
import jax.numpy as jnp
from jax import lax
from jax.sharding import PartitionSpec as P

epsilon = 1e-05
precise = lax.Precision.HIGH
everyone = ("branch", "gi", "gj")
columns = ("branch", "gj")


def layer_normalise(values, norm_gain):
    average = jnp.mean(values, axis=-1, keepdims=True)
    centred = values - average
    variance = jnp.mean(centred * centred, axis=-1, keepdims=True)
    return centred * lax.rsqrt(variance + epsilon) * norm_gain


def apply_projection(values, weight):
    return jnp.einsum("...c,cd->...d", values, weight, precision=precise)


def direct_gather(block, axes):
    n, me = lax.axis_size(axes), lax.axis_index(axes)
    parts = [block]
    for step in range(1, n):
        parts.append(lax.ppermute(block, axes, [((t + step) % n, t) for t in range(n)]))
    stacked = jnp.stack(parts + parts)
    return lax.dynamic_slice_in_dim(stacked, lax.rem(n - me, n), n, axis=0)


def per_device(
    homolog_embedding,
    pair_input_tensor,
    layernorm_scales,
    pair_norm_gains,
    pair_bias_matrix,
    horizontal_qkvg_kernel,
    horizontal_final_kernel,
    vertical_qkvg_kernel,
    vertical_final_kernel,
    feedforward_expand_kernel,
    feedforward_shrink_kernel,
    dyadic_sides_kernel,
    outer_output_matrix,
    triangle_input_matrix,
    triangle_output_matrix,
):
    rows, residues, width = homolog_embedding.shape
    pair_cols, pair_width = pair_input_tensor.shape[1:]
    heads = pair_bias_matrix.shape[1]
    inner = horizontal_final_kernel.shape[0]
    size = inner // heads
    outer_width = dyadic_sides_kernel.shape[1] // 2
    n_cols, n_gi = lax.axis_size(columns), lax.axis_size("gi")
    n_all = n_cols * n_gi
    length = residues * n_gi
    scale = 1.0 / math.sqrt(size)

    msa_rows = direct_gather(homolog_embedding, "gi")
    bias_local = apply_projection(
        layer_normalise(pair_input_tensor, pair_norm_gains[0]), pair_bias_matrix
    )
    bias_local = jnp.transpose(bias_local, (2, 0, 1))
    bias = direct_gather(bias_local, columns)
    bias = jnp.transpose(bias, (1, 2, 0, 3)).reshape(heads, residues, length)
    own = layer_normalise(homolog_embedding, layernorm_scales[0])
    query = apply_projection(own, horizontal_qkvg_kernel[:, :inner])
    gate = apply_projection(own, horizontal_qkvg_kernel[:, 3 * inner :])
    rest = layer_normalise(msa_rows, layernorm_scales[0])
    pair_kv = apply_projection(rest, horizontal_qkvg_kernel[:, inner : 3 * inner])
    key = pair_kv[..., :inner].reshape(n_gi, rows, residues, heads, size)
    value = pair_kv[..., inner:].reshape(n_gi, rows, residues, heads, size)
    query = query.reshape(rows, residues, heads, size)
    scores = jnp.einsum("sihd,gsjhd->shigj", query, key, precision=precise) * scale
    scores = scores.reshape(rows, heads, residues, length) + bias[None]
    weights = jnp.exp(scores - jnp.max(scores, axis=-1, keepdims=True))
    total = jnp.sum(weights, axis=-1)
    weights = weights.reshape(rows, heads, residues, n_gi, residues)
    attended = jnp.einsum("shigj,gsjhd->sihd", weights, value, precision=precise)
    attended = attended / jnp.transpose(total, (0, 2, 1))[..., None]
    attended = attended.reshape(rows, residues, inner)
    msa_first = homolog_embedding + apply_projection(
        jax.nn.sigmoid(gate) * attended, horizontal_final_kernel
    )

    msa_first = lax.all_to_all(msa_first, columns, 1, 0, tiled=True)
    all_rows, few = msa_first.shape[:2]
    projected = apply_projection(
        layer_normalise(msa_first, layernorm_scales[1]), vertical_qkvg_kernel
    )
    query, key, value = (
        projected[..., k * inner : (k + 1) * inner].reshape(all_rows, few, heads, size)
        for k in range(3)
    )
    gate = projected[..., 3 * inner :]
    scores = jnp.einsum("sihd,tihd->ihst", query, key, precision=precise) * scale
    weights = jax.nn.softmax(scores, axis=-1)
    attended = jnp.einsum("ihst,tihd->sihd", weights, value, precision=precise)
    attended = attended.reshape(all_rows, few, inner)
    msa_second = msa_first + apply_projection(
        jax.nn.sigmoid(gate) * attended, vertical_final_kernel
    )
    expanded = jax.nn.relu(
        apply_projection(
            layer_normalise(msa_second, layernorm_scales[2]), feedforward_expand_kernel
        )
    )
    alignment = msa_second + apply_projection(expanded, feedforward_shrink_kernel)
    alignment_output = lax.all_to_all(alignment, columns, 0, 1, tiled=True)

    factors = apply_projection(
        layer_normalise(alignment, layernorm_scales[3]), dyadic_sides_kernel
    )
    left = jnp.transpose(factors[..., :outer_width], (1, 0, 2))
    right = jnp.transpose(factors[..., outer_width:], (1, 0, 2))
    left = direct_gather(left, columns).reshape(residues, all_rows, outer_width)
    groups = n_gi // n_cols
    n_branch, n_gj = lax.axis_size("branch"), lax.axis_size("gj")

    def flat(c, g):
        return (c // n_gj * n_gi + g) * n_gj + c % n_gj

    parts = []
    for step in range(n_gi):
        pairs = []
        for c in range(n_cols):
            for g in range(n_gi):
                other = (g + step) % n_gi
                source = flat(other // groups, c * groups + other % groups)
                pairs.append((source, flat(c, g)))
        parts.append(lax.ppermute(right, everyone, pairs))
    stacked = jnp.stack(parts + parts)
    me = lax.axis_index("gi")
    right = lax.dynamic_slice_in_dim(stacked, lax.rem(n_gi - me, n_gi), n_gi, axis=0)
    right = right.reshape(n_cols, groups, few, all_rows, outer_width)
    right = jnp.transpose(right, (1, 0, 2, 3, 4)).reshape(pair_cols, all_rows, outer_width)
    outer = jnp.einsum("isc,jsd->ijcd", left, right, precision=precise) / all_rows
    pair_first = pair_input_tensor + apply_projection(
        outer.reshape(residues, pair_cols, outer_width * outer_width), outer_output_matrix
    )

    projected = apply_projection(
        layer_normalise(pair_first, pair_norm_gains[1]), triangle_input_matrix
    )
    la, ga, lb, gb, go = (
        projected[..., k * pair_width : (k + 1) * pair_width] for k in range(5)
    )
    left_tri = jax.nn.sigmoid(ga) * la
    right_tri = jax.nn.sigmoid(gb) * lb
    if pair_width % n_all == 0:
        share = pair_width // n_all
        both = jnp.stack([left_tri, right_tri]).reshape(2, residues, pair_cols, n_all, share)
        both = jnp.transpose(both, (3, 0, 4, 1, 2))
        both = lax.all_to_all(both, everyone, 0, 0, tiled=True)
        both = both.reshape(n_branch, n_gi, n_gj, 2, share, residues, pair_cols)
        both = jnp.transpose(both, (3, 4, 1, 5, 0, 2, 6)).reshape(2, share, length, length)
        product = jnp.einsum("cik,cjk->cij", both[0], both[1], precision=precise)
        product = product.reshape(share, n_gi, residues, n_branch, n_gj, pair_cols)
        product = jnp.transpose(product, (3, 1, 4, 0, 2, 5)).reshape(
            n_all, share, residues, pair_cols
        )
        product = lax.all_to_all(product, everyone, 0, 0, tiled=True)
        product = jnp.transpose(
            product.reshape(pair_width, residues, pair_cols), (1, 2, 0)
        )
    else:
        right_columns = lax.all_gather(right_tri, "gi", axis=0, tiled=True)
        product = lax.psum_scatter(
            jnp.einsum("jkc,ikc->jic", right_columns, left_tri, precision=precise),
            columns,
            scatter_dimension=0,
            tiled=True,
        )
        product = jnp.transpose(product, (1, 0, 2))
    pair_output_tensor = pair_first + jax.nn.sigmoid(go) * apply_projection(
        layer_normalise(product, pair_norm_gains[2]), triangle_output_matrix
    )
    return (alignment_output, pair_output_tensor)


def solution(mesh):
    tile, grid = P(("branch", "gj"), "gi", None), P("gi", ("branch", "gj"), None)
    return jax.shard_map(
        per_device,
        mesh=mesh,
        in_specs=(tile, grid) + (P(),) * 13,
        out_specs=(tile, grid),
        check_vma=False,
    )
```

```python
import functools
import math

import jax
import jax.numpy as jnp
from jax import lax
from jax.experimental import pallas as pl
from jax.experimental.pallas import tpu as pltpu
from jax.sharding import PartitionSpec as P

epsilon = 1e-05
precise = lax.Precision.HIGH
everyone = ("branch", "gi", "gj")
columns = ("branch", "gj")
lanes = 128
vmem = pl.BlockSpec(memory_space=pltpu.VMEM)
smem = pl.BlockSpec(memory_space=pltpu.SMEM)
params = pltpu.CompilerParams(vmem_limit_bytes=48 * 1024 * 1024)


def layer_normalise(values, norm_gain, axis=-1):
    average = jnp.mean(values, axis=axis, keepdims=True)
    centred = values - average
    variance = jnp.mean(centred * centred, axis=axis, keepdims=True)
    return centred * lax.rsqrt(variance + epsilon) * norm_gain


def apply_projection(values, weight):
    return jnp.einsum("...c,cd->...d", values, weight, precision=precise)


def sigmoid(values):
    return 1.0 / (1.0 + jnp.exp(-values))


def split(values):
    high = values.astype(jnp.bfloat16)
    return high, (values - high.astype(jnp.float32)).astype(jnp.bfloat16)


def multiply(left, right, across=False):
    numbers = (((1,), (1 if across else 0,)), ((), ()))

    def one(a, b):
        return lax.dot_general(a, b, numbers, preferred_element_type=jnp.float32)

    (lh, ll), (rh, rl) = split(left), split(right)
    return one(lh, rh) + (one(lh, rl) + one(ll, rh))


def swap_lane_groups(arrays):
    n, arrays = len(arrays), list(arrays)
    width = lanes // n
    wide = arrays[0].shape[-1]
    lane = lax.broadcasted_iota(jnp.int32, arrays[0].shape, arrays[0].ndim - 1)
    group = lax.rem(lane, lanes) // width
    axis = arrays[0].ndim - 1
    step = 1
    while step < n:
        upper = (group // step) % 2 == 1
        for low in range(n):
            if low & step:
                continue
            a, b = arrays[low], arrays[low + step]
            arrays[low] = jnp.where(upper, pltpu.roll(b, step * width, axis), a)
            arrays[low + step] = jnp.where(
                upper, b, pltpu.roll(a, wide - step * width, axis)
            )
        step *= 2
    return arrays


def head_masks(shape, heads):
    column = lax.broadcasted_iota(jnp.int32, shape, 1)
    return [column // (shape[1] // heads) == h for h in range(heads)]


def attend(query, key, value, bias, heads, allowed=None):
    count, inner = query.shape
    masks = head_masks((count, inner), heads)
    spread = jnp.concatenate([jnp.where(m, query, 0.0) for m in masks], axis=0)
    scores = multiply(spread, key, across=True) * (1.0 / math.sqrt(inner // heads))
    if bias is not None:
        scores = scores + bias
    if allowed is not None:
        scores = jnp.where(allowed, scores, -1e30)
    weights = jnp.exp(scores - jnp.max(scores, axis=-1, keepdims=True))
    weights = weights / jnp.sum(weights, axis=-1, keepdims=True)
    mixed = multiply(weights, value)
    result = jnp.where(masks[0], mixed[:count], 0.0)
    for h in range(1, heads):
        result = result + jnp.where(masks[h], mixed[h * count : (h + 1) * count], 0.0)
    return result


def bias_kernel(pair_ref, gains_ref, matrix_ref, out_ref):
    residues, pair_cols, _ = pair_ref.shape
    heads = matrix_ref.shape[0]
    per = lanes // pair_cols
    normal = layer_normalise(pair_ref[...], gains_ref[0:1, :][None])
    for i in range(residues):
        here = multiply(matrix_ref[...], normal[i], across=True)
        for h in range(heads):
            out_ref[h // per, i : i + 1, pl.ds(h % per * pair_cols, pair_cols)] = here[h : h + 1]


def row_kernel(
    n_branch, n_gj, parts, few, part_ref, msa_ref, bias_ref, gains_ref, qkvg_ref, final_ref, out_ref
):
    _, residues, width = msa_ref.shape
    n_src, blocks, _, _ = bias_ref.shape
    n_cols = n_branch * n_gj
    per_part = n_src // n_cols
    n_gi = per_part * parts
    rows = msa_ref.shape[0] // n_gi
    inner = final_ref.shape[0]
    queries = per_part * residues
    length = n_gi * residues
    heads = blocks * lanes // (length // n_cols)
    per = heads // blocks
    gain = gains_ref[0:1, :]
    tokens = jnp.concatenate(
        [msa_ref[g * rows + r] for r in range(rows) for g in range(n_gi)], axis=0
    )
    first = part_ref[0] * (per_part * rows)
    asking = msa_ref[pl.ds(first, per_part * rows)]
    asking = jnp.concatenate(
        [asking[g * rows + r] for r in range(rows) for g in range(per_part)], axis=0
    )
    key_value = multiply(layer_normalise(tokens, gain), qkvg_ref[:, inner : 3 * inner])
    normal = layer_normalise(asking, gain)
    query = multiply(normal, qkvg_ref[:, :inner])
    gate = multiply(normal, qkvg_ref[:, 3 * inner :])
    pieces = [[] for _ in range(heads)]
    for block in range(blocks):
        for g in range(per_part):
            tiles = [[] for _ in range(per)]
            for tile in range(n_cols // per):
                group = []
                for c in range(tile * per, (tile + 1) * per):
                    source = (c // n_gj * per_part + g) * n_gj + c % n_gj
                    group.append(bias_ref[source, block])
                for k, piece in enumerate(swap_lane_groups(group)):
                    tiles[k].append(piece)
            for k in range(per):
                pieces[block * per + k].append(jnp.concatenate(tiles[k], axis=1))
    bias = jnp.concatenate([p for head in pieces for p in head], axis=0)
    attended = []
    for r in range(rows):
        keys = key_value[r * length : (r + 1) * length, :inner]
        values = key_value[r * length : (r + 1) * length, inner:]
        attended.append(
            attend(query[r * queries : (r + 1) * queries], keys, values, bias, heads)
        )
    attended = jnp.concatenate(attended, axis=0)
    result = asking + multiply(sigmoid(gate) * attended, final_ref[...])
    for b in range(n_branch):
        for g in range(per_part):
            for j in range(n_gj):
                start = g * residues + (b * n_gj + j) * few
                out_ref[(b * per_part + g) * n_gj + j] = jnp.concatenate(
                    [result[r * queries + start : r * queries + start + few] for r in range(rows)],
                    axis=0,
                )


def column_kernel(
    n_branch, n_gj, few, heads, msa_ref, gains_ref, qkvg_ref, final_ref, expand_ref, shrink_ref,
    sides_ref, out_ref, left_ref, right_ref
):
    count, width = msa_ref.shape
    inner = final_ref.shape[0]
    half = sides_ref.shape[0] // 2
    first = msa_ref[...]
    projected = multiply(layer_normalise(first, gains_ref[1:2, :]), qkvg_ref[...])
    query, key, value, gate = (projected[:, k * inner : (k + 1) * inner] for k in range(4))
    allowed = None
    if few > 1:
        shape = (heads * count, count)
        asks = lax.broadcasted_iota(jnp.int32, shape, 0)
        holds = lax.broadcasted_iota(jnp.int32, shape, 1)
        allowed = lax.rem(asks, few) == lax.rem(holds, few)
    attended = attend(query, key, value, None, heads, allowed)
    second = first + multiply(sigmoid(gate) * attended, final_ref[...])
    expanded = multiply(layer_normalise(second, gains_ref[2:3, :]), expand_ref[...])
    third = second + multiply(jnp.maximum(expanded, 0.0), shrink_ref[...])
    per_part = out_ref.shape[1]
    each = out_ref.shape[2]
    for b in range(n_branch):
        for g in range(per_part):
            for j in range(n_gj):
                start = ((b * per_part + g) * n_gj + j) * each
                out_ref[b * n_gj + j, g] = third[start : start + each]
    factors = multiply(sides_ref[...], layer_normalise(third, gains_ref[3:4, :]), across=True)
    left_ref[...] = factors[:half]
    right_ref[...] = factors[half:]


def pair_kernel(
    few, n_gi, left_ref, right_ref, pair_ref, gain_ref, matrix_ref, triangle_ref,
    tri_ref, first_ref, gate_ref
):
    n_cols, wide, count = left_ref.shape
    all_rows = count // few
    residues = n_cols * few
    pair_cols = n_gi * few
    per = lanes // pair_cols
    groups = residues // per
    width = pair_ref.shape[1]
    owner = lax.rem(lax.broadcasted_iota(jnp.int32, (1, count), 1), few)
    left = []
    for c in range(n_cols):
        here = left_ref[c]
        for f in range(few):
            own = jnp.where(owner == f, here, 0.0)
            total = own
            for other in range(few):
                if other != f:
                    total = total + pltpu.roll(own, (other - f) % count, 1)
            left.append(total)
    left = jnp.concatenate(left, axis=0) * (1.0 / all_rows)
    right = []
    for d in range(wide):
        here = right_ref[pl.ds(d, n_gi, stride=wide), :]
        right += [jnp.where(owner == f, here, 0.0) for f in range(few)]
    right = jnp.concatenate(right, axis=0)
    outer = multiply(left, right, across=True)
    outputs = []
    for g in range(groups):
        swapped = swap_lane_groups(
            [outer[(g * per + i) * wide : (g * per + i + 1) * wide] for i in range(per)]
        )
        stacked = [
            s[:, t * lanes : (t + 1) * lanes] for s in swapped for t in range(wide // per)
        ]
        outputs.append(jnp.concatenate(stacked, axis=0))
    update = multiply(matrix_ref[...], jnp.concatenate(outputs, axis=1))
    first = pair_ref[...].T + update
    projected = multiply(triangle_ref[...], layer_normalise(first, gain_ref[...], axis=0))
    tri = sigmoid(projected[2 * width : 4 * width]) * projected[: 2 * width]
    tri_ref[...] = tri.reshape(tri_ref.shape)
    first_ref[...] = first.T
    gate_ref[...] = sigmoid(projected[4 * width :]).T


def per_device(
    homolog_embedding,
    pair_input_tensor,
    layernorm_scales,
    pair_norm_gains,
    pair_bias_matrix,
    horizontal_qkvg_kernel,
    horizontal_final_kernel,
    vertical_qkvg_kernel,
    vertical_final_kernel,
    feedforward_expand_kernel,
    feedforward_shrink_kernel,
    dyadic_sides_kernel,
    outer_output_matrix,
    triangle_input_matrix,
    triangle_output_matrix,
):
    rows, residues, width = homolog_embedding.shape
    pair_cols, pair_width = pair_input_tensor.shape[1:]
    heads = pair_bias_matrix.shape[1]
    outer_width = dyadic_sides_kernel.shape[1] // 2
    n_branch, n_gi, n_gj = (lax.axis_size(name) for name in everyone)
    n_cols = n_branch * n_gj
    n_all = n_cols * n_gi
    length = residues * n_gi
    few = residues // n_cols
    groups = n_gi // n_cols
    parts = 2
    per_part = n_gi // parts
    own_rows = rows // per_part
    f32 = jnp.float32

    def call(kernel, outs, *operands, scalars=0):
        return pl.pallas_call(
            kernel,
            out_shape=[jax.ShapeDtypeStruct(shape, f32) for shape in outs],
            in_specs=[smem] * scalars + [vmem] * (len(operands) - scalars),
            out_specs=[vmem] * len(outs),
            compiler_params=params,
        )(*operands)

    halves = [
        [
            (b * n_gi + part * per_part + g) * n_gj + j
            for b in range(n_branch)
            for g in range(per_part)
            for j in range(n_gj)
        ]
        for part in range(parts)
    ]
    n_half = n_cols * per_part

    msa = lax.all_to_all(
        jnp.concatenate([homolog_embedding] * parts, axis=0), "gi", 0, 0, tiled=True
    )
    per = lanes // pair_cols
    (bias,) = call(
        bias_kernel,
        [(heads // per, residues, lanes)],
        pair_input_tensor,
        pair_norm_gains,
        pair_bias_matrix.T,
    )
    bias = jnp.broadcast_to(bias[None], (n_half,) + bias.shape)
    bias = lax.all_to_all(bias, everyone, 0, 0, tiled=True, axis_index_groups=halves)
    part = (lax.axis_index("gi") // per_part).astype(jnp.int32).reshape(1)
    (msa_first,) = call(
        functools.partial(row_kernel, n_branch, n_gj, parts, few),
        [(n_half, own_rows * few, width)],
        part,
        msa,
        bias,
        layernorm_scales,
        horizontal_qkvg_kernel,
        horizontal_final_kernel,
        scalars=1,
    )

    msa_first = lax.all_to_all(msa_first, everyone, 0, 0, tiled=True, axis_index_groups=halves)
    count = n_half * own_rows * few
    alignment, left, right = call(
        functools.partial(column_kernel, n_branch, n_gj, few, heads),
        [(n_cols, per_part, own_rows * few, width)] + [(outer_width, count)] * 2,
        msa_first.reshape(count, width),
        layernorm_scales,
        vertical_qkvg_kernel,
        vertical_final_kernel,
        feedforward_expand_kernel,
        feedforward_shrink_kernel,
        dyadic_sides_kernel.T,
    )
    alignment = lax.all_to_all(
        alignment.reshape(n_cols, rows, few, width), columns, 0, 0, tiled=True
    )
    alignment_output = jnp.transpose(alignment, (1, 0, 2, 3)).reshape(rows, residues, width)

    left = lax.all_to_all(
        jnp.broadcast_to(left[None], (n_cols,) + left.shape), columns, 0, 0, tiled=True
    )
    right = lax.all_to_all(
        jnp.broadcast_to(right[None], (n_gi,) + right.shape), "gi", 0, 0, tiled=True
    )
    pair = pair_input_tensor.reshape(residues, groups, n_cols, few, pair_width)
    pair = lax.all_to_all(jnp.transpose(pair, (2, 0, 1, 3, 4)), columns, 0, 0, tiled=True)
    pair = jnp.transpose(pair, (1, 3, 0, 2, 4)).reshape(residues * pair_cols, pair_width)
    share = max(pair_width // n_all, 1)
    slots = pair_width // share
    triangle = triangle_input_matrix.T.reshape(5, slots, share, pair_width)
    sides = jnp.stack([triangle[0], triangle[2]], axis=1)
    gates = jnp.stack([triangle[1], triangle[3]], axis=1)
    triangle = jnp.concatenate(
        [side.reshape(2 * pair_width, pair_width) for side in (sides, gates)]
        + [triangle[4].reshape(pair_width, pair_width)],
        axis=0,
    )
    matrix = outer_output_matrix.reshape(outer_width, outer_width // per, per, pair_width)
    matrix = jnp.transpose(matrix, (3, 2, 1, 0)).reshape(pair_width, -1)
    positions = residues * pair_cols
    tri, pair_first, out_gate = call(
        functools.partial(pair_kernel, few, n_gi),
        [(slots, 2 * share, positions)] + [(positions, pair_width)] * 2,
        left,
        right.reshape(n_gi * outer_width, count),
        pair,
        pair_norm_gains[1][:, None],
        matrix,
        triangle,
    )

    both = jnp.stack([pair_first, out_gate]).reshape(
        2, residues, few, n_cols, groups, pair_width
    )
    both = lax.all_to_all(jnp.transpose(both, (3, 0, 1, 4, 2, 5)), columns, 0, 0, tiled=True)
    both = jnp.transpose(both, (1, 2, 3, 0, 4, 5)).reshape(
        2, residues, pair_cols, pair_width
    )
    pair_first, out_gate = both[0], both[1]

    if pair_width % n_all == 0:
        tri = lax.all_to_all(tri, everyone, 0, 0, tiled=True)
        tri = tri.reshape(n_branch, n_gi, n_gj, 2, share, residues, pair_cols)
        tri = jnp.transpose(tri, (3, 4, 1, 5, 0, 2, 6)).reshape(2, share, length, length)
        product = jnp.einsum("cik,cjk->cij", tri[0], tri[1], precision=precise)
        product = product.reshape(share, n_gi, residues, n_branch, n_gj, pair_cols)
        product = jnp.transpose(product, (3, 1, 4, 0, 2, 5)).reshape(
            n_all, share, residues * pair_cols
        )
        product = lax.all_to_all(product, everyone, 0, 0, tiled=True)
        product = product.reshape(pair_width, positions).T.reshape(
            residues, pair_cols, pair_width
        )
    else:
        tri = jnp.transpose(tri.reshape(slots, 2, share, positions), (1, 3, 0, 2))
        tri = tri.reshape(2, residues, pair_cols, pair_width)
        right_columns = lax.all_gather(tri[1], "gi", axis=0, tiled=True)
        product = lax.psum_scatter(
            jnp.einsum("jkc,ikc->jic", right_columns, tri[0], precision=precise),
            columns,
            scatter_dimension=0,
            tiled=True,
        )
        product = jnp.transpose(product, (1, 0, 2))
    pair_output_tensor = pair_first + out_gate * apply_projection(
        layer_normalise(product, pair_norm_gains[2]), triangle_output_matrix
    )
    return (alignment_output, pair_output_tensor)


def solution(mesh):
    tile, grid = P(("branch", "gj"), "gi", None), P("gi", ("branch", "gj"), None)
    return jax.shard_map(
        per_device,
        mesh=mesh,
        in_specs=(tile, grid) + (P(),) * 13,
        out_specs=(tile, grid),
        check_vma=False,
    )
```

```python
import functools
import math

import jax
import jax.numpy as jnp
from jax import lax
from jax.experimental import pallas as pl
from jax.experimental.pallas import tpu as pltpu
from jax.sharding import PartitionSpec as P

epsilon = 1e-05
precise = lax.Precision.HIGH
everyone = ("branch", "gi", "gj")
columns = ("branch", "gj")
lanes = 128
vmem = pl.BlockSpec(memory_space=pltpu.VMEM)
smem = pl.BlockSpec(memory_space=pltpu.SMEM)
params = pltpu.CompilerParams(vmem_limit_bytes=48 * 1024 * 1024)


def layer_normalise(values, norm_gain, axis=-1):
    average = jnp.mean(values, axis=axis, keepdims=True)
    centred = values - average
    variance = jnp.mean(centred * centred, axis=axis, keepdims=True)
    return centred * lax.rsqrt(variance + epsilon) * norm_gain


def apply_projection(values, weight):
    return jnp.einsum("...c,cd->...d", values, weight, precision=precise)


def sigmoid(values):
    return 1.0 / (1.0 + jnp.exp(-values))


def split(values):
    high = values.astype(jnp.bfloat16)
    return high, (values - high.astype(jnp.float32)).astype(jnp.bfloat16)


def multiply(left, right, across=False):
    numbers = (((1,), (1 if across else 0,)), ((), ()))

    def one(a, b):
        return lax.dot_general(a, b, numbers, preferred_element_type=jnp.float32)

    (lh, ll), (rh, rl) = split(left), split(right)
    return one(lh, rh) + (one(lh, rl) + one(ll, rh))


def swap_lane_groups(arrays):
    n, arrays = len(arrays), list(arrays)
    width = lanes // n
    wide = arrays[0].shape[-1]
    lane = lax.broadcasted_iota(jnp.int32, arrays[0].shape, arrays[0].ndim - 1)
    group = lax.rem(lane, lanes) // width
    axis = arrays[0].ndim - 1
    step = 1
    while step < n:
        upper = (group // step) % 2 == 1
        for low in range(n):
            if low & step:
                continue
            a, b = arrays[low], arrays[low + step]
            arrays[low] = jnp.where(upper, pltpu.roll(b, step * width, axis), a)
            arrays[low + step] = jnp.where(
                upper, b, pltpu.roll(a, wide - step * width, axis)
            )
        step *= 2
    return arrays


def head_masks(shape, heads):
    column = lax.broadcasted_iota(jnp.int32, shape, 1)
    return [column // (shape[1] // heads) == h for h in range(heads)]


def attend(query, key, value, bias, heads, allowed=None):
    count, inner = query.shape
    masks = head_masks((count, inner), heads)
    spread = jnp.concatenate([jnp.where(m, query, 0.0) for m in masks], axis=0)
    scores = multiply(spread, key, across=True) * (1.0 / math.sqrt(inner // heads))
    if bias is not None:
        scores = scores + bias
    if allowed is not None:
        scores = jnp.where(allowed, scores, -1e30)
    weights = jnp.exp(scores - jnp.max(scores, axis=-1, keepdims=True))
    weights = weights / jnp.sum(weights, axis=-1, keepdims=True)
    mixed = multiply(weights, value)
    result = jnp.where(masks[0], mixed[:count], 0.0)
    for h in range(1, heads):
        result = result + jnp.where(masks[h], mixed[h * count : (h + 1) * count], 0.0)
    return result


def spread(me, refs, slots):
    for k, ref in enumerate(refs):
        slots[me ^ k] = ref[...]


def spread_rows(me, refs, slots):
    for k, ref in enumerate(refs):
        count = ref.shape[0]
        slots[pl.ds(pl.multiple_of((me ^ k) * count, 8), count), :] = ref[...]


def bias_kernel(few, me_ref, pair_ref, gains_ref, matrix_ref, out_ref, *rest):
    chunks, slots = rest[:-1], rest[-1]
    residues, pair_cols, _ = pair_ref.shape
    heads = matrix_ref.shape[0]
    n_cols = len(chunks)
    groups = pair_cols // (n_cols * few)
    per = lanes // pair_cols
    normal = layer_normalise(pair_ref[...], gains_ref[0:1, :][None])
    for i in range(residues):
        here = multiply(matrix_ref[...], normal[i], across=True)
        for h in range(heads):
            out_ref[h // per, i : i + 1, pl.ds(h % per * pair_cols, pair_cols)] = here[h : h + 1]
    for c in range(n_cols):
        for o in range(groups):
            for f in range(few):
                start = (o * n_cols + c) * few + f
                slots[c, :, f * groups + o, :] = pair_ref[:, start, :]
    for k in range(n_cols):
        chunks[k][...] = slots[me_ref[0] ^ k]


def bias_rows_kernel(n_cols, me_ref, *rest):
    blocks, (out_ref, slots) = rest[:n_cols], rest[n_cols:]
    spread(me_ref[0], blocks, slots)
    count = slots.shape[1]
    per = out_ref.shape[0] // count
    for block in range(count):
        tiles = [[] for _ in range(per)]
        for tile in range(n_cols // per):
            group = [slots[c, block] for c in range(tile * per, (tile + 1) * per)]
            for k, piece in enumerate(swap_lane_groups(group)):
                tiles[k].append(piece)
        for k in range(per):
            out_ref[block * per + k] = jnp.concatenate(tiles[k], axis=1)


def row_kernel(n_branch, n_gj, per_part, few, me_ref, msa_ref, *rest):
    bias_refs, (gains_ref, qkvg_ref, final_ref, out_ref, slots) = (
        rest[:per_part],
        rest[per_part:],
    )
    _, residues, width = msa_ref.shape
    heads, _, length = bias_refs[0].shape
    n_gi = length // residues
    rows = msa_ref.shape[0] // n_gi
    inner = final_ref.shape[0]
    queries = per_part * residues
    gain = gains_ref[0:1, :]
    spread(me_ref[1], bias_refs, slots)
    bias = jnp.concatenate(
        [slots[g, h] for h in range(heads) for g in range(per_part)], axis=0
    )
    tokens = jnp.concatenate(
        [msa_ref[g * rows + r] for r in range(rows) for g in range(n_gi)], axis=0
    )
    first = me_ref[2] * (per_part * rows)
    asking = msa_ref[pl.ds(first, per_part * rows)]
    asking = jnp.concatenate(
        [asking[g * rows + r] for r in range(rows) for g in range(per_part)], axis=0
    )
    key_value = multiply(layer_normalise(tokens, gain), qkvg_ref[:, inner : 3 * inner])
    normal = layer_normalise(asking, gain)
    query = multiply(normal, qkvg_ref[:, :inner])
    gate = multiply(normal, qkvg_ref[:, 3 * inner :])
    attended = []
    for r in range(rows):
        keys = key_value[r * length : (r + 1) * length, :inner]
        values = key_value[r * length : (r + 1) * length, inner:]
        attended.append(
            attend(query[r * queries : (r + 1) * queries], keys, values, bias, heads)
        )
    attended = jnp.concatenate(attended, axis=0)
    result = asking + multiply(sigmoid(gate) * attended, final_ref[...])
    for b in range(n_branch):
        for g in range(per_part):
            for j in range(n_gj):
                start = g * residues + (b * n_gj + j) * few
                out_ref[(b * per_part + g) * n_gj + j] = jnp.concatenate(
                    [result[r * queries + start : r * queries + start + few] for r in range(rows)],
                    axis=0,
                )


def column_kernel(
    n_branch, n_gj, few, heads, me_ref, msa_ref, gains_ref, qkvg_ref, final_ref, expand_ref,
    shrink_ref, sides_ref, left_ref, right_ref, *rest
):
    count, width = msa_ref.shape
    inner = final_ref.shape[0]
    half = sides_ref.shape[0] // 2
    first = msa_ref[...]
    projected = multiply(layer_normalise(first, gains_ref[1:2, :]), qkvg_ref[...])
    query, key, value, gate = (projected[:, k * inner : (k + 1) * inner] for k in range(4))
    allowed = None
    if few > 1:
        shape = (heads * count, count)
        asks = lax.broadcasted_iota(jnp.int32, shape, 0)
        holds = lax.broadcasted_iota(jnp.int32, shape, 1)
        allowed = lax.rem(asks, few) == lax.rem(holds, few)
    attended = attend(query, key, value, None, heads, allowed)
    second = first + multiply(sigmoid(gate) * attended, final_ref[...])
    expanded = multiply(layer_normalise(second, gains_ref[2:3, :]), expand_ref[...])
    third = second + multiply(jnp.maximum(expanded, 0.0), shrink_ref[...])
    factors = multiply(sides_ref[...], layer_normalise(third, gains_ref[3:4, :]), across=True)
    left_ref[...] = factors[:half]
    for g in range(right_ref.shape[0]):
        right_ref[g] = factors[half:]
    chunks, slots = rest[:-1], rest[-1]
    per_part, each = slots.shape[1:3]
    for b in range(n_branch):
        for g in range(per_part):
            for j in range(n_gj):
                start = ((b * per_part + g) * n_gj + j) * each
                slots[b * n_gj + j, g] = third[start : start + each]
    for k, chunk in enumerate(chunks):
        chunk[...] = slots[me_ref[0] ^ k]


def alignment_kernel(n_cols, few, me_ref, *rest):
    blocks, (out_ref, slots) = rest[:n_cols], rest[n_cols:]
    spread(me_ref[0], blocks, slots)
    rows, residues, _ = out_ref.shape
    for r in range(rows):
        out_ref[r] = jnp.concatenate(
            [slots[c, r * few : (r + 1) * few] for c in range(n_cols)], axis=0
        )


def pair_kernel(
    few, n_gi, n_cols, me_ref, *rest
):
    left_refs, pair_refs = rest[:n_cols], rest[n_cols : 2 * n_cols]
    right_ref, gain_ref, matrix_ref, triangle_ref, tri_ref = rest[2 * n_cols : 2 * n_cols + 5]
    chunks = rest[2 * n_cols + 5 : 3 * n_cols + 5]
    left_ref, slots, pair_ref, first_ref, gate_ref = rest[3 * n_cols + 5 :]
    me = me_ref[0]
    groups_j = n_gi // n_cols
    spread(me, left_refs, left_ref)
    spread_rows(me, pair_refs, slots)
    _, wide, count = left_ref.shape
    block = pair_refs[0].shape[0]
    half = block // groups_j
    for c in range(n_cols):
        for o in range(groups_j):
            pair_ref[pl.ds(c * groups_j + o, half, stride=n_gi), :] = slots[
                pl.ds(c * block + o, half, stride=groups_j), :
            ]
    all_rows = count // few
    residues = n_cols * few
    pair_cols = n_gi * few
    per = lanes // pair_cols
    groups = residues // per
    width = pair_ref.shape[1]
    owner = lax.rem(lax.broadcasted_iota(jnp.int32, (1, count), 1), few)
    left = []
    for c in range(n_cols):
        here = left_ref[c]
        for f in range(few):
            own = jnp.where(owner == f, here, 0.0)
            total = own
            for other in range(few):
                if other != f:
                    total = total + pltpu.roll(own, (other - f) % count, 1)
            left.append(total)
    left = jnp.concatenate(left, axis=0) * (1.0 / all_rows)
    right = []
    for d in range(wide):
        here = right_ref[pl.ds(d, n_gi, stride=wide), :]
        right += [jnp.where(owner == f, here, 0.0) for f in range(few)]
    right = jnp.concatenate(right, axis=0)
    outer = multiply(left, right, across=True)
    outputs = []
    for g in range(groups):
        swapped = swap_lane_groups(
            [outer[(g * per + i) * wide : (g * per + i + 1) * wide] for i in range(per)]
        )
        stacked = [
            s[:, t * lanes : (t + 1) * lanes] for s in swapped for t in range(wide // per)
        ]
        outputs.append(jnp.concatenate(stacked, axis=0))
    update = multiply(matrix_ref[...], jnp.concatenate(outputs, axis=1))
    first = pair_ref[...].T + update
    projected = multiply(triangle_ref[...], layer_normalise(first, gain_ref[...], axis=0))
    tri = sigmoid(projected[2 * width : 4 * width]) * projected[: 2 * width]
    tri_ref[...] = tri.reshape(tri_ref.shape)
    first_ref[...] = first.T
    gate_ref[...] = sigmoid(projected[4 * width :]).T
    for k in range(n_cols):
        for o in range(groups_j):
            rows = pl.ds((me ^ k) * groups_j + o, half, stride=n_gi)
            chunks[k][pl.ds(o * half, half), :] = first_ref[rows, :]
            chunks[k][pl.ds(block + o * half, half), :] = gate_ref[rows, :]


def final_kernel(n_cols, few, residues, me_ref, product_ref, *rest):
    blocks, (gain_ref, matrix_ref, out_ref, slots, first_ref, gate_ref) = (
        rest[:n_cols],
        rest[n_cols:],
    )
    spread_rows(me_ref[0], blocks, slots)
    block = blocks[0].shape[0]
    pair_cols = product_ref.shape[1] // residues
    groups = pair_cols // (n_cols * few)
    for c in range(n_cols):
        for o in range(groups):
            for f in range(few):
                rows = pl.ds((o * n_cols + c) * few + f, residues, stride=pair_cols)
                start = c * block + o * residues * few + f
                first_ref[rows, :] = slots[pl.ds(start, residues, stride=few), :]
                start += block // 2
                gate_ref[rows, :] = slots[pl.ds(start, residues, stride=few), :]
    normal = layer_normalise(product_ref[...], gain_ref[...], axis=0)
    update = multiply(matrix_ref[...], normal)
    out_ref[...] = first_ref[...] + gate_ref[...] * update.T


def per_device(
    homolog_embedding,
    pair_input_tensor,
    layernorm_scales,
    pair_norm_gains,
    pair_bias_matrix,
    horizontal_qkvg_kernel,
    horizontal_final_kernel,
    vertical_qkvg_kernel,
    vertical_final_kernel,
    feedforward_expand_kernel,
    feedforward_shrink_kernel,
    dyadic_sides_kernel,
    outer_output_matrix,
    triangle_input_matrix,
    triangle_output_matrix,
):
    rows, residues, width = homolog_embedding.shape
    pair_cols, pair_width = pair_input_tensor.shape[1:]
    heads = pair_bias_matrix.shape[1]
    outer_width = dyadic_sides_kernel.shape[1] // 2
    n_branch, n_gi, n_gj = (lax.axis_size(name) for name in everyone)
    n_cols = n_branch * n_gj
    n_all = n_cols * n_gi
    length = residues * n_gi
    few = residues // n_cols
    groups = n_gi // n_cols
    parts = 2
    per_part = n_gi // parts
    own_rows = rows // per_part
    f32 = jnp.float32

    def call(kernel, outs, *operands, scratch=()):
        return pl.pallas_call(
            kernel,
            out_shape=[jax.ShapeDtypeStruct(shape, f32) for shape in outs],
            in_specs=[smem] + [vmem] * (len(operands) - 1),
            out_specs=[vmem] * len(outs),
            scratch_shapes=[pltpu.VMEM(shape, f32) for shape in scratch],
            compiler_params=params,
        )(*operands)

    def trade(blocks, axes):
        n = lax.axis_size(axes)
        return [blocks[0]] + [
            lax.ppermute(blocks[k], axes, [(t ^ k, t) for t in range(n) if t ^ k < n])
            for k in range(1, len(blocks))
        ]

    halves = [
        [
            (b * n_gi + part * per_part + g) * n_gj + j
            for b in range(n_branch)
            for g in range(per_part)
            for j in range(n_gj)
        ]
        for part in range(parts)
    ]
    n_half = n_cols * per_part
    mine = lax.axis_index("gi")
    me = jnp.stack([lax.axis_index(columns), mine % per_part, mine // per_part])
    me = me.astype(jnp.int32)
    positions = residues * pair_cols
    each = own_rows * few

    msa = lax.all_to_all(
        jnp.concatenate([homolog_embedding] * parts, axis=0), "gi", 0, 0, tiled=True
    )
    per = lanes // pair_cols
    bias_block = (heads // per, residues, lanes)
    bias, *pair = call(
        functools.partial(bias_kernel, few),
        [bias_block] + [(residues, groups * few, pair_width)] * n_cols,
        me,
        pair_input_tensor,
        pair_norm_gains,
        pair_bias_matrix.T,
        scratch=[(n_cols, residues, groups * few, pair_width)],
    )
    (bias,) = call(
        functools.partial(bias_rows_kernel, n_cols),
        [(heads, residues, length)],
        me,
        *trade([bias] * n_cols, columns),
        scratch=[(n_cols,) + bias_block],
    )
    bias = trade([bias] * per_part, "gi")
    pair = [block.reshape(-1, pair_width) for block in trade(pair, columns)]
    (msa_first,) = call(
        functools.partial(row_kernel, n_branch, n_gj, per_part, few),
        [(n_half, each, width)],
        me,
        msa,
        *bias,
        layernorm_scales,
        horizontal_qkvg_kernel,
        horizontal_final_kernel,
        scratch=[(per_part, heads, residues, length)],
    )

    msa_first = lax.all_to_all(msa_first, everyone, 0, 0, tiled=True, axis_index_groups=halves)
    count = n_half * each
    left, right, *alignment = call(
        functools.partial(column_kernel, n_branch, n_gj, few, heads),
        [(outer_width, count), (n_gi, outer_width, count)] + [(per_part, each, width)] * n_cols,
        me,
        msa_first.reshape(count, width),
        layernorm_scales,
        vertical_qkvg_kernel,
        vertical_final_kernel,
        feedforward_expand_kernel,
        feedforward_shrink_kernel,
        dyadic_sides_kernel.T,
        scratch=[(n_cols, per_part, each, width)],
    )
    right = lax.all_to_all(right, "gi", 0, 0, tiled=True)
    left = trade([left] * n_cols, columns)
    alignment = [block.reshape(-1, width) for block in trade(alignment, columns)]
    (alignment_output,) = call(
        functools.partial(alignment_kernel, n_cols, few),
        [(rows, residues, width)],
        me,
        *alignment,
        scratch=[(n_cols, rows * few, width)],
    )

    share = max(pair_width // n_all, 1)
    slots = pair_width // share
    triangle = triangle_input_matrix.T.reshape(5, slots, share, pair_width)
    sides = jnp.stack([triangle[0], triangle[2]], axis=1)
    gates = jnp.stack([triangle[1], triangle[3]], axis=1)
    triangle = jnp.concatenate(
        [side.reshape(2 * pair_width, pair_width) for side in (sides, gates)]
        + [triangle[4].reshape(pair_width, pair_width)],
        axis=0,
    )
    matrix = outer_output_matrix.reshape(outer_width, outer_width // per, per, pair_width)
    matrix = jnp.transpose(matrix, (3, 2, 1, 0)).reshape(pair_width, -1)
    tri, *first_gate = call(
        functools.partial(pair_kernel, few, n_gi, n_cols),
        [(slots, 2 * share, positions)]
        + [(2 * positions // n_cols, pair_width)] * n_cols,
        me,
        *left,
        *pair,
        right.reshape(n_gi * outer_width, count),
        pair_norm_gains[1][:, None],
        matrix,
        triangle,
        scratch=[
            (n_cols, outer_width, count),
            (positions, pair_width),
            (positions, pair_width),
            (positions, pair_width),
            (positions, pair_width),
        ],
    )

    if pair_width % n_all == 0:
        tri = lax.all_to_all(tri, everyone, 0, 0, tiled=True)
        tri = tri.reshape(n_branch, n_gi, n_gj, 2, share, residues, pair_cols)
        tri = jnp.transpose(tri, (3, 4, 1, 5, 0, 2, 6)).reshape(2, share, length, length)
        product = jnp.einsum("cik,cjk->cij", tri[0], tri[1], precision=precise)
        product = product.reshape(share, n_gi, residues, n_branch, n_gj, pair_cols)
        product = jnp.transpose(product, (3, 1, 4, 0, 2, 5)).reshape(
            n_all, share, positions
        )
        product = lax.all_to_all(product, everyone, 0, 0, tiled=True)
        product = product.reshape(pair_width, positions)
    else:
        tri = jnp.transpose(tri.reshape(slots, 2, share, positions), (1, 3, 0, 2))
        tri = tri.reshape(2, residues, pair_cols, pair_width)
        right_columns = lax.all_gather(tri[1], "gi", axis=0, tiled=True)
        product = lax.psum_scatter(
            jnp.einsum("jkc,ikc->jic", right_columns, tri[0], precision=precise),
            columns,
            scatter_dimension=0,
            tiled=True,
        )
        product = jnp.transpose(product, (2, 1, 0)).reshape(pair_width, positions)
    (pair_output_tensor,) = call(
        functools.partial(final_kernel, n_cols, few, residues),
        [(positions, pair_width)],
        me,
        product,
        *trade(first_gate, columns),
        pair_norm_gains[2][:, None],
        triangle_output_matrix.T,
        scratch=[
            (2 * positions, pair_width),
            (positions, pair_width),
            (positions, pair_width),
        ],
    )
    return (
        alignment_output,
        pair_output_tensor.reshape(residues, pair_cols, pair_width),
    )


def solution(mesh):
    tile, grid = P(("branch", "gj"), "gi", None), P("gi", ("branch", "gj"), None)
    return jax.shard_map(
        per_device,
        mesh=mesh,
        in_specs=(tile, grid) + (P(),) * 13,
        out_specs=(tile, grid),
        check_vma=False,
    )
```

```python
import functools
import math

import jax
import jax.numpy as jnp
from jax import lax
from jax.experimental import pallas as pl
from jax.experimental.pallas import tpu as pltpu
from jax.sharding import PartitionSpec as P

epsilon = 1e-05
precise = lax.Precision.HIGH
everyone = ("branch", "gi", "gj")
columns = ("branch", "gj")
lanes = 128
vmem = pl.BlockSpec(memory_space=pltpu.VMEM)
smem = pl.BlockSpec(memory_space=pltpu.SMEM)
params = pltpu.CompilerParams(vmem_limit_bytes=16 * 1024 * 1024)


def layer_normalise(values, norm_gain, axis=-1):
    average = jnp.mean(values, axis=axis, keepdims=True)
    centred = values - average
    variance = jnp.mean(centred * centred, axis=axis, keepdims=True)
    return centred * lax.rsqrt(variance + epsilon) * norm_gain


def apply_projection(values, weight):
    return jnp.einsum("...c,cd->...d", values, weight, precision=precise)


def sigmoid(values):
    return 1.0 / (1.0 + jnp.exp(-values))


def split(values):
    high = values.astype(jnp.bfloat16)
    return high, (values - high.astype(jnp.float32)).astype(jnp.bfloat16)


def multiply(left, right, across=False):
    numbers = (((1,), (1 if across else 0,)), ((), ()))

    def one(a, b):
        return lax.dot_general(a, b, numbers, preferred_element_type=jnp.float32)

    (lh, ll), (rh, rl) = split(left), split(right)
    return one(lh, rh) + (one(lh, rl) + one(ll, rh))


def swap_lane_groups(arrays):
    n, arrays = len(arrays), list(arrays)
    width = lanes // n
    wide = arrays[0].shape[-1]
    lane = lax.broadcasted_iota(jnp.int32, arrays[0].shape, arrays[0].ndim - 1)
    group = lax.rem(lane, lanes) // width
    axis = arrays[0].ndim - 1
    step = 1
    while step < n:
        upper = (group // step) % 2 == 1
        for low in range(n):
            if low & step:
                continue
            a, b = arrays[low], arrays[low + step]
            arrays[low] = jnp.where(upper, pltpu.roll(b, step * width, axis), a)
            arrays[low + step] = jnp.where(
                upper, b, pltpu.roll(a, wide - step * width, axis)
            )
        step *= 2
    return arrays


def head_masks(shape, heads):
    column = lax.broadcasted_iota(jnp.int32, shape, 1)
    return [column // (shape[1] // heads) == h for h in range(heads)]


def attend(query, key, value, bias, heads, allowed=None):
    count, inner = query.shape
    masks = head_masks((count, inner), heads)
    spread = jnp.concatenate([jnp.where(m, query, 0.0) for m in masks], axis=0)
    scores = multiply(spread, key, across=True) * (1.0 / math.sqrt(inner // heads))
    if bias is not None:
        scores = scores + bias
    if allowed is not None:
        scores = jnp.where(allowed, scores, -1e30)
    weights = jnp.exp(scores - jnp.max(scores, axis=-1, keepdims=True))
    weights = weights / jnp.sum(weights, axis=-1, keepdims=True)
    mixed = multiply(weights, value)
    result = jnp.where(masks[0], mixed[:count], 0.0)
    for h in range(1, heads):
        result = result + jnp.where(masks[h], mixed[h * count : (h + 1) * count], 0.0)
    return result


def spread(me, refs, slots):
    for k, ref in enumerate(refs):
        slots[me ^ k] = ref[...]


def spread_rows(me, refs, slots):
    for k, ref in enumerate(refs):
        count = ref.shape[0]
        slots[pl.ds(pl.multiple_of((me ^ k) * count, 8), count), :] = ref[...]


def bias_kernel(few, me_ref, msa_ref, pair_ref, gains_ref, matrix_ref, copies_ref, out_ref, *rest):
    chunks, slots = rest[:-1], rest[-1]
    rows = msa_ref.shape[0]
    for copy in range(copies_ref.shape[0] // rows):
        copies_ref[pl.ds(copy * rows, rows)] = msa_ref[...]
    residues, pair_cols, _ = pair_ref.shape
    heads = matrix_ref.shape[0]
    n_cols = len(chunks)
    groups = pair_cols // (n_cols * few)
    per = lanes // pair_cols
    normal = layer_normalise(pair_ref[...], gains_ref[0:1, :][None])
    for i in range(residues):
        here = multiply(matrix_ref[...], normal[i], across=True)
        for h in range(heads):
            out_ref[h // per, i : i + 1, pl.ds(h % per * pair_cols, pair_cols)] = here[h : h + 1]
    for c in range(n_cols):
        for o in range(groups):
            for f in range(few):
                start = (o * n_cols + c) * few + f
                slots[c, :, f * groups + o, :] = pair_ref[:, start, :]
    for k in range(n_cols):
        chunks[k][...] = slots[me_ref[0] ^ k]


def bias_rows_kernel(n_cols, me_ref, *rest):
    blocks, (out_ref, slots) = rest[:n_cols], rest[n_cols:]
    spread(me_ref[0], blocks, slots)
    count = slots.shape[1]
    per = out_ref.shape[0] // count
    for block in range(count):
        tiles = [[] for _ in range(per)]
        for tile in range(n_cols // per):
            group = [slots[c, block] for c in range(tile * per, (tile + 1) * per)]
            for k, piece in enumerate(swap_lane_groups(group)):
                tiles[k].append(piece)
        for k in range(per):
            out_ref[block * per + k] = jnp.concatenate(tiles[k], axis=1)


def row_kernel(n_branch, n_gj, per_part, few, me_ref, msa_ref, *rest):
    bias_refs, (gains_ref, qkvg_ref, final_ref, out_ref, slots) = (
        rest[:per_part],
        rest[per_part:],
    )
    _, residues, width = msa_ref.shape
    heads, _, length = bias_refs[0].shape
    n_gi = length // residues
    rows = msa_ref.shape[0] // n_gi
    inner = final_ref.shape[0]
    queries = per_part * residues
    gain = gains_ref[0:1, :]
    spread(me_ref[1], bias_refs, slots)
    bias = jnp.concatenate(
        [slots[g, h] for h in range(heads) for g in range(per_part)], axis=0
    )
    tokens = jnp.concatenate(
        [msa_ref[g * rows + r] for r in range(rows) for g in range(n_gi)], axis=0
    )
    first = me_ref[2] * (per_part * rows)
    asking = msa_ref[pl.ds(first, per_part * rows)]
    asking = jnp.concatenate(
        [asking[g * rows + r] for r in range(rows) for g in range(per_part)], axis=0
    )
    key_value = multiply(layer_normalise(tokens, gain), qkvg_ref[:, inner : 3 * inner])
    normal = layer_normalise(asking, gain)
    query = multiply(normal, qkvg_ref[:, :inner])
    gate = multiply(normal, qkvg_ref[:, 3 * inner :])
    attended = []
    for r in range(rows):
        keys = key_value[r * length : (r + 1) * length, :inner]
        values = key_value[r * length : (r + 1) * length, inner:]
        attended.append(
            attend(query[r * queries : (r + 1) * queries], keys, values, bias, heads)
        )
    attended = jnp.concatenate(attended, axis=0)
    result = asking + multiply(sigmoid(gate) * attended, final_ref[...])
    for b in range(n_branch):
        for g in range(per_part):
            for j in range(n_gj):
                start = g * residues + (b * n_gj + j) * few
                out_ref[(b * per_part + g) * n_gj + j] = jnp.concatenate(
                    [result[r * queries + start : r * queries + start + few] for r in range(rows)],
                    axis=0,
                )


def column_kernel(
    n_branch, n_gj, few, heads, me_ref, msa_ref, gains_ref, qkvg_ref, final_ref, expand_ref,
    shrink_ref, sides_ref, left_ref, right_ref, *rest
):
    count, width = msa_ref.shape
    inner = final_ref.shape[0]
    half = sides_ref.shape[0] // 2
    first = msa_ref[...]
    projected = multiply(layer_normalise(first, gains_ref[1:2, :]), qkvg_ref[...])
    query, key, value, gate = (projected[:, k * inner : (k + 1) * inner] for k in range(4))
    allowed = None
    if few > 1:
        shape = (heads * count, count)
        asks = lax.broadcasted_iota(jnp.int32, shape, 0)
        holds = lax.broadcasted_iota(jnp.int32, shape, 1)
        allowed = lax.rem(asks, few) == lax.rem(holds, few)
    attended = attend(query, key, value, None, heads, allowed)
    second = first + multiply(sigmoid(gate) * attended, final_ref[...])
    expanded = multiply(layer_normalise(second, gains_ref[2:3, :]), expand_ref[...])
    third = second + multiply(jnp.maximum(expanded, 0.0), shrink_ref[...])
    factors = multiply(sides_ref[...], layer_normalise(third, gains_ref[3:4, :]), across=True)
    left_ref[...] = factors[:half]
    for g in range(right_ref.shape[0]):
        right_ref[g] = factors[half:]
    chunks, slots = rest[:-1], rest[-1]
    per_part, each = slots.shape[1:3]
    for b in range(n_branch):
        for g in range(per_part):
            for j in range(n_gj):
                start = ((b * per_part + g) * n_gj + j) * each
                slots[b * n_gj + j, g] = third[start : start + each]
    for k, chunk in enumerate(chunks):
        chunk[...] = slots[me_ref[0] ^ k]


def gather_tiles(few, me, alignment_refs, pair_refs, msa_out, pair_out, msa_slots, slots):
    n_cols = len(alignment_refs)
    spread(me, alignment_refs, msa_slots)
    for r in range(msa_out.shape[0]):
        msa_out[r] = jnp.concatenate(
            [msa_slots[c, r * few : (r + 1) * few] for c in range(n_cols)], axis=0
        )
    spread_rows(me, pair_refs, slots)
    block = pair_refs[0].shape[0]
    positions = n_cols * block // 2
    residues = msa_out.shape[1]
    groups = positions // (residues * few * n_cols)
    count = residues * few
    for c in range(n_cols):
        for part in range(2):
            for o in range(groups):
                start = part * positions + o * n_cols + c
                pair_out[pl.ds(start, count, stride=groups * n_cols), :] = slots[
                    pl.ds(c * block + (part * groups + o) * count, count), :
                ]


def gather_kernel(few, n_cols, me_ref, *rest):
    gather_tiles(few, me_ref[0], rest[:n_cols], rest[n_cols : 2 * n_cols], *rest[2 * n_cols :])


def triangle_kernel(few, n_cols, me_ref, tri_ref, *rest):
    blocks, (out_ref, msa_out, pair_out, product_ref, msa_slots, slots) = (
        rest[: 2 * n_cols],
        rest[2 * n_cols :],
    )
    gather_tiles(
        few, me_ref[0], blocks[:n_cols], blocks[n_cols:], msa_out, pair_out, msa_slots, slots
    )
    n_all, rows, _ = out_ref.shape
    n_gi = n_all // n_cols
    share = few
    tiles = rows // few
    each = 2 * share
    wide = lanes // few
    group = lax.broadcasted_iota(jnp.int32, (n_gi * tiles, lanes), 1) // wide
    products = []
    for q in range(share):
        left, right = [], []
        for c in range(n_cols):
            base = c * n_gi * tiles * each
            here = jnp.concatenate(
                [
                    tri_ref[pl.ds(base + t * each + q, n_gi, stride=tiles * each), :]
                    for t in range(tiles)
                ],
                axis=0,
            )
            left.append(
                jnp.concatenate(
                    [jnp.where(group == i, here, 0.0) for i in range(few)], axis=0
                )
            )
            here = tri_ref[pl.ds(base + share + q, n_gi * tiles, stride=each), :]
            rolled = [here] + [pltpu.roll(here, k * wide, 1) for k in range(1, few)]
            copies = []
            for j in range(few):
                copy = rolled[0]
                for k in range(1, few):
                    copy = jnp.where(group == (j + k) % few, rolled[k], copy)
                copies.append(copy)
            step = n_gi * tiles // n_cols
            right.append(
                jnp.concatenate(
                    [copy[k * step : (k + 1) * step] for k in range(n_cols) for copy in copies],
                    axis=0,
                )
            )
        products.append(
            multiply(
                jnp.concatenate(left, axis=1), jnp.concatenate(right, axis=1), across=True
            )
        )
    for c, product in enumerate(swap_lane_groups(products)):
        product_ref[...] = product
        for g in range(n_gi):
            out_ref[c * n_gi + g] = product_ref[pl.ds(g, rows, stride=n_gi), :]


def pair_kernel(
    few, n_gi, n_cols, me_ref, *rest
):
    left_refs, pair_refs = rest[:n_cols], rest[n_cols : 2 * n_cols]
    right_ref, gain_ref, matrix_ref, triangle_ref, tri_ref = rest[2 * n_cols : 2 * n_cols + 5]
    chunks = rest[2 * n_cols + 5 : 3 * n_cols + 5]
    left_ref, slots, pair_ref, first_ref, gate_ref = rest[3 * n_cols + 5 :]
    me = me_ref[0]
    groups_j = n_gi // n_cols
    spread(me, left_refs, left_ref)
    spread_rows(me, pair_refs, slots)
    _, wide, count = left_ref.shape
    block = pair_refs[0].shape[0]
    half = block // groups_j
    for c in range(n_cols):
        for o in range(groups_j):
            pair_ref[pl.ds(c * groups_j + o, half, stride=n_gi), :] = slots[
                pl.ds(c * block + o, half, stride=groups_j), :
            ]
    all_rows = count // few
    residues = n_cols * few
    pair_cols = n_gi * few
    per = lanes // pair_cols
    groups = residues // per
    width = pair_ref.shape[1]
    owner = lax.rem(lax.broadcasted_iota(jnp.int32, (1, count), 1), few)
    left = []
    for c in range(n_cols):
        here = left_ref[c]
        for f in range(few):
            own = jnp.where(owner == f, here, 0.0)
            total = own
            for other in range(few):
                if other != f:
                    total = total + pltpu.roll(own, (other - f) % count, 1)
            left.append(total)
    left = jnp.concatenate(left, axis=0) * (1.0 / all_rows)
    right = []
    for d in range(wide):
        here = right_ref[pl.ds(d, n_gi, stride=wide), :]
        right += [jnp.where(owner == f, here, 0.0) for f in range(few)]
    right = jnp.concatenate(right, axis=0)
    outer = multiply(left, right, across=True)
    outputs = []
    for g in range(groups):
        swapped = swap_lane_groups(
            [outer[(g * per + i) * wide : (g * per + i + 1) * wide] for i in range(per)]
        )
        stacked = [
            s[:, t * lanes : (t + 1) * lanes] for s in swapped for t in range(wide // per)
        ]
        outputs.append(jnp.concatenate(stacked, axis=0))
    update = multiply(matrix_ref[...], jnp.concatenate(outputs, axis=1))
    first = pair_ref[...].T + update
    projected = multiply(triangle_ref[...], layer_normalise(first, gain_ref[...], axis=0))
    tri = sigmoid(projected[2 * width : 4 * width]) * projected[: 2 * width]
    slot_count, _, each, _ = tri_ref.shape
    for g in range(groups):
        tri_ref[:, g] = tri[:, g * lanes : (g + 1) * lanes].reshape(slot_count, each, lanes)
    first_ref[...] = first.T
    gate_ref[...] = sigmoid(projected[4 * width :]).T
    for k in range(n_cols):
        for o in range(groups_j):
            rows = pl.ds((me ^ k) * groups_j + o, half, stride=n_gi)
            chunks[k][pl.ds(o * half, half), :] = first_ref[rows, :]
            chunks[k][pl.ds(block + o * half, half), :] = gate_ref[rows, :]


def final_kernel(few, n_cols, residues, packed, product_ref, pair_ref, gain_ref, matrix_ref, out_ref):
    positions = out_ref.shape[0]
    if packed:
        tiles = residues // few
        tall = product_ref.shape[0] // residues
        product = []
        for t in range(tiles):
            here = [
                product_ref[pl.ds(i * tiles + t, tall, stride=residues), :] for i in range(few)
            ]
            product.append(jnp.concatenate(swap_lane_groups(here), axis=0))
        product = jnp.concatenate(product, axis=1)
    else:
        product = product_ref[...]
    update = multiply(matrix_ref[...], layer_normalise(product, gain_ref[...], axis=0))
    result = pair_ref[pl.ds(0, positions), :] + pair_ref[pl.ds(positions, positions), :] * update.T
    count = positions // (residues * few)
    for i in range(residues):
        for f in range(few):
            start = (i * few + f) * count
            out_ref[pl.ds(i * few * count + f, count, stride=few), :] = result[
                start : start + count
            ]


def per_device(
    homolog_embedding,
    pair_input_tensor,
    layernorm_scales,
    pair_norm_gains,
    pair_bias_matrix,
    horizontal_qkvg_kernel,
    horizontal_final_kernel,
    vertical_qkvg_kernel,
    vertical_final_kernel,
    feedforward_expand_kernel,
    feedforward_shrink_kernel,
    dyadic_sides_kernel,
    outer_output_matrix,
    triangle_input_matrix,
    triangle_output_matrix,
):
    rows, residues, width = homolog_embedding.shape
    pair_cols, pair_width = pair_input_tensor.shape[1:]
    heads = pair_bias_matrix.shape[1]
    outer_width = dyadic_sides_kernel.shape[1] // 2
    n_branch, n_gi, n_gj = (lax.axis_size(name) for name in everyone)
    n_cols = n_branch * n_gj
    n_all = n_cols * n_gi
    length = residues * n_gi
    few = residues // n_cols
    groups = n_gi // n_cols
    parts = 2
    per_part = n_gi // parts
    own_rows = rows // per_part
    f32 = jnp.float32

    def call(kernel, outs, *operands, scratch=()):
        return pl.pallas_call(
            kernel,
            out_shape=[jax.ShapeDtypeStruct(shape, f32) for shape in outs],
            in_specs=[smem] + [vmem] * (len(operands) - 1),
            out_specs=[vmem] * len(outs),
            scratch_shapes=[pltpu.VMEM(shape, f32) for shape in scratch],
            compiler_params=params,
        )(*operands)

    def trade(blocks, axes):
        n = lax.axis_size(axes)
        return [blocks[0]] + [
            lax.ppermute(blocks[k], axes, [(t ^ k, t) for t in range(n) if t ^ k < n])
            for k in range(1, len(blocks))
        ]

    halves = [
        [
            (b * n_gi + part * per_part + g) * n_gj + j
            for b in range(n_branch)
            for g in range(per_part)
            for j in range(n_gj)
        ]
        for part in range(parts)
    ]
    n_half = n_cols * per_part
    mine = lax.axis_index("gi")
    me = jnp.stack([lax.axis_index(columns), mine % per_part, mine // per_part])
    me = me.astype(jnp.int32)
    positions = residues * pair_cols
    each = own_rows * few

    per = lanes // pair_cols
    bias_block = (heads // per, residues, lanes)
    msa, bias, *pair = call(
        functools.partial(bias_kernel, few),
        [(parts * rows, residues, width), bias_block]
        + [(residues, groups * few, pair_width)] * n_cols,
        me,
        homolog_embedding,
        pair_input_tensor,
        pair_norm_gains,
        pair_bias_matrix.T,
        scratch=[(n_cols, residues, groups * few, pair_width)],
    )
    msa = lax.all_to_all(msa, "gi", 0, 0, tiled=True)
    (bias,) = call(
        functools.partial(bias_rows_kernel, n_cols),
        [(heads, residues, length)],
        me,
        *trade([bias] * n_cols, columns),
        scratch=[(n_cols,) + bias_block],
    )
    bias = trade([bias] * per_part, "gi")
    pair = [block.reshape(-1, pair_width) for block in trade(pair, columns)]
    (msa_first,) = call(
        functools.partial(row_kernel, n_branch, n_gj, per_part, few),
        [(n_half, each, width)],
        me,
        msa,
        *bias,
        layernorm_scales,
        horizontal_qkvg_kernel,
        horizontal_final_kernel,
        scratch=[(per_part, heads, residues, length)],
    )

    msa_first = lax.all_to_all(msa_first, everyone, 0, 0, tiled=True, axis_index_groups=halves)
    count = n_half * each
    left, right, *alignment = call(
        functools.partial(column_kernel, n_branch, n_gj, few, heads),
        [(outer_width, count), (n_gi, outer_width, count)] + [(per_part, each, width)] * n_cols,
        me,
        msa_first.reshape(count, width),
        layernorm_scales,
        vertical_qkvg_kernel,
        vertical_final_kernel,
        feedforward_expand_kernel,
        feedforward_shrink_kernel,
        dyadic_sides_kernel.T,
        scratch=[(n_cols, per_part, each, width)],
    )
    right = lax.all_to_all(right, "gi", 0, 0, tiled=True)
    left = trade([left] * n_cols, columns)
    alignment = [block.reshape(-1, width) for block in trade(alignment, columns)]
    share = max(pair_width // n_all, 1)
    slots = pair_width // share
    triangle = triangle_input_matrix.T.reshape(5, slots, share, pair_width)
    sides = jnp.stack([triangle[0], triangle[2]], axis=1)
    gates = jnp.stack([triangle[1], triangle[3]], axis=1)
    triangle = jnp.concatenate(
        [side.reshape(2 * pair_width, pair_width) for side in (sides, gates)]
        + [triangle[4].reshape(pair_width, pair_width)],
        axis=0,
    )
    matrix = outer_output_matrix.reshape(outer_width, outer_width // per, per, pair_width)
    matrix = jnp.transpose(matrix, (3, 2, 1, 0)).reshape(pair_width, -1)
    tri, *first_gate = call(
        functools.partial(pair_kernel, few, n_gi, n_cols),
        [(slots, positions // lanes, 2 * share, lanes)]
        + [(2 * positions // n_cols, pair_width)] * n_cols,
        me,
        *left,
        *pair,
        right.reshape(n_gi * outer_width, count),
        pair_norm_gains[1][:, None],
        matrix,
        triangle,
        scratch=[
            (n_cols, outer_width, count),
            (positions, pair_width),
            (positions, pair_width),
            (positions, pair_width),
            (positions, pair_width),
        ],
    )

    first_gate = trade(first_gate, columns)
    tiles = [(rows, residues, width), (2 * positions, pair_width)]
    scratch = [(n_cols, rows * few, width), (2 * positions, pair_width)]
    packed = share * n_all == pair_width and share == few and few == per
    gain, last = pair_norm_gains[2], triangle_output_matrix
    if packed:
        order = [[(c // n_gj * n_gi + g) * n_gj + c % n_gj for c in range(n_cols) for g in range(n_gi)]]
        tri = lax.all_to_all(tri, everyone, 0, 0, tiled=True, axis_index_groups=order)
        product, alignment_output, first_gate = call(
            functools.partial(triangle_kernel, few, n_cols),
            [(n_all, residues, lanes)] + tiles,
            me,
            tri.reshape(-1, lanes),
            *alignment,
            *first_gate,
            scratch=[(lanes, lanes)] + scratch,
        )
        product = lax.all_to_all(product, everyone, 0, 0, tiled=True, axis_index_groups=order)
        product = product.reshape(n_all * residues, lanes)
        gain = gain.reshape(n_all, share).T.reshape(-1)
        last = jnp.swapaxes(last.reshape(n_all, share, pair_width), 0, 1).reshape(last.shape)
    else:
        alignment_output, first_gate = call(
            functools.partial(gather_kernel, few, n_cols),
            tiles,
            me,
            *alignment,
            *first_gate,
            scratch=scratch,
        )
        tri = jnp.transpose(tri.reshape(slots, -1, 2, share, lanes), (2, 1, 4, 0, 3))
        tri = tri.reshape(2, residues, pair_cols, pair_width)
        right_columns = lax.all_gather(tri[1], "gi", axis=0, tiled=True)
        product = lax.psum_scatter(
            jnp.einsum("jkc,ikc->jic", right_columns, tri[0], precision=precise),
            columns,
            scatter_dimension=0,
            tiled=True,
        ).reshape(groups, n_cols, few, residues, pair_width)
        product = jnp.transpose(product, (4, 3, 2, 0, 1)).reshape(pair_width, positions)
    (pair_output_tensor,) = pl.pallas_call(
        functools.partial(final_kernel, few, n_cols, residues, packed),
        out_shape=[jax.ShapeDtypeStruct((positions, pair_width), f32)],
        in_specs=[vmem] * 4,
        out_specs=[vmem],
        compiler_params=params,
    )(product, first_gate, gain[:, None], last.T)
    return (
        alignment_output,
        pair_output_tensor.reshape(residues, pair_cols, pair_width),
    )


def solution(mesh):
    tile, grid = P(("branch", "gj"), "gi", None), P("gi", ("branch", "gj"), None)
    return jax.shard_map(
        per_device,
        mesh=mesh,
        in_specs=(tile, grid) + (P(),) * 13,
        out_specs=(tile, grid),
        check_vma=False,
    )
```

```python
import functools
import math

import jax
import jax.numpy as jnp
from jax import lax
from jax.experimental import pallas as pl
from jax.experimental.pallas import tpu as pltpu
from jax.sharding import PartitionSpec as P

epsilon = 1e-05
precise = lax.Precision.HIGH
everyone = ("branch", "gi", "gj")
columns = ("branch", "gj")
lanes = 128
vmem = pl.BlockSpec(memory_space=pltpu.VMEM)
smem = pl.BlockSpec(memory_space=pltpu.SMEM)
hbm = pl.BlockSpec(memory_space=pltpu.HBM)
params = pltpu.CompilerParams(vmem_limit_bytes=16 * 1024 * 1024)


def layer_normalise(values, norm_gain, axis=-1):
    average = jnp.mean(values, axis=axis, keepdims=True)
    centred = values - average
    variance = jnp.mean(centred * centred, axis=axis, keepdims=True)
    return centred * lax.rsqrt(variance + epsilon) * norm_gain


def apply_projection(values, weight):
    return jnp.einsum("...c,cd->...d", values, weight, precision=precise)


def sigmoid(values):
    return 1.0 / (1.0 + jnp.exp(-values))


def split(values):
    high = values.astype(jnp.bfloat16)
    return high, (values - high.astype(jnp.float32)).astype(jnp.bfloat16)


def multiply(left, right, across=False):
    numbers = (((1,), (1 if across else 0,)), ((), ()))

    def one(a, b):
        return lax.dot_general(a, b, numbers, preferred_element_type=jnp.float32)

    (lh, ll), (rh, rl) = split(left), split(right)
    return one(lh, rh) + (one(lh, rl) + one(ll, rh))


def swap_lane_groups(arrays):
    n, arrays = len(arrays), list(arrays)
    width = lanes // n
    wide = arrays[0].shape[-1]
    lane = lax.broadcasted_iota(jnp.int32, arrays[0].shape, arrays[0].ndim - 1)
    group = lax.rem(lane, lanes) // width
    axis = arrays[0].ndim - 1
    step = 1
    while step < n:
        upper = (group // step) % 2 == 1
        for low in range(n):
            if low & step:
                continue
            a, b = arrays[low], arrays[low + step]
            arrays[low] = jnp.where(upper, pltpu.roll(b, step * width, axis), a)
            arrays[low + step] = jnp.where(
                upper, b, pltpu.roll(a, wide - step * width, axis)
            )
        step *= 2
    return arrays


def head_masks(shape, heads):
    column = lax.broadcasted_iota(jnp.int32, shape, 1)
    return [column // (shape[1] // heads) == h for h in range(heads)]


def attend(query, key, value, bias, heads, allowed=None):
    count, inner = query.shape
    masks = head_masks((count, inner), heads)
    spread = jnp.concatenate([jnp.where(m, query, 0.0) for m in masks], axis=0)
    scores = multiply(spread, key, across=True) * (1.0 / math.sqrt(inner // heads))
    if bias is not None:
        scores = scores + bias
    if allowed is not None:
        scores = jnp.where(allowed, scores, -1e30)
    weights = jnp.exp(scores - jnp.max(scores, axis=-1, keepdims=True))
    weights = weights / jnp.sum(weights, axis=-1, keepdims=True)
    mixed = multiply(weights, value)
    result = jnp.where(masks[0], mixed[:count], 0.0)
    for h in range(1, heads):
        result = result + jnp.where(masks[h], mixed[h * count : (h + 1) * count], 0.0)
    return result


def start_copies(pairs, sems):
    copies = [pltpu.make_async_copy(a, b, sems.at[n]) for n, (a, b) in enumerate(pairs)]
    for copy in copies:
        copy.start()
    return copies


def wait_all(copies):
    for copy in copies:
        copy.wait()


def spread(me, refs, slots):
    for k, ref in enumerate(refs):
        slots[me ^ k] = ref[...]


def spread_rows(me, refs, slots):
    for k, ref in enumerate(refs):
        count = ref.shape[0]
        slots[pl.ds(pl.multiple_of((me ^ k) * count, 8), count), :] = ref[...]


def bias_kernel(
    msa_far, pair_far, gains_far, matrix_far, copies_far, out_ref, pair_ref, gains_ref, matrix_ref, sems
):
    rows = msa_far.shape[0]
    repeats = copies_far.shape[0] // rows
    copies = start_copies(
        [(gains_far, gains_ref), (matrix_far, matrix_ref), (pair_far, pair_ref)]
        + [(msa_far, copies_far.at[pl.ds(n * rows, rows)]) for n in range(repeats)],
        sems,
    )
    residues, pair_cols, _ = pair_ref.shape
    heads = matrix_ref.shape[0]
    per = lanes // pair_cols
    wait_all(copies[:3])
    normal = layer_normalise(pair_ref[...], gains_ref[0:1, :][None])
    for i in range(residues):
        here = multiply(matrix_ref[...], normal[i], across=True)
        for h in range(heads):
            out_ref[h // per, i : i + 1, pl.ds(h % per * pair_cols, pair_cols)] = here[h : h + 1]
    wait_all(copies[3:])


def pair_blocks_kernel(few, residues, me_ref, pair_ref, *rest):
    chunks, slots = rest[:-1], rest[-1]
    n_cols = len(chunks)
    block = chunks[0].shape[0]
    groups = block // (residues * few)
    for c in range(n_cols):
        for o in range(groups):
            for f in range(few):
                source = pl.ds((o * n_cols + c) * few + f, residues, stride=groups * n_cols * few)
                target = pl.ds(c * block + f * groups + o, residues, stride=few * groups)
                slots[target, :] = pair_ref[source, :]
    for k in range(n_cols):
        start = pl.multiple_of((me_ref[0] ^ k) * block, 8)
        chunks[k][...] = slots[pl.ds(start, block), :]


def bias_rows_kernel(n_cols, me_ref, *rest):
    blocks, (out_ref, slots) = rest[:n_cols], rest[n_cols:]
    spread(me_ref[0], blocks, slots)
    count = slots.shape[1]
    per = out_ref.shape[0] // count
    for block in range(count):
        tiles = [[] for _ in range(per)]
        for tile in range(n_cols // per):
            group = [slots[c, block] for c in range(tile * per, (tile + 1) * per)]
            for k, piece in enumerate(swap_lane_groups(group)):
                tiles[k].append(piece)
        for k in range(per):
            out_ref[block * per + k] = jnp.concatenate(tiles[k], axis=1)


def row_kernel(n_branch, n_gj, per_part, few, me_ref, msa_ref, *rest):
    bias_refs, rest = rest[:per_part], rest[per_part:]
    gains_far, qkvg_far, final_far, out_ref, slots, gains_ref, qkvg_ref, final_ref, sems = rest
    copies = start_copies(
        [(gains_far, gains_ref), (qkvg_far, qkvg_ref), (final_far, final_ref)]
        + [(ref, slots.at[me_ref[1] ^ k]) for k, ref in enumerate(bias_refs)],
        sems,
    )
    _, residues, width = msa_ref.shape
    _, heads, _, length = slots.shape
    n_gi = length // residues
    rows = msa_ref.shape[0] // n_gi
    inner = final_ref.shape[0]
    queries = per_part * residues
    tokens = jnp.concatenate(
        [msa_ref[g * rows + r] for r in range(rows) for g in range(n_gi)], axis=0
    )
    first = me_ref[2] * (per_part * rows)
    asking = msa_ref[pl.ds(first, per_part * rows)]
    asking = jnp.concatenate(
        [asking[g * rows + r] for r in range(rows) for g in range(per_part)], axis=0
    )
    tokens = layer_normalise(tokens, 1.0)
    normal = layer_normalise(asking, 1.0)
    wait_all(copies[:2])
    gain = gains_ref[0:1, :]
    key_value = multiply(tokens * gain, qkvg_ref[:, inner : 3 * inner])
    normal = normal * gain
    query = multiply(normal, qkvg_ref[:, :inner])
    gate = multiply(normal, qkvg_ref[:, 3 * inner :])
    wait_all(copies[2:])
    bias = jnp.concatenate(
        [slots[g, h] for h in range(heads) for g in range(per_part)], axis=0
    )
    attended = []
    for r in range(rows):
        keys = key_value[r * length : (r + 1) * length, :inner]
        values = key_value[r * length : (r + 1) * length, inner:]
        attended.append(
            attend(query[r * queries : (r + 1) * queries], keys, values, bias, heads)
        )
    attended = jnp.concatenate(attended, axis=0)
    result = asking + multiply(sigmoid(gate) * attended, final_ref[...])
    for b in range(n_branch):
        for g in range(per_part):
            for j in range(n_gj):
                start = g * residues + (b * n_gj + j) * few
                out_ref[(b * per_part + g) * n_gj + j] = jnp.concatenate(
                    [result[r * queries + start : r * queries + start + few] for r in range(rows)],
                    axis=0,
                )


def column_kernel(n_branch, n_gj, few, heads, me_ref, msa_ref, *rest):
    n_cols = n_branch * n_gj
    far, rest = rest[:6], rest[6:]
    left_far, right_far, chunks, rest = rest[0], rest[1], rest[2 : 2 + n_cols], rest[2 + n_cols :]
    gains_ref, qkvg_ref, final_ref, expand_ref, shrink_ref, sides_ref = rest[:6]
    slots, factors_ref, sems, out_sems = rest[6:]
    copies = start_copies(list(zip(far, rest[:6])), sems)
    count, width = msa_ref.shape
    inner = final_ref.shape[0]
    half = sides_ref.shape[0] // 2
    first = msa_ref[...]
    normal = layer_normalise(first, 1.0)
    wait_all(copies[:2])
    projected = multiply(normal * gains_ref[1:2, :], qkvg_ref[...])
    query, key, value, gate = (projected[:, k * inner : (k + 1) * inner] for k in range(4))
    allowed = None
    if few > 1:
        shape = (heads * count, count)
        asks = lax.broadcasted_iota(jnp.int32, shape, 0)
        holds = lax.broadcasted_iota(jnp.int32, shape, 1)
        allowed = lax.rem(asks, few) == lax.rem(holds, few)
    attended = attend(query, key, value, None, heads, allowed)
    wait_all(copies[2:])
    second = first + multiply(sigmoid(gate) * attended, final_ref[...])
    expanded = multiply(layer_normalise(second, gains_ref[2:3, :]), expand_ref[...])
    third = second + multiply(jnp.maximum(expanded, 0.0), shrink_ref[...])
    factors_ref[...] = multiply(
        sides_ref[...], layer_normalise(third, gains_ref[3:4, :]), across=True
    )
    pairs = [(factors_ref.at[pl.ds(0, half)], left_far)]
    for g in range(right_far.shape[0]):
        pairs.append((factors_ref.at[pl.ds(half, half)], right_far.at[g]))
    copies = start_copies(pairs, out_sems)
    per_part, each = slots.shape[1:3]
    for b in range(n_branch):
        for g in range(per_part):
            for j in range(n_gj):
                start = ((b * per_part + g) * n_gj + j) * each
                slots[b * n_gj + j, g] = third[start : start + each]
    for k, chunk in enumerate(chunks):
        chunk[...] = slots[me_ref[0] ^ k]
    wait_all(copies)


def gather_tiles(few, me, alignment_refs, pair_refs, msa_out, pair_out, msa_slots, slots):
    n_cols = len(alignment_refs)
    spread(me, alignment_refs, msa_slots)
    for r in range(msa_out.shape[0]):
        msa_out[r] = jnp.concatenate(
            [msa_slots[c, r * few : (r + 1) * few] for c in range(n_cols)], axis=0
        )
    spread_rows(me, pair_refs, slots)
    block = pair_refs[0].shape[0]
    positions = n_cols * block // 2
    residues = msa_out.shape[1]
    groups = positions // (residues * few * n_cols)
    count = residues * few
    for c in range(n_cols):
        for part in range(2):
            for o in range(groups):
                start = part * positions + o * n_cols + c
                pair_out[pl.ds(start, count, stride=groups * n_cols), :] = slots[
                    pl.ds(c * block + (part * groups + o) * count, count), :
                ]


def gather_kernel(few, n_cols, me_ref, *rest):
    gather_tiles(few, me_ref[0], rest[:n_cols], rest[n_cols : 2 * n_cols], *rest[2 * n_cols :])


def triangle_kernel(few, n_cols, me_ref, tri_ref, *rest):
    blocks, (out_ref, msa_out, pair_out, product_ref, msa_slots, slots) = (
        rest[: 2 * n_cols],
        rest[2 * n_cols :],
    )
    gather_tiles(
        few, me_ref[0], blocks[:n_cols], blocks[n_cols:], msa_out, pair_out, msa_slots, slots
    )
    n_all, rows, _ = out_ref.shape
    n_gi = n_all // n_cols
    share = few
    tiles = rows // few
    each = 2 * share
    wide = lanes // few
    group = lax.broadcasted_iota(jnp.int32, (n_gi * tiles, lanes), 1) // wide
    products = []
    for q in range(share):
        left, right = [], []
        for c in range(n_cols):
            base = c * n_gi * tiles * each
            here = jnp.concatenate(
                [
                    tri_ref[pl.ds(base + t * each + q, n_gi, stride=tiles * each), :]
                    for t in range(tiles)
                ],
                axis=0,
            )
            left.append(
                jnp.concatenate(
                    [jnp.where(group == i, here, 0.0) for i in range(few)], axis=0
                )
            )
            here = tri_ref[pl.ds(base + share + q, n_gi * tiles, stride=each), :]
            rolled = [here] + [pltpu.roll(here, k * wide, 1) for k in range(1, few)]
            copies = []
            for j in range(few):
                copy = rolled[0]
                for k in range(1, few):
                    copy = jnp.where(group == (j + k) % few, rolled[k], copy)
                copies.append(copy)
            step = n_gi * tiles // n_cols
            right.append(
                jnp.concatenate(
                    [copy[k * step : (k + 1) * step] for k in range(n_cols) for copy in copies],
                    axis=0,
                )
            )
        products.append(
            multiply(
                jnp.concatenate(left, axis=1), jnp.concatenate(right, axis=1), across=True
            )
        )
    for c, product in enumerate(swap_lane_groups(products)):
        product_ref[...] = product
        for g in range(n_gi):
            out_ref[c * n_gi + g] = product_ref[pl.ds(g, rows, stride=n_gi), :]


def pair_kernel(
    few, n_gi, n_cols, me_ref, *rest
):
    left_refs, pair_refs = rest[:n_cols], rest[n_cols : 2 * n_cols]
    right_ref, gain_ref, matrix_ref, triangle_ref, tri_ref = rest[2 * n_cols : 2 * n_cols + 5]
    matrix_far, triangle_far = matrix_ref, triangle_ref
    chunks = rest[2 * n_cols + 5 : 3 * n_cols + 5]
    rest = rest[3 * n_cols + 5 :]
    left_ref, slots, pair_ref, first_ref, gate_ref, matrix_ref, triangle_ref, sems = rest
    me = me_ref[0]
    groups_j = n_gi // n_cols
    block = pair_refs[0].shape[0]
    pairs = [(ref, left_ref.at[me ^ k]) for k, ref in enumerate(left_refs)]
    for k, ref in enumerate(pair_refs):
        start = pl.multiple_of((me ^ k) * block, 8)
        pairs.append((ref, slots.at[pl.ds(start, block)]))
    pairs += [(matrix_far, matrix_ref), (triangle_far, triangle_ref)]
    copies = start_copies(pairs, sems)
    _, wide, count = left_ref.shape
    half = block // groups_j
    wait_all(copies[:n_cols])
    all_rows = count // few
    residues = n_cols * few
    pair_cols = n_gi * few
    per = lanes // pair_cols
    groups = residues // per
    width = pair_ref.shape[1]
    owner = lax.rem(lax.broadcasted_iota(jnp.int32, (1, count), 1), few)
    left = []
    for c in range(n_cols):
        here = left_ref[c]
        for f in range(few):
            own = jnp.where(owner == f, here, 0.0)
            total = own
            for other in range(few):
                if other != f:
                    total = total + pltpu.roll(own, (other - f) % count, 1)
            left.append(total)
    left = jnp.concatenate(left, axis=0) * (1.0 / all_rows)
    right = []
    for d in range(wide):
        here = right_ref[pl.ds(d, n_gi, stride=wide), :]
        right += [jnp.where(owner == f, here, 0.0) for f in range(few)]
    right = jnp.concatenate(right, axis=0)
    outer = multiply(left, right, across=True)
    outputs = []
    for g in range(groups):
        swapped = swap_lane_groups(
            [outer[(g * per + i) * wide : (g * per + i + 1) * wide] for i in range(per)]
        )
        stacked = [
            s[:, t * lanes : (t + 1) * lanes] for s in swapped for t in range(wide // per)
        ]
        outputs.append(jnp.concatenate(stacked, axis=0))
    wait_all(copies[n_cols:])
    for c in range(n_cols):
        for o in range(groups_j):
            pair_ref[pl.ds(c * groups_j + o, half, stride=n_gi), :] = slots[
                pl.ds(c * block + o, half, stride=groups_j), :
            ]
    update = multiply(matrix_ref[...], jnp.concatenate(outputs, axis=1))
    first = pair_ref[...].T + update
    projected = multiply(triangle_ref[...], layer_normalise(first, gain_ref[...], axis=0))
    tri = sigmoid(projected[2 * width : 4 * width]) * projected[: 2 * width]
    slot_count, _, each, _ = tri_ref.shape
    for g in range(groups):
        tri_ref[:, g] = tri[:, g * lanes : (g + 1) * lanes].reshape(slot_count, each, lanes)
    first_ref[...] = first.T
    gate_ref[...] = sigmoid(projected[4 * width :]).T
    for k in range(n_cols):
        for o in range(groups_j):
            rows = pl.ds((me ^ k) * groups_j + o, half, stride=n_gi)
            chunks[k][pl.ds(o * half, half), :] = first_ref[rows, :]
            chunks[k][pl.ds(block + o * half, half), :] = gate_ref[rows, :]


def final_kernel(few, n_cols, residues, packed, product_ref, pair_ref, gain_ref, matrix_ref, out_ref):
    positions = out_ref.shape[0]
    if packed:
        tiles = residues // few
        tall = product_ref.shape[0] // residues
        product = []
        for t in range(tiles):
            here = [
                product_ref[pl.ds(i * tiles + t, tall, stride=residues), :] for i in range(few)
            ]
            product.append(jnp.concatenate(swap_lane_groups(here), axis=0))
        product = jnp.concatenate(product, axis=1)
    else:
        product = product_ref[...]
    update = multiply(matrix_ref[...], layer_normalise(product, gain_ref[...], axis=0))
    result = pair_ref[pl.ds(0, positions), :] + pair_ref[pl.ds(positions, positions), :] * update.T
    count = positions // (residues * few)
    for i in range(residues):
        for f in range(few):
            start = (i * few + f) * count
            out_ref[pl.ds(i * few * count + f, count, stride=few), :] = result[
                start : start + count
            ]


def per_device(
    homolog_embedding,
    pair_input_tensor,
    layernorm_scales,
    pair_norm_gains,
    pair_bias_matrix,
    horizontal_qkvg_kernel,
    horizontal_final_kernel,
    vertical_qkvg_kernel,
    vertical_final_kernel,
    feedforward_expand_kernel,
    feedforward_shrink_kernel,
    dyadic_sides_kernel,
    outer_output_matrix,
    triangle_input_matrix,
    triangle_output_matrix,
):
    rows, residues, width = homolog_embedding.shape
    pair_cols, pair_width = pair_input_tensor.shape[1:]
    heads = pair_bias_matrix.shape[1]
    outer_width = dyadic_sides_kernel.shape[1] // 2
    n_branch, n_gi, n_gj = (lax.axis_size(name) for name in everyone)
    n_cols = n_branch * n_gj
    n_all = n_cols * n_gi
    length = residues * n_gi
    few = residues // n_cols
    groups = n_gi // n_cols
    parts = 2
    per_part = n_gi // parts
    own_rows = rows // per_part
    f32 = jnp.float32

    def call(kernel, outs, *operands, scratch=(), sems=()):
        def bare(item):
            return item[0] if isinstance(item, list) else item

        def spec(item):
            return hbm if isinstance(item, list) else vmem

        return pl.pallas_call(
            kernel,
            out_shape=[jax.ShapeDtypeStruct(bare(out), f32) for out in outs],
            in_specs=[
                smem if getattr(operand, "dtype", f32) == jnp.int32 else spec(operand)
                for operand in operands
            ],
            out_specs=[spec(out) for out in outs],
            scratch_shapes=[pltpu.VMEM(shape, f32) for shape in scratch]
            + [pltpu.SemaphoreType.DMA((n,)) for n in sems],
            compiler_params=params,
        )(*[bare(operand) for operand in operands])

    def trade(blocks, axes):
        n = lax.axis_size(axes)
        return [blocks[0]] + [
            lax.ppermute(blocks[k], axes, [(t ^ k, t) for t in range(n) if t ^ k < n])
            for k in range(1, len(blocks))
        ]

    halves = [
        [
            (b * n_gi + part * per_part + g) * n_gj + j
            for b in range(n_branch)
            for g in range(per_part)
            for j in range(n_gj)
        ]
        for part in range(parts)
    ]
    n_half = n_cols * per_part
    mine = lax.axis_index("gi")
    me = jnp.stack([lax.axis_index(columns), mine % per_part, mine // per_part])
    me = me.astype(jnp.int32)
    positions = residues * pair_cols
    each = own_rows * few

    per = lanes // pair_cols
    bias_block = (heads // per, residues, lanes)
    msa, bias = call(
        bias_kernel,
        [[(parts * rows, residues, width)], bias_block],
        [homolog_embedding],
        [pair_input_tensor],
        [pair_norm_gains],
        [pair_bias_matrix.T],
        scratch=[pair_input_tensor.shape, pair_norm_gains.shape, (heads, pair_width)],
        sems=[3 + parts],
    )
    msa = lax.all_to_all(msa, "gi", 0, 0, tiled=True)
    (bias,) = call(
        functools.partial(bias_rows_kernel, n_cols),
        [(heads, residues, length)],
        me,
        *trade([bias] * n_cols, columns),
        scratch=[(n_cols,) + bias_block],
    )
    bias = trade([bias] * per_part, "gi")
    (msa_first,) = call(
        functools.partial(row_kernel, n_branch, n_gj, per_part, few),
        [(n_half, each, width)],
        me,
        msa,
        *[[block] for block in bias],
        [layernorm_scales],
        [horizontal_qkvg_kernel],
        [horizontal_final_kernel],
        scratch=[(per_part, heads, residues, length)]
        + [w.shape for w in (layernorm_scales, horizontal_qkvg_kernel, horizontal_final_kernel)],
        sems=[3 + per_part],
    )
    pair, msa_first = lax.optimization_barrier((pair_input_tensor, msa_first))

    msa_first = lax.all_to_all(msa_first, everyone, 0, 0, tiled=True, axis_index_groups=halves)
    count = n_half * each
    weights = (
        layernorm_scales,
        vertical_qkvg_kernel,
        vertical_final_kernel,
        feedforward_expand_kernel,
        feedforward_shrink_kernel,
        dyadic_sides_kernel.T,
    )
    left, right, *alignment = call(
        functools.partial(column_kernel, n_branch, n_gj, few, heads),
        [[(outer_width, count)], [(n_gi, outer_width, count)]] + [(per_part, each, width)] * n_cols,
        me,
        msa_first.reshape(count, width),
        *[[w] for w in weights],
        scratch=[w.shape for w in weights]
        + [(n_cols, per_part, each, width), (2 * outer_width, count)],
        sems=[len(weights), 1 + n_gi],
    )
    pair = call(
        functools.partial(pair_blocks_kernel, few, residues),
        [(positions // n_cols, pair_width)] * n_cols,
        me,
        pair.reshape(positions, pair_width),
        scratch=[(positions, pair_width)],
    )
    pair = trade(pair, columns)
    right = lax.all_to_all(right, "gi", 0, 0, tiled=True)
    left = trade([left] * n_cols, columns)
    alignment = [block.reshape(-1, width) for block in trade(alignment, columns)]
    share = max(pair_width // n_all, 1)
    slots = pair_width // share
    triangle = triangle_input_matrix.T.reshape(5, slots, share, pair_width)
    sides = jnp.stack([triangle[0], triangle[2]], axis=1)
    gates = jnp.stack([triangle[1], triangle[3]], axis=1)
    triangle = jnp.concatenate(
        [side.reshape(2 * pair_width, pair_width) for side in (sides, gates)]
        + [triangle[4].reshape(pair_width, pair_width)],
        axis=0,
    )
    matrix = outer_output_matrix.reshape(outer_width, outer_width // per, per, pair_width)
    matrix = jnp.transpose(matrix, (3, 2, 1, 0)).reshape(pair_width, -1)
    tri, *first_gate = call(
        functools.partial(pair_kernel, few, n_gi, n_cols),
        [(slots, positions // lanes, 2 * share, lanes)]
        + [(2 * positions // n_cols, pair_width)] * n_cols,
        me,
        *[[block] for block in left + pair],
        right.reshape(n_gi * outer_width, count),
        pair_norm_gains[1][:, None],
        [matrix],
        [triangle],
        scratch=[
            (n_cols, outer_width, count),
            (positions, pair_width),
            (positions, pair_width),
            (positions, pair_width),
            (positions, pair_width),
            matrix.shape,
            triangle.shape,
        ],
        sems=[2 * n_cols + 2],
    )

    first_gate = trade(first_gate, columns)
    tiles = [(rows, residues, width), (2 * positions, pair_width)]
    scratch = [(n_cols, rows * few, width), (2 * positions, pair_width)]
    packed = share * n_all == pair_width and share == few and few == per
    gain, last = pair_norm_gains[2], triangle_output_matrix
    if packed:
        order = [[(c // n_gj * n_gi + g) * n_gj + c % n_gj for c in range(n_cols) for g in range(n_gi)]]
        tri = lax.all_to_all(tri, everyone, 0, 0, tiled=True, axis_index_groups=order)
        product, alignment_output, first_gate = call(
            functools.partial(triangle_kernel, few, n_cols),
            [(n_all, residues, lanes)] + tiles,
            me,
            tri.reshape(-1, lanes),
            *alignment,
            *first_gate,
            scratch=[(lanes, lanes)] + scratch,
        )
        product = lax.all_to_all(product, everyone, 0, 0, tiled=True, axis_index_groups=order)
        product = product.reshape(n_all * residues, lanes)
        gain = gain.reshape(n_all, share).T.reshape(-1)
        last = jnp.swapaxes(last.reshape(n_all, share, pair_width), 0, 1).reshape(last.shape)
    else:
        alignment_output, first_gate = call(
            functools.partial(gather_kernel, few, n_cols),
            tiles,
            me,
            *alignment,
            *first_gate,
            scratch=scratch,
        )
        tri = jnp.transpose(tri.reshape(slots, -1, 2, share, lanes), (2, 1, 4, 0, 3))
        tri = tri.reshape(2, residues, pair_cols, pair_width)
        right_columns = lax.all_gather(tri[1], "gi", axis=0, tiled=True)
        product = lax.psum_scatter(
            jnp.einsum("jkc,ikc->jic", right_columns, tri[0], precision=precise),
            columns,
            scatter_dimension=0,
            tiled=True,
        ).reshape(groups, n_cols, few, residues, pair_width)
        product = jnp.transpose(product, (4, 3, 2, 0, 1)).reshape(pair_width, positions)
    (pair_output_tensor,) = pl.pallas_call(
        functools.partial(final_kernel, few, n_cols, residues, packed),
        out_shape=[jax.ShapeDtypeStruct((positions, pair_width), f32)],
        in_specs=[vmem] * 4,
        out_specs=[vmem],
        compiler_params=params,
    )(product, first_gate, gain[:, None], last.T)
    return (
        alignment_output,
        pair_output_tensor.reshape(residues, pair_cols, pair_width),
    )


def solution(mesh):
    tile, grid = P(("branch", "gj"), "gi", None), P("gi", ("branch", "gj"), None)
    return jax.shard_map(
        per_device,
        mesh=mesh,
        in_specs=(tile, grid) + (P(),) * 13,
        out_specs=(tile, grid),
        check_vma=False,
    )
```

```python
import functools
import math

import jax
import jax.numpy as jnp
from jax import lax
from jax.experimental import pallas as pl
from jax.experimental.pallas import tpu as pltpu
from jax.sharding import PartitionSpec as P

epsilon = 1e-05
precise = lax.Precision.HIGH
everyone = ("branch", "gi", "gj")
columns = ("branch", "gj")
lanes = 128
far = pl.BlockSpec(memory_space=pl.ANY)


def layer_normalise(values, norm_gain, axis=-1):
    average = jnp.mean(values, axis=axis, keepdims=True)
    centred = values - average
    variance = jnp.mean(centred * centred, axis=axis, keepdims=True)
    return centred * lax.rsqrt(variance + epsilon) * norm_gain


def apply_projection(values, weight):
    return jnp.einsum("...c,cd->...d", values, weight, precision=precise)


def sigmoid(values):
    return 1.0 / (1.0 + jnp.exp(-values))


def split(values):
    high = values.astype(jnp.bfloat16)
    return high, (values - high.astype(jnp.float32)).astype(jnp.bfloat16)


def multiply(left, right, across=False):
    numbers = (((1,), (1 if across else 0,)), ((), ()))

    def one(a, b):
        return lax.dot_general(a, b, numbers, preferred_element_type=jnp.float32)

    (lh, ll), (rh, rl) = split(left), split(right)
    return one(lh, rh) + (one(lh, rl) + one(ll, rh))


def swap_lane_groups(arrays):
    n, arrays = len(arrays), list(arrays)
    width = lanes // n
    wide = arrays[0].shape[-1]
    lane = lax.broadcasted_iota(jnp.int32, arrays[0].shape, arrays[0].ndim - 1)
    group = lax.rem(lane, lanes) // width
    axis = arrays[0].ndim - 1
    step = 1
    while step < n:
        upper = (group // step) % 2 == 1
        for low in range(n):
            if low & step:
                continue
            a, b = arrays[low], arrays[low + step]
            arrays[low] = jnp.where(upper, pltpu.roll(b, step * width, axis), a)
            arrays[low + step] = jnp.where(
                upper, b, pltpu.roll(a, wide - step * width, axis)
            )
        step *= 2
    return arrays


def head_masks(shape, heads):
    column = lax.broadcasted_iota(jnp.int32, shape, 1)
    return [column // (shape[1] // heads) == h for h in range(heads)]


def attend(query, key, value, bias, heads, allowed=None):
    count, inner = query.shape
    masks = head_masks((count, inner), heads)
    spread = jnp.concatenate([jnp.where(m, query, 0.0) for m in masks], axis=0)
    scores = multiply(spread, key, across=True) * (1.0 / math.sqrt(inner // heads))
    if bias is not None:
        scores = scores + bias
    if allowed is not None:
        scores = jnp.where(allowed, scores, -1e30)
    weights = jnp.exp(scores - jnp.max(scores, axis=-1, keepdims=True))
    weights = weights / jnp.sum(weights, axis=-1, keepdims=True)
    mixed = multiply(weights, value)
    result = jnp.where(masks[0], mixed[:count], 0.0)
    for h in range(1, heads):
        result = result + jnp.where(masks[h], mixed[h * count : (h + 1) * count], 0.0)
    return result


def start_copies(pairs, sems):
    copies = [pltpu.make_async_copy(a, b, sems.at[n]) for n, (a, b) in enumerate(pairs)]
    for copy in copies:
        copy.start()
    return copies


def wait_all(copies):
    for copy in copies:
        copy.wait()


def column_index():
    return lax.axis_index("branch") * lax.axis_size("gj") + lax.axis_index("gj")


def call(kernel, outs, *operands, scratch=(), sems=()):
    def bare(item):
        return item[0] if isinstance(item, list) else item

    n_in, n_out = len(operands), len(outs)
    near_in = [n for n, item in enumerate(operands) if not isinstance(item, list)]
    near_out = [n for n, item in enumerate(outs) if not isinstance(item, list)]
    shapes = [operands[n].shape for n in near_in] + [outs[n] for n in near_out]

    def body(*refs):
        inputs, results = list(refs[:n_in]), list(refs[n_in : n_in + n_out])
        local = refs[n_in + n_out : n_in + n_out + len(shapes)]
        rest, own_sems = refs[n_in + n_out + len(shapes) : -1], refs[-1]
        pairs = list(zip([inputs[n] for n in near_in], local))
        back = list(zip(local[len(near_in) :], [results[n] for n in near_out]))
        for n, ref in zip(near_in, local):
            inputs[n] = ref
        for n, ref in zip(near_out, local[len(near_in) :]):
            results[n] = ref
        copies = start_copies(pairs, own_sems)
        kernel(lambda: wait_all(copies), *inputs, *results, *rest)
        wait_all(start_copies(back, own_sems))

    return pl.pallas_call(
        body,
        out_shape=[jax.ShapeDtypeStruct(bare(out), jnp.float32) for out in outs],
        in_specs=[far] * n_in,
        out_specs=[far] * n_out,
        scratch_shapes=[pltpu.VMEM(shape, jnp.float32) for shape in shapes + list(scratch)]
        + [pltpu.SemaphoreType.DMA((n,)) for n in sems]
        + [pltpu.SemaphoreType.DMA((max(len(near_in), len(near_out), 1),))],
    )(*[bare(operand) for operand in operands])


def spread(me, refs, slots):
    for k, ref in enumerate(refs):
        slots[me ^ k] = ref[...]


def spread_rows(me, refs, slots):
    for k, ref in enumerate(refs):
        count = ref.shape[0]
        slots[pl.ds(pl.multiple_of((me ^ k) * count, 8), count), :] = ref[...]


def bias_kernel(
    ready, msa_far, pair_far, gains_far, matrix_far, copies_far, out_ref, pair_ref, gains_ref, matrix_ref, sems
):
    rows = msa_far.shape[0]
    repeats = copies_far.shape[0] // rows
    copies = start_copies(
        [(gains_far, gains_ref), (matrix_far, matrix_ref), (pair_far, pair_ref)]
        + [(msa_far, copies_far.at[pl.ds(n * rows, rows)]) for n in range(repeats)],
        sems,
    )
    residues, pair_cols, _ = pair_ref.shape
    heads = matrix_ref.shape[0]
    per = lanes // pair_cols
    ready()
    wait_all(copies[:3])
    normal = layer_normalise(pair_ref[...], gains_ref[0:1, :][None])
    for i in range(residues):
        here = multiply(matrix_ref[...], normal[i], across=True)
        for h in range(heads):
            out_ref[h // per, i : i + 1, pl.ds(h % per * pair_cols, pair_cols)] = here[h : h + 1]
    wait_all(copies[3:])


def pair_blocks_kernel(few, residues, ready, pair_ref, *rest):
    chunks, slots = rest[:-1], rest[-1]
    n_cols = len(chunks)
    block = chunks[0].shape[0]
    groups = block // (residues * few)
    me = column_index()
    ready()
    for c in range(n_cols):
        for o in range(groups):
            for f in range(few):
                source = pl.ds((o * n_cols + c) * few + f, residues, stride=groups * n_cols * few)
                target = pl.ds(c * block + f * groups + o, residues, stride=few * groups)
                slots[target, :] = pair_ref[source, :]
    for k in range(n_cols):
        start = pl.multiple_of((me ^ k) * block, 8)
        chunks[k][...] = slots[pl.ds(start, block), :]


def bias_rows_kernel(n_cols, ready, *rest):
    blocks, (out_ref, slots) = rest[:n_cols], rest[n_cols:]
    ready()
    spread(column_index(), blocks, slots)
    count = slots.shape[1]
    per = out_ref.shape[0] // count
    for block in range(count):
        tiles = [[] for _ in range(per)]
        for tile in range(n_cols // per):
            group = [slots[c, block] for c in range(tile * per, (tile + 1) * per)]
            for k, piece in enumerate(swap_lane_groups(group)):
                tiles[k].append(piece)
        for k in range(per):
            out_ref[block * per + k] = jnp.concatenate(tiles[k], axis=1)


def row_kernel(n_branch, n_gj, per_part, few, ready, msa_ref, *rest):
    bias_refs, rest = rest[:per_part], rest[per_part:]
    gains_far, qkvg_far, final_far, out_ref, slots, gains_ref, qkvg_ref, final_ref, sems = rest
    mine = lax.axis_index("gi")
    me, part = lax.rem(mine, per_part), lax.div(mine, per_part)
    copies = start_copies(
        [(gains_far, gains_ref), (qkvg_far, qkvg_ref), (final_far, final_ref)]
        + [(ref, slots.at[me ^ k]) for k, ref in enumerate(bias_refs)],
        sems,
    )
    ready()
    _, residues, width = msa_ref.shape
    _, heads, _, length = slots.shape
    n_gi = length // residues
    rows = msa_ref.shape[0] // n_gi
    inner = final_ref.shape[0]
    queries = per_part * residues
    tokens = jnp.concatenate(
        [msa_ref[g * rows + r] for r in range(rows) for g in range(n_gi)], axis=0
    )
    first = part * (per_part * rows)
    asking = msa_ref[pl.ds(first, per_part * rows)]
    asking = jnp.concatenate(
        [asking[g * rows + r] for r in range(rows) for g in range(per_part)], axis=0
    )
    tokens = layer_normalise(tokens, 1.0)
    normal = layer_normalise(asking, 1.0)
    wait_all(copies[:2])
    gain = gains_ref[0:1, :]
    key_value = multiply(tokens * gain, qkvg_ref[:, inner : 3 * inner])
    normal = normal * gain
    query = multiply(normal, qkvg_ref[:, :inner])
    gate = multiply(normal, qkvg_ref[:, 3 * inner :])
    wait_all(copies[2:])
    bias = jnp.concatenate(
        [slots[g, h] for h in range(heads) for g in range(per_part)], axis=0
    )
    attended = []
    for r in range(rows):
        keys = key_value[r * length : (r + 1) * length, :inner]
        values = key_value[r * length : (r + 1) * length, inner:]
        attended.append(
            attend(query[r * queries : (r + 1) * queries], keys, values, bias, heads)
        )
    attended = jnp.concatenate(attended, axis=0)
    result = asking + multiply(sigmoid(gate) * attended, final_ref[...])
    for b in range(n_branch):
        for g in range(per_part):
            for j in range(n_gj):
                start = g * residues + (b * n_gj + j) * few
                out_ref[(b * per_part + g) * n_gj + j] = jnp.concatenate(
                    [result[r * queries + start : r * queries + start + few] for r in range(rows)],
                    axis=0,
                )


def column_kernel(n_branch, n_gj, few, heads, ready, msa_ref, *rest):
    n_cols = n_branch * n_gj
    weights, rest = rest[:6], rest[6:]
    left_far, right_far, chunks, rest = rest[0], rest[1], rest[2 : 2 + n_cols], rest[2 + n_cols :]
    gains_ref, qkvg_ref, final_ref, expand_ref, shrink_ref, sides_ref = rest[:6]
    slots, factors_ref, sems, out_sems = rest[6:]
    copies = start_copies(list(zip(weights, rest[:6])), sems)
    ready()
    count, width = msa_ref.shape
    inner = final_ref.shape[0]
    half = sides_ref.shape[0] // 2
    first = msa_ref[...]
    normal = layer_normalise(first, 1.0)
    wait_all(copies[:2])
    projected = multiply(normal * gains_ref[1:2, :], qkvg_ref[...])
    query, key, value, gate = (projected[:, k * inner : (k + 1) * inner] for k in range(4))
    allowed = None
    if few > 1:
        shape = (heads * count, count)
        asks = lax.broadcasted_iota(jnp.int32, shape, 0)
        holds = lax.broadcasted_iota(jnp.int32, shape, 1)
        allowed = lax.rem(asks, few) == lax.rem(holds, few)
    attended = attend(query, key, value, None, heads, allowed)
    wait_all(copies[2:])
    second = first + multiply(sigmoid(gate) * attended, final_ref[...])
    expanded = multiply(layer_normalise(second, gains_ref[2:3, :]), expand_ref[...])
    third = second + multiply(jnp.maximum(expanded, 0.0), shrink_ref[...])
    factors_ref[...] = multiply(
        sides_ref[...], layer_normalise(third, gains_ref[3:4, :]), across=True
    )
    pairs = [(factors_ref.at[pl.ds(0, half)], left_far)]
    for g in range(right_far.shape[0]):
        pairs.append((factors_ref.at[pl.ds(half, half)], right_far.at[g]))
    copies = start_copies(pairs, out_sems)
    per_part, each = slots.shape[1:3]
    for b in range(n_branch):
        for g in range(per_part):
            for j in range(n_gj):
                start = ((b * per_part + g) * n_gj + j) * each
                slots[b * n_gj + j, g] = third[start : start + each]
    for k, chunk in enumerate(chunks):
        chunk[...] = slots[column_index() ^ k]
    wait_all(copies)


def gather_tiles(few, me, alignment_refs, pair_refs, msa_out, pair_out, msa_slots, slots):
    n_cols = len(alignment_refs)
    spread(me, alignment_refs, msa_slots)
    for r in range(msa_out.shape[0]):
        msa_out[r] = jnp.concatenate(
            [msa_slots[c, r * few : (r + 1) * few] for c in range(n_cols)], axis=0
        )
    spread_rows(me, pair_refs, slots)
    block = pair_refs[0].shape[0]
    positions = n_cols * block // 2
    residues = msa_out.shape[1]
    groups = positions // (residues * few * n_cols)
    count = residues * few
    for c in range(n_cols):
        for part in range(2):
            for o in range(groups):
                start = part * positions + o * n_cols + c
                pair_out[pl.ds(start, count, stride=groups * n_cols), :] = slots[
                    pl.ds(c * block + (part * groups + o) * count, count), :
                ]


def gather_kernel(few, n_cols, ready, *rest):
    ready()
    gather_tiles(few, column_index(), rest[:n_cols], rest[n_cols : 2 * n_cols], *rest[2 * n_cols :])


def triangle_kernel(few, n_cols, ready, tri_ref, *rest):
    blocks, (out_ref, msa_out, pair_out, product_ref, msa_slots, slots) = (
        rest[: 2 * n_cols],
        rest[2 * n_cols :],
    )
    ready()
    gather_tiles(
        few, column_index(), blocks[:n_cols], blocks[n_cols:], msa_out, pair_out, msa_slots, slots
    )
    n_all, rows, _ = out_ref.shape
    n_gi = n_all // n_cols
    share = few
    tiles = rows // few
    each = 2 * share
    wide = lanes // few
    group = lax.broadcasted_iota(jnp.int32, (n_gi * tiles, lanes), 1) // wide
    products = []
    for q in range(share):
        left, right = [], []
        for c in range(n_cols):
            base = c * n_gi * tiles * each
            here = jnp.concatenate(
                [
                    tri_ref[pl.ds(base + t * each + q, n_gi, stride=tiles * each), :]
                    for t in range(tiles)
                ],
                axis=0,
            )
            left.append(
                jnp.concatenate(
                    [jnp.where(group == i, here, 0.0) for i in range(few)], axis=0
                )
            )
            here = tri_ref[pl.ds(base + share + q, n_gi * tiles, stride=each), :]
            rolled = [here] + [pltpu.roll(here, k * wide, 1) for k in range(1, few)]
            copies = []
            for j in range(few):
                copy = rolled[0]
                for k in range(1, few):
                    copy = jnp.where(group == (j + k) % few, rolled[k], copy)
                copies.append(copy)
            step = n_gi * tiles // n_cols
            right.append(
                jnp.concatenate(
                    [copy[k * step : (k + 1) * step] for k in range(n_cols) for copy in copies],
                    axis=0,
                )
            )
        products.append(
            multiply(
                jnp.concatenate(left, axis=1), jnp.concatenate(right, axis=1), across=True
            )
        )
    for c, product in enumerate(swap_lane_groups(products)):
        product_ref[...] = product
        for g in range(n_gi):
            out_ref[c * n_gi + g] = product_ref[pl.ds(g, rows, stride=n_gi), :]


def pair_kernel(
    few, n_gi, n_cols, ready, *rest
):
    left_refs, pair_refs = rest[:n_cols], rest[n_cols : 2 * n_cols]
    right_ref, gain_ref, matrix_ref, triangle_ref, tri_ref = rest[2 * n_cols : 2 * n_cols + 5]
    matrix_far, triangle_far = matrix_ref, triangle_ref
    chunks = rest[2 * n_cols + 5 : 3 * n_cols + 5]
    rest = rest[3 * n_cols + 5 :]
    left_ref, slots, pair_ref, first_ref, gate_ref, matrix_ref, triangle_ref, sems = rest
    me = column_index()
    groups_j = n_gi // n_cols
    block = pair_refs[0].shape[0]
    pairs = [(ref, left_ref.at[me ^ k]) for k, ref in enumerate(left_refs)]
    for k, ref in enumerate(pair_refs):
        start = pl.multiple_of((me ^ k) * block, 8)
        pairs.append((ref, slots.at[pl.ds(start, block)]))
    pairs += [(matrix_far, matrix_ref), (triangle_far, triangle_ref)]
    copies = start_copies(pairs, sems)
    _, wide, count = left_ref.shape
    half = block // groups_j
    ready()
    wait_all(copies[:n_cols])
    all_rows = count // few
    residues = n_cols * few
    pair_cols = n_gi * few
    per = lanes // pair_cols
    groups = residues // per
    width = pair_ref.shape[1]
    owner = lax.rem(lax.broadcasted_iota(jnp.int32, (1, count), 1), few)
    left = []
    for c in range(n_cols):
        here = left_ref[c]
        for f in range(few):
            own = jnp.where(owner == f, here, 0.0)
            total = own
            for other in range(few):
                if other != f:
                    total = total + pltpu.roll(own, (other - f) % count, 1)
            left.append(total)
    left = jnp.concatenate(left, axis=0) * (1.0 / all_rows)
    right = []
    for d in range(wide):
        here = right_ref[pl.ds(d, n_gi, stride=wide), :]
        right += [jnp.where(owner == f, here, 0.0) for f in range(few)]
    right = jnp.concatenate(right, axis=0)
    outer = multiply(left, right, across=True)
    outputs = []
    for g in range(groups):
        swapped = swap_lane_groups(
            [outer[(g * per + i) * wide : (g * per + i + 1) * wide] for i in range(per)]
        )
        stacked = [
            s[:, t * lanes : (t + 1) * lanes] for s in swapped for t in range(wide // per)
        ]
        outputs.append(jnp.concatenate(stacked, axis=0))
    wait_all(copies[n_cols:])
    for c in range(n_cols):
        for o in range(groups_j):
            pair_ref[pl.ds(c * groups_j + o, half, stride=n_gi), :] = slots[
                pl.ds(c * block + o, half, stride=groups_j), :
            ]
    update = multiply(matrix_ref[...], jnp.concatenate(outputs, axis=1))
    first = pair_ref[...].T + update
    projected = multiply(triangle_ref[...], layer_normalise(first, gain_ref[...], axis=0))
    tri = sigmoid(projected[2 * width : 4 * width]) * projected[: 2 * width]
    slot_count, _, each, _ = tri_ref.shape
    for g in range(groups):
        tri_ref[:, g] = tri[:, g * lanes : (g + 1) * lanes].reshape(slot_count, each, lanes)
    first_ref[...] = first.T
    gate_ref[...] = sigmoid(projected[4 * width :]).T
    for k in range(n_cols):
        for o in range(groups_j):
            rows = pl.ds((me ^ k) * groups_j + o, half, stride=n_gi)
            chunks[k][pl.ds(o * half, half), :] = first_ref[rows, :]
            chunks[k][pl.ds(block + o * half, half), :] = gate_ref[rows, :]


def final_kernel(
    few, n_cols, residues, packed, ready, product_ref, pair_ref, gain_ref, matrix_ref, out_ref
):
    positions = out_ref.shape[0]
    ready()
    if packed:
        tiles = residues // few
        tall = product_ref.shape[0] // residues
        product = []
        for t in range(tiles):
            here = [
                product_ref[pl.ds(i * tiles + t, tall, stride=residues), :] for i in range(few)
            ]
            product.append(jnp.concatenate(swap_lane_groups(here), axis=0))
        product = jnp.concatenate(product, axis=1)
    else:
        product = product_ref[...]
    update = multiply(matrix_ref[...], layer_normalise(product, gain_ref[...], axis=0))
    result = pair_ref[pl.ds(0, positions), :] + pair_ref[pl.ds(positions, positions), :] * update.T
    count = positions // (residues * few)
    for i in range(residues):
        for f in range(few):
            start = (i * few + f) * count
            out_ref[pl.ds(i * few * count + f, count, stride=few), :] = result[
                start : start + count
            ]


def per_device(
    homolog_embedding,
    pair_input_tensor,
    layernorm_scales,
    pair_norm_gains,
    pair_bias_matrix,
    horizontal_qkvg_kernel,
    horizontal_final_kernel,
    vertical_qkvg_kernel,
    vertical_final_kernel,
    feedforward_expand_kernel,
    feedforward_shrink_kernel,
    dyadic_sides_kernel,
    outer_output_matrix,
    triangle_input_matrix,
    triangle_output_matrix,
):
    rows, residues, width = homolog_embedding.shape
    pair_cols, pair_width = pair_input_tensor.shape[1:]
    heads = pair_bias_matrix.shape[1]
    outer_width = dyadic_sides_kernel.shape[1] // 2
    n_branch, n_gi, n_gj = (lax.axis_size(name) for name in everyone)
    n_cols = n_branch * n_gj
    n_all = n_cols * n_gi
    length = residues * n_gi
    few = residues // n_cols
    groups = n_gi // n_cols
    parts = 2
    per_part = n_gi // parts
    own_rows = rows // per_part

    def trade(blocks, axes):
        n = lax.axis_size(axes)
        return [blocks[0]] + [
            lax.ppermute(blocks[k], axes, [(t ^ k, t) for t in range(n) if t ^ k < n])
            for k in range(1, len(blocks))
        ]

    halves = [
        [
            (b * n_gi + part * per_part + g) * n_gj + j
            for b in range(n_branch)
            for g in range(per_part)
            for j in range(n_gj)
        ]
        for part in range(parts)
    ]
    n_half = n_cols * per_part
    positions = residues * pair_cols
    each = own_rows * few

    per = lanes // pair_cols
    bias_block = (heads // per, residues, lanes)
    msa, bias = call(
        bias_kernel,
        [[(parts * rows, residues, width)], bias_block],
        [homolog_embedding],
        [pair_input_tensor],
        [pair_norm_gains],
        [pair_bias_matrix.T],
        scratch=[pair_input_tensor.shape, pair_norm_gains.shape, (heads, pair_width)],
        sems=[3 + parts],
    )
    msa = lax.all_to_all(msa, "gi", 0, 0, tiled=True)
    (bias,) = call(
        functools.partial(bias_rows_kernel, n_cols),
        [(heads, residues, length)],
        *trade([bias] * n_cols, columns),
        scratch=[(n_cols,) + bias_block],
    )
    bias = trade([bias] * per_part, "gi")
    (msa_first,) = call(
        functools.partial(row_kernel, n_branch, n_gj, per_part, few),
        [(n_half, each, width)],
        msa,
        *[[block] for block in bias],
        [layernorm_scales],
        [horizontal_qkvg_kernel],
        [horizontal_final_kernel],
        scratch=[(per_part, heads, residues, length)]
        + [w.shape for w in (layernorm_scales, horizontal_qkvg_kernel, horizontal_final_kernel)],
        sems=[3 + per_part],
    )
    pair, msa_first = lax.optimization_barrier((pair_input_tensor, msa_first))

    msa_first = lax.all_to_all(msa_first, everyone, 0, 0, tiled=True, axis_index_groups=halves)
    count = n_half * each
    weights = (
        layernorm_scales,
        vertical_qkvg_kernel,
        vertical_final_kernel,
        feedforward_expand_kernel,
        feedforward_shrink_kernel,
        dyadic_sides_kernel.T,
    )
    left, right, *alignment = call(
        functools.partial(column_kernel, n_branch, n_gj, few, heads),
        [[(outer_width, count)], [(n_gi, outer_width, count)]] + [(per_part, each, width)] * n_cols,
        msa_first.reshape(count, width),
        *[[w] for w in weights],
        scratch=[w.shape for w in weights]
        + [(n_cols, per_part, each, width), (2 * outer_width, count)],
        sems=[len(weights), 1 + n_gi],
    )
    pair = call(
        functools.partial(pair_blocks_kernel, few, residues),
        [(positions // n_cols, pair_width)] * n_cols,
        pair.reshape(positions, pair_width),
        scratch=[(positions, pair_width)],
    )
    pair = trade(pair, columns)
    right = lax.all_to_all(right, "gi", 0, 0, tiled=True)
    left = trade([left] * n_cols, columns)
    alignment = [block.reshape(-1, width) for block in trade(alignment, columns)]
    share = max(pair_width // n_all, 1)
    slots = pair_width // share
    triangle = triangle_input_matrix.T.reshape(5, slots, share, pair_width)
    sides = jnp.stack([triangle[0], triangle[2]], axis=1)
    gates = jnp.stack([triangle[1], triangle[3]], axis=1)
    triangle = jnp.concatenate(
        [side.reshape(2 * pair_width, pair_width) for side in (sides, gates)]
        + [triangle[4].reshape(pair_width, pair_width)],
        axis=0,
    )
    matrix = outer_output_matrix.reshape(outer_width, outer_width // per, per, pair_width)
    matrix = jnp.transpose(matrix, (3, 2, 1, 0)).reshape(pair_width, -1)
    tri, *first_gate = call(
        functools.partial(pair_kernel, few, n_gi, n_cols),
        [(slots, positions // lanes, 2 * share, lanes)]
        + [(2 * positions // n_cols, pair_width)] * n_cols,
        *[[block] for block in left + pair],
        right.reshape(n_gi * outer_width, count),
        pair_norm_gains[1][:, None],
        [matrix],
        [triangle],
        scratch=[
            (n_cols, outer_width, count),
            (positions, pair_width),
            (positions, pair_width),
            (positions, pair_width),
            (positions, pair_width),
            matrix.shape,
            triangle.shape,
        ],
        sems=[2 * n_cols + 2],
    )

    first_gate = trade(first_gate, columns)
    tiles = [(rows, residues, width), (2 * positions, pair_width)]
    scratch = [(n_cols, rows * few, width), (2 * positions, pair_width)]
    packed = share * n_all == pair_width and share == few and few == per
    gain, last = pair_norm_gains[2], triangle_output_matrix
    if packed:
        order = [[(c // n_gj * n_gi + g) * n_gj + c % n_gj for c in range(n_cols) for g in range(n_gi)]]
        tri = lax.all_to_all(tri, everyone, 0, 0, tiled=True, axis_index_groups=order)
        product, alignment_output, first_gate = call(
            functools.partial(triangle_kernel, few, n_cols),
            [(n_all, residues, lanes)] + tiles,
                tri.reshape(-1, lanes),
            *alignment,
            *first_gate,
            scratch=[(lanes, lanes)] + scratch,
        )
        product = lax.all_to_all(product, everyone, 0, 0, tiled=True, axis_index_groups=order)
        product = product.reshape(n_all * residues, lanes)
        gain = gain.reshape(n_all, share).T.reshape(-1)
        last = jnp.swapaxes(last.reshape(n_all, share, pair_width), 0, 1).reshape(last.shape)
    else:
        alignment_output, first_gate = call(
            functools.partial(gather_kernel, few, n_cols),
            tiles,
                *alignment,
            *first_gate,
            scratch=scratch,
        )
        tri = jnp.transpose(tri.reshape(slots, -1, 2, share, lanes), (2, 1, 4, 0, 3))
        tri = tri.reshape(2, residues, pair_cols, pair_width)
        right_columns = lax.all_gather(tri[1], "gi", axis=0, tiled=True)
        product = lax.psum_scatter(
            jnp.einsum("jkc,ikc->jic", right_columns, tri[0], precision=precise),
            columns,
            scatter_dimension=0,
            tiled=True,
        ).reshape(groups, n_cols, few, residues, pair_width)
        product = jnp.transpose(product, (4, 3, 2, 0, 1)).reshape(pair_width, positions)
    (pair_output_tensor,) = call(
        functools.partial(final_kernel, few, n_cols, residues, packed),
        [(positions, pair_width)],
        product,
        first_gate,
        gain[:, None],
        last.T,
    )
    return (
        alignment_output,
        pair_output_tensor.reshape(residues, pair_cols, pair_width),
    )


def solution(mesh):
    tile, grid = P(("branch", "gj"), "gi", None), P("gi", ("branch", "gj"), None)
    return jax.shard_map(
        per_device,
        mesh=mesh,
        in_specs=(tile, grid) + (P(),) * 13,
        out_specs=(tile, grid),
        check_vma=False,
    )
```

```python
import functools
import math

import jax
import jax.numpy as jnp
from jax import lax
from jax.experimental import pallas as pl
from jax.experimental.pallas import tpu as pltpu
from jax.sharding import PartitionSpec as P

epsilon = 1e-05
precise = lax.Precision.HIGH
everyone = ("branch", "gi", "gj")
columns = ("branch", "gj")
lanes = 128
far = pl.BlockSpec(memory_space=pl.ANY)
vmem = pl.BlockSpec(memory_space=pltpu.VMEM)
params = pltpu.CompilerParams(vmem_limit_bytes=16 * 1024 * 1024)


def layer_normalise(values, norm_gain, axis=-1):
    average = jnp.mean(values, axis=axis, keepdims=True)
    centred = values - average
    variance = jnp.mean(centred * centred, axis=axis, keepdims=True)
    return centred * lax.rsqrt(variance + epsilon) * norm_gain


def apply_projection(values, weight):
    return jnp.einsum("...c,cd->...d", values, weight, precision=precise)


def sigmoid(values):
    return 1.0 / (1.0 + jnp.exp(-values))


def split(values):
    high = values.astype(jnp.bfloat16)
    return high, (values - high.astype(jnp.float32)).astype(jnp.bfloat16)


def multiply(left, right, across=False):
    numbers = (((1,), (1 if across else 0,)), ((), ()))

    def one(a, b):
        return lax.dot_general(a, b, numbers, preferred_element_type=jnp.float32)

    (lh, ll), (rh, rl) = split(left), split(right)
    return one(lh, rh) + (one(lh, rl) + one(ll, rh))


def swap_lane_groups(arrays):
    n, arrays = len(arrays), list(arrays)
    width = lanes // n
    wide = arrays[0].shape[-1]
    lane = lax.broadcasted_iota(jnp.int32, arrays[0].shape, arrays[0].ndim - 1)
    group = lax.rem(lane, lanes) // width
    axis = arrays[0].ndim - 1
    step = 1
    while step < n:
        upper = (group // step) % 2 == 1
        for low in range(n):
            if low & step:
                continue
            a, b = arrays[low], arrays[low + step]
            arrays[low] = jnp.where(upper, pltpu.roll(b, step * width, axis), a)
            arrays[low + step] = jnp.where(
                upper, b, pltpu.roll(a, wide - step * width, axis)
            )
        step *= 2
    return arrays


def head_masks(shape, heads):
    column = lax.broadcasted_iota(jnp.int32, shape, 1)
    return [column // (shape[1] // heads) == h for h in range(heads)]


def attend(query, key, value, bias, heads, allowed=None):
    count, inner = query.shape
    masks = head_masks((count, inner), heads)
    spread = jnp.concatenate([jnp.where(m, query, 0.0) for m in masks], axis=0)
    scores = multiply(spread, key, across=True) * (1.0 / math.sqrt(inner // heads))
    if bias is not None:
        scores = scores + bias
    if allowed is not None:
        scores = jnp.where(allowed, scores, -1e30)
    weights = jnp.exp(scores - jnp.max(scores, axis=-1, keepdims=True))
    weights = weights / jnp.sum(weights, axis=-1, keepdims=True)
    mixed = multiply(weights, value)
    result = jnp.where(masks[0], mixed[:count], 0.0)
    for h in range(1, heads):
        result = result + jnp.where(masks[h], mixed[h * count : (h + 1) * count], 0.0)
    return result


def start_copies(pairs, sems):
    copies = [pltpu.make_async_copy(a, b, sems.at[n]) for n, (a, b) in enumerate(pairs)]
    for copy in copies:
        copy.start()
    return copies


def wait_all(copies):
    for copy in copies:
        copy.wait()


def column_index():
    return lax.axis_index("branch") * lax.axis_size("gj") + lax.axis_index("gj")


def call(kernel, outs, *operands, scratch=(), sems=()):
    def bare(item):
        return item[0] if isinstance(item, list) else item

    n_in, n_out = len(operands), len(outs)
    near_in = [n for n, item in enumerate(operands) if not isinstance(item, list)]
    near_out = [n for n, item in enumerate(outs) if not isinstance(item, list)]
    shapes = [operands[n].shape for n in near_in] + [outs[n] for n in near_out]

    def body(*refs):
        inputs, results = list(refs[:n_in]), list(refs[n_in : n_in + n_out])
        local = refs[n_in + n_out : n_in + n_out + len(shapes)]
        rest, own_sems = refs[n_in + n_out + len(shapes) : -1], refs[-1]
        pairs = list(zip([inputs[n] for n in near_in], local))
        back = list(zip(local[len(near_in) :], [results[n] for n in near_out]))
        for n, ref in zip(near_in, local):
            inputs[n] = ref
        for n, ref in zip(near_out, local[len(near_in) :]):
            results[n] = ref
        copies = start_copies(pairs, own_sems)
        kernel(lambda: wait_all(copies), *inputs, *results, *rest)
        wait_all(start_copies(back, own_sems))

    return pl.pallas_call(
        body,
        out_shape=[jax.ShapeDtypeStruct(bare(out), jnp.float32) for out in outs],
        in_specs=[far] * n_in,
        out_specs=[far] * n_out,
        scratch_shapes=[pltpu.VMEM(shape, jnp.float32) for shape in shapes + list(scratch)]
        + [pltpu.SemaphoreType.DMA((n,)) for n in sems]
        + [pltpu.SemaphoreType.DMA((max(len(near_in), len(near_out), 1),))],
    )(*[bare(operand) for operand in operands])


def call_near(kernel, outs, *operands, scratch=()):
    return pl.pallas_call(
        lambda *refs: kernel(lambda: None, *refs),
        out_shape=[jax.ShapeDtypeStruct(out, jnp.float32) for out in outs],
        in_specs=[vmem] * len(operands),
        out_specs=[vmem] * len(outs),
        scratch_shapes=[pltpu.VMEM(shape, jnp.float32) for shape in scratch],
        compiler_params=params,
    )(*operands)


def spread(me, refs, slots):
    for k, ref in enumerate(refs):
        slots[me ^ k] = ref[...]


def spread_rows(me, refs, slots):
    for k, ref in enumerate(refs):
        count = ref.shape[0]
        slots[pl.ds(pl.multiple_of((me ^ k) * count, 8), count), :] = ref[...]


def bias_kernel(
    ready, msa_far, pair_far, gains_far, matrix_far, copies_far, out_ref, msa_ref, pair_ref,
    gains_ref, matrix_ref, sems, out_sems
):
    rows = msa_far.shape[0]
    repeats = copies_far.shape[0] // rows
    copies = start_copies(
        [(msa_far, msa_ref), (gains_far, gains_ref), (matrix_far, matrix_ref), (pair_far, pair_ref)],
        sems,
    )
    residues, pair_cols, _ = pair_ref.shape
    heads = matrix_ref.shape[0]
    per = lanes // pair_cols
    ready()
    wait_all(copies)
    copies = start_copies(
        [(msa_ref, copies_far.at[pl.ds(n * rows, rows)]) for n in range(repeats)], out_sems
    )
    normal = layer_normalise(pair_ref[...], gains_ref[0:1, :][None])
    for i in range(residues):
        here = multiply(matrix_ref[...], normal[i], across=True)
        for h in range(heads):
            out_ref[h // per, i : i + 1, pl.ds(h % per * pair_cols, pair_cols)] = here[h : h + 1]
    wait_all(copies)


def pair_blocks_kernel(few, residues, ready, pair_ref, *rest):
    chunks, slots = rest[:-1], rest[-1]
    n_cols = len(chunks)
    block = chunks[0].shape[0]
    groups = block // (residues * few)
    me = column_index()
    ready()
    for c in range(n_cols):
        for o in range(groups):
            for f in range(few):
                source = pl.ds((o * n_cols + c) * few + f, residues, stride=groups * n_cols * few)
                target = pl.ds(c * block + f * groups + o, residues, stride=few * groups)
                slots[target, :] = pair_ref[source, :]
    for k in range(n_cols):
        start = pl.multiple_of((me ^ k) * block, 8)
        chunks[k][...] = slots[pl.ds(start, block), :]


def bias_rows_kernel(n_cols, ready, *rest):
    blocks, (out_ref, slots) = rest[:n_cols], rest[n_cols:]
    ready()
    spread(column_index(), blocks, slots)
    count = slots.shape[1]
    per = out_ref.shape[0] // count
    for block in range(count):
        tiles = [[] for _ in range(per)]
        for tile in range(n_cols // per):
            group = [slots[c, block] for c in range(tile * per, (tile + 1) * per)]
            for k, piece in enumerate(swap_lane_groups(group)):
                tiles[k].append(piece)
        for k in range(per):
            out_ref[block * per + k] = jnp.concatenate(tiles[k], axis=1)


def row_kernel(n_branch, n_gj, per_part, few, ready, msa_ref, *rest):
    bias_refs, rest = rest[:per_part], rest[per_part:]
    gains_far, qkvg_far, final_far, out_ref, slots, gains_ref, qkvg_ref, final_ref, sems = rest
    mine = lax.axis_index("gi")
    me, part = lax.rem(mine, per_part), lax.div(mine, per_part)
    copies = start_copies(
        [(gains_far, gains_ref), (qkvg_far, qkvg_ref), (final_far, final_ref)]
        + [(ref, slots.at[me ^ k]) for k, ref in enumerate(bias_refs)],
        sems,
    )
    ready()
    _, residues, width = msa_ref.shape
    _, heads, _, length = slots.shape
    n_gi = length // residues
    rows = msa_ref.shape[0] // n_gi
    inner = final_ref.shape[0]
    queries = per_part * residues
    tokens = jnp.concatenate(
        [msa_ref[g * rows + r] for r in range(rows) for g in range(n_gi)], axis=0
    )
    first = part * (per_part * rows)
    asking = msa_ref[pl.ds(first, per_part * rows)]
    asking = jnp.concatenate(
        [asking[g * rows + r] for r in range(rows) for g in range(per_part)], axis=0
    )
    tokens = layer_normalise(tokens, 1.0)
    normal = layer_normalise(asking, 1.0)
    wait_all(copies[:2])
    gain = gains_ref[0:1, :]
    key_value = multiply(tokens * gain, qkvg_ref[:, inner : 3 * inner])
    normal = normal * gain
    query = multiply(normal, qkvg_ref[:, :inner])
    gate = multiply(normal, qkvg_ref[:, 3 * inner :])
    wait_all(copies[2:])
    bias = jnp.concatenate(
        [slots[g, h] for h in range(heads) for g in range(per_part)], axis=0
    )
    attended = []
    for r in range(rows):
        keys = key_value[r * length : (r + 1) * length, :inner]
        values = key_value[r * length : (r + 1) * length, inner:]
        attended.append(
            attend(query[r * queries : (r + 1) * queries], keys, values, bias, heads)
        )
    attended = jnp.concatenate(attended, axis=0)
    result = asking + multiply(sigmoid(gate) * attended, final_ref[...])
    for b in range(n_branch):
        for g in range(per_part):
            for j in range(n_gj):
                start = g * residues + (b * n_gj + j) * few
                out_ref[(b * per_part + g) * n_gj + j] = jnp.concatenate(
                    [result[r * queries + start : r * queries + start + few] for r in range(rows)],
                    axis=0,
                )


def column_kernel(
    few, heads, ready, msa_ref, gains_ref, qkvg_ref, final_ref, expand_ref, shrink_ref, sides_ref,
    left_ref, right_ref, out_ref
):
    ready()
    count, width = msa_ref.shape
    inner = final_ref.shape[0]
    half = sides_ref.shape[0] // 2
    first = msa_ref[...]
    projected = multiply(layer_normalise(first, gains_ref[1:2, :]), qkvg_ref[...])
    query, key, value, gate = (projected[:, k * inner : (k + 1) * inner] for k in range(4))
    allowed = None
    if few > 1:
        shape = (heads * count, count)
        asks = lax.broadcasted_iota(jnp.int32, shape, 0)
        holds = lax.broadcasted_iota(jnp.int32, shape, 1)
        allowed = lax.rem(asks, few) == lax.rem(holds, few)
    attended = attend(query, key, value, None, heads, allowed)
    second = first + multiply(sigmoid(gate) * attended, final_ref[...])
    expanded = multiply(layer_normalise(second, gains_ref[2:3, :]), expand_ref[...])
    third = second + multiply(jnp.maximum(expanded, 0.0), shrink_ref[...])
    out_ref[...] = third
    factors = multiply(sides_ref[...], layer_normalise(third, gains_ref[3:4, :]), across=True)
    left_ref[...] = factors[:half]
    for g in range(right_ref.shape[0]):
        right_ref[g] = factors[half:]


def msa_blocks_kernel(n_branch, n_gj, ready, msa_ref, *rest):
    chunks, slots = rest[:-1], rest[-1]
    per_part, each = slots.shape[1:3]
    ready()
    for b in range(n_branch):
        for g in range(per_part):
            for j in range(n_gj):
                start = ((b * per_part + g) * n_gj + j) * each
                slots[b * n_gj + j, g] = msa_ref[start : start + each]
    for k, chunk in enumerate(chunks):
        chunk[...] = slots[column_index() ^ k]


def gather_tiles(few, me, alignment_refs, pair_refs, msa_out, pair_out, msa_slots, slots):
    n_cols = len(alignment_refs)
    spread(me, alignment_refs, msa_slots)
    for r in range(msa_out.shape[0]):
        msa_out[r] = jnp.concatenate(
            [msa_slots[c, r * few : (r + 1) * few] for c in range(n_cols)], axis=0
        )
    spread_rows(me, pair_refs, slots)
    block = pair_refs[0].shape[0]
    positions = n_cols * block // 2
    residues = msa_out.shape[1]
    groups = positions // (residues * few * n_cols)
    count = residues * few
    for c in range(n_cols):
        for part in range(2):
            for o in range(groups):
                start = part * positions + o * n_cols + c
                pair_out[pl.ds(start, count, stride=groups * n_cols), :] = slots[
                    pl.ds(c * block + (part * groups + o) * count, count), :
                ]


def gather_kernel(few, n_cols, ready, *rest):
    ready()
    gather_tiles(few, column_index(), rest[:n_cols], rest[n_cols : 2 * n_cols], *rest[2 * n_cols :])


def triangle_kernel(few, n_branch, n_gj, ready, tri_ref, *rest):
    n_cols = n_branch * n_gj
    blocks, (out_ref, msa_out, pair_out, product_ref, msa_slots, slots) = (
        rest[: 2 * n_cols],
        rest[2 * n_cols :],
    )
    ready()
    gather_tiles(
        few, column_index(), blocks[:n_cols], blocks[n_cols:], msa_out, pair_out, msa_slots, slots
    )
    n_all, rows, _ = out_ref.shape
    n_gi = n_all // n_cols
    share = few
    tiles = rows // few
    each = 2 * share
    wide = lanes // few
    group = lax.broadcasted_iota(jnp.int32, (n_gi * tiles, lanes), 1) // wide
    products = []
    for q in range(share):
        left, right = [], []
        for c in range(n_cols):
            base = (c // n_gj * n_all // n_branch + c % n_gj) * tiles * each
            step = n_gj * tiles * each
            here = jnp.concatenate(
                [
                    tri_ref[pl.ds(base + t * each + q, n_gi, stride=step), :]
                    for t in range(tiles)
                ],
                axis=0,
            )
            left.append(
                jnp.concatenate(
                    [jnp.where(group == i, here, 0.0) for i in range(few)], axis=0
                )
            )
            here = jnp.concatenate(
                [
                    tri_ref[pl.ds(base + g * step + share + q, tiles, stride=each), :]
                    for g in range(n_gi)
                ],
                axis=0,
            )
            rolled = [here] + [pltpu.roll(here, k * wide, 1) for k in range(1, few)]
            copies = []
            for j in range(few):
                copy = rolled[0]
                for k in range(1, few):
                    copy = jnp.where(group == (j + k) % few, rolled[k], copy)
                copies.append(copy)
            step = n_gi * tiles // n_cols
            right.append(
                jnp.concatenate(
                    [copy[k * step : (k + 1) * step] for k in range(n_cols) for copy in copies],
                    axis=0,
                )
            )
        products.append(
            multiply(
                jnp.concatenate(left, axis=1), jnp.concatenate(right, axis=1), across=True
            )
        )
    for c, product in enumerate(swap_lane_groups(products)):
        product_ref[...] = product
        for g in range(n_gi):
            out_ref[(c // n_gj * n_gi + g) * n_gj + c % n_gj] = product_ref[pl.ds(g, rows, stride=n_gi), :]


def pair_kernel(
    few, n_gi, n_cols, ready, *rest
):
    left_refs, pair_refs = rest[:n_cols], rest[n_cols : 2 * n_cols]
    right_ref, gain_ref, matrix_ref, triangle_ref, tri_ref = rest[2 * n_cols : 2 * n_cols + 5]
    chunks = rest[2 * n_cols + 5 : 3 * n_cols + 5]
    rest = rest[3 * n_cols + 5 :]
    left_ref, slots, pair_ref, first_ref, gate_ref = rest
    me = column_index()
    groups_j = n_gi // n_cols
    block = pair_refs[0].shape[0]
    ready()
    spread(me, left_refs, left_ref)
    spread_rows(me, pair_refs, slots)
    _, wide, count = left_ref.shape
    half = block // groups_j
    all_rows = count // few
    residues = n_cols * few
    pair_cols = n_gi * few
    per = lanes // pair_cols
    groups = residues // per
    width = pair_ref.shape[1]
    owner = lax.rem(lax.broadcasted_iota(jnp.int32, (1, count), 1), few)
    left = []
    for c in range(n_cols):
        here = left_ref[c]
        for f in range(few):
            own = jnp.where(owner == f, here, 0.0)
            total = own
            for other in range(few):
                if other != f:
                    total = total + pltpu.roll(own, (other - f) % count, 1)
            left.append(total)
    left = jnp.concatenate(left, axis=0) * (1.0 / all_rows)
    right = []
    for d in range(wide):
        here = right_ref[pl.ds(d, n_gi, stride=wide), :]
        right += [jnp.where(owner == f, here, 0.0) for f in range(few)]
    right = jnp.concatenate(right, axis=0)
    outer = multiply(left, right, across=True)
    outputs = []
    for g in range(groups):
        swapped = swap_lane_groups(
            [outer[(g * per + i) * wide : (g * per + i + 1) * wide] for i in range(per)]
        )
        stacked = [
            s[:, t * lanes : (t + 1) * lanes] for s in swapped for t in range(wide // per)
        ]
        outputs.append(jnp.concatenate(stacked, axis=0))
    for c in range(n_cols):
        for o in range(groups_j):
            pair_ref[pl.ds(c * groups_j + o, half, stride=n_gi), :] = slots[
                pl.ds(c * block + o, half, stride=groups_j), :
            ]
    update = multiply(matrix_ref[...], jnp.concatenate(outputs, axis=1))
    first = pair_ref[...].T + update
    projected = multiply(triangle_ref[...], layer_normalise(first, gain_ref[...], axis=0))
    tri = sigmoid(projected[2 * width : 4 * width]) * projected[: 2 * width]
    slot_count, _, each, _ = tri_ref.shape
    for g in range(groups):
        tri_ref[:, g] = tri[:, g * lanes : (g + 1) * lanes].reshape(slot_count, each, lanes)
    first_ref[...] = first.T
    gate_ref[...] = sigmoid(projected[4 * width :]).T
    for k in range(n_cols):
        for o in range(groups_j):
            rows = pl.ds((me ^ k) * groups_j + o, half, stride=n_gi)
            chunks[k][pl.ds(o * half, half), :] = first_ref[rows, :]
            chunks[k][pl.ds(block + o * half, half), :] = gate_ref[rows, :]


def final_kernel(
    few, n_cols, residues, packed, ready, product_ref, pair_ref, gain_ref, matrix_ref, out_ref
):
    positions = out_ref.shape[0]
    ready()
    if packed:
        tiles = residues // few
        tall = product_ref.shape[0] // residues
        product = []
        for t in range(tiles):
            here = [
                product_ref[pl.ds(i * tiles + t, tall, stride=residues), :] for i in range(few)
            ]
            product.append(jnp.concatenate(swap_lane_groups(here), axis=0))
        product = jnp.concatenate(product, axis=1)
    else:
        product = product_ref[...]
    update = multiply(matrix_ref[...], layer_normalise(product, gain_ref[...], axis=0))
    result = pair_ref[pl.ds(0, positions), :] + pair_ref[pl.ds(positions, positions), :] * update.T
    count = positions // (residues * few)
    for i in range(residues):
        for f in range(few):
            start = (i * few + f) * count
            out_ref[pl.ds(i * few * count + f, count, stride=few), :] = result[
                start : start + count
            ]


def per_device(
    homolog_embedding,
    pair_input_tensor,
    layernorm_scales,
    pair_norm_gains,
    pair_bias_matrix,
    horizontal_qkvg_kernel,
    horizontal_final_kernel,
    vertical_qkvg_kernel,
    vertical_final_kernel,
    feedforward_expand_kernel,
    feedforward_shrink_kernel,
    dyadic_sides_kernel,
    outer_output_matrix,
    triangle_input_matrix,
    triangle_output_matrix,
):
    rows, residues, width = homolog_embedding.shape
    pair_cols, pair_width = pair_input_tensor.shape[1:]
    heads = pair_bias_matrix.shape[1]
    outer_width = dyadic_sides_kernel.shape[1] // 2
    n_branch, n_gi, n_gj = (lax.axis_size(name) for name in everyone)
    n_cols = n_branch * n_gj
    n_all = n_cols * n_gi
    length = residues * n_gi
    few = residues // n_cols
    groups = n_gi // n_cols
    parts = 2
    per_part = n_gi // parts
    own_rows = rows // per_part

    def trade(blocks, axes):
        n = lax.axis_size(axes)
        return [blocks[0]] + [
            lax.ppermute(blocks[k], axes, [(t ^ k, t) for t in range(n) if t ^ k < n])
            for k in range(1, len(blocks))
        ]

    halves = [
        [
            (b * n_gi + part * per_part + g) * n_gj + j
            for b in range(n_branch)
            for g in range(per_part)
            for j in range(n_gj)
        ]
        for part in range(parts)
    ]
    n_half = n_cols * per_part
    positions = residues * pair_cols
    each = own_rows * few

    per = lanes // pair_cols
    bias_block = (heads // per, residues, lanes)
    msa, bias = call(
        bias_kernel,
        [[(parts * rows, residues, width)], bias_block],
        [homolog_embedding],
        [pair_input_tensor],
        [pair_norm_gains],
        [pair_bias_matrix.T],
        scratch=[
            homolog_embedding.shape,
            pair_input_tensor.shape,
            pair_norm_gains.shape,
            (heads, pair_width),
        ],
        sems=[4, parts],
    )
    msa = lax.all_to_all(msa, "gi", 0, 0, tiled=True)
    (bias,) = call_near(
        functools.partial(bias_rows_kernel, n_cols),
        [(heads, residues, length)],
        *trade([bias] * n_cols, columns),
        scratch=[(n_cols,) + bias_block],
    )
    bias = trade([bias] * per_part, "gi")
    (msa_first,) = call(
        functools.partial(row_kernel, n_branch, n_gj, per_part, few),
        [(n_half, each, width)],
        msa,
        *[[block] for block in bias],
        [layernorm_scales],
        [horizontal_qkvg_kernel],
        [horizontal_final_kernel],
        scratch=[(per_part, heads, residues, length)]
        + [w.shape for w in (layernorm_scales, horizontal_qkvg_kernel, horizontal_final_kernel)],
        sems=[3 + per_part],
    )
    pair, msa_first = lax.optimization_barrier((pair_input_tensor, msa_first))

    msa_first = lax.all_to_all(msa_first, everyone, 0, 0, tiled=True, axis_index_groups=halves)
    count = n_half * each
    weights = (
        layernorm_scales,
        vertical_qkvg_kernel,
        vertical_final_kernel,
        feedforward_expand_kernel,
        feedforward_shrink_kernel,
        dyadic_sides_kernel.T,
    )
    left, right, alignment = call_near(
        functools.partial(column_kernel, few, heads),
        [(outer_width, count), (n_gi, outer_width, count), (count, width)],
        msa_first.reshape(count, width),
        *weights,
    )
    alignment = call_near(
        functools.partial(msa_blocks_kernel, n_branch, n_gj),
        [(per_part, each, width)] * n_cols,
        alignment,
        scratch=[(n_cols, per_part, each, width)],
    )
    pair = call_near(
        functools.partial(pair_blocks_kernel, few, residues),
        [(positions // n_cols, pair_width)] * n_cols,
        pair.reshape(positions, pair_width),
        scratch=[(positions, pair_width)],
    )
    pair = trade(pair, columns)
    right = lax.all_to_all(right, "gi", 0, 0, tiled=True)
    left = trade([left] * n_cols, columns)
    alignment = [block.reshape(-1, width) for block in trade(alignment, columns)]
    share = max(pair_width // n_all, 1)
    slots = pair_width // share
    triangle = triangle_input_matrix.T.reshape(5, slots, share, pair_width)
    sides = jnp.stack([triangle[0], triangle[2]], axis=1)
    gates = jnp.stack([triangle[1], triangle[3]], axis=1)
    triangle = jnp.concatenate(
        [side.reshape(2 * pair_width, pair_width) for side in (sides, gates)]
        + [triangle[4].reshape(pair_width, pair_width)],
        axis=0,
    )
    matrix = outer_output_matrix.reshape(outer_width, outer_width // per, per, pair_width)
    matrix = jnp.transpose(matrix, (3, 2, 1, 0)).reshape(pair_width, -1)
    tri, *first_gate = call_near(
        functools.partial(pair_kernel, few, n_gi, n_cols),
        [(slots, positions // lanes, 2 * share, lanes)]
        + [(2 * positions // n_cols, pair_width)] * n_cols,
        *left,
        *pair,
        right.reshape(n_gi * outer_width, count),
        pair_norm_gains[1][:, None],
        matrix,
        triangle,
        scratch=[
            (n_cols, outer_width, count),
            (positions, pair_width),
            (positions, pair_width),
            (positions, pair_width),
            (positions, pair_width),
        ],
    )

    first_gate = trade(first_gate, columns)
    tiles = [(rows, residues, width), (2 * positions, pair_width)]
    scratch = [(n_cols, rows * few, width), (2 * positions, pair_width)]
    packed = share * n_all == pair_width and share == few and few == per
    gain, last = pair_norm_gains[2], triangle_output_matrix
    if packed:
        tri = lax.all_to_all(tri, everyone, 0, 0, tiled=True)
        product, alignment_output, first_gate = call_near(
            functools.partial(triangle_kernel, few, n_branch, n_gj),
            [(n_all, residues, lanes)] + tiles,
                tri.reshape(-1, lanes),
            *alignment,
            *first_gate,
            scratch=[(lanes, lanes)] + scratch,
        )
        product = lax.all_to_all(product, everyone, 0, 0, tiled=True)
        product = product.reshape(n_all * residues, lanes)
        gain = gain.reshape(n_all, share).T.reshape(-1)
        last = jnp.swapaxes(last.reshape(n_all, share, pair_width), 0, 1).reshape(last.shape)
    else:
        alignment_output, first_gate = call_near(
            functools.partial(gather_kernel, few, n_cols),
            tiles,
                *alignment,
            *first_gate,
            scratch=scratch,
        )
        tri = jnp.transpose(tri.reshape(slots, -1, 2, share, lanes), (2, 1, 4, 0, 3))
        tri = tri.reshape(2, residues, pair_cols, pair_width)
        right_columns = lax.all_gather(tri[1], "gi", axis=0, tiled=True)
        product = lax.psum_scatter(
            jnp.einsum("jkc,ikc->jic", right_columns, tri[0], precision=precise),
            columns,
            scatter_dimension=0,
            tiled=True,
        ).reshape(groups, n_cols, few, residues, pair_width)
        product = jnp.transpose(product, (4, 3, 2, 0, 1)).reshape(pair_width, positions)
    (pair_output_tensor,) = call_near(
        functools.partial(final_kernel, few, n_cols, residues, packed),
        [(positions, pair_width)],
        product,
        first_gate,
        gain[:, None],
        last.T,
    )
    return (
        alignment_output,
        pair_output_tensor.reshape(residues, pair_cols, pair_width),
    )


def solution(mesh):
    tile, grid = P(("branch", "gj"), "gi", None), P("gi", ("branch", "gj"), None)
    return jax.shard_map(
        per_device,
        mesh=mesh,
        in_specs=(tile, grid) + (P(),) * 13,
        out_specs=(tile, grid),
        check_vma=False,
    )
```

```python
import functools
import math

import jax
import jax.numpy as jnp
from jax import lax
from jax.experimental import pallas as pl
from jax.experimental.pallas import tpu as pltpu
from jax.sharding import PartitionSpec as P

epsilon = 1e-05
precise = lax.Precision.HIGH
everyone = ("branch", "gi", "gj")
columns = ("branch", "gj")
lanes = 128
far = pl.BlockSpec(memory_space=pl.ANY)
vmem = pl.BlockSpec(memory_space=pltpu.VMEM)
params = pltpu.CompilerParams(vmem_limit_bytes=16 * 1024 * 1024)


def layer_normalise(values, norm_gain, axis=-1):
    average = jnp.mean(values, axis=axis, keepdims=True)
    centred = values - average
    variance = jnp.mean(centred * centred, axis=axis, keepdims=True)
    return centred * lax.rsqrt(variance + epsilon) * norm_gain


def apply_projection(values, weight):
    return jnp.einsum("...c,cd->...d", values, weight, precision=precise)


def sigmoid(values):
    return 1.0 / (1.0 + jnp.exp(-values))


def split(values):
    high = values.astype(jnp.bfloat16)
    return high, (values - high.astype(jnp.float32)).astype(jnp.bfloat16)


def multiply(left, right, across=False):
    numbers = (((1,), (1 if across else 0,)), ((), ()))

    def one(a, b):
        return lax.dot_general(a, b, numbers, preferred_element_type=jnp.float32)

    (lh, ll), (rh, rl) = split(left), split(right)
    return one(lh, rh) + (one(lh, rl) + one(ll, rh))


def swap_lane_groups(arrays):
    n, arrays = len(arrays), list(arrays)
    width = lanes // n
    wide = arrays[0].shape[-1]
    lane = lax.broadcasted_iota(jnp.int32, arrays[0].shape, arrays[0].ndim - 1)
    group = lax.rem(lane, lanes) // width
    axis = arrays[0].ndim - 1
    step = 1
    while step < n:
        upper = (group // step) % 2 == 1
        for low in range(n):
            if low & step:
                continue
            a, b = arrays[low], arrays[low + step]
            arrays[low] = jnp.where(upper, pltpu.roll(b, step * width, axis), a)
            arrays[low + step] = jnp.where(
                upper, b, pltpu.roll(a, wide - step * width, axis)
            )
        step *= 2
    return arrays


def head_masks(shape, heads):
    column = lax.broadcasted_iota(jnp.int32, shape, 1)
    return [column // (shape[1] // heads) == h for h in range(heads)]


def attend(query, key, value, bias, heads, allowed=None):
    count, inner = query.shape
    masks = head_masks((count, inner), heads)
    spread = jnp.concatenate([jnp.where(m, query, 0.0) for m in masks], axis=0)
    scores = multiply(spread, key, across=True) * (1.0 / math.sqrt(inner // heads))
    if bias is not None:
        scores = scores + bias
    if allowed is not None:
        scores = jnp.where(allowed, scores, -1e30)
    weights = jnp.exp(scores - jnp.max(scores, axis=-1, keepdims=True))
    weights = weights / jnp.sum(weights, axis=-1, keepdims=True)
    mixed = multiply(weights, value)
    result = jnp.where(masks[0], mixed[:count], 0.0)
    for h in range(1, heads):
        result = result + jnp.where(masks[h], mixed[h * count : (h + 1) * count], 0.0)
    return result


def start_copies(pairs, sems):
    copies = [pltpu.make_async_copy(a, b, sems.at[n]) for n, (a, b) in enumerate(pairs)]
    for copy in copies:
        copy.start()
    return copies


def wait_all(copies):
    for copy in copies:
        copy.wait()


def column_index():
    return lax.axis_index("branch") * lax.axis_size("gj") + lax.axis_index("gj")


def call(kernel, outs, *operands, scratch=(), sems=()):
    def bare(item):
        return item[0] if isinstance(item, list) else item

    n_in, n_out = len(operands), len(outs)
    near_in = [n for n, item in enumerate(operands) if not isinstance(item, list)]
    near_out = [n for n, item in enumerate(outs) if not isinstance(item, list)]
    shapes = [operands[n].shape for n in near_in] + [outs[n] for n in near_out]

    def body(*refs):
        inputs, results = list(refs[:n_in]), list(refs[n_in : n_in + n_out])
        local = refs[n_in + n_out : n_in + n_out + len(shapes)]
        rest, own_sems = refs[n_in + n_out + len(shapes) : -1], refs[-1]
        pairs = list(zip([inputs[n] for n in near_in], local))
        back = list(zip(local[len(near_in) :], [results[n] for n in near_out]))
        for n, ref in zip(near_in, local):
            inputs[n] = ref
        for n, ref in zip(near_out, local[len(near_in) :]):
            results[n] = ref
        copies = start_copies(pairs, own_sems)
        kernel(lambda: wait_all(copies), *inputs, *results, *rest)
        wait_all(start_copies(back, own_sems))

    return pl.pallas_call(
        body,
        out_shape=[jax.ShapeDtypeStruct(bare(out), jnp.float32) for out in outs],
        in_specs=[far] * n_in,
        out_specs=[far] * n_out,
        scratch_shapes=[pltpu.VMEM(shape, jnp.float32) for shape in shapes + list(scratch)]
        + [pltpu.SemaphoreType.DMA((n,)) for n in sems]
        + [pltpu.SemaphoreType.DMA((max(len(near_in), len(near_out), 1),))],
    )(*[bare(operand) for operand in operands])


def call_near(kernel, outs, *operands, scratch=()):
    return pl.pallas_call(
        lambda *refs: kernel(lambda: None, *refs),
        out_shape=[jax.ShapeDtypeStruct(out, jnp.float32) for out in outs],
        in_specs=[vmem] * len(operands),
        out_specs=[vmem] * len(outs),
        scratch_shapes=[pltpu.VMEM(shape, jnp.float32) for shape in scratch],
        compiler_params=params,
    )(*operands)


def spread(me, refs, slots):
    for k, ref in enumerate(refs):
        slots[me ^ k] = ref[...]


def spread_rows(me, refs, slots):
    for k, ref in enumerate(refs):
        count = ref.shape[0]
        slots[pl.ds(pl.multiple_of((me ^ k) * count, 8), count), :] = ref[...]


def bias_kernel(
    ready, msa_far, pair_far, gains_far, matrix_far, copies_far, out_ref, msa_ref, pair_ref,
    gains_ref, matrix_ref, sems, out_sems
):
    rows = msa_far.shape[0]
    repeats = copies_far.shape[0] // rows
    copies = start_copies(
        [(msa_far, msa_ref), (gains_far, gains_ref), (matrix_far, matrix_ref), (pair_far, pair_ref)],
        sems,
    )
    residues, pair_cols, _ = pair_ref.shape
    heads = matrix_ref.shape[0]
    per = lanes // pair_cols
    ready()
    wait_all(copies)
    copies = start_copies(
        [(msa_ref, copies_far.at[pl.ds(n * rows, rows)]) for n in range(repeats)], out_sems
    )
    normal = layer_normalise(pair_ref[...], gains_ref[0:1, :][None])
    for i in range(residues):
        here = multiply(matrix_ref[...], normal[i], across=True)
        for h in range(heads):
            out_ref[h // per, i : i + 1, pl.ds(h % per * pair_cols, pair_cols)] = here[h : h + 1]
    wait_all(copies)


def pair_blocks_kernel(few, residues, ready, pair_ref, *rest):
    chunks, slots = rest[:-1], rest[-1]
    n_cols = len(chunks)
    block = chunks[0].shape[0]
    groups = block // (residues * few)
    me = column_index()
    ready()
    for c in range(n_cols):
        for o in range(groups):
            for f in range(few):
                source = pl.ds((o * n_cols + c) * few + f, residues, stride=groups * n_cols * few)
                target = pl.ds(c * block + f * groups + o, residues, stride=few * groups)
                slots[target, :] = pair_ref[source, :]
    for k in range(n_cols):
        start = pl.multiple_of((me ^ k) * block, 8)
        chunks[k][...] = slots[pl.ds(start, block), :]


def bias_rows_kernel(n_cols, ready, *rest):
    blocks, (out_ref, slots) = rest[:n_cols], rest[n_cols:]
    ready()
    spread(column_index(), blocks, slots)
    count = slots.shape[1]
    per = out_ref.shape[0] // count
    for block in range(count):
        tiles = [[] for _ in range(per)]
        for tile in range(n_cols // per):
            group = [slots[c, block] for c in range(tile * per, (tile + 1) * per)]
            for k, piece in enumerate(swap_lane_groups(group)):
                tiles[k].append(piece)
        for k in range(per):
            out_ref[block * per + k] = jnp.concatenate(tiles[k], axis=1)


def row_kernel(n_branch, n_gj, per_part, few, ready, msa_ref, *rest):
    bias_refs, rest = rest[:per_part], rest[per_part:]
    gains_far, qkvg_far, final_far, out_ref, slots, gains_ref, qkvg_ref, final_ref, sems = rest
    mine = lax.axis_index("gi")
    me, part = lax.rem(mine, per_part), lax.div(mine, per_part)
    copies = start_copies(
        [(gains_far, gains_ref), (qkvg_far, qkvg_ref), (final_far, final_ref)]
        + [(ref, slots.at[me ^ k]) for k, ref in enumerate(bias_refs)],
        sems,
    )
    ready()
    _, residues, width = msa_ref.shape
    _, heads, _, length = slots.shape
    n_gi = length // residues
    rows = msa_ref.shape[0] // n_gi
    inner = final_ref.shape[0]
    queries = per_part * residues
    tokens = jnp.concatenate(
        [msa_ref[g * rows + r] for r in range(rows) for g in range(n_gi)], axis=0
    )
    first = part * (per_part * rows)
    asking = msa_ref[pl.ds(first, per_part * rows)]
    asking = jnp.concatenate(
        [asking[g * rows + r] for r in range(rows) for g in range(per_part)], axis=0
    )
    tokens = layer_normalise(tokens, 1.0)
    normal = layer_normalise(asking, 1.0)
    wait_all(copies[:2])
    gain = gains_ref[0:1, :]
    key_value = multiply(tokens * gain, qkvg_ref[:, inner : 3 * inner])
    normal = normal * gain
    query = multiply(normal, qkvg_ref[:, :inner])
    gate = multiply(normal, qkvg_ref[:, 3 * inner :])
    wait_all(copies[2:])
    bias = jnp.concatenate(
        [slots[g, h] for h in range(heads) for g in range(per_part)], axis=0
    )
    attended = []
    for r in range(rows):
        keys = key_value[r * length : (r + 1) * length, :inner]
        values = key_value[r * length : (r + 1) * length, inner:]
        attended.append(
            attend(query[r * queries : (r + 1) * queries], keys, values, bias, heads)
        )
    attended = jnp.concatenate(attended, axis=0)
    result = asking + multiply(sigmoid(gate) * attended, final_ref[...])
    for b in range(n_branch):
        for g in range(per_part):
            for j in range(n_gj):
                start = g * residues + (b * n_gj + j) * few
                out_ref[(b * per_part + g) * n_gj + j] = jnp.concatenate(
                    [result[r * queries + start : r * queries + start + few] for r in range(rows)],
                    axis=0,
                )


def column_kernel(
    few, heads, ready, msa_ref, gains_ref, qkvg_ref, final_ref, expand_ref, shrink_ref, sides_ref,
    left_ref, right_ref, out_ref
):
    ready()
    count, width = msa_ref.shape
    inner = final_ref.shape[0]
    half = sides_ref.shape[0] // 2
    first = msa_ref[...]
    projected = multiply(layer_normalise(first, gains_ref[1:2, :]), qkvg_ref[...])
    query, key, value, gate = (projected[:, k * inner : (k + 1) * inner] for k in range(4))
    allowed = None
    if few > 1:
        shape = (heads * count, count)
        asks = lax.broadcasted_iota(jnp.int32, shape, 0)
        holds = lax.broadcasted_iota(jnp.int32, shape, 1)
        allowed = lax.rem(asks, few) == lax.rem(holds, few)
    attended = attend(query, key, value, None, heads, allowed)
    second = first + multiply(sigmoid(gate) * attended, final_ref[...])
    expanded = multiply(layer_normalise(second, gains_ref[2:3, :]), expand_ref[...])
    third = second + multiply(jnp.maximum(expanded, 0.0), shrink_ref[...])
    out_ref[...] = third
    factors = multiply(sides_ref[...], layer_normalise(third, gains_ref[3:4, :]), across=True)
    left_ref[...] = factors[:half]
    for g in range(right_ref.shape[0]):
        right_ref[g] = factors[half:]


def msa_blocks_kernel(n_branch, n_gj, ready, msa_ref, *rest):
    chunks, slots = rest[:-1], rest[-1]
    per_part, each = slots.shape[1:3]
    ready()
    for b in range(n_branch):
        for g in range(per_part):
            for j in range(n_gj):
                start = ((b * per_part + g) * n_gj + j) * each
                slots[b * n_gj + j, g] = msa_ref[start : start + each]
    for k, chunk in enumerate(chunks):
        chunk[...] = slots[column_index() ^ k]


def gather_msa(few, me, blocks, out_ref, slots):
    n_cols = len(blocks)
    spread(me, blocks, slots)
    for r in range(out_ref.shape[0]):
        out_ref[r] = jnp.concatenate(
            [slots[c, r * few : (r + 1) * few] for c in range(n_cols)], axis=0
        )


def gather_msa_kernel(few, n_cols, ready, *rest):
    ready()
    gather_msa(few, column_index(), rest[:n_cols], *rest[n_cols:])


def gather_pair_kernel(few, n_cols, residues, ready, gain_ref, matrix_ref, *rest):
    blocks, (first_ref, gate_ref, slots) = rest[:n_cols], rest[n_cols:]
    ready()
    spread_rows(column_index(), blocks, slots)
    block = blocks[0].shape[0]
    count = residues * few
    groups = block // count
    for c in range(n_cols):
        for o in range(groups):
            first_ref[pl.ds(o * n_cols + c, count, stride=groups * n_cols), :] = slots[
                pl.ds(c * block + o * count, count), :
            ]
    normal = layer_normalise(first_ref[...], gain_ref[...])
    gate_ref[...] = sigmoid(multiply(normal, matrix_ref[...]))


def triangle_kernel(few, n_branch, n_gj, ready, tri_ref, *rest):
    n_cols = n_branch * n_gj
    blocks, (out_ref, msa_out, product_ref, slots) = rest[:n_cols], rest[n_cols:]
    ready()
    gather_msa(few, column_index(), blocks, msa_out, slots)
    n_all, rows, _ = out_ref.shape
    n_gi = n_all // n_cols
    share = few
    tiles = rows // few
    each = 2 * share
    wide = lanes // few
    group = lax.broadcasted_iota(jnp.int32, (n_gi * tiles, lanes), 1) // wide
    products = []
    for q in range(share):
        left, right = [], []
        for c in range(n_cols):
            base = (c // n_gj * n_all // n_branch + c % n_gj) * tiles * each
            step = n_gj * tiles * each
            here = jnp.concatenate(
                [
                    tri_ref[pl.ds(base + t * each + q, n_gi, stride=step), :]
                    for t in range(tiles)
                ],
                axis=0,
            )
            left.append(
                jnp.concatenate(
                    [jnp.where(group == i, here, 0.0) for i in range(few)], axis=0
                )
            )
            here = jnp.concatenate(
                [
                    tri_ref[pl.ds(base + g * step + share + q, tiles, stride=each), :]
                    for g in range(n_gi)
                ],
                axis=0,
            )
            rolled = [here] + [pltpu.roll(here, k * wide, 1) for k in range(1, few)]
            copies = []
            for j in range(few):
                copy = rolled[0]
                for k in range(1, few):
                    copy = jnp.where(group == (j + k) % few, rolled[k], copy)
                copies.append(copy)
            step = n_gi * tiles // n_cols
            right.append(
                jnp.concatenate(
                    [copy[k * step : (k + 1) * step] for k in range(n_cols) for copy in copies],
                    axis=0,
                )
            )
        products.append(
            multiply(
                jnp.concatenate(left, axis=1), jnp.concatenate(right, axis=1), across=True
            )
        )
    for c, product in enumerate(swap_lane_groups(products)):
        product_ref[...] = product
        for g in range(n_gi):
            out_ref[(c // n_gj * n_gi + g) * n_gj + c % n_gj] = product_ref[pl.ds(g, rows, stride=n_gi), :]


def pair_kernel(
    few, n_gi, n_cols, ready, *rest
):
    left_refs, pair_refs = rest[:n_cols], rest[n_cols : 2 * n_cols]
    right_ref, gain_ref, matrix_ref, triangle_ref, tri_ref = rest[2 * n_cols : 2 * n_cols + 5]
    chunks = rest[2 * n_cols + 5 : 3 * n_cols + 5]
    rest = rest[3 * n_cols + 5 :]
    left_ref, slots, pair_ref, first_ref = rest
    me = column_index()
    groups_j = n_gi // n_cols
    block = pair_refs[0].shape[0]
    ready()
    spread(me, left_refs, left_ref)
    spread_rows(me, pair_refs, slots)
    _, wide, count = left_ref.shape
    half = block // groups_j
    all_rows = count // few
    residues = n_cols * few
    pair_cols = n_gi * few
    per = lanes // pair_cols
    groups = residues // per
    width = pair_ref.shape[1]
    owner = lax.rem(lax.broadcasted_iota(jnp.int32, (1, count), 1), few)
    left = []
    for c in range(n_cols):
        here = left_ref[c]
        for f in range(few):
            own = jnp.where(owner == f, here, 0.0)
            total = own
            for other in range(few):
                if other != f:
                    total = total + pltpu.roll(own, (other - f) % count, 1)
            left.append(total)
    left = jnp.concatenate(left, axis=0) * (1.0 / all_rows)
    right = []
    for d in range(wide):
        here = right_ref[pl.ds(d, n_gi, stride=wide), :]
        right += [jnp.where(owner == f, here, 0.0) for f in range(few)]
    right = jnp.concatenate(right, axis=0)
    outer = multiply(left, right, across=True)
    outputs = []
    for g in range(groups):
        swapped = swap_lane_groups(
            [outer[(g * per + i) * wide : (g * per + i + 1) * wide] for i in range(per)]
        )
        stacked = [
            s[:, t * lanes : (t + 1) * lanes] for s in swapped for t in range(wide // per)
        ]
        outputs.append(jnp.concatenate(stacked, axis=0))
    for c in range(n_cols):
        for o in range(groups_j):
            pair_ref[pl.ds(c * groups_j + o, half, stride=n_gi), :] = slots[
                pl.ds(c * block + o, half, stride=groups_j), :
            ]
    update = multiply(matrix_ref[...], jnp.concatenate(outputs, axis=1))
    first = pair_ref[...].T + update
    projected = multiply(triangle_ref[...], layer_normalise(first, gain_ref[...], axis=0))
    tri = sigmoid(projected[2 * width : 4 * width]) * projected[: 2 * width]
    slot_count, _, each, _ = tri_ref.shape
    for g in range(groups):
        tri_ref[:, g] = tri[:, g * lanes : (g + 1) * lanes].reshape(slot_count, each, lanes)
    first_ref[...] = first.T
    for k in range(n_cols):
        for o in range(groups_j):
            rows = pl.ds((me ^ k) * groups_j + o, half, stride=n_gi)
            chunks[k][pl.ds(o * half, half), :] = first_ref[rows, :]


def final_kernel(
    few, n_cols, residues, packed, ready, product_ref, first_ref, gate_ref, gain_ref, matrix_ref,
    out_ref
):
    positions = out_ref.shape[0]
    ready()
    if packed:
        tiles = residues // few
        tall = product_ref.shape[0] // residues
        product = []
        for t in range(tiles):
            here = [
                product_ref[pl.ds(i * tiles + t, tall, stride=residues), :] for i in range(few)
            ]
            product.append(jnp.concatenate(swap_lane_groups(here), axis=0))
        product = jnp.concatenate(product, axis=1)
    else:
        product = product_ref[...]
    update = multiply(matrix_ref[...], layer_normalise(product, gain_ref[...], axis=0))
    result = first_ref[...] + gate_ref[...] * update.T
    count = positions // (residues * few)
    for i in range(residues):
        for f in range(few):
            start = (i * few + f) * count
            out_ref[pl.ds(i * few * count + f, count, stride=few), :] = result[
                start : start + count
            ]


def per_device(
    homolog_embedding,
    pair_input_tensor,
    layernorm_scales,
    pair_norm_gains,
    pair_bias_matrix,
    horizontal_qkvg_kernel,
    horizontal_final_kernel,
    vertical_qkvg_kernel,
    vertical_final_kernel,
    feedforward_expand_kernel,
    feedforward_shrink_kernel,
    dyadic_sides_kernel,
    outer_output_matrix,
    triangle_input_matrix,
    triangle_output_matrix,
):
    rows, residues, width = homolog_embedding.shape
    pair_cols, pair_width = pair_input_tensor.shape[1:]
    heads = pair_bias_matrix.shape[1]
    outer_width = dyadic_sides_kernel.shape[1] // 2
    n_branch, n_gi, n_gj = (lax.axis_size(name) for name in everyone)
    n_cols = n_branch * n_gj
    n_all = n_cols * n_gi
    length = residues * n_gi
    few = residues // n_cols
    groups = n_gi // n_cols
    parts = 2
    per_part = n_gi // parts
    own_rows = rows // per_part

    def trade(blocks, axes):
        n = lax.axis_size(axes)
        return [blocks[0]] + [
            lax.ppermute(blocks[k], axes, [(t ^ k, t) for t in range(n) if t ^ k < n])
            for k in range(1, len(blocks))
        ]

    halves = [
        [
            (b * n_gi + part * per_part + g) * n_gj + j
            for b in range(n_branch)
            for g in range(per_part)
            for j in range(n_gj)
        ]
        for part in range(parts)
    ]
    n_half = n_cols * per_part
    positions = residues * pair_cols
    each = own_rows * few

    per = lanes // pair_cols
    bias_block = (heads // per, residues, lanes)
    msa, bias = call(
        bias_kernel,
        [[(parts * rows, residues, width)], bias_block],
        [homolog_embedding],
        [pair_input_tensor],
        [pair_norm_gains],
        [pair_bias_matrix.T],
        scratch=[
            homolog_embedding.shape,
            pair_input_tensor.shape,
            pair_norm_gains.shape,
            (heads, pair_width),
        ],
        sems=[4, parts],
    )
    (bias,) = call_near(
        functools.partial(bias_rows_kernel, n_cols),
        [(heads, residues, length)],
        *trade([bias] * n_cols, columns),
        scratch=[(n_cols,) + bias_block],
    )
    msa, bias = lax.optimization_barrier((msa, bias))
    msa = lax.all_to_all(msa, "gi", 0, 0, tiled=True)
    bias = trade([bias] * per_part, "gi")
    (msa_first,) = call(
        functools.partial(row_kernel, n_branch, n_gj, per_part, few),
        [(n_half, each, width)],
        msa,
        *[[block] for block in bias],
        [layernorm_scales],
        [horizontal_qkvg_kernel],
        [horizontal_final_kernel],
        scratch=[(per_part, heads, residues, length)]
        + [w.shape for w in (layernorm_scales, horizontal_qkvg_kernel, horizontal_final_kernel)],
        sems=[3 + per_part],
    )
    pair, msa_first = lax.optimization_barrier((pair_input_tensor, msa_first))

    msa_first = lax.all_to_all(msa_first, everyone, 0, 0, tiled=True, axis_index_groups=halves)
    count = n_half * each
    weights = (
        layernorm_scales,
        vertical_qkvg_kernel,
        vertical_final_kernel,
        feedforward_expand_kernel,
        feedforward_shrink_kernel,
        dyadic_sides_kernel.T,
    )
    left, right, alignment = call_near(
        functools.partial(column_kernel, few, heads),
        [(outer_width, count), (n_gi, outer_width, count), (count, width)],
        msa_first.reshape(count, width),
        *weights,
    )
    alignment = call_near(
        functools.partial(msa_blocks_kernel, n_branch, n_gj),
        [(per_part, each, width)] * n_cols,
        alignment,
        scratch=[(n_cols, per_part, each, width)],
    )
    pair = call_near(
        functools.partial(pair_blocks_kernel, few, residues),
        [(positions // n_cols, pair_width)] * n_cols,
        pair.reshape(positions, pair_width),
        scratch=[(positions, pair_width)],
    )
    pair = trade(pair, columns)
    right = lax.all_to_all(right, "gi", 0, 0, tiled=True)
    left = trade([left] * n_cols, columns)
    alignment = [block.reshape(-1, width) for block in trade(alignment, columns)]
    share = max(pair_width // n_all, 1)
    slots = pair_width // share
    triangle = triangle_input_matrix[:, : 4 * pair_width].T.reshape(4, slots, share, pair_width)
    triangle = jnp.stack(
        [jnp.stack([triangle[n], triangle[n + 2]], axis=1) for n in range(2)]
    ).reshape(4 * pair_width, pair_width)
    matrix = outer_output_matrix.reshape(outer_width, outer_width // per, per, pair_width)
    matrix = jnp.transpose(matrix, (3, 2, 1, 0)).reshape(pair_width, -1)
    tri, *first = call_near(
        functools.partial(pair_kernel, few, n_gi, n_cols),
        [(slots, positions // lanes, 2 * share, lanes)]
        + [(positions // n_cols, pair_width)] * n_cols,
        *left,
        *pair,
        right.reshape(n_gi * outer_width, count),
        pair_norm_gains[1][:, None],
        matrix,
        triangle,
        scratch=[
            (n_cols, outer_width, count),
            (positions, pair_width),
            (positions, pair_width),
            (positions, pair_width),
        ],
    )

    first, gate = call_near(
        functools.partial(gather_pair_kernel, few, n_cols, residues),
        [(positions, pair_width)] * 2,
        pair_norm_gains[1:2],
        triangle_input_matrix[:, 4 * pair_width :],
        *trade(first, columns),
        scratch=[(positions, pair_width)],
    )
    tile = (rows, residues, width)
    scratch = [(n_cols, rows * few, width)]
    packed = share * n_all == pair_width and share == few and few == per
    gain, last = pair_norm_gains[2], triangle_output_matrix
    if packed:
        tri = lax.all_to_all(tri, everyone, 0, 0, tiled=True)
        product, alignment_output = call_near(
            functools.partial(triangle_kernel, few, n_branch, n_gj),
            [(n_all, residues, lanes), tile],
            tri.reshape(-1, lanes),
            *alignment,
            scratch=[(lanes, lanes)] + scratch,
        )
        product = lax.all_to_all(product, everyone, 0, 0, tiled=True)
        product = product.reshape(n_all * residues, lanes)
        gain = gain.reshape(n_all, share).T.reshape(-1)
        last = jnp.swapaxes(last.reshape(n_all, share, pair_width), 0, 1).reshape(last.shape)
    else:
        (alignment_output,) = call_near(
            functools.partial(gather_msa_kernel, few, n_cols),
            [tile],
            *alignment,
            scratch=scratch,
        )
        tri = jnp.transpose(tri.reshape(slots, -1, 2, share, lanes), (2, 1, 4, 0, 3))
        tri = tri.reshape(2, residues, pair_cols, pair_width)
        right_columns = lax.all_gather(tri[1], "gi", axis=0, tiled=True)
        product = lax.psum_scatter(
            jnp.einsum("jkc,ikc->jic", right_columns, tri[0], precision=precise),
            columns,
            scatter_dimension=0,
            tiled=True,
        ).reshape(groups, n_cols, few, residues, pair_width)
        product = jnp.transpose(product, (4, 3, 2, 0, 1)).reshape(pair_width, positions)
    (pair_output_tensor,) = call_near(
        functools.partial(final_kernel, few, n_cols, residues, packed),
        [(positions, pair_width)],
        product,
        first,
        gate,
        gain[:, None],
        last.T,
    )
    return (
        alignment_output,
        pair_output_tensor.reshape(residues, pair_cols, pair_width),
    )


def solution(mesh):
    tile, grid = P(("branch", "gj"), "gi", None), P("gi", ("branch", "gj"), None)
    return jax.shard_map(
        per_device,
        mesh=mesh,
        in_specs=(tile, grid) + (P(),) * 13,
        out_specs=(tile, grid),
        check_vma=False,
    )
```

```python
import functools
import math

import jax
import jax.numpy as jnp
from jax import lax
from jax.experimental import pallas as pl
from jax.experimental.pallas import tpu as pltpu
from jax.sharding import PartitionSpec as P

epsilon = 1e-05
precise = lax.Precision.HIGH
everyone = ("branch", "gi", "gj")
columns = ("branch", "gj")
lanes = 128
far = pl.BlockSpec(memory_space=pl.ANY)
vmem = pl.BlockSpec(memory_space=pltpu.VMEM)
params = pltpu.CompilerParams(vmem_limit_bytes=16 * 1024 * 1024)


def layer_normalise(values, norm_gain, axis=-1):
    average = jnp.mean(values, axis=axis, keepdims=True)
    centred = values - average
    variance = jnp.mean(centred * centred, axis=axis, keepdims=True)
    return centred * lax.rsqrt(variance + epsilon) * norm_gain


def apply_projection(values, weight):
    return jnp.einsum("...c,cd->...d", values, weight, precision=precise)


def sigmoid(values):
    return 1.0 / (1.0 + jnp.exp(-values))


def split(values):
    high = values.astype(jnp.bfloat16)
    return high, (values - high.astype(jnp.float32)).astype(jnp.bfloat16)


def multiply(left, right, across=False):
    numbers = (((1,), (1 if across else 0,)), ((), ()))

    def one(a, b):
        return lax.dot_general(a, b, numbers, preferred_element_type=jnp.float32)

    (lh, ll), (rh, rl) = split(left), split(right)
    return one(lh, rh) + (one(lh, rl) + one(ll, rh))


def swap_lane_groups(arrays):
    n, arrays = len(arrays), list(arrays)
    width = lanes // n
    wide = arrays[0].shape[-1]
    lane = lax.broadcasted_iota(jnp.int32, arrays[0].shape, arrays[0].ndim - 1)
    group = lax.rem(lane, lanes) // width
    axis = arrays[0].ndim - 1
    step = 1
    while step < n:
        upper = (group // step) % 2 == 1
        for low in range(n):
            if low & step:
                continue
            a, b = arrays[low], arrays[low + step]
            arrays[low] = jnp.where(upper, pltpu.roll(b, step * width, axis), a)
            arrays[low + step] = jnp.where(
                upper, b, pltpu.roll(a, wide - step * width, axis)
            )
        step *= 2
    return arrays


def head_masks(shape, heads):
    column = lax.broadcasted_iota(jnp.int32, shape, 1)
    return [column // (shape[1] // heads) == h for h in range(heads)]


def attend(query, key, value, bias, heads, allowed=None):
    count, inner = query.shape
    masks = head_masks((count, inner), heads)
    spread = jnp.concatenate([jnp.where(m, query, 0.0) for m in masks], axis=0)
    scores = multiply(spread, key, across=True) * (1.0 / math.sqrt(inner // heads))
    if bias is not None:
        scores = scores + bias
    if allowed is not None:
        scores = jnp.where(allowed, scores, -1e30)
    weights = jnp.exp(scores - jnp.max(scores, axis=-1, keepdims=True))
    weights = weights / jnp.sum(weights, axis=-1, keepdims=True)
    mixed = multiply(weights, value)
    result = jnp.where(masks[0], mixed[:count], 0.0)
    for h in range(1, heads):
        result = result + jnp.where(masks[h], mixed[h * count : (h + 1) * count], 0.0)
    return result


def start_copies(pairs, sems):
    copies = [pltpu.make_async_copy(a, b, sems.at[n]) for n, (a, b) in enumerate(pairs)]
    for copy in copies:
        copy.start()
    return copies


def wait_all(copies):
    for copy in copies:
        copy.wait()


def column_index():
    return lax.axis_index("branch") * lax.axis_size("gj") + lax.axis_index("gj")


def call(kernel, outs, *operands, scratch=(), sems=(), grant=None):
    def bare(item):
        return item[0] if isinstance(item, list) else item

    n_in, n_out = len(operands), len(outs)
    near_in = [n for n, item in enumerate(operands) if not isinstance(item, list)]
    near_out = [n for n, item in enumerate(outs) if not isinstance(item, list)]
    shapes = [operands[n].shape for n in near_in] + [outs[n] for n in near_out]

    def body(*refs):
        inputs, results = list(refs[:n_in]), list(refs[n_in : n_in + n_out])
        local = refs[n_in + n_out : n_in + n_out + len(shapes)]
        rest, own_sems = refs[n_in + n_out + len(shapes) : -1], refs[-1]
        pairs = list(zip([inputs[n] for n in near_in], local))
        back = list(zip(local[len(near_in) :], [results[n] for n in near_out]))
        for n, ref in zip(near_in, local):
            inputs[n] = ref
        for n, ref in zip(near_out, local[len(near_in) :]):
            results[n] = ref
        copies = start_copies(pairs, own_sems)
        kernel(lambda: wait_all(copies), *inputs, *results, *rest)
        wait_all(start_copies(back, own_sems))

    return pl.pallas_call(
        body,
        out_shape=[jax.ShapeDtypeStruct(bare(out), jnp.float32) for out in outs],
        in_specs=[far] * n_in,
        out_specs=[far] * n_out,
        scratch_shapes=[pltpu.VMEM(shape, jnp.float32) for shape in shapes + list(scratch)]
        + [pltpu.SemaphoreType.DMA((n,)) for n in sems]
        + [pltpu.SemaphoreType.DMA((max(len(near_in), len(near_out), 1),))],
        compiler_params=pltpu.CompilerParams(vmem_limit_bytes=grant),
    )(*[bare(operand) for operand in operands])


def call_near(kernel, outs, *operands, scratch=()):
    return pl.pallas_call(
        lambda *refs: kernel(lambda: None, *refs),
        out_shape=[jax.ShapeDtypeStruct(out, jnp.float32) for out in outs],
        in_specs=[vmem] * len(operands),
        out_specs=[vmem] * len(outs),
        scratch_shapes=[pltpu.VMEM(shape, jnp.float32) for shape in scratch],
        compiler_params=params,
    )(*operands)


def spread(me, refs, slots):
    for k, ref in enumerate(refs):
        slots[me ^ k] = ref[...]


def spread_rows(me, refs, slots):
    for k, ref in enumerate(refs):
        count = ref.shape[0]
        slots[pl.ds(pl.multiple_of((me ^ k) * count, 8), count), :] = ref[...]


def bias_kernel(ready, pair_ref, gains_ref, matrix_ref, out_ref):
    residues, pair_cols, _ = pair_ref.shape
    heads = matrix_ref.shape[0]
    per = lanes // pair_cols
    ready()
    normal = layer_normalise(pair_ref[...], gains_ref[0:1, :][None])
    for i in range(residues):
        here = multiply(matrix_ref[...], normal[i], across=True)
        for h in range(heads):
            out_ref[h // per, i : i + 1, pl.ds(h % per * pair_cols, pair_cols)] = here[h : h + 1]


def repeat_kernel(ready, msa_ref, copies_far, sems):
    rows = msa_ref.shape[0]
    ready()
    wait_all(
        start_copies(
            [
                (msa_ref, copies_far.at[pl.ds(n * rows, rows)])
                for n in range(copies_far.shape[0] // rows)
            ],
            sems,
        )
    )


def pair_blocks_kernel(few, residues, ready, pair_ref, *rest):
    chunks, slots = rest[:-1], rest[-1]
    n_cols = len(chunks)
    block = chunks[0].shape[0]
    groups = block // (residues * few)
    me = column_index()
    ready()
    for c in range(n_cols):
        for o in range(groups):
            for f in range(few):
                source = pl.ds((o * n_cols + c) * few + f, residues, stride=groups * n_cols * few)
                target = pl.ds(c * block + f * groups + o, residues, stride=few * groups)
                slots[target, :] = pair_ref[source, :]
    for k in range(n_cols):
        start = pl.multiple_of((me ^ k) * block, 8)
        chunks[k][...] = slots[pl.ds(start, block), :]


def bias_rows_kernel(n_cols, ready, *rest):
    blocks, (out_ref, slots) = rest[:n_cols], rest[n_cols:]
    ready()
    spread(column_index(), blocks, slots)
    count = slots.shape[1]
    per = out_ref.shape[0] // count
    for block in range(count):
        tiles = [[] for _ in range(per)]
        for tile in range(n_cols // per):
            group = [slots[c, block] for c in range(tile * per, (tile + 1) * per)]
            for k, piece in enumerate(swap_lane_groups(group)):
                tiles[k].append(piece)
        for k in range(per):
            out_ref[block * per + k] = jnp.concatenate(tiles[k], axis=1)


def row_kernel(n_branch, n_gj, per_part, few, ready, msa_ref, *rest):
    bias_refs, rest = rest[:per_part], rest[per_part:]
    gains_far, qkvg_far, final_far, out_ref, slots, gains_ref, qkvg_ref, final_ref, sems = rest
    mine = lax.axis_index("gi")
    me, part = lax.rem(mine, per_part), lax.div(mine, per_part)
    copies = start_copies(
        [(gains_far, gains_ref), (qkvg_far, qkvg_ref), (final_far, final_ref)]
        + [(ref, slots.at[me ^ k]) for k, ref in enumerate(bias_refs)],
        sems,
    )
    ready()
    _, residues, width = msa_ref.shape
    _, heads, _, length = slots.shape
    n_gi = length // residues
    rows = msa_ref.shape[0] // n_gi
    inner = final_ref.shape[0]
    queries = per_part * residues
    tokens = jnp.concatenate(
        [msa_ref[g * rows + r] for r in range(rows) for g in range(n_gi)], axis=0
    )
    first = part * (per_part * rows)
    asking = msa_ref[pl.ds(first, per_part * rows)]
    asking = jnp.concatenate(
        [asking[g * rows + r] for r in range(rows) for g in range(per_part)], axis=0
    )
    tokens = layer_normalise(tokens, 1.0)
    normal = layer_normalise(asking, 1.0)
    wait_all(copies[:2])
    gain = gains_ref[0:1, :]
    key_value = multiply(tokens * gain, qkvg_ref[:, inner : 3 * inner])
    normal = normal * gain
    query = multiply(normal, qkvg_ref[:, :inner])
    gate = multiply(normal, qkvg_ref[:, 3 * inner :])
    wait_all(copies[2:])
    bias = jnp.concatenate(
        [slots[g, h] for h in range(heads) for g in range(per_part)], axis=0
    )
    attended = []
    for r in range(rows):
        keys = key_value[r * length : (r + 1) * length, :inner]
        values = key_value[r * length : (r + 1) * length, inner:]
        attended.append(
            attend(query[r * queries : (r + 1) * queries], keys, values, bias, heads)
        )
    attended = jnp.concatenate(attended, axis=0)
    result = asking + multiply(sigmoid(gate) * attended, final_ref[...])
    for b in range(n_branch):
        for g in range(per_part):
            for j in range(n_gj):
                start = g * residues + (b * n_gj + j) * few
                out_ref[(b * per_part + g) * n_gj + j] = jnp.concatenate(
                    [result[r * queries + start : r * queries + start + few] for r in range(rows)],
                    axis=0,
                )


def column_kernel(
    few, heads, ready, msa_ref, gains_ref, qkvg_ref, final_ref, expand_ref, shrink_ref, sides_ref,
    left_ref, right_ref, out_ref
):
    ready()
    count, width = msa_ref.shape
    inner = final_ref.shape[0]
    half = sides_ref.shape[0] // 2
    first = msa_ref[...]
    projected = multiply(layer_normalise(first, gains_ref[1:2, :]), qkvg_ref[...])
    query, key, value, gate = (projected[:, k * inner : (k + 1) * inner] for k in range(4))
    allowed = None
    if few > 1:
        shape = (heads * count, count)
        asks = lax.broadcasted_iota(jnp.int32, shape, 0)
        holds = lax.broadcasted_iota(jnp.int32, shape, 1)
        allowed = lax.rem(asks, few) == lax.rem(holds, few)
    attended = attend(query, key, value, None, heads, allowed)
    second = first + multiply(sigmoid(gate) * attended, final_ref[...])
    expanded = multiply(layer_normalise(second, gains_ref[2:3, :]), expand_ref[...])
    third = second + multiply(jnp.maximum(expanded, 0.0), shrink_ref[...])
    out_ref[...] = third
    factors = multiply(sides_ref[...], layer_normalise(third, gains_ref[3:4, :]), across=True)
    left_ref[...] = factors[:half]
    for g in range(right_ref.shape[0]):
        right_ref[g] = factors[half:]


def msa_blocks_kernel(n_branch, n_gj, ready, msa_ref, *rest):
    chunks, slots = rest[:-1], rest[-1]
    per_part, each = slots.shape[1:3]
    ready()
    for b in range(n_branch):
        for g in range(per_part):
            for j in range(n_gj):
                start = ((b * per_part + g) * n_gj + j) * each
                slots[b * n_gj + j, g] = msa_ref[start : start + each]
    for k, chunk in enumerate(chunks):
        chunk[...] = slots[column_index() ^ k]


def gather_msa(few, me, blocks, out_ref, slots):
    n_cols = len(blocks)
    spread(me, blocks, slots)
    for r in range(out_ref.shape[0]):
        out_ref[r] = jnp.concatenate(
            [slots[c, r * few : (r + 1) * few] for c in range(n_cols)], axis=0
        )


def gather_msa_kernel(few, n_cols, ready, *rest):
    ready()
    gather_msa(few, column_index(), rest[:n_cols], *rest[n_cols:])


def gather_pair_kernel(few, n_cols, residues, ready, gains_ref, matrix_ref, *rest):
    blocks, (first_ref, gate_ref, slots) = rest[:n_cols], rest[n_cols:]
    ready()
    spread_rows(column_index(), blocks, slots)
    block = blocks[0].shape[0]
    count = residues * few
    groups = block // count
    for c in range(n_cols):
        for o in range(groups):
            first_ref[pl.ds(o * n_cols + c, count, stride=groups * n_cols), :] = slots[
                pl.ds(c * block + o * count, count), :
            ]
    width = first_ref.shape[1]
    normal = layer_normalise(first_ref[...], gains_ref[1:2, :])
    gate_ref[...] = sigmoid(
        multiply(normal, matrix_ref[pl.ds(4 * width, width), :], across=True)
    )


def triangle_kernel(few, n_branch, n_gj, ready, tri_ref, *rest):
    n_cols = n_branch * n_gj
    blocks, (out_ref, msa_out, product_ref, slots) = rest[:n_cols], rest[n_cols:]
    ready()
    gather_msa(few, column_index(), blocks, msa_out, slots)
    n_all, rows, _ = out_ref.shape
    n_gi = n_all // n_cols
    share = few
    tiles = rows // few
    each = 2 * share
    wide = lanes // few
    group = lax.broadcasted_iota(jnp.int32, (n_gi * tiles, lanes), 1) // wide
    products = []
    for q in range(share):
        left, right = [], []
        for c in range(n_cols):
            base = (c // n_gj * n_all // n_branch + c % n_gj) * tiles * each
            step = n_gj * tiles * each
            here = jnp.concatenate(
                [
                    tri_ref[pl.ds(base + t * each + q, n_gi, stride=step), :]
                    for t in range(tiles)
                ],
                axis=0,
            )
            left.append(
                jnp.concatenate(
                    [jnp.where(group == i, here, 0.0) for i in range(few)], axis=0
                )
            )
            here = jnp.concatenate(
                [
                    tri_ref[pl.ds(base + g * step + share + q, tiles, stride=each), :]
                    for g in range(n_gi)
                ],
                axis=0,
            )
            rolled = [here] + [pltpu.roll(here, k * wide, 1) for k in range(1, few)]
            copies = []
            for j in range(few):
                copy = rolled[0]
                for k in range(1, few):
                    copy = jnp.where(group == (j + k) % few, rolled[k], copy)
                copies.append(copy)
            step = n_gi * tiles // n_cols
            right.append(
                jnp.concatenate(
                    [copy[k * step : (k + 1) * step] for k in range(n_cols) for copy in copies],
                    axis=0,
                )
            )
        products.append(
            multiply(
                jnp.concatenate(left, axis=1), jnp.concatenate(right, axis=1), across=True
            )
        )
    for c, product in enumerate(swap_lane_groups(products)):
        product_ref[...] = product
        for g in range(n_gi):
            out_ref[(c // n_gj * n_gi + g) * n_gj + c % n_gj] = product_ref[pl.ds(g, rows, stride=n_gi), :]


def pair_kernel(
    few, n_gi, n_cols, share, ready, *rest
):
    left_refs, pair_refs = rest[:n_cols], rest[n_cols : 2 * n_cols]
    right_ref, gains_ref, matrix_ref, triangle_ref, tri_ref = rest[2 * n_cols : 2 * n_cols + 5]
    chunks = rest[2 * n_cols + 5 : 3 * n_cols + 5]
    rest = rest[3 * n_cols + 5 :]
    left_ref, slots, pair_ref, first_ref, sides_ref = rest
    me = column_index()
    groups_j = n_gi // n_cols
    block = pair_refs[0].shape[0]
    ready()
    spread(me, left_refs, left_ref)
    spread_rows(me, pair_refs, slots)
    _, wide, count = left_ref.shape
    half = block // groups_j
    all_rows = count // few
    residues = n_cols * few
    pair_cols = n_gi * few
    per = lanes // pair_cols
    groups = residues // per
    width = pair_ref.shape[1]
    owner = lax.rem(lax.broadcasted_iota(jnp.int32, (1, count), 1), few)
    left = []
    for c in range(n_cols):
        here = left_ref[c]
        for f in range(few):
            own = jnp.where(owner == f, here, 0.0)
            total = own
            for other in range(few):
                if other != f:
                    total = total + pltpu.roll(own, (other - f) % count, 1)
            left.append(total)
    left = jnp.concatenate(left, axis=0) * (1.0 / all_rows)
    right = []
    for d in range(wide):
        here = right_ref[pl.ds(d, n_gi, stride=wide), :]
        right += [jnp.where(owner == f, here, 0.0) for f in range(few)]
    right = jnp.concatenate(right, axis=0)
    outer = multiply(left, right, across=True)
    outputs = []
    for g in range(groups):
        swapped = swap_lane_groups(
            [outer[(g * per + i) * wide : (g * per + i + 1) * wide] for i in range(per)]
        )
        stacked = [
            s[:, t * lanes : (t + 1) * lanes] for s in swapped for t in range(wide // per)
        ]
        outputs.append(jnp.concatenate(stacked, axis=0))
    for c in range(n_cols):
        for o in range(groups_j):
            pair_ref[pl.ds(c * groups_j + o, half, stride=n_gi), :] = slots[
                pl.ds(c * block + o, half, stride=groups_j), :
            ]
    update = multiply(matrix_ref[...], jnp.concatenate(outputs, axis=1))
    first = pair_ref[...].T + update
    projected = multiply(
        triangle_ref[pl.ds(0, 4 * width), :] * gains_ref[1:2, :],
        layer_normalise(first, 1.0, axis=0),
    )
    for n in range(2):
        value = projected[2 * n * width : (2 * n + 1) * width]
        tri = sigmoid(projected[(2 * n + 1) * width : (2 * n + 2) * width]) * value
        for g in range(groups):
            sides_ref[...] = tri[:, g * lanes : (g + 1) * lanes]
            for q in range(share):
                rows = pl.ds(g * 2 * share + n * share + q, width // share, stride=2 * share * groups)
                tri_ref[rows, :] = sides_ref[pl.ds(q, width // share, stride=share), :]
    first_ref[...] = first.T
    for k in range(n_cols):
        for o in range(groups_j):
            rows = pl.ds((me ^ k) * groups_j + o, half, stride=n_gi)
            chunks[k][pl.ds(o * half, half), :] = first_ref[rows, :]


def final_kernel(
    few, residues, packed, ready, product_ref, first_ref, gate_ref, gains_ref, matrix_ref, out_ref,
    channels_ref
):
    positions = out_ref.shape[0]
    ready()
    if packed:
        tiles = residues // few
        tall = product_ref.shape[0] // residues
        product = []
        for t in range(tiles):
            here = [
                product_ref[pl.ds(i * tiles + t, tall, stride=residues), :] for i in range(few)
            ]
            for q, piece in enumerate(swap_lane_groups(here)):
                channels_ref[pl.ds(q, tall, stride=few), :] = piece
            product.append(channels_ref[...])
        product = jnp.concatenate(product, axis=1)
    else:
        product = product_ref[...]
    normal = layer_normalise(product, 1.0, axis=0).T * gains_ref[2:3, :]
    result = first_ref[...] + gate_ref[...] * multiply(normal, matrix_ref[...])
    count = positions // (residues * few)
    for i in range(residues):
        for f in range(few):
            start = (i * few + f) * count
            out_ref[pl.ds(i * few * count + f, count, stride=few), :] = result[
                start : start + count
            ]


def per_device(
    homolog_embedding,
    pair_input_tensor,
    layernorm_scales,
    pair_norm_gains,
    pair_bias_matrix,
    horizontal_qkvg_kernel,
    horizontal_final_kernel,
    vertical_qkvg_kernel,
    vertical_final_kernel,
    feedforward_expand_kernel,
    feedforward_shrink_kernel,
    dyadic_sides_kernel,
    outer_output_matrix,
    triangle_input_matrix,
    triangle_output_matrix,
):
    rows, residues, width = homolog_embedding.shape
    pair_cols, pair_width = pair_input_tensor.shape[1:]
    heads = pair_bias_matrix.shape[1]
    outer_width = dyadic_sides_kernel.shape[1] // 2
    n_branch, n_gi, n_gj = (lax.axis_size(name) for name in everyone)
    n_cols = n_branch * n_gj
    n_all = n_cols * n_gi
    length = residues * n_gi
    few = residues // n_cols
    groups = n_gi // n_cols
    parts = 2
    per_part = n_gi // parts
    own_rows = rows // per_part

    def trade(blocks, axes):
        n = lax.axis_size(axes)
        return [blocks[0]] + [
            lax.ppermute(blocks[k], axes, [(t ^ k, t) for t in range(n) if t ^ k < n])
            for k in range(1, len(blocks))
        ]

    halves = [
        [
            (b * n_gi + part * per_part + g) * n_gj + j
            for b in range(n_branch)
            for g in range(per_part)
            for j in range(n_gj)
        ]
        for part in range(parts)
    ]
    n_half = n_cols * per_part
    positions = residues * pair_cols
    each = own_rows * few

    per = lanes // pair_cols
    bias_block = (heads // per, residues, lanes)
    (bias,) = call(
        bias_kernel, [bias_block], pair_input_tensor, pair_norm_gains, pair_bias_matrix.T
    )
    msa, bias = lax.optimization_barrier((homolog_embedding, bias))
    (msa,) = call(repeat_kernel, [[(parts * rows, residues, width)]], msa, sems=[parts])
    msa = lax.all_to_all(msa, "gi", 0, 0, tiled=True)
    (bias,) = call_near(
        functools.partial(bias_rows_kernel, n_cols),
        [(heads, residues, length)],
        *trade([bias] * n_cols, columns),
        scratch=[(n_cols,) + bias_block],
    )
    bias = trade([bias] * per_part, "gi")
    (msa_first,) = call(
        functools.partial(row_kernel, n_branch, n_gj, per_part, few),
        [(n_half, each, width)],
        msa,
        *[[block] for block in bias],
        [layernorm_scales],
        [horizontal_qkvg_kernel],
        [horizontal_final_kernel],
        scratch=[(per_part, heads, residues, length)]
        + [w.shape for w in (layernorm_scales, horizontal_qkvg_kernel, horizontal_final_kernel)],
        sems=[3 + per_part],
        grant=63 * 1024 * 1024,
    )
    pair, msa_first = lax.optimization_barrier((pair_input_tensor, msa_first))

    msa_first = lax.all_to_all(msa_first, everyone, 0, 0, tiled=True, axis_index_groups=halves)
    count = n_half * each
    weights = (
        layernorm_scales,
        vertical_qkvg_kernel,
        vertical_final_kernel,
        feedforward_expand_kernel,
        feedforward_shrink_kernel,
        dyadic_sides_kernel.T,
    )
    left, right, alignment = call_near(
        functools.partial(column_kernel, few, heads),
        [(outer_width, count), (n_gi, outer_width, count), (count, width)],
        msa_first.reshape(count, width),
        *weights,
    )
    alignment = call_near(
        functools.partial(msa_blocks_kernel, n_branch, n_gj),
        [(per_part, each, width)] * n_cols,
        alignment,
        scratch=[(n_cols, per_part, each, width)],
    )
    pair = call_near(
        functools.partial(pair_blocks_kernel, few, residues),
        [(positions // n_cols, pair_width)] * n_cols,
        pair.reshape(positions, pair_width),
        scratch=[(positions, pair_width)],
    )
    pair = trade(pair, columns)
    right = lax.all_to_all(right, "gi", 0, 0, tiled=True)
    left = trade([left] * n_cols, columns)
    alignment = [block.reshape(-1, width) for block in trade(alignment, columns)]
    share = max(pair_width // n_all, 1)
    slots = pair_width // share
    matrix = outer_output_matrix.reshape(outer_width, outer_width // per, per, pair_width)
    matrix = jnp.transpose(matrix, (3, 2, 1, 0)).reshape(pair_width, -1)
    tri, *first = call_near(
        functools.partial(pair_kernel, few, n_gi, n_cols, share),
        [(2 * pair_width * positions // lanes, lanes)]
        + [(positions // n_cols, pair_width)] * n_cols,
        *left,
        *pair,
        right.reshape(n_gi * outer_width, count),
        pair_norm_gains,
        matrix,
        triangle_input_matrix.T,
        scratch=[
            (n_cols, outer_width, count),
            (positions, pair_width),
            (positions, pair_width),
            (positions, pair_width),
            (pair_width, lanes),
        ],
    )

    first, gate = call_near(
        functools.partial(gather_pair_kernel, few, n_cols, residues),
        [(positions, pair_width)] * 2,
        pair_norm_gains,
        triangle_input_matrix.T,
        *trade(first, columns),
        scratch=[(positions, pair_width)],
    )
    tile = (rows, residues, width)
    scratch = [(n_cols, rows * few, width)]
    packed = share * n_all == pair_width and share == few and few == per
    if packed:
        tri = lax.all_to_all(tri.reshape(n_all, -1, lanes), everyone, 0, 0, tiled=True)
        product, alignment_output = call_near(
            functools.partial(triangle_kernel, few, n_branch, n_gj),
            [(n_all, residues, lanes), tile],
            tri.reshape(-1, lanes),
            *alignment,
            scratch=[(lanes, lanes)] + scratch,
        )
        product = lax.all_to_all(product, everyone, 0, 0, tiled=True)
        product = product.reshape(n_all * residues, lanes)
    else:
        (alignment_output,) = call_near(
            functools.partial(gather_msa_kernel, few, n_cols),
            [tile],
            *alignment,
            scratch=scratch,
        )
        tri = jnp.transpose(tri.reshape(slots, -1, 2, share, lanes), (2, 1, 4, 0, 3))
        tri = tri.reshape(2, residues, pair_cols, pair_width)
        right_columns = lax.all_gather(tri[1], "gi", axis=0, tiled=True)
        product = lax.psum_scatter(
            jnp.einsum("jkc,ikc->jic", right_columns, tri[0], precision=precise),
            columns,
            scatter_dimension=0,
            tiled=True,
        ).reshape(groups, n_cols, few, residues, pair_width)
        product = jnp.transpose(product, (4, 3, 2, 0, 1)).reshape(pair_width, positions)
    (pair_output_tensor,) = call_near(
        functools.partial(final_kernel, few, residues, packed),
        [(positions, pair_width)],
        product,
        first,
        gate,
        pair_norm_gains,
        triangle_output_matrix,
        scratch=[(pair_width, lanes)],
    )
    return (
        alignment_output,
        pair_output_tensor.reshape(residues, pair_cols, pair_width),
    )


def solution(mesh):
    tile, grid = P(("branch", "gj"), "gi", None), P("gi", ("branch", "gj"), None)
    return jax.shard_map(
        per_device,
        mesh=mesh,
        in_specs=(tile, grid) + (P(),) * 13,
        out_specs=(tile, grid),
        check_vma=False,
    )
```

```python
import functools
import math

import jax
import jax.numpy as jnp
from jax import lax
from jax.experimental import pallas as pl
from jax.experimental.pallas import tpu as pltpu
from jax.sharding import PartitionSpec as P

epsilon = 1e-05
precise = lax.Precision.HIGH
everyone = ("branch", "gi", "gj")
columns = ("branch", "gj")
lanes = 128
far = pl.BlockSpec(memory_space=pl.ANY)
vmem = pl.BlockSpec(memory_space=pltpu.VMEM)
params = pltpu.CompilerParams(vmem_limit_bytes=16 * 1024 * 1024)


def layer_normalise(values, norm_gain, axis=-1):
    average = jnp.mean(values, axis=axis, keepdims=True)
    centred = values - average
    variance = jnp.mean(centred * centred, axis=axis, keepdims=True)
    return centred * lax.rsqrt(variance + epsilon) * norm_gain


def apply_projection(values, weight):
    return jnp.einsum("...c,cd->...d", values, weight, precision=precise)


def sigmoid(values):
    return 1.0 / (1.0 + jnp.exp(-values))


def split(values):
    high = values.astype(jnp.bfloat16)
    return high, (values - high.astype(jnp.float32)).astype(jnp.bfloat16)


def multiply(left, right, across=False):
    numbers = (((1,), (1 if across else 0,)), ((), ()))

    def one(a, b):
        return lax.dot_general(a, b, numbers, preferred_element_type=jnp.float32)

    lh, ll = left if isinstance(left, tuple) else split(left)
    rh, rl = right if isinstance(right, tuple) else split(right)
    return one(lh, rh) + (one(lh, rl) + one(ll, rh))


def swap_lane_groups(arrays):
    n, arrays = len(arrays), list(arrays)
    width = lanes // n
    wide = arrays[0].shape[-1]
    lane = lax.broadcasted_iota(jnp.int32, arrays[0].shape, arrays[0].ndim - 1)
    group = lax.rem(lane, lanes) // width
    axis = arrays[0].ndim - 1
    step = 1
    while step < n:
        upper = (group // step) % 2 == 1
        for low in range(n):
            if low & step:
                continue
            a, b = arrays[low], arrays[low + step]
            arrays[low] = jnp.where(upper, pltpu.roll(b, step * width, axis), a)
            arrays[low + step] = jnp.where(
                upper, b, pltpu.roll(a, wide - step * width, axis)
            )
        step *= 2
    return arrays


def head_masks(shape, heads):
    column = lax.broadcasted_iota(jnp.int32, shape, 1)
    return [column // (shape[1] // heads) == h for h in range(heads)]


def attend(query, key, value, bias, heads, allowed=None):
    count, inner = query.shape
    masks = head_masks((count, inner), heads)
    spread = jnp.concatenate([jnp.where(m, query, 0.0) for m in masks], axis=0)
    scores = multiply(spread, key, across=True) * (1.0 / math.sqrt(inner // heads))
    if bias is not None:
        scores = scores + bias
    if allowed is not None:
        scores = jnp.where(allowed, scores, -1e30)
    weights = jnp.exp(scores - jnp.max(scores, axis=-1, keepdims=True))
    weights = weights / jnp.sum(weights, axis=-1, keepdims=True)
    mixed = multiply(weights, value)
    result = jnp.where(masks[0], mixed[:count], 0.0)
    for h in range(1, heads):
        result = result + jnp.where(masks[h], mixed[h * count : (h + 1) * count], 0.0)
    return result


def start_copies(pairs, sems):
    copies = [pltpu.make_async_copy(a, b, sems.at[n]) for n, (a, b) in enumerate(pairs)]
    for copy in copies:
        copy.start()
    return copies


def wait_all(copies):
    for copy in copies:
        copy.wait()


def column_index():
    return lax.axis_index("branch") * lax.axis_size("gj") + lax.axis_index("gj")


def call(kernel, outs, *operands, scratch=(), sems=(), grant=None):
    def bare(item):
        return item[0] if isinstance(item, list) else item

    n_in, n_out = len(operands), len(outs)
    near_in = [n for n, item in enumerate(operands) if not isinstance(item, list)]
    near_out = [n for n, item in enumerate(outs) if not isinstance(item, list)]
    shapes = [operands[n].shape for n in near_in] + [outs[n] for n in near_out]

    def body(*refs):
        inputs, results = list(refs[:n_in]), list(refs[n_in : n_in + n_out])
        local = refs[n_in + n_out : n_in + n_out + len(shapes)]
        rest, own_sems = refs[n_in + n_out + len(shapes) : -1], refs[-1]
        pairs = list(zip([inputs[n] for n in near_in], local))
        back = list(zip(local[len(near_in) :], [results[n] for n in near_out]))
        for n, ref in zip(near_in, local):
            inputs[n] = ref
        for n, ref in zip(near_out, local[len(near_in) :]):
            results[n] = ref
        copies = start_copies(pairs, own_sems)
        kernel(lambda: wait_all(copies), *inputs, *results, *rest)
        wait_all(start_copies(back, own_sems))

    return pl.pallas_call(
        body,
        out_shape=[jax.ShapeDtypeStruct(bare(out), jnp.float32) for out in outs],
        in_specs=[far] * n_in,
        out_specs=[far] * n_out,
        scratch_shapes=[pltpu.VMEM(shape, jnp.float32) for shape in shapes + list(scratch)]
        + [pltpu.SemaphoreType.DMA((n,)) for n in sems]
        + [pltpu.SemaphoreType.DMA((max(len(near_in), len(near_out), 1),))],
        compiler_params=pltpu.CompilerParams(vmem_limit_bytes=grant),
    )(*[bare(operand) for operand in operands])


def call_near(kernel, outs, *operands, scratch=()):
    return pl.pallas_call(
        lambda *refs: kernel(lambda: None, *refs),
        out_shape=[
            out if hasattr(out, "dtype") else jax.ShapeDtypeStruct(out, jnp.float32)
            for out in outs
        ],
        in_specs=[vmem] * len(operands),
        out_specs=[vmem] * len(outs),
        scratch_shapes=[pltpu.VMEM(shape, jnp.float32) for shape in scratch],
        compiler_params=params,
    )(*operands)


def spread(me, refs, slots):
    for k, ref in enumerate(refs):
        slots[me ^ k] = ref[...]


def spread_rows(me, refs, slots):
    for k, ref in enumerate(refs):
        count = ref.shape[0]
        slots[pl.ds(pl.multiple_of((me ^ k) * count, 8), count), :] = ref[...]


def bias_kernel(
    ready, msa_far, pair_far, gains_far, matrix_far, copies_far, out_ref, msa_ref, pair_ref,
    gains_ref, matrix_ref, sems, out_sems
):
    rows = msa_far.shape[0]
    repeats = copies_far.shape[0] // rows
    copies = start_copies(
        [(msa_far, msa_ref), (gains_far, gains_ref), (matrix_far, matrix_ref), (pair_far, pair_ref)],
        sems,
    )
    residues, pair_cols, _ = pair_ref.shape
    heads = matrix_ref.shape[0]
    per = lanes // pair_cols
    ready()
    wait_all(copies)
    copies = start_copies(
        [(msa_ref, copies_far.at[pl.ds(n * rows, rows)]) for n in range(repeats)], out_sems
    )
    normal = layer_normalise(pair_ref[...], gains_ref[0:1, :][None])
    for i in range(residues):
        here = multiply(matrix_ref[...], normal[i], across=True)
        for h in range(heads):
            out_ref[h // per, i : i + 1, pl.ds(h % per * pair_cols, pair_cols)] = here[h : h + 1]
    wait_all(copies)


def store_pair(value, high_ref, low_ref):
    high_ref[...], low_ref[...] = split(value)


def column_stage_kernel(few, residues, n_cols, ready, gains_ref, *rest):
    weights, pair_ref, gains_out, rest = rest[:5], rest[5], rest[6], rest[7:]
    pairs, chunks, slots = rest[:10], rest[10 : 10 + n_cols], rest[-1]
    ready()
    gains_out[...] = gains_ref[...]
    for n, ref in enumerate(weights):
        store_pair(ref[...], pairs[2 * n], pairs[2 * n + 1])
    block = chunks[0].shape[0]
    groups = block // (residues * few)
    me = column_index()
    for c in range(n_cols):
        for o in range(groups):
            for f in range(few):
                source = pl.ds((o * n_cols + c) * few + f, residues, stride=groups * n_cols * few)
                target = pl.ds(c * block + f * groups + o, residues, stride=few * groups)
                slots[target, :] = pair_ref[source, :]
    for k in range(n_cols):
        start = pl.multiple_of((me ^ k) * block, 8)
        chunks[k][...] = slots[pl.ds(start, block), :]


def pair_stage_kernel(wide, per, ready, gains_ref, matrix_ref, triangle_ref, *pairs):
    ready()
    width = triangle_ref.shape[0]
    rows = [
        matrix_ref[pl.ds(t * per + d, wide, stride=wide), :]
        for d in range(per)
        for t in range(wide // per)
    ]
    store_pair(jnp.concatenate(rows, axis=0).T, *pairs[:2])
    store_pair(triangle_ref[:, : 4 * width].T * gains_ref[1:2, :], *pairs[2:])


def bias_rows_kernel(n_cols, ready, *rest):
    blocks, (out_ref, slots) = rest[:n_cols], rest[n_cols:]
    ready()
    spread(column_index(), blocks, slots)
    count = slots.shape[1]
    per = out_ref.shape[0] // count
    for block in range(count):
        tiles = [[] for _ in range(per)]
        for tile in range(n_cols // per):
            group = [slots[c, block] for c in range(tile * per, (tile + 1) * per)]
            for k, piece in enumerate(swap_lane_groups(group)):
                tiles[k].append(piece)
        for k in range(per):
            out_ref[block * per + k] = jnp.concatenate(tiles[k], axis=1)


def row_kernel(n_branch, n_gj, per_part, few, ready, msa_ref, *rest):
    bias_refs, rest = rest[:per_part], rest[per_part:]
    gains_far, qkvg_far, final_far, out_ref, slots, gains_ref, qkvg_ref, final_ref, sems = rest
    mine = lax.axis_index("gi")
    me, part = lax.rem(mine, per_part), lax.div(mine, per_part)
    copies = start_copies(
        [(gains_far, gains_ref), (qkvg_far, qkvg_ref), (final_far, final_ref)]
        + [(ref, slots.at[me ^ k]) for k, ref in enumerate(bias_refs)],
        sems,
    )
    ready()
    _, residues, width = msa_ref.shape
    _, heads, _, length = slots.shape
    n_gi = length // residues
    rows = msa_ref.shape[0] // n_gi
    inner = final_ref.shape[0]
    queries = per_part * residues
    tokens = jnp.concatenate(
        [msa_ref[g * rows + r] for r in range(rows) for g in range(n_gi)], axis=0
    )
    first = part * (per_part * rows)
    asking = msa_ref[pl.ds(first, per_part * rows)]
    asking = jnp.concatenate(
        [asking[g * rows + r] for r in range(rows) for g in range(per_part)], axis=0
    )
    tokens = layer_normalise(tokens, 1.0)
    normal = layer_normalise(asking, 1.0)
    wait_all(copies[:2])
    gain = gains_ref[0:1, :]
    key_value = multiply(tokens * gain, qkvg_ref[:, inner : 3 * inner])
    normal = normal * gain
    query = multiply(normal, qkvg_ref[:, :inner])
    gate = multiply(normal, qkvg_ref[:, 3 * inner :])
    wait_all(copies[2:])
    bias = jnp.concatenate(
        [slots[g, h] for h in range(heads) for g in range(per_part)], axis=0
    )
    attended = []
    for r in range(rows):
        keys = key_value[r * length : (r + 1) * length, :inner]
        values = key_value[r * length : (r + 1) * length, inner:]
        attended.append(
            attend(query[r * queries : (r + 1) * queries], keys, values, bias, heads)
        )
    attended = jnp.concatenate(attended, axis=0)
    result = asking + multiply(sigmoid(gate) * attended, final_ref[...])
    for b in range(n_branch):
        for g in range(per_part):
            for j in range(n_gj):
                start = g * residues + (b * n_gj + j) * few
                out_ref[(b * per_part + g) * n_gj + j] = jnp.concatenate(
                    [result[r * queries + start : r * queries + start + few] for r in range(rows)],
                    axis=0,
                )


def column_kernel(few, heads, ready, msa_ref, gains_ref, *rest):
    left_ref, right_ref, out_ref = rest[10:]
    qkvg, final, expand, shrink, sides = (
        (rest[2 * n][...], rest[2 * n + 1][...]) for n in range(5)
    )
    ready()
    count, width = msa_ref.shape
    inner = final[0].shape[0]
    half = sides[0].shape[0] // 2
    first = msa_ref[...]
    projected = multiply(layer_normalise(first, gains_ref[1:2, :]), qkvg)
    query, key, value, gate = (projected[:, k * inner : (k + 1) * inner] for k in range(4))
    allowed = None
    if few > 1:
        shape = (heads * count, count)
        asks = lax.broadcasted_iota(jnp.int32, shape, 0)
        holds = lax.broadcasted_iota(jnp.int32, shape, 1)
        allowed = lax.rem(asks, few) == lax.rem(holds, few)
    attended = attend(query, key, value, None, heads, allowed)
    second = first + multiply(sigmoid(gate) * attended, final)
    expanded = multiply(layer_normalise(second, gains_ref[2:3, :]), expand)
    third = second + multiply(jnp.maximum(expanded, 0.0), shrink)
    out_ref[...] = third
    factors = multiply(sides, layer_normalise(third, gains_ref[3:4, :]), across=True)
    left_ref[...] = factors[:half]
    for g in range(right_ref.shape[0]):
        right_ref[g] = factors[half:]


def msa_blocks_kernel(n_branch, n_gj, ready, msa_ref, *rest):
    chunks, slots = rest[:-1], rest[-1]
    per_part, each = slots.shape[1:3]
    ready()
    for b in range(n_branch):
        for g in range(per_part):
            for j in range(n_gj):
                start = ((b * per_part + g) * n_gj + j) * each
                slots[b * n_gj + j, g] = msa_ref[start : start + each]
    for k, chunk in enumerate(chunks):
        chunk[...] = slots[column_index() ^ k]


def gather_msa(few, me, blocks, out_ref, slots):
    n_cols = len(blocks)
    spread(me, blocks, slots)
    for r in range(out_ref.shape[0]):
        out_ref[r] = jnp.concatenate(
            [slots[c, r * few : (r + 1) * few] for c in range(n_cols)], axis=0
        )


def gather_msa_kernel(few, n_cols, ready, *rest):
    ready()
    gather_msa(few, column_index(), rest[:n_cols], *rest[n_cols:])


def gather_pair_kernel(few, n_cols, residues, ready, gains_ref, matrix_ref, *rest):
    blocks, (first_ref, gate_ref, slots) = rest[:n_cols], rest[n_cols:]
    ready()
    spread_rows(column_index(), blocks, slots)
    block = blocks[0].shape[0]
    count = residues * few
    groups = block // count
    for c in range(n_cols):
        for o in range(groups):
            first_ref[pl.ds(o * n_cols + c, count, stride=groups * n_cols), :] = slots[
                pl.ds(c * block + o * count, count), :
            ]
    width = first_ref.shape[1]
    normal = layer_normalise(first_ref[...], gains_ref[1:2, :])
    gate_ref[...] = sigmoid(
        multiply(normal, matrix_ref[:, 4 * width :])
    )


def triangle_kernel(few, n_branch, n_gj, ready, tri_ref, *rest):
    n_cols = n_branch * n_gj
    blocks, (out_ref, msa_out, product_ref, slots) = rest[:n_cols], rest[n_cols:]
    ready()
    gather_msa(few, column_index(), blocks, msa_out, slots)
    n_all, rows, _ = out_ref.shape
    n_gi = n_all // n_cols
    share = few
    tiles = rows // few
    each = 2 * share
    wide = lanes // few
    group = lax.broadcasted_iota(jnp.int32, (n_gi * tiles, lanes), 1) // wide
    products = []
    for q in range(share):
        left, right = [], []
        for c in range(n_cols):
            base = (c // n_gj * n_all // n_branch + c % n_gj) * tiles * each
            step = n_gj * tiles * each
            here = jnp.concatenate(
                [
                    tri_ref[pl.ds(base + t * each + q, n_gi, stride=step), :]
                    for t in range(tiles)
                ],
                axis=0,
            )
            left.append(
                jnp.concatenate(
                    [jnp.where(group == i, here, 0.0) for i in range(few)], axis=0
                )
            )
            here = jnp.concatenate(
                [
                    tri_ref[pl.ds(base + g * step + share + q, tiles, stride=each), :]
                    for g in range(n_gi)
                ],
                axis=0,
            )
            rolled = [here] + [pltpu.roll(here, k * wide, 1) for k in range(1, few)]
            copies = []
            for j in range(few):
                copy = rolled[0]
                for k in range(1, few):
                    copy = jnp.where(group == (j + k) % few, rolled[k], copy)
                copies.append(copy)
            step = n_gi * tiles // n_cols
            right.append(
                jnp.concatenate(
                    [copy[k * step : (k + 1) * step] for k in range(n_cols) for copy in copies],
                    axis=0,
                )
            )
        products.append(
            multiply(
                jnp.concatenate(left, axis=1), jnp.concatenate(right, axis=1), across=True
            )
        )
    for c, product in enumerate(swap_lane_groups(products)):
        product_ref[...] = product
        for g in range(n_gi):
            out_ref[(c // n_gj * n_gi + g) * n_gj + c % n_gj] = product_ref[pl.ds(g, rows, stride=n_gi), :]


def pair_kernel(
    few, n_gi, n_cols, share, ready, *rest
):
    left_refs, pair_refs = rest[:n_cols], rest[n_cols : 2 * n_cols]
    right_ref, *staged, tri_ref = rest[2 * n_cols : 2 * n_cols + 6]
    chunks, rest = rest[2 * n_cols + 6 : 3 * n_cols + 6], rest[3 * n_cols + 6 :]
    left_ref, slots, pair_ref, first_ref, sides_ref = rest
    me = column_index()
    groups_j = n_gi // n_cols
    block = pair_refs[0].shape[0]
    ready()
    spread(me, left_refs, left_ref)
    spread_rows(me, pair_refs, slots)
    _, wide, count = left_ref.shape
    half = block // groups_j
    all_rows = count // few
    residues = n_cols * few
    pair_cols = n_gi * few
    per = lanes // pair_cols
    groups = residues // per
    width = pair_ref.shape[1]
    owner = lax.rem(lax.broadcasted_iota(jnp.int32, (1, count), 1), few)
    left = []
    for c in range(n_cols):
        here = left_ref[c]
        for f in range(few):
            own = jnp.where(owner == f, here, 0.0)
            total = own
            for other in range(few):
                if other != f:
                    total = total + pltpu.roll(own, (other - f) % count, 1)
            left.append(total)
    left = jnp.concatenate(left, axis=0) * (1.0 / all_rows)
    right = []
    for d in range(wide):
        here = right_ref[pl.ds(d, n_gi, stride=wide), :]
        right += [jnp.where(owner == f, here, 0.0) for f in range(few)]
    right = jnp.concatenate(right, axis=0)
    outer = multiply(left, right, across=True)
    outputs = []
    for g in range(groups):
        swapped = swap_lane_groups(
            [outer[(g * per + i) * wide : (g * per + i + 1) * wide] for i in range(per)]
        )
        stacked = [
            s[:, t * lanes : (t + 1) * lanes] for s in swapped for t in range(wide // per)
        ]
        outputs.append(jnp.concatenate(stacked, axis=0))
    for c in range(n_cols):
        for o in range(groups_j):
            pair_ref[pl.ds(c * groups_j + o, half, stride=n_gi), :] = slots[
                pl.ds(c * block + o, half, stride=groups_j), :
            ]
    matrix, triangle = ((staged[n][...], staged[n + 1][...]) for n in (0, 2))
    update = multiply(matrix, jnp.concatenate(outputs, axis=1))
    first = pair_ref[...].T + update
    projected = multiply(triangle, layer_normalise(first, 1.0, axis=0))
    for n in range(2):
        value = projected[2 * n * width : (2 * n + 1) * width]
        tri = sigmoid(projected[(2 * n + 1) * width : (2 * n + 2) * width]) * value
        for g in range(groups):
            sides_ref[...] = tri[:, g * lanes : (g + 1) * lanes]
            for q in range(share):
                rows = pl.ds(g * 2 * share + n * share + q, width // share, stride=2 * share * groups)
                tri_ref[rows, :] = sides_ref[pl.ds(q, width // share, stride=share), :]
    first_ref[...] = first.T
    for k in range(n_cols):
        for o in range(groups_j):
            rows = pl.ds((me ^ k) * groups_j + o, half, stride=n_gi)
            chunks[k][pl.ds(o * half, half), :] = first_ref[rows, :]


def final_kernel(
    few, residues, packed, ready, product_ref, first_ref, gate_ref, gains_ref, matrix_ref, out_ref,
    channels_ref
):
    positions = out_ref.shape[0]
    ready()
    if packed:
        tiles = residues // few
        tall = product_ref.shape[0] // residues
        product = []
        for t in range(tiles):
            here = [
                product_ref[pl.ds(i * tiles + t, tall, stride=residues), :] for i in range(few)
            ]
            for q, piece in enumerate(swap_lane_groups(here)):
                channels_ref[pl.ds(q, tall, stride=few), :] = piece
            product.append(channels_ref[...])
        product = jnp.concatenate(product, axis=1)
    else:
        product = product_ref[...]
    normal = layer_normalise(product, 1.0, axis=0).T * gains_ref[2:3, :]
    result = first_ref[...] + gate_ref[...] * multiply(normal, matrix_ref[...])
    count = positions // (residues * few)
    for i in range(residues):
        for f in range(few):
            start = (i * few + f) * count
            out_ref[pl.ds(i * few * count + f, count, stride=few), :] = result[
                start : start + count
            ]


def per_device(
    homolog_embedding,
    pair_input_tensor,
    layernorm_scales,
    pair_norm_gains,
    pair_bias_matrix,
    horizontal_qkvg_kernel,
    horizontal_final_kernel,
    vertical_qkvg_kernel,
    vertical_final_kernel,
    feedforward_expand_kernel,
    feedforward_shrink_kernel,
    dyadic_sides_kernel,
    outer_output_matrix,
    triangle_input_matrix,
    triangle_output_matrix,
):
    rows, residues, width = homolog_embedding.shape
    pair_cols, pair_width = pair_input_tensor.shape[1:]
    heads = pair_bias_matrix.shape[1]
    outer_width = dyadic_sides_kernel.shape[1] // 2
    n_branch, n_gi, n_gj = (lax.axis_size(name) for name in everyone)
    n_cols = n_branch * n_gj
    n_all = n_cols * n_gi
    length = residues * n_gi
    few = residues // n_cols
    groups = n_gi // n_cols
    parts = 2
    per_part = n_gi // parts
    own_rows = rows // per_part

    def trade(blocks, axes):
        n = lax.axis_size(axes)
        return [blocks[0]] + [
            lax.ppermute(blocks[k], axes, [(t ^ k, t) for t in range(n) if t ^ k < n])
            for k in range(1, len(blocks))
        ]

    halves = [
        [
            (b * n_gi + part * per_part + g) * n_gj + j
            for b in range(n_branch)
            for g in range(per_part)
            for j in range(n_gj)
        ]
        for part in range(parts)
    ]
    n_half = n_cols * per_part
    positions = residues * pair_cols
    each = own_rows * few

    per = lanes // pair_cols
    bias_block = (heads // per, residues, lanes)
    msa, bias = call(
        bias_kernel,
        [[(parts * rows, residues, width)], bias_block],
        [homolog_embedding],
        [pair_input_tensor],
        [pair_norm_gains],
        [pair_bias_matrix.T],
        scratch=[
            homolog_embedding.shape,
            pair_input_tensor.shape,
            pair_norm_gains.shape,
            (heads, pair_width),
        ],
        sems=[4, parts],
    )
    msa = lax.all_to_all(msa, "gi", 0, 0, tiled=True)
    (bias,) = call_near(
        functools.partial(bias_rows_kernel, n_cols),
        [(heads, residues, length)],
        *trade([bias] * n_cols, columns),
        scratch=[(n_cols,) + bias_block],
    )
    bias = trade([bias] * per_part, "gi")
    (msa_first,) = call(
        functools.partial(row_kernel, n_branch, n_gj, per_part, few),
        [(n_half, each, width)],
        msa,
        *[[block] for block in bias],
        [layernorm_scales],
        [horizontal_qkvg_kernel],
        [horizontal_final_kernel],
        scratch=[(per_part, heads, residues, length)]
        + [w.shape for w in (layernorm_scales, horizontal_qkvg_kernel, horizontal_final_kernel)],
        sems=[3 + per_part],
        grant=63 * 1024 * 1024,
    )
    pair, msa_first = lax.optimization_barrier((pair_input_tensor, msa_first))
    msa_first = lax.all_to_all(msa_first, everyone, 0, 0, tiled=True, axis_index_groups=halves)
    count = n_half * each
    weights = (
        vertical_qkvg_kernel,
        vertical_final_kernel,
        feedforward_expand_kernel,
        feedforward_shrink_kernel,
        dyadic_sides_kernel.T,
    )
    gains, *weights = call_near(
        functools.partial(column_stage_kernel, few, residues, n_cols),
        [layernorm_scales.shape]
        + [jax.ShapeDtypeStruct(w.shape, jnp.bfloat16) for w in weights for _ in range(2)]
        + [(positions // n_cols, pair_width)] * n_cols,
        layernorm_scales,
        *weights,
        pair.reshape(positions, pair_width),
        scratch=[(positions, pair_width)],
    )
    weights, pair = weights[:-n_cols], trade(weights[-n_cols:], columns)
    left, right, alignment = call_near(
        functools.partial(column_kernel, few, heads),
        [(outer_width, count), (n_gi, outer_width, count), (count, width)],
        msa_first.reshape(count, width),
        gains,
        *weights,
    )
    alignment = call_near(
        functools.partial(msa_blocks_kernel, n_branch, n_gj),
        [(per_part, each, width)] * n_cols,
        alignment,
        scratch=[(n_cols, per_part, each, width)],
    )
    right = lax.all_to_all(right, "gi", 0, 0, tiled=True)
    left = trade([left] * n_cols, columns)
    alignment = [block.reshape(-1, width) for block in trade(alignment, columns)]
    share = max(pair_width // n_all, 1)
    slots = pair_width // share
    matrix, left[0] = lax.optimization_barrier((outer_output_matrix, left[0]))
    staged = call_near(
        functools.partial(pair_stage_kernel, outer_width, per),
        [
            jax.ShapeDtypeStruct(shape, jnp.bfloat16)
            for shape in (matrix.shape[::-1], (4 * pair_width, pair_width))
            for _ in range(2)
        ],
        pair_norm_gains,
        matrix,
        triangle_input_matrix,
    )
    tri, *first = call_near(
        functools.partial(pair_kernel, few, n_gi, n_cols, share),
        [(2 * pair_width * positions // lanes, lanes)]
        + [(positions // n_cols, pair_width)] * n_cols,
        *left,
        *pair,
        right.reshape(n_gi * outer_width, count),
        *staged,
        scratch=[
            (n_cols, outer_width, count),
            (positions, pair_width),
            (positions, pair_width),
            (positions, pair_width),
            (pair_width, lanes),
        ],
    )

    first, gate = call_near(
        functools.partial(gather_pair_kernel, few, n_cols, residues),
        [(positions, pair_width)] * 2,
        pair_norm_gains,
        triangle_input_matrix,
        *trade(first, columns),
        scratch=[(positions, pair_width)],
    )
    tile = (rows, residues, width)
    scratch = [(n_cols, rows * few, width)]
    packed = share * n_all == pair_width and share == few and few == per
    if packed:
        tri = lax.all_to_all(tri.reshape(n_all, -1, lanes), everyone, 0, 0, tiled=True)
        product, alignment_output = call_near(
            functools.partial(triangle_kernel, few, n_branch, n_gj),
            [(n_all, residues, lanes), tile],
            tri.reshape(-1, lanes),
            *alignment,
            scratch=[(lanes, lanes)] + scratch,
        )
        product = lax.all_to_all(product, everyone, 0, 0, tiled=True)
        product = product.reshape(n_all * residues, lanes)
    else:
        (alignment_output,) = call_near(
            functools.partial(gather_msa_kernel, few, n_cols),
            [tile],
            *alignment,
            scratch=scratch,
        )
        tri = jnp.transpose(tri.reshape(slots, -1, 2, share, lanes), (2, 1, 4, 0, 3))
        tri = tri.reshape(2, residues, pair_cols, pair_width)
        right_columns = lax.all_gather(tri[1], "gi", axis=0, tiled=True)
        product = lax.psum_scatter(
            jnp.einsum("jkc,ikc->jic", right_columns, tri[0], precision=precise),
            columns,
            scatter_dimension=0,
            tiled=True,
        ).reshape(groups, n_cols, few, residues, pair_width)
        product = jnp.transpose(product, (4, 3, 2, 0, 1)).reshape(pair_width, positions)
    (pair_output_tensor,) = call_near(
        functools.partial(final_kernel, few, residues, packed),
        [(positions, pair_width)],
        product,
        first,
        gate,
        pair_norm_gains,
        triangle_output_matrix,
        scratch=[(pair_width, lanes)],
    )
    return (
        alignment_output,
        pair_output_tensor.reshape(residues, pair_cols, pair_width),
    )


def solution(mesh):
    tile, grid = P(("branch", "gj"), "gi", None), P("gi", ("branch", "gj"), None)
    return jax.shard_map(
        per_device,
        mesh=mesh,
        in_specs=(tile, grid) + (P(),) * 13,
        out_specs=(tile, grid),
        check_vma=False,
    )
```

```python
import functools
import math

import jax
import jax.numpy as jnp
from jax import lax
from jax.experimental import pallas as pl
from jax.experimental.pallas import tpu as pltpu
from jax.sharding import PartitionSpec as P

epsilon = 1e-05
precise = lax.Precision.HIGH
everyone = ("branch", "gi", "gj")
columns = ("branch", "gj")
lanes = 128
far = pl.BlockSpec(memory_space=pl.ANY)
vmem = pl.BlockSpec(memory_space=pltpu.VMEM)
params = pltpu.CompilerParams(vmem_limit_bytes=16 * 1024 * 1024)


def layer_normalise(values, norm_gain, axis=-1):
    average = jnp.mean(values, axis=axis, keepdims=True)
    centred = values - average
    variance = jnp.mean(centred * centred, axis=axis, keepdims=True)
    return centred * lax.rsqrt(variance + epsilon) * norm_gain


def apply_projection(values, weight):
    return jnp.einsum("...c,cd->...d", values, weight, precision=precise)


def sigmoid(values):
    return 1.0 / (1.0 + jnp.exp(-values))


def split(values):
    high = values.astype(jnp.bfloat16)
    return high, (values - high.astype(jnp.float32)).astype(jnp.bfloat16)


def multiply(left, right, across=False):
    numbers = (((1,), (1 if across else 0,)), ((), ()))

    def one(a, b):
        return lax.dot_general(a, b, numbers, preferred_element_type=jnp.float32)

    (lh, ll), (rh, rl) = split(left), split(right)
    return one(lh, rh) + (one(lh, rl) + one(ll, rh))


def swap_lane_groups(arrays):
    n, arrays = len(arrays), list(arrays)
    width = lanes // n
    wide = arrays[0].shape[-1]
    lane = lax.broadcasted_iota(jnp.int32, arrays[0].shape, arrays[0].ndim - 1)
    group = lax.rem(lane, lanes) // width
    axis = arrays[0].ndim - 1
    step = 1
    while step < n:
        upper = (group // step) % 2 == 1
        for low in range(n):
            if low & step:
                continue
            a, b = arrays[low], arrays[low + step]
            arrays[low] = jnp.where(upper, pltpu.roll(b, step * width, axis), a)
            arrays[low + step] = jnp.where(
                upper, b, pltpu.roll(a, wide - step * width, axis)
            )
        step *= 2
    return arrays


def head_masks(shape, heads):
    column = lax.broadcasted_iota(jnp.int32, shape, 1)
    return [column // (shape[1] // heads) == h for h in range(heads)]


def attend(query, key, value, bias, heads, allowed=None):
    count, inner = query.shape
    masks = head_masks((count, inner), heads)
    spread = jnp.concatenate([jnp.where(m, query, 0.0) for m in masks], axis=0)
    scores = multiply(spread, key, across=True) * (1.0 / math.sqrt(inner // heads))
    if bias is not None:
        scores = scores + bias
    if allowed is not None:
        scores = jnp.where(allowed, scores, -1e30)
    weights = jnp.exp(scores - jnp.max(scores, axis=-1, keepdims=True))
    weights = weights / jnp.sum(weights, axis=-1, keepdims=True)
    mixed = multiply(weights, value)
    result = jnp.where(masks[0], mixed[:count], 0.0)
    for h in range(1, heads):
        result = result + jnp.where(masks[h], mixed[h * count : (h + 1) * count], 0.0)
    return result


def start_copies(pairs, sems):
    copies = [pltpu.make_async_copy(a, b, sems.at[n]) for n, (a, b) in enumerate(pairs)]
    for copy in copies:
        copy.start()
    return copies


def wait_all(copies):
    for copy in copies:
        copy.wait()


def column_index():
    return lax.axis_index("branch") * lax.axis_size("gj") + lax.axis_index("gj")


def call(kernel, outs, *operands, scratch=(), sems=()):
    def bare(item):
        return item[0] if isinstance(item, list) else item

    n_in, n_out = len(operands), len(outs)
    near_in = [n for n, item in enumerate(operands) if not isinstance(item, list)]
    near_out = [n for n, item in enumerate(outs) if not isinstance(item, list)]
    shapes = [operands[n].shape for n in near_in] + [outs[n] for n in near_out]

    def body(*refs):
        inputs, results = list(refs[:n_in]), list(refs[n_in : n_in + n_out])
        local = refs[n_in + n_out : n_in + n_out + len(shapes)]
        rest, own_sems = refs[n_in + n_out + len(shapes) : -1], refs[-1]
        pairs = list(zip([inputs[n] for n in near_in], local))
        back = list(zip(local[len(near_in) :], [results[n] for n in near_out]))
        for n, ref in zip(near_in, local):
            inputs[n] = ref
        for n, ref in zip(near_out, local[len(near_in) :]):
            results[n] = ref
        copies = start_copies(pairs, own_sems)
        kernel(lambda: wait_all(copies), *inputs, *results, *rest)
        wait_all(start_copies(back, own_sems))

    return pl.pallas_call(
        body,
        out_shape=[jax.ShapeDtypeStruct(bare(out), jnp.float32) for out in outs],
        in_specs=[far] * n_in,
        out_specs=[far] * n_out,
        scratch_shapes=[pltpu.VMEM(shape, jnp.float32) for shape in shapes + list(scratch)]
        + [pltpu.SemaphoreType.DMA((n,)) for n in sems]
        + [pltpu.SemaphoreType.DMA((max(len(near_in), len(near_out), 1),))],
    )(*[bare(operand) for operand in operands])


def call_near(kernel, outs, *operands, scratch=()):
    return pl.pallas_call(
        lambda *refs: kernel(lambda: None, *refs),
        out_shape=[jax.ShapeDtypeStruct(out, jnp.float32) for out in outs],
        in_specs=[vmem] * len(operands),
        out_specs=[vmem] * len(outs),
        scratch_shapes=[pltpu.VMEM(shape, jnp.float32) for shape in scratch],
        compiler_params=params,
    )(*operands)


def spread(me, refs, slots):
    for k, ref in enumerate(refs):
        slots[me ^ k] = ref[...]


def spread_rows(me, refs, slots):
    for k, ref in enumerate(refs):
        count = ref.shape[0]
        slots[pl.ds(pl.multiple_of((me ^ k) * count, 8), count), :] = ref[...]


def bias_kernel(
    ready, msa_far, pair_far, gains_far, matrix_far, copies_far, out_ref, msa_ref, pair_ref,
    gains_ref, matrix_ref, sems, out_sems
):
    rows = msa_far.shape[0]
    repeats = copies_far.shape[0] // rows
    copies = start_copies(
        [(msa_far, msa_ref), (gains_far, gains_ref), (matrix_far, matrix_ref), (pair_far, pair_ref)],
        sems,
    )
    residues, pair_cols, _ = pair_ref.shape
    heads = matrix_ref.shape[0]
    per = lanes // pair_cols
    ready()
    wait_all(copies)
    copies = start_copies(
        [(msa_ref, copies_far.at[pl.ds(n * rows, rows)]) for n in range(repeats)], out_sems
    )
    normal = layer_normalise(pair_ref[...], gains_ref[0:1, :][None])
    for i in range(residues):
        here = multiply(matrix_ref[...], normal[i], across=True)
        for h in range(heads):
            out_ref[h // per, i : i + 1, pl.ds(h % per * pair_cols, pair_cols)] = here[h : h + 1]
    wait_all(copies)


def pair_blocks_kernel(few, residues, ready, pair_ref, *rest):
    chunks, slots = rest[:-1], rest[-1]
    n_cols = len(chunks)
    block = chunks[0].shape[0]
    groups = block // (residues * few)
    me = column_index()
    ready()
    for c in range(n_cols):
        for o in range(groups):
            for f in range(few):
                source = pl.ds((o * n_cols + c) * few + f, residues, stride=groups * n_cols * few)
                target = pl.ds(c * block + f * groups + o, residues, stride=few * groups)
                slots[target, :] = pair_ref[source, :]
    for k in range(n_cols):
        start = pl.multiple_of((me ^ k) * block, 8)
        chunks[k][...] = slots[pl.ds(start, block), :]


def bias_part_kernel(per_part, ready, *rest):
    blocks, (out_ref,) = rest[:per_part], rest[per_part:]
    ready()
    spread(lax.rem(lax.axis_index("gi"), per_part), blocks, out_ref)


def row_kernel(n_branch, n_gj, per_part, few, ready, msa_ref, *rest):
    n_cols = n_branch * n_gj
    bias_refs, rest = rest[:n_cols], rest[n_cols:]
    gains_far, qkvg_far, final_far, out_ref, slots, gains_ref, qkvg_ref, final_ref, sems = rest
    me, part = column_index(), lax.div(lax.axis_index("gi"), per_part)
    copies = start_copies(
        [(gains_far, gains_ref), (qkvg_far, qkvg_ref), (final_far, final_ref)]
        + [(ref, slots.at[me ^ k]) for k, ref in enumerate(bias_refs)],
        sems,
    )
    ready()
    _, residues, width = msa_ref.shape
    blocks = slots.shape[2]
    n_gi = lax.axis_size("gi")
    length = n_gi * residues
    per = lanes * n_cols // length
    heads = blocks * per
    rows = msa_ref.shape[0] // n_gi
    inner = final_ref.shape[0]
    queries = per_part * residues
    tokens = jnp.concatenate(
        [msa_ref[g * rows + r] for r in range(rows) for g in range(n_gi)], axis=0
    )
    first = part * (per_part * rows)
    asking = msa_ref[pl.ds(first, per_part * rows)]
    asking = jnp.concatenate(
        [asking[g * rows + r] for r in range(rows) for g in range(per_part)], axis=0
    )
    tokens = layer_normalise(tokens, 1.0)
    normal = layer_normalise(asking, 1.0)
    wait_all(copies[:2])
    gain = gains_ref[0:1, :]
    key_value = multiply(tokens * gain, qkvg_ref[:, inner : 3 * inner])
    normal = normal * gain
    query = multiply(normal, qkvg_ref[:, :inner])
    gate = multiply(normal, qkvg_ref[:, 3 * inner :])
    wait_all(copies[2:])
    pieces = [[] for _ in range(heads)]
    for block in range(blocks):
        for g in range(per_part):
            tiles = [[] for _ in range(per)]
            for tile in range(n_cols // per):
                group = [slots[c, g, block] for c in range(tile * per, (tile + 1) * per)]
                for k, piece in enumerate(swap_lane_groups(group)):
                    tiles[k].append(piece)
            for k in range(per):
                pieces[block * per + k].append(jnp.concatenate(tiles[k], axis=1))
    bias = jnp.concatenate([piece for head in pieces for piece in head], axis=0)
    attended = []
    for r in range(rows):
        keys = key_value[r * length : (r + 1) * length, :inner]
        values = key_value[r * length : (r + 1) * length, inner:]
        attended.append(
            attend(query[r * queries : (r + 1) * queries], keys, values, bias, heads)
        )
    attended = jnp.concatenate(attended, axis=0)
    result = asking + multiply(sigmoid(gate) * attended, final_ref[...])
    for b in range(n_branch):
        for g in range(per_part):
            for j in range(n_gj):
                start = g * residues + (b * n_gj + j) * few
                out_ref[(b * per_part + g) * n_gj + j] = jnp.concatenate(
                    [result[r * queries + start : r * queries + start + few] for r in range(rows)],
                    axis=0,
                )


def column_kernel(
    few, heads, ready, msa_ref, gains_ref, qkvg_ref, final_ref, expand_ref, shrink_ref, sides_ref,
    left_ref, right_ref, out_ref
):
    ready()
    count, width = msa_ref.shape
    inner = final_ref.shape[0]
    half = sides_ref.shape[0] // 2
    first = msa_ref[...]
    projected = multiply(layer_normalise(first, gains_ref[1:2, :]), qkvg_ref[...])
    query, key, value, gate = (projected[:, k * inner : (k + 1) * inner] for k in range(4))
    allowed = None
    if few > 1:
        shape = (heads * count, count)
        asks = lax.broadcasted_iota(jnp.int32, shape, 0)
        holds = lax.broadcasted_iota(jnp.int32, shape, 1)
        allowed = lax.rem(asks, few) == lax.rem(holds, few)
    attended = attend(query, key, value, None, heads, allowed)
    second = first + multiply(sigmoid(gate) * attended, final_ref[...])
    expanded = multiply(layer_normalise(second, gains_ref[2:3, :]), expand_ref[...])
    third = second + multiply(jnp.maximum(expanded, 0.0), shrink_ref[...])
    out_ref[...] = third
    factors = multiply(sides_ref[...], layer_normalise(third, gains_ref[3:4, :]), across=True)
    left_ref[...] = factors[:half]
    for g in range(right_ref.shape[0]):
        right_ref[g] = factors[half:]


def msa_blocks_kernel(n_branch, n_gj, ready, msa_ref, *rest):
    chunks, slots = rest[:-1], rest[-1]
    per_part, each = slots.shape[1:3]
    ready()
    for b in range(n_branch):
        for g in range(per_part):
            for j in range(n_gj):
                start = ((b * per_part + g) * n_gj + j) * each
                slots[b * n_gj + j, g] = msa_ref[start : start + each]
    for k, chunk in enumerate(chunks):
        chunk[...] = slots[column_index() ^ k]


def gather_msa(few, me, blocks, out_ref, slots):
    n_cols = len(blocks)
    spread(me, blocks, slots)
    for r in range(out_ref.shape[0]):
        out_ref[r] = jnp.concatenate(
            [slots[c, r * few : (r + 1) * few] for c in range(n_cols)], axis=0
        )


def gather_msa_kernel(few, n_cols, ready, *rest):
    ready()
    gather_msa(few, column_index(), rest[:n_cols], *rest[n_cols:])


def gather_pair_kernel(few, n_cols, residues, ready, gains_ref, matrix_ref, *rest):
    blocks, (first_ref, gate_ref, slots) = rest[:n_cols], rest[n_cols:]
    ready()
    spread_rows(column_index(), blocks, slots)
    block = blocks[0].shape[0]
    count = residues * few
    groups = block // count
    for c in range(n_cols):
        for o in range(groups):
            first_ref[pl.ds(o * n_cols + c, count, stride=groups * n_cols), :] = slots[
                pl.ds(c * block + o * count, count), :
            ]
    width = first_ref.shape[1]
    normal = layer_normalise(first_ref[...], gains_ref[1:2, :])
    gate_ref[...] = sigmoid(multiply(normal, matrix_ref[:, 4 * width :]))


def triangle_kernel(few, n_branch, n_gj, ready, tri_ref, *rest):
    n_cols = n_branch * n_gj
    blocks, (out_ref, msa_out, product_ref, slots) = rest[:n_cols], rest[n_cols:]
    ready()
    gather_msa(few, column_index(), blocks, msa_out, slots)
    n_all, rows, _ = out_ref.shape
    n_gi = n_all // n_cols
    share = few
    tiles = rows // few
    each = 2 * share
    wide = lanes // few
    group = lax.broadcasted_iota(jnp.int32, (n_gi * tiles, lanes), 1) // wide
    products = []
    for q in range(share):
        left, right = [], []
        for c in range(n_cols):
            base = (c // n_gj * n_all // n_branch + c % n_gj) * tiles * each
            step = n_gj * tiles * each
            here = jnp.concatenate(
                [
                    tri_ref[pl.ds(base + t * each + q, n_gi, stride=step), :]
                    for t in range(tiles)
                ],
                axis=0,
            )
            left.append(
                jnp.concatenate(
                    [jnp.where(group == i, here, 0.0) for i in range(few)], axis=0
                )
            )
            here = jnp.concatenate(
                [
                    tri_ref[pl.ds(base + g * step + share + q, tiles, stride=each), :]
                    for g in range(n_gi)
                ],
                axis=0,
            )
            rolled = [here] + [pltpu.roll(here, k * wide, 1) for k in range(1, few)]
            copies = []
            for j in range(few):
                copy = rolled[0]
                for k in range(1, few):
                    copy = jnp.where(group == (j + k) % few, rolled[k], copy)
                copies.append(copy)
            step = n_gi * tiles // n_cols
            right.append(
                jnp.concatenate(
                    [copy[k * step : (k + 1) * step] for k in range(n_cols) for copy in copies],
                    axis=0,
                )
            )
        products.append(
            multiply(
                jnp.concatenate(left, axis=1), jnp.concatenate(right, axis=1), across=True
            )
        )
    for c, product in enumerate(swap_lane_groups(products)):
        product_ref[...] = product
        for g in range(n_gi):
            out_ref[(c // n_gj * n_gi + g) * n_gj + c % n_gj] = product_ref[pl.ds(g, rows, stride=n_gi), :]


def pair_kernel(
    few, n_gi, n_cols, ready, *rest
):
    left_refs, pair_refs = rest[:n_cols], rest[n_cols : 2 * n_cols]
    right_ref, gain_ref, matrix_ref, triangle_ref, tri_ref = rest[2 * n_cols : 2 * n_cols + 5]
    chunks = rest[2 * n_cols + 5 : 3 * n_cols + 5]
    rest = rest[3 * n_cols + 5 :]
    left_ref, slots, pair_ref, first_ref = rest
    me = column_index()
    groups_j = n_gi // n_cols
    block = pair_refs[0].shape[0]
    ready()
    spread(me, left_refs, left_ref)
    spread_rows(me, pair_refs, slots)
    _, wide, count = left_ref.shape
    half = block // groups_j
    all_rows = count // few
    residues = n_cols * few
    pair_cols = n_gi * few
    per = lanes // pair_cols
    groups = residues // per
    width = pair_ref.shape[1]
    owner = lax.rem(lax.broadcasted_iota(jnp.int32, (1, count), 1), few)
    left = []
    for c in range(n_cols):
        here = left_ref[c]
        for f in range(few):
            own = jnp.where(owner == f, here, 0.0)
            total = own
            for other in range(few):
                if other != f:
                    total = total + pltpu.roll(own, (other - f) % count, 1)
            left.append(total)
    left = jnp.concatenate(left, axis=0) * (1.0 / all_rows)
    right = []
    for d in range(wide):
        here = right_ref[pl.ds(d, n_gi, stride=wide), :]
        right += [jnp.where(owner == f, here, 0.0) for f in range(few)]
    right = jnp.concatenate(right, axis=0)
    outer = multiply(left, right, across=True)
    outputs = []
    for g in range(groups):
        swapped = swap_lane_groups(
            [outer[(g * per + i) * wide : (g * per + i + 1) * wide] for i in range(per)]
        )
        stacked = [
            s[:, t * lanes : (t + 1) * lanes] for s in swapped for t in range(wide // per)
        ]
        outputs.append(jnp.concatenate(stacked, axis=0))
    for c in range(n_cols):
        for o in range(groups_j):
            pair_ref[pl.ds(c * groups_j + o, half, stride=n_gi), :] = slots[
                pl.ds(c * block + o, half, stride=groups_j), :
            ]
    update = multiply(matrix_ref[...], jnp.concatenate(outputs, axis=1))
    first = pair_ref[...].T + update
    projected = multiply(
        triangle_ref[pl.ds(0, 4 * width), :], layer_normalise(first, gain_ref[...], axis=0)
    )
    tri = sigmoid(projected[2 * width : 4 * width]) * projected[: 2 * width]
    slot_count, _, each, _ = tri_ref.shape
    for g in range(groups):
        tri_ref[:, g] = tri[:, g * lanes : (g + 1) * lanes].reshape(slot_count, each, lanes)
    first_ref[...] = first.T
    for k in range(n_cols):
        for o in range(groups_j):
            rows = pl.ds((me ^ k) * groups_j + o, half, stride=n_gi)
            chunks[k][pl.ds(o * half, half), :] = first_ref[rows, :]


def final_kernel(
    few, residues, packed, ready, product_ref, first_ref, gate_ref, gains_ref, matrix_ref, out_ref,
    channels_ref
):
    positions = out_ref.shape[0]
    ready()
    if packed:
        tiles = residues // few
        tall = product_ref.shape[0] // residues
        product = []
        for t in range(tiles):
            here = [
                product_ref[pl.ds(i * tiles + t, tall, stride=residues), :] for i in range(few)
            ]
            for q, piece in enumerate(swap_lane_groups(here)):
                channels_ref[pl.ds(q, tall, stride=few), :] = piece
            product.append(channels_ref[...])
        product = jnp.concatenate(product, axis=1)
    else:
        product = product_ref[...]
    normal = layer_normalise(product, 1.0, axis=0).T * gains_ref[2:3, :]
    result = first_ref[...] + gate_ref[...] * multiply(normal, matrix_ref[...])
    count = positions // (residues * few)
    for i in range(residues):
        for f in range(few):
            start = (i * few + f) * count
            out_ref[pl.ds(i * few * count + f, count, stride=few), :] = result[
                start : start + count
            ]


def per_device(
    homolog_embedding,
    pair_input_tensor,
    layernorm_scales,
    pair_norm_gains,
    pair_bias_matrix,
    horizontal_qkvg_kernel,
    horizontal_final_kernel,
    vertical_qkvg_kernel,
    vertical_final_kernel,
    feedforward_expand_kernel,
    feedforward_shrink_kernel,
    dyadic_sides_kernel,
    outer_output_matrix,
    triangle_input_matrix,
    triangle_output_matrix,
):
    rows, residues, width = homolog_embedding.shape
    pair_cols, pair_width = pair_input_tensor.shape[1:]
    heads = pair_bias_matrix.shape[1]
    outer_width = dyadic_sides_kernel.shape[1] // 2
    n_branch, n_gi, n_gj = (lax.axis_size(name) for name in everyone)
    n_cols = n_branch * n_gj
    n_all = n_cols * n_gi
    length = residues * n_gi
    few = residues // n_cols
    groups = n_gi // n_cols
    parts = 2
    per_part = n_gi // parts
    own_rows = rows // per_part

    def trade(blocks, axes):
        n = lax.axis_size(axes)
        return [blocks[0]] + [
            lax.ppermute(blocks[k], axes, [(t ^ k, t) for t in range(n) if t ^ k < n])
            for k in range(1, len(blocks))
        ]

    halves = [
        [
            (b * n_gi + part * per_part + g) * n_gj + j
            for b in range(n_branch)
            for g in range(per_part)
            for j in range(n_gj)
        ]
        for part in range(parts)
    ]
    n_half = n_cols * per_part
    positions = residues * pair_cols
    each = own_rows * few

    per = lanes // pair_cols
    bias_block = (heads // per, residues, lanes)
    msa, bias = call(
        bias_kernel,
        [[(parts * rows, residues, width)], bias_block],
        [homolog_embedding],
        [pair_input_tensor],
        [pair_norm_gains],
        [pair_bias_matrix.T],
        scratch=[
            homolog_embedding.shape,
            pair_input_tensor.shape,
            pair_norm_gains.shape,
            (heads, pair_width),
        ],
        sems=[4, parts],
    )
    msa = lax.all_to_all(msa, "gi", 0, 0, tiled=True)
    (bias,) = call_near(
        functools.partial(bias_part_kernel, per_part),
        [(per_part,) + bias_block],
        *trade([bias] * per_part, "gi"),
    )
    bias = trade([bias] * n_cols, columns)
    (msa_first,) = call(
        functools.partial(row_kernel, n_branch, n_gj, per_part, few),
        [(n_half, each, width)],
        msa,
        *[[block] for block in bias],
        [layernorm_scales],
        [horizontal_qkvg_kernel],
        [horizontal_final_kernel],
        scratch=[(n_cols, per_part) + bias_block]
        + [w.shape for w in (layernorm_scales, horizontal_qkvg_kernel, horizontal_final_kernel)],
        sems=[3 + n_cols],
    )
    pair, msa_first = lax.optimization_barrier((pair_input_tensor, msa_first))

    msa_first = lax.all_to_all(msa_first, everyone, 0, 0, tiled=True, axis_index_groups=halves)
    count = n_half * each
    weights = (
        layernorm_scales,
        vertical_qkvg_kernel,
        vertical_final_kernel,
        feedforward_expand_kernel,
        feedforward_shrink_kernel,
        dyadic_sides_kernel.T,
    )
    left, right, alignment = call_near(
        functools.partial(column_kernel, few, heads),
        [(outer_width, count), (n_gi, outer_width, count), (count, width)],
        msa_first.reshape(count, width),
        *weights,
    )
    alignment = call_near(
        functools.partial(msa_blocks_kernel, n_branch, n_gj),
        [(per_part, each, width)] * n_cols,
        alignment,
        scratch=[(n_cols, per_part, each, width)],
    )
    pair = call_near(
        functools.partial(pair_blocks_kernel, few, residues),
        [(positions // n_cols, pair_width)] * n_cols,
        pair.reshape(positions, pair_width),
        scratch=[(positions, pair_width)],
    )
    pair = trade(pair, columns)
    right = lax.all_to_all(right, "gi", 0, 0, tiled=True)
    left = trade([left] * n_cols, columns)
    alignment = [block.reshape(-1, width) for block in trade(alignment, columns)]
    share = max(pair_width // n_all, 1)
    slots = pair_width // share
    triangle = triangle_input_matrix.T.reshape(5, slots, share, pair_width)
    sides = jnp.stack([triangle[0], triangle[2]], axis=1)
    gates = jnp.stack([triangle[1], triangle[3]], axis=1)
    triangle = jnp.concatenate(
        [side.reshape(2 * pair_width, pair_width) for side in (sides, gates)]
        + [triangle[4].reshape(pair_width, pair_width)],
        axis=0,
    )
    matrix = outer_output_matrix.reshape(outer_width, outer_width // per, per, pair_width)
    matrix = jnp.transpose(matrix, (3, 2, 1, 0)).reshape(pair_width, -1)
    tri, *first = call_near(
        functools.partial(pair_kernel, few, n_gi, n_cols),
        [(slots, positions // lanes, 2 * share, lanes)]
        + [(positions // n_cols, pair_width)] * n_cols,
        *left,
        *pair,
        right.reshape(n_gi * outer_width, count),
        pair_norm_gains[1][:, None],
        matrix,
        triangle,
        scratch=[
            (n_cols, outer_width, count),
            (positions, pair_width),
            (positions, pair_width),
            (positions, pair_width),
        ],
    )

    first, gate = call_near(
        functools.partial(gather_pair_kernel, few, n_cols, residues),
        [(positions, pair_width)] * 2,
        pair_norm_gains,
        triangle_input_matrix,
        *trade(first, columns),
        scratch=[(positions, pair_width)],
    )
    tile = (rows, residues, width)
    scratch = [(n_cols, rows * few, width)]
    packed = share * n_all == pair_width and share == few and few == per
    if packed:
        tri = lax.all_to_all(tri, everyone, 0, 0, tiled=True)
        product, alignment_output = call_near(
            functools.partial(triangle_kernel, few, n_branch, n_gj),
            [(n_all, residues, lanes), tile],
            tri.reshape(-1, lanes),
            *alignment,
            scratch=[(lanes, lanes)] + scratch,
        )
        product = lax.all_to_all(product, everyone, 0, 0, tiled=True)
        product = product.reshape(n_all * residues, lanes)
    else:
        (alignment_output,) = call_near(
            functools.partial(gather_msa_kernel, few, n_cols),
            [tile],
            *alignment,
            scratch=scratch,
        )
        tri = jnp.transpose(tri.reshape(slots, -1, 2, share, lanes), (2, 1, 4, 0, 3))
        tri = tri.reshape(2, residues, pair_cols, pair_width)
        right_columns = lax.all_gather(tri[1], "gi", axis=0, tiled=True)
        product = lax.psum_scatter(
            jnp.einsum("jkc,ikc->jic", right_columns, tri[0], precision=precise),
            columns,
            scatter_dimension=0,
            tiled=True,
        ).reshape(groups, n_cols, few, residues, pair_width)
        product = jnp.transpose(product, (4, 3, 2, 0, 1)).reshape(pair_width, positions)
    (pair_output_tensor,) = call_near(
        functools.partial(final_kernel, few, residues, packed),
        [(positions, pair_width)],
        product,
        first,
        gate,
        pair_norm_gains,
        triangle_output_matrix,
        scratch=[(pair_width, lanes)],
    )
    return (
        alignment_output,
        pair_output_tensor.reshape(residues, pair_cols, pair_width),
    )


def solution(mesh):
    tile, grid = P(("branch", "gj"), "gi", None), P("gi", ("branch", "gj"), None)
    return jax.shard_map(
        per_device,
        mesh=mesh,
        in_specs=(tile, grid) + (P(),) * 13,
        out_specs=(tile, grid),
        check_vma=False,
    )
```

```python
import functools
import math

import jax
import jax.numpy as jnp
from jax import lax
from jax.experimental import pallas as pl
from jax.experimental.pallas import tpu as pltpu
from jax.sharding import PartitionSpec as P

epsilon = 1e-05
precise = lax.Precision.HIGH
everyone = ("branch", "gi", "gj")
columns = ("branch", "gj")
lanes = 128
far = pl.BlockSpec(memory_space=pl.ANY)
vmem = pl.BlockSpec(memory_space=pltpu.VMEM)
params = pltpu.CompilerParams(vmem_limit_bytes=16 * 1024 * 1024)


def layer_normalise(values, norm_gain, axis=-1):
    average = jnp.mean(values, axis=axis, keepdims=True)
    centred = values - average
    variance = jnp.mean(centred * centred, axis=axis, keepdims=True)
    return centred * lax.rsqrt(variance + epsilon) * norm_gain


def apply_projection(values, weight):
    return jnp.einsum("...c,cd->...d", values, weight, precision=precise)


def sigmoid(values):
    return 1.0 / (1.0 + jnp.exp(-values))


def split(values):
    high = values.astype(jnp.bfloat16)
    return high, (values - high.astype(jnp.float32)).astype(jnp.bfloat16)


def multiply(left, right, across=False):
    numbers = (((1,), (1 if across else 0,)), ((), ()))

    def one(a, b):
        return lax.dot_general(a, b, numbers, preferred_element_type=jnp.float32)

    (lh, ll), (rh, rl) = split(left), split(right)
    return one(lh, rh) + (one(lh, rl) + one(ll, rh))


def swap_lane_groups(arrays):
    n, arrays = len(arrays), list(arrays)
    width = lanes // n
    wide = arrays[0].shape[-1]
    lane = lax.broadcasted_iota(jnp.int32, arrays[0].shape, arrays[0].ndim - 1)
    group = lax.rem(lane, lanes) // width
    axis = arrays[0].ndim - 1
    step = 1
    while step < n:
        upper = (group // step) % 2 == 1
        for low in range(n):
            if low & step:
                continue
            a, b = arrays[low], arrays[low + step]
            arrays[low] = jnp.where(upper, pltpu.roll(b, step * width, axis), a)
            arrays[low + step] = jnp.where(
                upper, b, pltpu.roll(a, wide - step * width, axis)
            )
        step *= 2
    return arrays


def head_masks(shape, heads):
    column = lax.broadcasted_iota(jnp.int32, shape, 1)
    return [column // (shape[1] // heads) == h for h in range(heads)]


def attend(query, key, value, bias, heads, allowed=None):
    count, inner = query.shape
    masks = head_masks((count, inner), heads)
    spread = jnp.concatenate([jnp.where(m, query, 0.0) for m in masks], axis=0)
    scores = multiply(spread, key, across=True) * (1.0 / math.sqrt(inner // heads))
    if bias is not None:
        scores = scores + bias
    if allowed is not None:
        scores = jnp.where(allowed, scores, -1e30)
    weights = jnp.exp(scores - jnp.max(scores, axis=-1, keepdims=True))
    weights = weights / jnp.sum(weights, axis=-1, keepdims=True)
    mixed = multiply(weights, value)
    result = jnp.where(masks[0], mixed[:count], 0.0)
    for h in range(1, heads):
        result = result + jnp.where(masks[h], mixed[h * count : (h + 1) * count], 0.0)
    return result


def start_copies(pairs, sems):
    copies = [pltpu.make_async_copy(a, b, sems.at[n]) for n, (a, b) in enumerate(pairs)]
    for copy in copies:
        copy.start()
    return copies


def wait_all(copies):
    for copy in copies:
        copy.wait()


def column_index():
    return lax.axis_index("branch") * lax.axis_size("gj") + lax.axis_index("gj")


def cost(kernel):
    name = getattr(kernel, "func", kernel).__name__
    work = {
        "bias_kernel": 2.0,
        "bias_part_kernel": 0.2,
        "row_kernel": 4.5,
        "pair_blocks_kernel": 3.0,
        "column_kernel": 4.5,
        "msa_blocks_kernel": 0.5,
        "pair_kernel": 4.0,
        "triangle_kernel": 2.0,
        "gather_pair_kernel": 1.0,
        "final_kernel": 1.3,
    }.get(name, 1.0)
    return pl.CostEstimate(
        flops=int(work * 1.1e9), bytes_accessed=int(work * 3.6e6), transcendentals=0
    )


def call(kernel, outs, *operands, scratch=(), sems=()):
    def bare(item):
        return item[0] if isinstance(item, list) else item

    n_in, n_out = len(operands), len(outs)
    near_in = [n for n, item in enumerate(operands) if not isinstance(item, list)]
    near_out = [n for n, item in enumerate(outs) if not isinstance(item, list)]
    shapes = [operands[n].shape for n in near_in] + [outs[n] for n in near_out]

    def body(*refs):
        inputs, results = list(refs[:n_in]), list(refs[n_in : n_in + n_out])
        local = refs[n_in + n_out : n_in + n_out + len(shapes)]
        rest, own_sems = refs[n_in + n_out + len(shapes) : -1], refs[-1]
        pairs = list(zip([inputs[n] for n in near_in], local))
        back = list(zip(local[len(near_in) :], [results[n] for n in near_out]))
        for n, ref in zip(near_in, local):
            inputs[n] = ref
        for n, ref in zip(near_out, local[len(near_in) :]):
            results[n] = ref
        copies = start_copies(pairs, own_sems)
        kernel(lambda: wait_all(copies), *inputs, *results, *rest)
        wait_all(start_copies(back, own_sems))

    return pl.pallas_call(
        body,
        out_shape=[jax.ShapeDtypeStruct(bare(out), jnp.float32) for out in outs],
        in_specs=[far] * n_in,
        out_specs=[far] * n_out,
        scratch_shapes=[pltpu.VMEM(shape, jnp.float32) for shape in shapes + list(scratch)]
        + [pltpu.SemaphoreType.DMA((n,)) for n in sems]
        + [pltpu.SemaphoreType.DMA((max(len(near_in), len(near_out), 1),))],
        cost_estimate=cost(kernel),
    )(*[bare(operand) for operand in operands])


def call_near(kernel, outs, *operands, scratch=()):
    return pl.pallas_call(
        lambda *refs: kernel(lambda: None, *refs),
        out_shape=[jax.ShapeDtypeStruct(out, jnp.float32) for out in outs],
        in_specs=[vmem] * len(operands),
        out_specs=[vmem] * len(outs),
        scratch_shapes=[pltpu.VMEM(shape, jnp.float32) for shape in scratch],
        compiler_params=params,
        cost_estimate=cost(kernel),
    )(*operands)


def spread(me, refs, slots):
    for k, ref in enumerate(refs):
        slots[me ^ k] = ref[...]


def spread_rows(me, refs, slots):
    for k, ref in enumerate(refs):
        count = ref.shape[0]
        slots[pl.ds(pl.multiple_of((me ^ k) * count, 8), count), :] = ref[...]


def bias_kernel(
    ready, msa_far, pair_far, gains_far, matrix_far, copies_far, out_ref, msa_ref, pair_ref,
    gains_ref, matrix_ref, sems, out_sems
):
    rows = msa_far.shape[0]
    repeats = copies_far.shape[0] // rows
    copies = start_copies(
        [(msa_far, msa_ref), (gains_far, gains_ref), (matrix_far, matrix_ref), (pair_far, pair_ref)],
        sems,
    )
    residues, pair_cols, _ = pair_ref.shape
    heads = matrix_ref.shape[0]
    per = lanes // pair_cols
    ready()
    wait_all(copies)
    copies = start_copies(
        [(msa_ref, copies_far.at[pl.ds(n * rows, rows)]) for n in range(repeats)], out_sems
    )
    normal = layer_normalise(pair_ref[...], gains_ref[0:1, :][None])
    for i in range(residues):
        here = multiply(matrix_ref[...], normal[i], across=True)
        for h in range(heads):
            out_ref[h // per, i : i + 1, pl.ds(h % per * pair_cols, pair_cols)] = here[h : h + 1]
    wait_all(copies)


def pair_blocks_kernel(few, residues, ready, pair_ref, *rest):
    chunks, slots = rest[:-1], rest[-1]
    n_cols = len(chunks)
    block = chunks[0].shape[0]
    groups = block // (residues * few)
    me = column_index()
    ready()
    for c in range(n_cols):
        for o in range(groups):
            for f in range(few):
                source = pl.ds((o * n_cols + c) * few + f, residues, stride=groups * n_cols * few)
                target = pl.ds(c * block + f * groups + o, residues, stride=few * groups)
                slots[target, :] = pair_ref[source, :]
    for k in range(n_cols):
        start = pl.multiple_of((me ^ k) * block, 8)
        chunks[k][...] = slots[pl.ds(start, block), :]


def bias_part_kernel(per_part, ready, *rest):
    blocks, (out_ref,) = rest[:per_part], rest[per_part:]
    ready()
    spread(lax.rem(lax.axis_index("gi"), per_part), blocks, out_ref)


def row_kernel(n_branch, n_gj, per_part, few, ready, msa_ref, *rest):
    n_cols = n_branch * n_gj
    bias_refs, rest = rest[:n_cols], rest[n_cols:]
    gains_far, qkvg_far, final_far, out_ref, slots, gains_ref, qkvg_ref, final_ref, sems = rest
    me, half = column_index(), lax.div(lax.axis_index("gi"), per_part)
    inner = final_ref.shape[0]
    parts = [pl.ds(n * inner, inner) for n in (1, 2, 0, 3)]
    copies = start_copies(
        [(gains_far, gains_ref)]
        + [(qkvg_far.at[:, part], qkvg_ref.at[:, part]) for part in parts]
        + [(final_far, final_ref)]
        + [(ref, slots.at[me ^ k]) for k, ref in enumerate(bias_refs)],
        sems,
    )
    ready()
    _, residues, width = msa_ref.shape
    blocks = slots.shape[2]
    n_gi = lax.axis_size("gi")
    length = n_gi * residues
    per = lanes * n_cols // length
    heads = blocks * per
    rows = msa_ref.shape[0] // n_gi
    inner = final_ref.shape[0]
    queries = per_part * residues
    tokens = jnp.concatenate(
        [msa_ref[g * rows + r] for r in range(rows) for g in range(n_gi)], axis=0
    )
    first = half * (per_part * rows)
    asking = msa_ref[pl.ds(first, per_part * rows)]
    asking = jnp.concatenate(
        [asking[g * rows + r] for r in range(rows) for g in range(per_part)], axis=0
    )
    tokens = layer_normalise(tokens, 1.0)
    normal = layer_normalise(asking, 1.0)
    wait_all(copies[:3])
    gain = gains_ref[0:1, :]
    key_value = multiply(tokens * gain, qkvg_ref[:, inner : 3 * inner])
    normal = normal * gain
    wait_all(copies[3:5])
    query = multiply(normal, qkvg_ref[:, :inner])
    gate = multiply(normal, qkvg_ref[:, 3 * inner :])
    wait_all(copies[5:])
    pieces = [[] for _ in range(heads)]
    for block in range(blocks):
        for g in range(per_part):
            tiles = [[] for _ in range(per)]
            for tile in range(n_cols // per):
                group = [slots[c, g, block] for c in range(tile * per, (tile + 1) * per)]
                for k, piece in enumerate(swap_lane_groups(group)):
                    tiles[k].append(piece)
            for k in range(per):
                pieces[block * per + k].append(jnp.concatenate(tiles[k], axis=1))
    bias = jnp.concatenate([piece for head in pieces for piece in head], axis=0)
    attended = []
    for r in range(rows):
        keys = key_value[r * length : (r + 1) * length, :inner]
        values = key_value[r * length : (r + 1) * length, inner:]
        attended.append(
            attend(query[r * queries : (r + 1) * queries], keys, values, bias, heads)
        )
    attended = jnp.concatenate(attended, axis=0)
    result = asking + multiply(sigmoid(gate) * attended, final_ref[...])
    for b in range(n_branch):
        for g in range(per_part):
            for j in range(n_gj):
                start = g * residues + (b * n_gj + j) * few
                out_ref[(b * per_part + g) * n_gj + j] = jnp.concatenate(
                    [result[r * queries + start : r * queries + start + few] for r in range(rows)],
                    axis=0,
                )


def column_kernel(
    few, heads, ready, msa_ref, gains_ref, qkvg_ref, final_ref, expand_ref, shrink_ref, sides_ref,
    left_ref, right_ref, out_ref
):
    ready()
    count, width = msa_ref.shape
    inner = final_ref.shape[0]
    half = sides_ref.shape[0] // 2
    first = msa_ref[...]
    projected = multiply(layer_normalise(first, gains_ref[1:2, :]), qkvg_ref[...])
    query, key, value, gate = (projected[:, k * inner : (k + 1) * inner] for k in range(4))
    allowed = None
    if few > 1:
        shape = (heads * count, count)
        asks = lax.broadcasted_iota(jnp.int32, shape, 0)
        holds = lax.broadcasted_iota(jnp.int32, shape, 1)
        allowed = lax.rem(asks, few) == lax.rem(holds, few)
    attended = attend(query, key, value, None, heads, allowed)
    second = first + multiply(sigmoid(gate) * attended, final_ref[...])
    expanded = multiply(layer_normalise(second, gains_ref[2:3, :]), expand_ref[...])
    third = second + multiply(jnp.maximum(expanded, 0.0), shrink_ref[...])
    out_ref[...] = third
    factors = multiply(sides_ref[...], layer_normalise(third, gains_ref[3:4, :]), across=True)
    left_ref[...] = factors[:half]
    for g in range(right_ref.shape[0]):
        right_ref[g] = factors[half:]


def msa_blocks_kernel(n_branch, n_gj, ready, msa_ref, *rest):
    chunks, slots = rest[:-1], rest[-1]
    per_part, each = slots.shape[1:3]
    ready()
    for b in range(n_branch):
        for g in range(per_part):
            for j in range(n_gj):
                start = ((b * per_part + g) * n_gj + j) * each
                slots[b * n_gj + j, g] = msa_ref[start : start + each]
    for k, chunk in enumerate(chunks):
        chunk[...] = slots[column_index() ^ k]


def gather_msa(few, me, blocks, out_ref, slots):
    n_cols = len(blocks)
    spread(me, blocks, slots)
    for r in range(out_ref.shape[0]):
        out_ref[r] = jnp.concatenate(
            [slots[c, r * few : (r + 1) * few] for c in range(n_cols)], axis=0
        )


def gather_msa_kernel(few, n_cols, ready, *rest):
    ready()
    gather_msa(few, column_index(), rest[:n_cols], *rest[n_cols:])


def gather_pair_kernel(few, n_cols, residues, ready, gains_ref, matrix_ref, *rest):
    blocks, (first_ref, gate_ref, slots) = rest[:n_cols], rest[n_cols:]
    ready()
    spread_rows(column_index(), blocks, slots)
    block = blocks[0].shape[0]
    count = residues * few
    groups = block // count
    for c in range(n_cols):
        for o in range(groups):
            first_ref[pl.ds(o * n_cols + c, count, stride=groups * n_cols), :] = slots[
                pl.ds(c * block + o * count, count), :
            ]
    width = first_ref.shape[1]
    normal = layer_normalise(first_ref[...], gains_ref[1:2, :])
    gate_ref[...] = sigmoid(multiply(normal, matrix_ref[:, 4 * width :]))


def triangle_kernel(few, n_branch, n_gj, ready, tri_ref, *rest):
    n_cols = n_branch * n_gj
    blocks, (out_ref, msa_out, product_ref, slots) = rest[:n_cols], rest[n_cols:]
    ready()
    gather_msa(few, column_index(), blocks, msa_out, slots)
    n_all, rows, _ = out_ref.shape
    n_gi = n_all // n_cols
    share = few
    tiles = rows // few
    each = 2 * share
    wide = lanes // few
    group = lax.broadcasted_iota(jnp.int32, (n_gi * tiles, lanes), 1) // wide
    products = []
    for q in range(share):
        left, right = [], []
        for c in range(n_cols):
            base = (c // n_gj * n_all // n_branch + c % n_gj) * tiles * each
            step = n_gj * tiles * each
            here = jnp.concatenate(
                [
                    tri_ref[pl.ds(base + t * each + q, n_gi, stride=step), :]
                    for t in range(tiles)
                ],
                axis=0,
            )
            left.append(
                jnp.concatenate(
                    [jnp.where(group == i, here, 0.0) for i in range(few)], axis=0
                )
            )
            here = jnp.concatenate(
                [
                    tri_ref[pl.ds(base + g * step + share + q, tiles, stride=each), :]
                    for g in range(n_gi)
                ],
                axis=0,
            )
            rolled = [here] + [pltpu.roll(here, k * wide, 1) for k in range(1, few)]
            copies = []
            for j in range(few):
                copy = rolled[0]
                for k in range(1, few):
                    copy = jnp.where(group == (j + k) % few, rolled[k], copy)
                copies.append(copy)
            step = n_gi * tiles // n_cols
            right.append(
                jnp.concatenate(
                    [copy[k * step : (k + 1) * step] for k in range(n_cols) for copy in copies],
                    axis=0,
                )
            )
        products.append(
            multiply(
                jnp.concatenate(left, axis=1), jnp.concatenate(right, axis=1), across=True
            )
        )
    for c, product in enumerate(swap_lane_groups(products)):
        product_ref[...] = product
        for g in range(n_gi):
            out_ref[(c // n_gj * n_gi + g) * n_gj + c % n_gj] = product_ref[pl.ds(g, rows, stride=n_gi), :]


def pair_kernel(
    few, n_gi, n_cols, ready, *rest
):
    left_refs, pair_refs = rest[:n_cols], rest[n_cols : 2 * n_cols]
    right_ref, gain_ref, matrix_ref, triangle_ref, tri_ref = rest[2 * n_cols : 2 * n_cols + 5]
    chunks = rest[2 * n_cols + 5 : 3 * n_cols + 5]
    rest = rest[3 * n_cols + 5 :]
    left_ref, slots, pair_ref, first_ref = rest
    me = column_index()
    groups_j = n_gi // n_cols
    block = pair_refs[0].shape[0]
    ready()
    spread(me, left_refs, left_ref)
    spread_rows(me, pair_refs, slots)
    _, wide, count = left_ref.shape
    half = block // groups_j
    all_rows = count // few
    residues = n_cols * few
    pair_cols = n_gi * few
    per = lanes // pair_cols
    groups = residues // per
    width = pair_ref.shape[1]
    owner = lax.rem(lax.broadcasted_iota(jnp.int32, (1, count), 1), few)
    left = []
    for c in range(n_cols):
        here = left_ref[c]
        for f in range(few):
            own = jnp.where(owner == f, here, 0.0)
            total = own
            for other in range(few):
                if other != f:
                    total = total + pltpu.roll(own, (other - f) % count, 1)
            left.append(total)
    left = jnp.concatenate(left, axis=0) * (1.0 / all_rows)
    right = []
    for d in range(wide):
        here = right_ref[pl.ds(d, n_gi, stride=wide), :]
        right += [jnp.where(owner == f, here, 0.0) for f in range(few)]
    right = jnp.concatenate(right, axis=0)
    outer = multiply(left, right, across=True)
    outputs = []
    for g in range(groups):
        swapped = swap_lane_groups(
            [outer[(g * per + i) * wide : (g * per + i + 1) * wide] for i in range(per)]
        )
        stacked = [
            s[:, t * lanes : (t + 1) * lanes] for s in swapped for t in range(wide // per)
        ]
        outputs.append(jnp.concatenate(stacked, axis=0))
    for c in range(n_cols):
        for o in range(groups_j):
            pair_ref[pl.ds(c * groups_j + o, half, stride=n_gi), :] = slots[
                pl.ds(c * block + o, half, stride=groups_j), :
            ]
    update = multiply(matrix_ref[...], jnp.concatenate(outputs, axis=1))
    first = pair_ref[...].T + update
    projected = multiply(
        triangle_ref[pl.ds(0, 4 * width), :], layer_normalise(first, gain_ref[...], axis=0)
    )
    tri = sigmoid(projected[2 * width : 4 * width]) * projected[: 2 * width]
    slot_count, _, each, _ = tri_ref.shape
    for g in range(groups):
        tri_ref[:, g] = tri[:, g * lanes : (g + 1) * lanes].reshape(slot_count, each, lanes)
    first_ref[...] = first.T
    for k in range(n_cols):
        for o in range(groups_j):
            rows = pl.ds((me ^ k) * groups_j + o, half, stride=n_gi)
            chunks[k][pl.ds(o * half, half), :] = first_ref[rows, :]


def final_kernel(
    few, residues, packed, ready, product_ref, first_ref, gate_ref, gains_ref, matrix_ref, out_ref,
    channels_ref
):
    positions = out_ref.shape[0]
    ready()
    if packed:
        tiles = residues // few
        tall = product_ref.shape[0] // residues
        product = []
        for t in range(tiles):
            here = [
                product_ref[pl.ds(i * tiles + t, tall, stride=residues), :] for i in range(few)
            ]
            for q, piece in enumerate(swap_lane_groups(here)):
                channels_ref[pl.ds(q, tall, stride=few), :] = piece
            product.append(channels_ref[...])
        product = jnp.concatenate(product, axis=1)
    else:
        product = product_ref[...]
    normal = layer_normalise(product, 1.0, axis=0).T * gains_ref[2:3, :]
    result = first_ref[...] + gate_ref[...] * multiply(normal, matrix_ref[...])
    count = positions // (residues * few)
    for i in range(residues):
        for f in range(few):
            start = (i * few + f) * count
            out_ref[pl.ds(i * few * count + f, count, stride=few), :] = result[
                start : start + count
            ]


def per_device(
    homolog_embedding,
    pair_input_tensor,
    layernorm_scales,
    pair_norm_gains,
    pair_bias_matrix,
    horizontal_qkvg_kernel,
    horizontal_final_kernel,
    vertical_qkvg_kernel,
    vertical_final_kernel,
    feedforward_expand_kernel,
    feedforward_shrink_kernel,
    dyadic_sides_kernel,
    outer_output_matrix,
    triangle_input_matrix,
    triangle_output_matrix,
):
    rows, residues, width = homolog_embedding.shape
    pair_cols, pair_width = pair_input_tensor.shape[1:]
    heads = pair_bias_matrix.shape[1]
    outer_width = dyadic_sides_kernel.shape[1] // 2
    n_branch, n_gi, n_gj = (lax.axis_size(name) for name in everyone)
    n_cols = n_branch * n_gj
    n_all = n_cols * n_gi
    length = residues * n_gi
    few = residues // n_cols
    groups = n_gi // n_cols
    parts = 2
    per_part = n_gi // parts
    own_rows = rows // per_part

    def trade(blocks, axes):
        n = lax.axis_size(axes)
        return [blocks[0]] + [
            lax.ppermute(blocks[k], axes, [(t ^ k, t) for t in range(n) if t ^ k < n])
            for k in range(1, len(blocks))
        ]

    halves = [
        [
            (b * n_gi + part * per_part + g) * n_gj + j
            for b in range(n_branch)
            for g in range(per_part)
            for j in range(n_gj)
        ]
        for part in range(parts)
    ]
    n_half = n_cols * per_part
    positions = residues * pair_cols
    each = own_rows * few

    per = lanes // pair_cols
    bias_block = (heads // per, residues, lanes)
    msa, bias = call(
        bias_kernel,
        [[(parts * rows, residues, width)], bias_block],
        [homolog_embedding],
        [pair_input_tensor],
        [pair_norm_gains],
        [pair_bias_matrix.T],
        scratch=[
            homolog_embedding.shape,
            pair_input_tensor.shape,
            pair_norm_gains.shape,
            (heads, pair_width),
        ],
        sems=[4, parts],
    )
    msa = lax.all_to_all(msa, "gi", 0, 0, tiled=True)
    (bias,) = call_near(
        functools.partial(bias_part_kernel, per_part),
        [(per_part,) + bias_block],
        *trade([bias] * per_part, "gi"),
    )
    bias = trade([bias] * n_cols, columns)
    (msa_first,) = call(
        functools.partial(row_kernel, n_branch, n_gj, per_part, few),
        [(n_half, each, width)],
        msa,
        *[[block] for block in bias],
        [layernorm_scales],
        [horizontal_qkvg_kernel],
        [horizontal_final_kernel],
        scratch=[(n_cols, per_part) + bias_block]
        + [w.shape for w in (layernorm_scales, horizontal_qkvg_kernel, horizontal_final_kernel)],
        sems=[6 + n_cols],
    )
    pair, msa_first = lax.optimization_barrier((pair_input_tensor, msa_first))

    msa_first = lax.all_to_all(msa_first, everyone, 0, 0, tiled=True, axis_index_groups=halves)
    count = n_half * each
    weights = (
        layernorm_scales,
        vertical_qkvg_kernel,
        vertical_final_kernel,
        feedforward_expand_kernel,
        feedforward_shrink_kernel,
        dyadic_sides_kernel.T,
    )
    left, right, alignment = call_near(
        functools.partial(column_kernel, few, heads),
        [(outer_width, count), (n_gi, outer_width, count), (count, width)],
        msa_first.reshape(count, width),
        *weights,
    )
    alignment = call_near(
        functools.partial(msa_blocks_kernel, n_branch, n_gj),
        [(per_part, each, width)] * n_cols,
        alignment,
        scratch=[(n_cols, per_part, each, width)],
    )
    pair = call_near(
        functools.partial(pair_blocks_kernel, few, residues),
        [(positions // n_cols, pair_width)] * n_cols,
        pair.reshape(positions, pair_width),
        scratch=[(positions, pair_width)],
    )
    pair = trade(pair, columns)
    right = lax.all_to_all(right, "gi", 0, 0, tiled=True)
    left = trade([left] * n_cols, columns)
    alignment = [block.reshape(-1, width) for block in trade(alignment, columns)]
    share = max(pair_width // n_all, 1)
    slots = pair_width // share
    triangle = triangle_input_matrix.T.reshape(5, slots, share, pair_width)
    sides = jnp.stack([triangle[0], triangle[2]], axis=1)
    gates = jnp.stack([triangle[1], triangle[3]], axis=1)
    triangle = jnp.concatenate(
        [side.reshape(2 * pair_width, pair_width) for side in (sides, gates)]
        + [triangle[4].reshape(pair_width, pair_width)],
        axis=0,
    )
    matrix = outer_output_matrix.reshape(outer_width, outer_width // per, per, pair_width)
    matrix = jnp.transpose(matrix, (3, 2, 1, 0)).reshape(pair_width, -1)
    tri, *first = call_near(
        functools.partial(pair_kernel, few, n_gi, n_cols),
        [(slots, positions // lanes, 2 * share, lanes)]
        + [(positions // n_cols, pair_width)] * n_cols,
        *left,
        *pair,
        right.reshape(n_gi * outer_width, count),
        pair_norm_gains[1][:, None],
        matrix,
        triangle,
        scratch=[
            (n_cols, outer_width, count),
            (positions, pair_width),
            (positions, pair_width),
            (positions, pair_width),
        ],
    )

    first, gate = call_near(
        functools.partial(gather_pair_kernel, few, n_cols, residues),
        [(positions, pair_width)] * 2,
        pair_norm_gains,
        triangle_input_matrix,
        *trade(first, columns),
        scratch=[(positions, pair_width)],
    )
    tile = (rows, residues, width)
    scratch = [(n_cols, rows * few, width)]
    packed = share * n_all == pair_width and share == few and few == per
    if packed:
        tri = lax.all_to_all(tri, everyone, 0, 0, tiled=True)
        product, alignment_output = call_near(
            functools.partial(triangle_kernel, few, n_branch, n_gj),
            [(n_all, residues, lanes), tile],
            tri.reshape(-1, lanes),
            *alignment,
            scratch=[(lanes, lanes)] + scratch,
        )
        product = lax.all_to_all(product, everyone, 0, 0, tiled=True)
        product = product.reshape(n_all * residues, lanes)
    else:
        (alignment_output,) = call_near(
            functools.partial(gather_msa_kernel, few, n_cols),
            [tile],
            *alignment,
            scratch=scratch,
        )
        tri = jnp.transpose(tri.reshape(slots, -1, 2, share, lanes), (2, 1, 4, 0, 3))
        tri = tri.reshape(2, residues, pair_cols, pair_width)
        right_columns = lax.all_gather(tri[1], "gi", axis=0, tiled=True)
        product = lax.psum_scatter(
            jnp.einsum("jkc,ikc->jic", right_columns, tri[0], precision=precise),
            columns,
            scatter_dimension=0,
            tiled=True,
        ).reshape(groups, n_cols, few, residues, pair_width)
        product = jnp.transpose(product, (4, 3, 2, 0, 1)).reshape(pair_width, positions)
    (pair_output_tensor,) = call_near(
        functools.partial(final_kernel, few, residues, packed),
        [(positions, pair_width)],
        product,
        first,
        gate,
        pair_norm_gains,
        triangle_output_matrix,
        scratch=[(pair_width, lanes)],
    )
    return (
        alignment_output,
        pair_output_tensor.reshape(residues, pair_cols, pair_width),
    )


def solution(mesh):
    tile, grid = P(("branch", "gj"), "gi", None), P("gi", ("branch", "gj"), None)
    return jax.shard_map(
        per_device,
        mesh=mesh,
        in_specs=(tile, grid) + (P(),) * 13,
        out_specs=(tile, grid),
        check_vma=False,
    )
```

```python
import functools
import math

import jax
import jax.numpy as jnp
from jax import lax
from jax.experimental import pallas as pl
from jax.experimental.pallas import tpu as pltpu
from jax.sharding import PartitionSpec as P

epsilon = 1e-05
precise = lax.Precision.HIGH
everyone = ("branch", "gi", "gj")
columns = ("branch", "gj")
lanes = 128
far = pl.BlockSpec(memory_space=pl.ANY)
vmem = pl.BlockSpec(memory_space=pltpu.VMEM)


def layer_normalise(values, norm_gain, axis=-1):
    average = jnp.mean(values, axis=axis, keepdims=True)
    centred = values - average
    variance = jnp.mean(centred * centred, axis=axis, keepdims=True)
    return centred * lax.rsqrt(variance + epsilon) * norm_gain


def apply_projection(values, weight):
    return jnp.einsum("...c,cd->...d", values, weight, precision=precise)


def sigmoid(values):
    return 1.0 / (1.0 + jnp.exp(-values))


def split(values):
    high = values.astype(jnp.bfloat16)
    return high, (values - high.astype(jnp.float32)).astype(jnp.bfloat16)


def multiply(left, right, across=False):
    numbers = (((1,), (1 if across else 0,)), ((), ()))

    def one(a, b):
        return lax.dot_general(a, b, numbers, preferred_element_type=jnp.float32)

    (lh, ll), (rh, rl) = split(left), split(right)
    return one(lh, rh) + (one(lh, rl) + one(ll, rh))


def swap_lane_groups(arrays):
    n, arrays = len(arrays), list(arrays)
    width = lanes // n
    wide = arrays[0].shape[-1]
    lane = lax.broadcasted_iota(jnp.int32, arrays[0].shape, arrays[0].ndim - 1)
    group = lax.rem(lane, lanes) // width
    axis = arrays[0].ndim - 1
    step = 1
    while step < n:
        upper = (group // step) % 2 == 1
        for low in range(n):
            if low & step:
                continue
            a, b = arrays[low], arrays[low + step]
            arrays[low] = jnp.where(upper, pltpu.roll(b, step * width, axis), a)
            arrays[low + step] = jnp.where(
                upper, b, pltpu.roll(a, wide - step * width, axis)
            )
        step *= 2
    return arrays


def head_masks(shape, heads):
    column = lax.broadcasted_iota(jnp.int32, shape, 1)
    return [column // (shape[1] // heads) == h for h in range(heads)]


def attend(query, key, value, bias, heads, allowed=None):
    count, inner = query.shape
    masks = head_masks((count, inner), heads)
    spread = jnp.concatenate([jnp.where(m, query, 0.0) for m in masks], axis=0)
    scores = multiply(spread, key, across=True) * (1.0 / math.sqrt(inner // heads))
    if bias is not None:
        scores = scores + bias
    if allowed is not None:
        scores = jnp.where(allowed, scores, -1e30)
    weights = jnp.exp(scores - jnp.max(scores, axis=-1, keepdims=True))
    weights = weights / jnp.sum(weights, axis=-1, keepdims=True)
    mixed = multiply(weights, value)
    result = jnp.where(masks[0], mixed[:count], 0.0)
    for h in range(1, heads):
        result = result + jnp.where(masks[h], mixed[h * count : (h + 1) * count], 0.0)
    return result


def start_copies(pairs, sems):
    copies = [pltpu.make_async_copy(a, b, sems.at[n]) for n, (a, b) in enumerate(pairs)]
    for copy in copies:
        copy.start()
    return copies


def wait_all(copies):
    for copy in copies:
        copy.wait()


def column_index():
    return lax.axis_index("branch") * lax.axis_size("gj") + lax.axis_index("gj")


def cost(kernel):
    name = getattr(kernel, "func", kernel).__name__
    work = {
        "bias_kernel": 2.0,
        "bias_part_kernel": 0.2,
        "row_kernel": 4.5,
        "pair_blocks_kernel": 3.0,
        "column_kernel": 4.5,
        "msa_blocks_kernel": 0.5,
        "pair_kernel": 4.0,
        "triangle_kernel": 2.0,
        "gather_pair_kernel": 1.0,
        "final_kernel": 1.3,
    }.get(name, 1.0)
    return pl.CostEstimate(
        flops=int(work * 1.1e9), bytes_accessed=int(work * 3.6e6), transcendentals=0
    )


def call(kernel, outs, *operands, scratch=(), sems=(), grant=None):
    def bare(item):
        return item[0] if isinstance(item, list) else item

    n_in, n_out = len(operands), len(outs)
    near_in = [n for n, item in enumerate(operands) if not isinstance(item, list)]
    near_out = [n for n, item in enumerate(outs) if not isinstance(item, list)]
    shapes = [operands[n].shape for n in near_in] + [outs[n] for n in near_out]

    def body(*refs):
        inputs, results = list(refs[:n_in]), list(refs[n_in : n_in + n_out])
        local = refs[n_in + n_out : n_in + n_out + len(shapes)]
        rest, own_sems = refs[n_in + n_out + len(shapes) : -1], refs[-1]
        pairs = list(zip([inputs[n] for n in near_in], local))
        back = list(zip(local[len(near_in) :], [results[n] for n in near_out]))
        for n, ref in zip(near_in, local):
            inputs[n] = ref
        for n, ref in zip(near_out, local[len(near_in) :]):
            results[n] = ref
        copies = start_copies(pairs, own_sems)
        kernel(lambda: wait_all(copies), *inputs, *results, *rest)
        wait_all(start_copies(back, own_sems))

    return pl.pallas_call(
        body,
        out_shape=[jax.ShapeDtypeStruct(bare(out), jnp.float32) for out in outs],
        in_specs=[far] * n_in,
        out_specs=[far] * n_out,
        scratch_shapes=[pltpu.VMEM(shape, jnp.float32) for shape in shapes + list(scratch)]
        + [pltpu.SemaphoreType.DMA((n,)) for n in sems]
        + [pltpu.SemaphoreType.DMA((max(len(near_in), len(near_out), 1),))],
        cost_estimate=cost(kernel),
        compiler_params=pltpu.CompilerParams(vmem_limit_bytes=grant),
    )(*[bare(operand) for operand in operands])


def call_near(kernel, outs, *operands, scratch=(), sems=(), grant=16 * 1024 * 1024):
    return pl.pallas_call(
        lambda *refs: kernel(lambda: None, *refs),
        out_shape=[jax.ShapeDtypeStruct(out, jnp.float32) for out in outs],
        in_specs=[far if isinstance(operand, list) else vmem for operand in operands],
        out_specs=[vmem] * len(outs),
        scratch_shapes=[pltpu.VMEM(shape, jnp.float32) for shape in scratch]
        + [pltpu.SemaphoreType.DMA((n,)) for n in sems],
        compiler_params=pltpu.CompilerParams(vmem_limit_bytes=grant),
        cost_estimate=cost(kernel),
    )(*[operand[0] if isinstance(operand, list) else operand for operand in operands])


def spread(me, refs, slots):
    for k, ref in enumerate(refs):
        slots[me ^ k] = ref[...]


def spread_rows(me, refs, slots):
    for k, ref in enumerate(refs):
        count = ref.shape[0]
        slots[pl.ds(pl.multiple_of((me ^ k) * count, 8), count), :] = ref[...]


def bias_kernel(
    ready, msa_far, pair_far, gains_far, matrix_far, copies_far, out_ref, msa_ref, pair_ref,
    gains_ref, matrix_ref, sems, out_sems
):
    rows = msa_far.shape[0]
    repeats = copies_far.shape[0] // rows
    copies = start_copies(
        [(msa_far, msa_ref), (gains_far, gains_ref), (matrix_far, matrix_ref), (pair_far, pair_ref)],
        sems,
    )
    residues, pair_cols, _ = pair_ref.shape
    heads = matrix_ref.shape[0]
    per = lanes // pair_cols
    ready()
    wait_all(copies)
    copies = start_copies(
        [(msa_ref, copies_far.at[pl.ds(n * rows, rows)]) for n in range(repeats)], out_sems
    )
    normal = layer_normalise(pair_ref[...], gains_ref[0:1, :][None])
    for i in range(residues):
        here = multiply(matrix_ref[...], normal[i], across=True)
        for h in range(heads):
            out_ref[h // per, i : i + 1, pl.ds(h % per * pair_cols, pair_cols)] = here[h : h + 1]
    wait_all(copies)


def pair_blocks_kernel(few, residues, ready, pair_ref, *rest):
    chunks, slots = rest[:-1], rest[-1]
    n_cols = len(chunks)
    block = chunks[0].shape[0]
    groups = block // (residues * few)
    me = column_index()
    ready()
    for c in range(n_cols):
        for o in range(groups):
            for f in range(few):
                source = pl.ds((o * n_cols + c) * few + f, residues, stride=groups * n_cols * few)
                target = pl.ds(c * block + f * groups + o, residues, stride=few * groups)
                slots[target, :] = pair_ref[source, :]
    for k in range(n_cols):
        start = pl.multiple_of((me ^ k) * block, 8)
        chunks[k][...] = slots[pl.ds(start, block), :]


def bias_part_kernel(per_part, ready, *rest):
    blocks, (out_ref,) = rest[:per_part], rest[per_part:]
    ready()
    spread(lax.rem(lax.axis_index("gi"), per_part), blocks, out_ref)


def row_kernel(n_branch, n_gj, per_part, few, ready, msa_ref, *rest):
    n_cols = n_branch * n_gj
    bias_refs, rest = rest[:n_cols], rest[n_cols:]
    gains_far, qkvg_far, final_far, out_ref, slots, gains_ref, qkvg_ref, final_ref, sems = rest
    me, half = column_index(), lax.div(lax.axis_index("gi"), per_part)
    inner = final_ref.shape[0]
    parts = [pl.ds(n * inner, inner) for n in (1, 2, 0, 3)]
    copies = start_copies(
        [(gains_far, gains_ref)]
        + [(qkvg_far.at[:, part], qkvg_ref.at[:, part]) for part in parts]
        + [(final_far, final_ref)]
        + [(ref, slots.at[me ^ k]) for k, ref in enumerate(bias_refs)],
        sems,
    )
    ready()
    _, residues, width = msa_ref.shape
    blocks = slots.shape[2]
    n_gi = lax.axis_size("gi")
    length = n_gi * residues
    per = lanes * n_cols // length
    heads = blocks * per
    rows = msa_ref.shape[0] // n_gi
    inner = final_ref.shape[0]
    queries = per_part * residues
    tokens = jnp.concatenate(
        [msa_ref[g * rows + r] for r in range(rows) for g in range(n_gi)], axis=0
    )
    first = half * (per_part * rows)
    asking = msa_ref[pl.ds(first, per_part * rows)]
    asking = jnp.concatenate(
        [asking[g * rows + r] for r in range(rows) for g in range(per_part)], axis=0
    )
    tokens = layer_normalise(tokens, 1.0)
    normal = layer_normalise(asking, 1.0)
    wait_all(copies[:3])
    gain = gains_ref[0:1, :]
    key_value = multiply(tokens * gain, qkvg_ref[:, inner : 3 * inner])
    normal = normal * gain
    wait_all(copies[3:5])
    query = multiply(normal, qkvg_ref[:, :inner])
    gate = multiply(normal, qkvg_ref[:, 3 * inner :])
    wait_all(copies[5:])
    pieces = [[] for _ in range(heads)]
    for block in range(blocks):
        for g in range(per_part):
            tiles = [[] for _ in range(per)]
            for tile in range(n_cols // per):
                group = [slots[c, g, block] for c in range(tile * per, (tile + 1) * per)]
                for k, piece in enumerate(swap_lane_groups(group)):
                    tiles[k].append(piece)
            for k in range(per):
                pieces[block * per + k].append(jnp.concatenate(tiles[k], axis=1))
    bias = jnp.concatenate([piece for head in pieces for piece in head], axis=0)
    attended = []
    for r in range(rows):
        keys = key_value[r * length : (r + 1) * length, :inner]
        values = key_value[r * length : (r + 1) * length, inner:]
        attended.append(
            attend(query[r * queries : (r + 1) * queries], keys, values, bias, heads)
        )
    attended = jnp.concatenate(attended, axis=0)
    result = asking + multiply(sigmoid(gate) * attended, final_ref[...])
    for b in range(n_branch):
        for g in range(per_part):
            for j in range(n_gj):
                start = g * residues + (b * n_gj + j) * few
                out_ref[(b * per_part + g) * n_gj + j] = jnp.concatenate(
                    [result[r * queries + start : r * queries + start + few] for r in range(rows)],
                    axis=0,
                )


def column_kernel(
    few, heads, ready, msa_ref, gains_ref, qkvg_ref, final_ref, expand_ref, shrink_far, sides_ref,
    left_ref, right_ref, out_ref, shrink_ref, sems
):
    copies = start_copies([(shrink_far, shrink_ref)], sems)
    ready()
    count, width = msa_ref.shape
    inner = final_ref.shape[0]
    half = sides_ref.shape[0] // 2
    first = msa_ref[...]
    projected = multiply(layer_normalise(first, gains_ref[1:2, :]), qkvg_ref[...])
    query, key, value, gate = (projected[:, k * inner : (k + 1) * inner] for k in range(4))
    allowed = None
    if few > 1:
        shape = (heads * count, count)
        asks = lax.broadcasted_iota(jnp.int32, shape, 0)
        holds = lax.broadcasted_iota(jnp.int32, shape, 1)
        allowed = lax.rem(asks, few) == lax.rem(holds, few)
    attended = attend(query, key, value, None, heads, allowed)
    second = first + multiply(sigmoid(gate) * attended, final_ref[...])
    expanded = multiply(layer_normalise(second, gains_ref[2:3, :]), expand_ref[...])
    wait_all(copies)
    third = second + multiply(jnp.maximum(expanded, 0.0), shrink_ref[...])
    out_ref[...] = third
    factors = multiply(sides_ref[...], layer_normalise(third, gains_ref[3:4, :]), across=True)
    left_ref[...] = factors[:half]
    for g in range(right_ref.shape[0]):
        right_ref[g] = factors[half:]


def msa_blocks_kernel(n_branch, n_gj, ready, msa_ref, *rest):
    chunks, slots = rest[:-1], rest[-1]
    per_part, each = slots.shape[1:3]
    ready()
    for b in range(n_branch):
        for g in range(per_part):
            for j in range(n_gj):
                start = ((b * per_part + g) * n_gj + j) * each
                slots[b * n_gj + j, g] = msa_ref[start : start + each]
    for k, chunk in enumerate(chunks):
        chunk[...] = slots[column_index() ^ k]


def gather_msa(few, me, blocks, out_ref, slots):
    n_cols = len(blocks)
    spread(me, blocks, slots)
    for r in range(out_ref.shape[0]):
        out_ref[r] = jnp.concatenate(
            [slots[c, r * few : (r + 1) * few] for c in range(n_cols)], axis=0
        )


def gather_msa_kernel(few, n_cols, ready, *rest):
    ready()
    gather_msa(few, column_index(), rest[:n_cols], *rest[n_cols:])


def gather_pair_kernel(few, n_cols, residues, ready, gains_ref, matrix_ref, *rest):
    blocks, (first_ref, gate_ref, slots) = rest[:n_cols], rest[n_cols:]
    ready()
    spread_rows(column_index(), blocks, slots)
    block = blocks[0].shape[0]
    count = residues * few
    groups = block // count
    for c in range(n_cols):
        for o in range(groups):
            first_ref[pl.ds(o * n_cols + c, count, stride=groups * n_cols), :] = slots[
                pl.ds(c * block + o * count, count), :
            ]
    width = first_ref.shape[1]
    normal = layer_normalise(first_ref[...], gains_ref[1:2, :])
    gate_ref[...] = sigmoid(multiply(normal, matrix_ref[:, 4 * width :]))


def triangle_kernel(few, n_branch, n_gj, ready, tri_ref, *rest):
    n_cols = n_branch * n_gj
    blocks, (out_ref, msa_out, product_ref, slots) = rest[:n_cols], rest[n_cols:]
    ready()
    gather_msa(few, column_index(), blocks, msa_out, slots)
    n_all, rows, _ = out_ref.shape
    n_gi = n_all // n_cols
    share = few
    tiles = rows // few
    each = 2 * share
    wide = lanes // few
    group = lax.broadcasted_iota(jnp.int32, (n_gi * tiles, lanes), 1) // wide
    products = []
    for q in range(share):
        left, right = [], []
        for c in range(n_cols):
            base = (c // n_gj * n_all // n_branch + c % n_gj) * tiles * each
            step = n_gj * tiles * each
            here = jnp.concatenate(
                [
                    tri_ref[pl.ds(base + t * each + q, n_gi, stride=step), :]
                    for t in range(tiles)
                ],
                axis=0,
            )
            left.append(
                jnp.concatenate(
                    [jnp.where(group == i, here, 0.0) for i in range(few)], axis=0
                )
            )
            here = jnp.concatenate(
                [
                    tri_ref[pl.ds(base + g * step + share + q, tiles, stride=each), :]
                    for g in range(n_gi)
                ],
                axis=0,
            )
            rolled = [here] + [pltpu.roll(here, k * wide, 1) for k in range(1, few)]
            copies = []
            for j in range(few):
                copy = rolled[0]
                for k in range(1, few):
                    copy = jnp.where(group == (j + k) % few, rolled[k], copy)
                copies.append(copy)
            step = n_gi * tiles // n_cols
            right.append(
                jnp.concatenate(
                    [copy[k * step : (k + 1) * step] for k in range(n_cols) for copy in copies],
                    axis=0,
                )
            )
        products.append(
            multiply(
                jnp.concatenate(left, axis=1), jnp.concatenate(right, axis=1), across=True
            )
        )
    for c, product in enumerate(swap_lane_groups(products)):
        product_ref[...] = product
        for g in range(n_gi):
            out_ref[(c // n_gj * n_gi + g) * n_gj + c % n_gj] = product_ref[pl.ds(g, rows, stride=n_gi), :]


def pair_kernel(
    few, n_gi, n_cols, ready, *rest
):
    left_refs, pair_refs = rest[:n_cols], rest[n_cols : 2 * n_cols]
    right_ref, gain_ref, matrix_ref, triangle_ref, tri_ref = rest[2 * n_cols : 2 * n_cols + 5]
    chunks = rest[2 * n_cols + 5 : 3 * n_cols + 5]
    rest = rest[3 * n_cols + 5 :]
    left_ref, slots, pair_ref, first_ref = rest
    me = column_index()
    groups_j = n_gi // n_cols
    block = pair_refs[0].shape[0]
    ready()
    spread(me, left_refs, left_ref)
    spread_rows(me, pair_refs, slots)
    _, wide, count = left_ref.shape
    half = block // groups_j
    all_rows = count // few
    residues = n_cols * few
    pair_cols = n_gi * few
    per = lanes // pair_cols
    groups = residues // per
    width = pair_ref.shape[1]
    owner = lax.rem(lax.broadcasted_iota(jnp.int32, (1, count), 1), few)
    left = []
    for c in range(n_cols):
        here = left_ref[c]
        for f in range(few):
            own = jnp.where(owner == f, here, 0.0)
            total = own
            for other in range(few):
                if other != f:
                    total = total + pltpu.roll(own, (other - f) % count, 1)
            left.append(total)
    left = jnp.concatenate(left, axis=0) * (1.0 / all_rows)
    right = []
    for d in range(wide):
        here = right_ref[pl.ds(d, n_gi, stride=wide), :]
        right += [jnp.where(owner == f, here, 0.0) for f in range(few)]
    right = jnp.concatenate(right, axis=0)
    outer = multiply(left, right, across=True)
    outputs = []
    for g in range(groups):
        swapped = swap_lane_groups(
            [outer[(g * per + i) * wide : (g * per + i + 1) * wide] for i in range(per)]
        )
        stacked = [
            s[:, t * lanes : (t + 1) * lanes] for s in swapped for t in range(wide // per)
        ]
        outputs.append(jnp.concatenate(stacked, axis=0))
    for c in range(n_cols):
        for o in range(groups_j):
            pair_ref[pl.ds(c * groups_j + o, half, stride=n_gi), :] = slots[
                pl.ds(c * block + o, half, stride=groups_j), :
            ]
    update = multiply(matrix_ref[...], jnp.concatenate(outputs, axis=1))
    first = pair_ref[...].T + update
    projected = multiply(
        triangle_ref[pl.ds(0, 4 * width), :], layer_normalise(first, gain_ref[...], axis=0)
    )
    tri = sigmoid(projected[2 * width : 4 * width]) * projected[: 2 * width]
    slot_count, _, each, _ = tri_ref.shape
    for g in range(groups):
        tri_ref[:, g] = tri[:, g * lanes : (g + 1) * lanes].reshape(slot_count, each, lanes)
    first_ref[...] = first.T
    for k in range(n_cols):
        for o in range(groups_j):
            rows = pl.ds((me ^ k) * groups_j + o, half, stride=n_gi)
            chunks[k][pl.ds(o * half, half), :] = first_ref[rows, :]


def final_kernel(
    few, residues, packed, ready, product_ref, first_ref, gate_ref, gains_ref, matrix_ref, out_ref,
    channels_ref
):
    positions = out_ref.shape[0]
    ready()
    if packed:
        tiles = residues // few
        tall = product_ref.shape[0] // residues
        product = []
        for t in range(tiles):
            here = [
                product_ref[pl.ds(i * tiles + t, tall, stride=residues), :] for i in range(few)
            ]
            for q, piece in enumerate(swap_lane_groups(here)):
                channels_ref[pl.ds(q, tall, stride=few), :] = piece
            product.append(channels_ref[...])
        product = jnp.concatenate(product, axis=1)
    else:
        product = product_ref[...]
    normal = layer_normalise(product, 1.0, axis=0).T * gains_ref[2:3, :]
    result = first_ref[...] + gate_ref[...] * multiply(normal, matrix_ref[...])
    count = positions // (residues * few)
    for i in range(residues):
        for f in range(few):
            start = (i * few + f) * count
            out_ref[pl.ds(i * few * count + f, count, stride=few), :] = result[
                start : start + count
            ]


def per_device(
    homolog_embedding,
    pair_input_tensor,
    layernorm_scales,
    pair_norm_gains,
    pair_bias_matrix,
    horizontal_qkvg_kernel,
    horizontal_final_kernel,
    vertical_qkvg_kernel,
    vertical_final_kernel,
    feedforward_expand_kernel,
    feedforward_shrink_kernel,
    dyadic_sides_kernel,
    outer_output_matrix,
    triangle_input_matrix,
    triangle_output_matrix,
):
    rows, residues, width = homolog_embedding.shape
    pair_cols, pair_width = pair_input_tensor.shape[1:]
    heads = pair_bias_matrix.shape[1]
    outer_width = dyadic_sides_kernel.shape[1] // 2
    n_branch, n_gi, n_gj = (lax.axis_size(name) for name in everyone)
    n_cols = n_branch * n_gj
    n_all = n_cols * n_gi
    length = residues * n_gi
    few = residues // n_cols
    groups = n_gi // n_cols
    parts = 2
    per_part = n_gi // parts
    own_rows = rows // per_part

    def trade(blocks, axes):
        n = lax.axis_size(axes)
        return [blocks[0]] + [
            lax.ppermute(blocks[k], axes, [(t ^ k, t) for t in range(n) if t ^ k < n])
            for k in range(1, len(blocks))
        ]

    halves = [
        [
            (b * n_gi + part * per_part + g) * n_gj + j
            for b in range(n_branch)
            for g in range(per_part)
            for j in range(n_gj)
        ]
        for part in range(parts)
    ]
    n_half = n_cols * per_part
    positions = residues * pair_cols
    each = own_rows * few

    per = lanes // pair_cols
    bias_block = (heads // per, residues, lanes)
    msa, bias = call(
        bias_kernel,
        [[(parts * rows, residues, width)], bias_block],
        [homolog_embedding],
        [pair_input_tensor],
        [pair_norm_gains],
        [pair_bias_matrix.T],
        scratch=[
            homolog_embedding.shape,
            pair_input_tensor.shape,
            pair_norm_gains.shape,
            (heads, pair_width),
        ],
        sems=[4, parts],
    )
    msa = lax.all_to_all(msa, "gi", 0, 0, tiled=True)
    (bias,) = call_near(
        functools.partial(bias_part_kernel, per_part),
        [(per_part,) + bias_block],
        *trade([bias] * per_part, "gi"),
    )
    bias = trade([bias] * n_cols, columns)
    (msa_first,) = call(
        functools.partial(row_kernel, n_branch, n_gj, per_part, few),
        [(n_half, each, width)],
        msa,
        *[[block] for block in bias],
        [layernorm_scales],
        [horizontal_qkvg_kernel],
        [horizontal_final_kernel],
        scratch=[(n_cols, per_part) + bias_block]
        + [w.shape for w in (layernorm_scales, horizontal_qkvg_kernel, horizontal_final_kernel)],
        sems=[6 + n_cols],
        grant=60 * 1024 * 1024,
    )
    pair, msa_first = lax.optimization_barrier((pair_input_tensor, msa_first))

    msa_first = lax.all_to_all(msa_first, everyone, 0, 0, tiled=True, axis_index_groups=halves)
    count = n_half * each
    weights = (
        layernorm_scales,
        vertical_qkvg_kernel,
        vertical_final_kernel,
        feedforward_expand_kernel,
        [feedforward_shrink_kernel],
        dyadic_sides_kernel.T,
    )
    left, right, alignment = call_near(
        functools.partial(column_kernel, few, heads),
        [(outer_width, count), (n_gi, outer_width, count), (count, width)],
        msa_first.reshape(count, width),
        *weights,
        scratch=[feedforward_shrink_kernel.shape],
        sems=[1],
        grant=60 * 1024 * 1024,
    )
    alignment = call_near(
        functools.partial(msa_blocks_kernel, n_branch, n_gj),
        [(per_part, each, width)] * n_cols,
        alignment,
        scratch=[(n_cols, per_part, each, width)],
    )
    pair = call_near(
        functools.partial(pair_blocks_kernel, few, residues),
        [(positions // n_cols, pair_width)] * n_cols,
        pair.reshape(positions, pair_width),
        scratch=[(positions, pair_width)],
    )
    pair = trade(pair, columns)
    right = lax.all_to_all(right, "gi", 0, 0, tiled=True)
    left = trade([left] * n_cols, columns)
    alignment = [block.reshape(-1, width) for block in trade(alignment, columns)]
    share = max(pair_width // n_all, 1)
    slots = pair_width // share
    triangle = triangle_input_matrix.T.reshape(5, slots, share, pair_width)
    sides = jnp.stack([triangle[0], triangle[2]], axis=1)
    gates = jnp.stack([triangle[1], triangle[3]], axis=1)
    triangle = jnp.concatenate(
        [side.reshape(2 * pair_width, pair_width) for side in (sides, gates)]
        + [triangle[4].reshape(pair_width, pair_width)],
        axis=0,
    )
    matrix = outer_output_matrix.reshape(outer_width, outer_width // per, per, pair_width)
    matrix = jnp.transpose(matrix, (3, 2, 1, 0)).reshape(pair_width, -1)
    tri, *first = call_near(
        functools.partial(pair_kernel, few, n_gi, n_cols),
        [(slots, positions // lanes, 2 * share, lanes)]
        + [(positions // n_cols, pair_width)] * n_cols,
        *left,
        *pair,
        right.reshape(n_gi * outer_width, count),
        pair_norm_gains[1][:, None],
        matrix,
        triangle,
        scratch=[
            (n_cols, outer_width, count),
            (positions, pair_width),
            (positions, pair_width),
            (positions, pair_width),
        ],
    )

    first, gate = call_near(
        functools.partial(gather_pair_kernel, few, n_cols, residues),
        [(positions, pair_width)] * 2,
        pair_norm_gains,
        triangle_input_matrix,
        *trade(first, columns),
        scratch=[(positions, pair_width)],
    )
    tile = (rows, residues, width)
    scratch = [(n_cols, rows * few, width)]
    packed = share * n_all == pair_width and share == few and few == per
    if packed:
        tri = lax.all_to_all(tri, everyone, 0, 0, tiled=True)
        product, alignment_output = call_near(
            functools.partial(triangle_kernel, few, n_branch, n_gj),
            [(n_all, residues, lanes), tile],
            tri.reshape(-1, lanes),
            *alignment,
            scratch=[(lanes, lanes)] + scratch,
        )
        product = lax.all_to_all(product, everyone, 0, 0, tiled=True)
        product = product.reshape(n_all * residues, lanes)
    else:
        (alignment_output,) = call_near(
            functools.partial(gather_msa_kernel, few, n_cols),
            [tile],
            *alignment,
            scratch=scratch,
        )
        tri = jnp.transpose(tri.reshape(slots, -1, 2, share, lanes), (2, 1, 4, 0, 3))
        tri = tri.reshape(2, residues, pair_cols, pair_width)
        right_columns = lax.all_gather(tri[1], "gi", axis=0, tiled=True)
        product = lax.psum_scatter(
            jnp.einsum("jkc,ikc->jic", right_columns, tri[0], precision=precise),
            columns,
            scatter_dimension=0,
            tiled=True,
        ).reshape(groups, n_cols, few, residues, pair_width)
        product = jnp.transpose(product, (4, 3, 2, 0, 1)).reshape(pair_width, positions)
    (pair_output_tensor,) = call_near(
        functools.partial(final_kernel, few, residues, packed),
        [(positions, pair_width)],
        product,
        first,
        gate,
        pair_norm_gains,
        triangle_output_matrix,
        scratch=[(pair_width, lanes)],
    )
    return (
        alignment_output,
        pair_output_tensor.reshape(residues, pair_cols, pair_width),
    )


def solution(mesh):
    tile, grid = P(("branch", "gj"), "gi", None), P("gi", ("branch", "gj"), None)
    return jax.shard_map(
        per_device,
        mesh=mesh,
        in_specs=(tile, grid) + (P(),) * 13,
        out_specs=(tile, grid),
        check_vma=False,
    )
```

```python
import functools
import math

import jax
import jax.numpy as jnp
from jax import lax
from jax.experimental import pallas as pl
from jax.experimental.pallas import tpu as pltpu
from jax.sharding import PartitionSpec as P

epsilon = 1e-05
precise = lax.Precision.HIGH
everyone = ("branch", "gi", "gj")
columns = ("branch", "gj")
lanes = 128
far = pl.BlockSpec(memory_space=pl.ANY)
vmem = pl.BlockSpec(memory_space=pltpu.VMEM)
params = pltpu.CompilerParams(vmem_limit_bytes=16 * 1024 * 1024)


def layer_normalise(values, norm_gain, axis=-1):
    average = jnp.mean(values, axis=axis, keepdims=True)
    centred = values - average
    variance = jnp.mean(centred * centred, axis=axis, keepdims=True)
    return centred * lax.rsqrt(variance + epsilon) * norm_gain


def apply_projection(values, weight):
    return jnp.einsum("...c,cd->...d", values, weight, precision=precise)


def sigmoid(values):
    return 1.0 / (1.0 + jnp.exp(-values))


def split(values):
    high = values.astype(jnp.bfloat16)
    return high, (values - high.astype(jnp.float32)).astype(jnp.bfloat16)


def multiply(left, right, across=False):
    numbers = (((1,), (1 if across else 0,)), ((), ()))

    def one(a, b):
        return lax.dot_general(a, b, numbers, preferred_element_type=jnp.float32)

    (lh, ll), (rh, rl) = split(left), split(right)
    return one(lh, rh) + (one(lh, rl) + one(ll, rh))


def swap_lane_groups(arrays):
    n, arrays = len(arrays), list(arrays)
    width = lanes // n
    wide = arrays[0].shape[-1]
    lane = lax.broadcasted_iota(jnp.int32, arrays[0].shape, arrays[0].ndim - 1)
    group = lax.rem(lane, lanes) // width
    axis = arrays[0].ndim - 1
    step = 1
    while step < n:
        upper = (group // step) % 2 == 1
        for low in range(n):
            if low & step:
                continue
            a, b = arrays[low], arrays[low + step]
            arrays[low] = jnp.where(upper, pltpu.roll(b, step * width, axis), a)
            arrays[low + step] = jnp.where(
                upper, b, pltpu.roll(a, wide - step * width, axis)
            )
        step *= 2
    return arrays


def head_masks(shape, heads):
    column = lax.broadcasted_iota(jnp.int32, shape, 1)
    return [column // (shape[1] // heads) == h for h in range(heads)]


def attend(query, key, value, bias, heads, allowed=None):
    count, inner = query.shape
    masks = head_masks((count, inner), heads)
    spread = jnp.concatenate([jnp.where(m, query, 0.0) for m in masks], axis=0)
    scores = multiply(spread, key, across=True) * (1.0 / math.sqrt(inner // heads))
    if bias is not None:
        scores = scores + bias
    if allowed is not None:
        scores = jnp.where(allowed, scores, -1e30)
    weights = jnp.exp(scores - jnp.max(scores, axis=-1, keepdims=True))
    weights = weights / jnp.sum(weights, axis=-1, keepdims=True)
    mixed = multiply(weights, value)
    result = jnp.where(masks[0], mixed[:count], 0.0)
    for h in range(1, heads):
        result = result + jnp.where(masks[h], mixed[h * count : (h + 1) * count], 0.0)
    return result


def start_copies(pairs, sems):
    copies = [pltpu.make_async_copy(a, b, sems.at[n]) for n, (a, b) in enumerate(pairs)]
    for copy in copies:
        copy.start()
    return copies


def wait_all(copies):
    for copy in copies:
        copy.wait()


def column_index():
    return lax.axis_index("branch") * lax.axis_size("gj") + lax.axis_index("gj")


def cost(kernel):
    name = getattr(kernel, "func", kernel).__name__
    work = {
        "bias_kernel": 2.0,
        "bias_part_kernel": 6.0,
        "row_kernel": 4.5,
        "pair_blocks_kernel": 8.0,
        "column_kernel": 4.5,
        "msa_blocks_kernel": 0.5,
        "pair_kernel": 4.0,
        "triangle_kernel": 2.0,
        "gather_pair_kernel": 1.0,
        "final_kernel": 1.3,
    }.get(name, 1.0)
    return pl.CostEstimate(
        flops=int(work * 1.1e9), bytes_accessed=int(work * 3.6e6), transcendentals=0
    )


def call(kernel, outs, *operands, scratch=(), sems=()):
    def bare(item):
        return item[0] if isinstance(item, list) else item

    n_in, n_out = len(operands), len(outs)
    near_in = [n for n, item in enumerate(operands) if not isinstance(item, list)]
    near_out = [n for n, item in enumerate(outs) if not isinstance(item, list)]
    shapes = [operands[n].shape for n in near_in] + [outs[n] for n in near_out]

    def body(*refs):
        inputs, results = list(refs[:n_in]), list(refs[n_in : n_in + n_out])
        local = refs[n_in + n_out : n_in + n_out + len(shapes)]
        rest, own_sems = refs[n_in + n_out + len(shapes) : -1], refs[-1]
        pairs = list(zip([inputs[n] for n in near_in], local))
        back = list(zip(local[len(near_in) :], [results[n] for n in near_out]))
        for n, ref in zip(near_in, local):
            inputs[n] = ref
        for n, ref in zip(near_out, local[len(near_in) :]):
            results[n] = ref
        copies = start_copies(pairs, own_sems)
        kernel(lambda: wait_all(copies), *inputs, *results, *rest)
        wait_all(start_copies(back, own_sems))

    return pl.pallas_call(
        body,
        out_shape=[jax.ShapeDtypeStruct(bare(out), jnp.float32) for out in outs],
        in_specs=[far] * n_in,
        out_specs=[far] * n_out,
        scratch_shapes=[pltpu.VMEM(shape, jnp.float32) for shape in shapes + list(scratch)]
        + [pltpu.SemaphoreType.DMA((n,)) for n in sems]
        + [pltpu.SemaphoreType.DMA((max(len(near_in), len(near_out), 1),))],
        cost_estimate=cost(kernel),
    )(*[bare(operand) for operand in operands])


def call_near(kernel, outs, *operands, scratch=()):
    return pl.pallas_call(
        lambda *refs: kernel(lambda: None, *refs),
        out_shape=[jax.ShapeDtypeStruct(out, jnp.float32) for out in outs],
        in_specs=[vmem] * len(operands),
        out_specs=[vmem] * len(outs),
        scratch_shapes=[pltpu.VMEM(shape, jnp.float32) for shape in scratch],
        compiler_params=params,
        cost_estimate=cost(kernel),
    )(*operands)


def spread(me, refs, slots):
    for k, ref in enumerate(refs):
        slots[me ^ k] = ref[...]


def spread_rows(me, refs, slots):
    for k, ref in enumerate(refs):
        count = ref.shape[0]
        slots[pl.ds(pl.multiple_of((me ^ k) * count, 8), count), :] = ref[...]


def bias_kernel(
    ready, msa_far, pair_far, gains_far, matrix_far, copies_far, out_ref, msa_ref, pair_ref,
    gains_ref, matrix_ref, sems, out_sems
):
    rows = msa_far.shape[0]
    repeats = copies_far.shape[0] // rows
    copies = start_copies(
        [(msa_far, msa_ref), (gains_far, gains_ref), (matrix_far, matrix_ref), (pair_far, pair_ref)],
        sems,
    )
    residues, pair_cols, _ = pair_ref.shape
    heads = matrix_ref.shape[0]
    per = lanes // pair_cols
    ready()
    wait_all(copies)
    copies = start_copies(
        [(msa_ref, copies_far.at[pl.ds(n * rows, rows)]) for n in range(repeats)], out_sems
    )
    normal = layer_normalise(pair_ref[...], gains_ref[0:1, :][None])
    for i in range(residues):
        here = multiply(matrix_ref[...], normal[i], across=True)
        for h in range(heads):
            out_ref[h // per, i : i + 1, pl.ds(h % per * pair_cols, pair_cols)] = here[h : h + 1]
    wait_all(copies)


def pair_blocks_kernel(few, residues, ready, pair_ref, *rest):
    chunks, slots = rest[:-1], rest[-1]
    n_cols = len(chunks)
    block = chunks[0].shape[0]
    groups = block // (residues * few)
    me = column_index()
    ready()
    for c in range(n_cols):
        for o in range(groups):
            for f in range(few):
                source = pl.ds((o * n_cols + c) * few + f, residues, stride=groups * n_cols * few)
                target = pl.ds(c * block + f * groups + o, residues, stride=few * groups)
                slots[target, :] = pair_ref[source, :]
    for k in range(n_cols):
        start = pl.multiple_of((me ^ k) * block, 8)
        chunks[k][...] = slots[pl.ds(start, block), :]


def bias_part_kernel(per_part, ready, *rest):
    blocks, (out_ref,) = rest[:per_part], rest[per_part:]
    ready()
    spread(lax.rem(lax.axis_index("gi"), per_part), blocks, out_ref)


def row_kernel(n_branch, n_gj, per_part, few, ready, msa_ref, *rest):
    n_cols = n_branch * n_gj
    bias_refs, (gains_ref, qkvg_ref, final_ref, out_ref, slots) = rest[:n_cols], rest[n_cols:]
    half = lax.div(lax.axis_index("gi"), per_part)
    ready()
    _, residues, width = msa_ref.shape
    blocks = slots.shape[2]
    n_gi = lax.axis_size("gi")
    length = n_gi * residues
    per = lanes * n_cols // length
    heads = blocks * per
    rows = msa_ref.shape[0] // n_gi
    inner = final_ref.shape[0]
    queries = per_part * residues
    tokens = jnp.concatenate(
        [msa_ref[g * rows + r] for r in range(rows) for g in range(n_gi)], axis=0
    )
    first = half * (per_part * rows)
    asking = msa_ref[pl.ds(first, per_part * rows)]
    asking = jnp.concatenate(
        [asking[g * rows + r] for r in range(rows) for g in range(per_part)], axis=0
    )
    tokens = layer_normalise(tokens, 1.0)
    normal = layer_normalise(asking, 1.0)
    gain = gains_ref[0:1, :]
    key_value = multiply(tokens * gain, qkvg_ref[:, inner : 3 * inner])
    normal = normal * gain
    query = multiply(normal, qkvg_ref[:, :inner])
    gate = multiply(normal, qkvg_ref[:, 3 * inner :])
    spread(column_index(), bias_refs, slots)
    pieces = [[] for _ in range(heads)]
    for block in range(blocks):
        for g in range(per_part):
            tiles = [[] for _ in range(per)]
            for tile in range(n_cols // per):
                group = [slots[c, g, block] for c in range(tile * per, (tile + 1) * per)]
                for k, piece in enumerate(swap_lane_groups(group)):
                    tiles[k].append(piece)
            for k in range(per):
                pieces[block * per + k].append(jnp.concatenate(tiles[k], axis=1))
    bias = jnp.concatenate([piece for head in pieces for piece in head], axis=0)
    attended = []
    for r in range(rows):
        keys = key_value[r * length : (r + 1) * length, :inner]
        values = key_value[r * length : (r + 1) * length, inner:]
        attended.append(
            attend(query[r * queries : (r + 1) * queries], keys, values, bias, heads)
        )
    attended = jnp.concatenate(attended, axis=0)
    result = asking + multiply(sigmoid(gate) * attended, final_ref[...])
    for b in range(n_branch):
        for g in range(per_part):
            for j in range(n_gj):
                start = g * residues + (b * n_gj + j) * few
                out_ref[(b * per_part + g) * n_gj + j] = jnp.concatenate(
                    [result[r * queries + start : r * queries + start + few] for r in range(rows)],
                    axis=0,
                )


def column_kernel(
    few, heads, ready, msa_ref, gains_ref, qkvg_ref, final_ref, expand_ref, shrink_ref, sides_ref,
    left_ref, right_ref, out_ref
):
    ready()
    count, width = msa_ref.shape
    inner = final_ref.shape[0]
    half = sides_ref.shape[0] // 2
    first = msa_ref[...]
    projected = multiply(layer_normalise(first, gains_ref[1:2, :]), qkvg_ref[...])
    query, key, value, gate = (projected[:, k * inner : (k + 1) * inner] for k in range(4))
    allowed = None
    if few > 1:
        shape = (heads * count, count)
        asks = lax.broadcasted_iota(jnp.int32, shape, 0)
        holds = lax.broadcasted_iota(jnp.int32, shape, 1)
        allowed = lax.rem(asks, few) == lax.rem(holds, few)
    attended = attend(query, key, value, None, heads, allowed)
    second = first + multiply(sigmoid(gate) * attended, final_ref[...])
    expanded = multiply(layer_normalise(second, gains_ref[2:3, :]), expand_ref[...])
    third = second + multiply(jnp.maximum(expanded, 0.0), shrink_ref[...])
    out_ref[...] = third
    factors = multiply(sides_ref[...], layer_normalise(third, gains_ref[3:4, :]), across=True)
    left_ref[...] = factors[:half]
    for g in range(right_ref.shape[0]):
        right_ref[g] = factors[half:]


def msa_blocks_kernel(n_branch, n_gj, ready, msa_ref, *rest):
    chunks, slots = rest[:-1], rest[-1]
    per_part, each = slots.shape[1:3]
    ready()
    for b in range(n_branch):
        for g in range(per_part):
            for j in range(n_gj):
                start = ((b * per_part + g) * n_gj + j) * each
                slots[b * n_gj + j, g] = msa_ref[start : start + each]
    for k, chunk in enumerate(chunks):
        chunk[...] = slots[column_index() ^ k]


def gather_msa(few, me, blocks, out_ref, slots):
    n_cols = len(blocks)
    spread(me, blocks, slots)
    for r in range(out_ref.shape[0]):
        out_ref[r] = jnp.concatenate(
            [slots[c, r * few : (r + 1) * few] for c in range(n_cols)], axis=0
        )


def gather_msa_kernel(few, n_cols, ready, *rest):
    ready()
    gather_msa(few, column_index(), rest[:n_cols], *rest[n_cols:])


def gather_pair_kernel(few, n_cols, residues, ready, gains_ref, matrix_ref, *rest):
    blocks, (first_ref, gate_ref, slots) = rest[:n_cols], rest[n_cols:]
    ready()
    spread_rows(column_index(), blocks, slots)
    block = blocks[0].shape[0]
    count = residues * few
    groups = block // count
    for c in range(n_cols):
        for o in range(groups):
            first_ref[pl.ds(o * n_cols + c, count, stride=groups * n_cols), :] = slots[
                pl.ds(c * block + o * count, count), :
            ]
    width = first_ref.shape[1]
    normal = layer_normalise(first_ref[...], gains_ref[1:2, :])
    gate_ref[...] = sigmoid(multiply(normal, matrix_ref[:, 4 * width :]))


def triangle_kernel(few, n_branch, n_gj, ready, tri_ref, *rest):
    n_cols = n_branch * n_gj
    blocks, (out_ref, msa_out, product_ref, slots) = rest[:n_cols], rest[n_cols:]
    ready()
    gather_msa(few, column_index(), blocks, msa_out, slots)
    n_all, rows, _ = out_ref.shape
    n_gi = n_all // n_cols
    share = few
    tiles = rows // few
    each = 2 * share
    wide = lanes // few
    group = lax.broadcasted_iota(jnp.int32, (n_gi * tiles, lanes), 1) // wide
    products = []
    for q in range(share):
        left, right = [], []
        for c in range(n_cols):
            base = (c // n_gj * n_all // n_branch + c % n_gj) * tiles * each
            step = n_gj * tiles * each
            here = jnp.concatenate(
                [
                    tri_ref[pl.ds(base + t * each + q, n_gi, stride=step), :]
                    for t in range(tiles)
                ],
                axis=0,
            )
            left.append(
                jnp.concatenate(
                    [jnp.where(group == i, here, 0.0) for i in range(few)], axis=0
                )
            )
            here = jnp.concatenate(
                [
                    tri_ref[pl.ds(base + g * step + share + q, tiles, stride=each), :]
                    for g in range(n_gi)
                ],
                axis=0,
            )
            rolled = [here] + [pltpu.roll(here, k * wide, 1) for k in range(1, few)]
            copies = []
            for j in range(few):
                copy = rolled[0]
                for k in range(1, few):
                    copy = jnp.where(group == (j + k) % few, rolled[k], copy)
                copies.append(copy)
            step = n_gi * tiles // n_cols
            right.append(
                jnp.concatenate(
                    [copy[k * step : (k + 1) * step] for k in range(n_cols) for copy in copies],
                    axis=0,
                )
            )
        products.append(
            multiply(
                jnp.concatenate(left, axis=1), jnp.concatenate(right, axis=1), across=True
            )
        )
    for c, product in enumerate(swap_lane_groups(products)):
        product_ref[...] = product
        for g in range(n_gi):
            out_ref[(c // n_gj * n_gi + g) * n_gj + c % n_gj] = product_ref[pl.ds(g, rows, stride=n_gi), :]


def pair_kernel(
    few, n_gi, n_cols, ready, *rest
):
    left_refs, pair_refs = rest[:n_cols], rest[n_cols : 2 * n_cols]
    right_ref, gain_ref, matrix_ref, triangle_ref, tri_ref = rest[2 * n_cols : 2 * n_cols + 5]
    chunks = rest[2 * n_cols + 5 : 3 * n_cols + 5]
    rest = rest[3 * n_cols + 5 :]
    left_ref, slots, pair_ref, first_ref = rest
    me = column_index()
    groups_j = n_gi // n_cols
    block = pair_refs[0].shape[0]
    ready()
    spread(me, left_refs, left_ref)
    spread_rows(me, pair_refs, slots)
    _, wide, count = left_ref.shape
    half = block // groups_j
    all_rows = count // few
    residues = n_cols * few
    pair_cols = n_gi * few
    per = lanes // pair_cols
    groups = residues // per
    width = pair_ref.shape[1]
    owner = lax.rem(lax.broadcasted_iota(jnp.int32, (1, count), 1), few)
    left = []
    for c in range(n_cols):
        here = left_ref[c]
        for f in range(few):
            own = jnp.where(owner == f, here, 0.0)
            total = own
            for other in range(few):
                if other != f:
                    total = total + pltpu.roll(own, (other - f) % count, 1)
            left.append(total)
    left = jnp.concatenate(left, axis=0) * (1.0 / all_rows)
    right = []
    for d in range(wide):
        here = right_ref[pl.ds(d, n_gi, stride=wide), :]
        right += [jnp.where(owner == f, here, 0.0) for f in range(few)]
    right = jnp.concatenate(right, axis=0)
    outer = multiply(left, right, across=True)
    outputs = []
    for g in range(groups):
        swapped = swap_lane_groups(
            [outer[(g * per + i) * wide : (g * per + i + 1) * wide] for i in range(per)]
        )
        stacked = [
            s[:, t * lanes : (t + 1) * lanes] for s in swapped for t in range(wide // per)
        ]
        outputs.append(jnp.concatenate(stacked, axis=0))
    for c in range(n_cols):
        for o in range(groups_j):
            pair_ref[pl.ds(c * groups_j + o, half, stride=n_gi), :] = slots[
                pl.ds(c * block + o, half, stride=groups_j), :
            ]
    update = multiply(matrix_ref[...], jnp.concatenate(outputs, axis=1))
    first = pair_ref[...].T + update
    projected = multiply(
        triangle_ref[pl.ds(0, 4 * width), :], layer_normalise(first, gain_ref[...], axis=0)
    )
    tri = sigmoid(projected[2 * width : 4 * width]) * projected[: 2 * width]
    slot_count, _, each, _ = tri_ref.shape
    for g in range(groups):
        tri_ref[:, g] = tri[:, g * lanes : (g + 1) * lanes].reshape(slot_count, each, lanes)
    first_ref[...] = first.T
    for k in range(n_cols):
        for o in range(groups_j):
            rows = pl.ds((me ^ k) * groups_j + o, half, stride=n_gi)
            chunks[k][pl.ds(o * half, half), :] = first_ref[rows, :]


def final_kernel(
    few, residues, packed, ready, product_ref, first_ref, gate_ref, gains_ref, matrix_ref, out_ref,
    channels_ref
):
    positions = out_ref.shape[0]
    ready()
    if packed:
        tiles = residues // few
        tall = product_ref.shape[0] // residues
        product = []
        for t in range(tiles):
            here = [
                product_ref[pl.ds(i * tiles + t, tall, stride=residues), :] for i in range(few)
            ]
            for q, piece in enumerate(swap_lane_groups(here)):
                channels_ref[pl.ds(q, tall, stride=few), :] = piece
            product.append(channels_ref[...])
        product = jnp.concatenate(product, axis=1)
    else:
        product = product_ref[...]
    normal = layer_normalise(product, 1.0, axis=0).T * gains_ref[2:3, :]
    result = first_ref[...] + gate_ref[...] * multiply(normal, matrix_ref[...])
    count = positions // (residues * few)
    for i in range(residues):
        for f in range(few):
            start = (i * few + f) * count
            out_ref[pl.ds(i * few * count + f, count, stride=few), :] = result[
                start : start + count
            ]


def per_device(
    homolog_embedding,
    pair_input_tensor,
    layernorm_scales,
    pair_norm_gains,
    pair_bias_matrix,
    horizontal_qkvg_kernel,
    horizontal_final_kernel,
    vertical_qkvg_kernel,
    vertical_final_kernel,
    feedforward_expand_kernel,
    feedforward_shrink_kernel,
    dyadic_sides_kernel,
    outer_output_matrix,
    triangle_input_matrix,
    triangle_output_matrix,
):
    rows, residues, width = homolog_embedding.shape
    pair_cols, pair_width = pair_input_tensor.shape[1:]
    heads = pair_bias_matrix.shape[1]
    outer_width = dyadic_sides_kernel.shape[1] // 2
    n_branch, n_gi, n_gj = (lax.axis_size(name) for name in everyone)
    n_cols = n_branch * n_gj
    n_all = n_cols * n_gi
    length = residues * n_gi
    few = residues // n_cols
    groups = n_gi // n_cols
    parts = 2
    per_part = n_gi // parts
    own_rows = rows // per_part

    def trade(blocks, axes):
        n = lax.axis_size(axes)
        return [blocks[0]] + [
            lax.ppermute(blocks[k], axes, [(t ^ k, t) for t in range(n) if t ^ k < n])
            for k in range(1, len(blocks))
        ]

    halves = [
        [
            (b * n_gi + part * per_part + g) * n_gj + j
            for b in range(n_branch)
            for g in range(per_part)
            for j in range(n_gj)
        ]
        for part in range(parts)
    ]
    n_half = n_cols * per_part
    positions = residues * pair_cols
    each = own_rows * few

    per = lanes // pair_cols
    bias_block = (heads // per, residues, lanes)
    msa, bias = call(
        bias_kernel,
        [[(parts * rows, residues, width)], bias_block],
        [homolog_embedding],
        [pair_input_tensor],
        [pair_norm_gains],
        [pair_bias_matrix.T],
        scratch=[
            homolog_embedding.shape,
            pair_input_tensor.shape,
            pair_norm_gains.shape,
            (heads, pair_width),
        ],
        sems=[4, parts],
    )
    msa = lax.all_to_all(msa, "gi", 0, 0, tiled=True)
    (bias,) = call_near(
        functools.partial(bias_part_kernel, per_part),
        [(per_part,) + bias_block],
        *trade([bias] * per_part, "gi"),
    )
    bias = trade([bias] * n_cols, columns)
    (msa_first,) = call_near(
        functools.partial(row_kernel, n_branch, n_gj, per_part, few),
        [(n_half, each, width)],
        msa,
        *bias,
        layernorm_scales,
        horizontal_qkvg_kernel,
        horizontal_final_kernel,
        scratch=[(n_cols, per_part) + bias_block],
    )
    pair, msa_first = lax.optimization_barrier((pair_input_tensor, msa_first))

    msa_first = lax.all_to_all(msa_first, everyone, 0, 0, tiled=True, axis_index_groups=halves)
    count = n_half * each
    weights = (
        layernorm_scales,
        vertical_qkvg_kernel,
        vertical_final_kernel,
        feedforward_expand_kernel,
        feedforward_shrink_kernel,
        dyadic_sides_kernel.T,
    )
    left, right, alignment = call_near(
        functools.partial(column_kernel, few, heads),
        [(outer_width, count), (n_gi, outer_width, count), (count, width)],
        msa_first.reshape(count, width),
        *weights,
    )
    alignment = call_near(
        functools.partial(msa_blocks_kernel, n_branch, n_gj),
        [(per_part, each, width)] * n_cols,
        alignment,
        scratch=[(n_cols, per_part, each, width)],
    )
    pair = call_near(
        functools.partial(pair_blocks_kernel, few, residues),
        [(positions // n_cols, pair_width)] * n_cols,
        pair.reshape(positions, pair_width),
        scratch=[(positions, pair_width)],
    )
    pair = trade(pair, columns)
    right = lax.all_to_all(right, "gi", 0, 0, tiled=True)
    left = trade([left] * n_cols, columns)
    alignment = [block.reshape(-1, width) for block in trade(alignment, columns)]
    share = max(pair_width // n_all, 1)
    slots = pair_width // share
    triangle = triangle_input_matrix.T.reshape(5, slots, share, pair_width)
    sides = jnp.stack([triangle[0], triangle[2]], axis=1)
    gates = jnp.stack([triangle[1], triangle[3]], axis=1)
    triangle = jnp.concatenate(
        [side.reshape(2 * pair_width, pair_width) for side in (sides, gates)]
        + [triangle[4].reshape(pair_width, pair_width)],
        axis=0,
    )
    matrix = outer_output_matrix.reshape(outer_width, outer_width // per, per, pair_width)
    matrix = jnp.transpose(matrix, (3, 2, 1, 0)).reshape(pair_width, -1)
    tri, *first = call_near(
        functools.partial(pair_kernel, few, n_gi, n_cols),
        [(slots, positions // lanes, 2 * share, lanes)]
        + [(positions // n_cols, pair_width)] * n_cols,
        *left,
        *pair,
        right.reshape(n_gi * outer_width, count),
        pair_norm_gains[1][:, None],
        matrix,
        triangle,
        scratch=[
            (n_cols, outer_width, count),
            (positions, pair_width),
            (positions, pair_width),
            (positions, pair_width),
        ],
    )

    first, gate = call_near(
        functools.partial(gather_pair_kernel, few, n_cols, residues),
        [(positions, pair_width)] * 2,
        pair_norm_gains,
        triangle_input_matrix,
        *trade(first, columns),
        scratch=[(positions, pair_width)],
    )
    tile = (rows, residues, width)
    scratch = [(n_cols, rows * few, width)]
    packed = share * n_all == pair_width and share == few and few == per
    if packed:
        tri = lax.all_to_all(tri, everyone, 0, 0, tiled=True)
        product, alignment_output = call_near(
            functools.partial(triangle_kernel, few, n_branch, n_gj),
            [(n_all, residues, lanes), tile],
            tri.reshape(-1, lanes),
            *alignment,
            scratch=[(lanes, lanes)] + scratch,
        )
        product = lax.all_to_all(product, everyone, 0, 0, tiled=True)
        product = product.reshape(n_all * residues, lanes)
    else:
        (alignment_output,) = call_near(
            functools.partial(gather_msa_kernel, few, n_cols),
            [tile],
            *alignment,
            scratch=scratch,
        )
        tri = jnp.transpose(tri.reshape(slots, -1, 2, share, lanes), (2, 1, 4, 0, 3))
        tri = tri.reshape(2, residues, pair_cols, pair_width)
        right_columns = lax.all_gather(tri[1], "gi", axis=0, tiled=True)
        product = lax.psum_scatter(
            jnp.einsum("jkc,ikc->jic", right_columns, tri[0], precision=precise),
            columns,
            scatter_dimension=0,
            tiled=True,
        ).reshape(groups, n_cols, few, residues, pair_width)
        product = jnp.transpose(product, (4, 3, 2, 0, 1)).reshape(pair_width, positions)
    (pair_output_tensor,) = call_near(
        functools.partial(final_kernel, few, residues, packed),
        [(positions, pair_width)],
        product,
        first,
        gate,
        pair_norm_gains,
        triangle_output_matrix,
        scratch=[(pair_width, lanes)],
    )
    return (
        alignment_output,
        pair_output_tensor.reshape(residues, pair_cols, pair_width),
    )


def solution(mesh):
    tile, grid = P(("branch", "gj"), "gi", None), P("gi", ("branch", "gj"), None)
    return jax.shard_map(
        per_device,
        mesh=mesh,
        in_specs=(tile, grid) + (P(),) * 13,
        out_specs=(tile, grid),
        check_vma=False,
    )
```

```python
import functools
import math

import jax
import jax.numpy as jnp
from jax import lax
from jax.experimental import pallas as pl
from jax.experimental.pallas import tpu as pltpu
from jax.sharding import PartitionSpec as P

epsilon = 1e-05
precise = lax.Precision.HIGH
everyone = ("branch", "gi", "gj")
columns = ("branch", "gj")
lanes = 128
far = pl.BlockSpec(memory_space=pl.ANY)
vmem = pl.BlockSpec(memory_space=pltpu.VMEM)
params = pltpu.CompilerParams(vmem_limit_bytes=16 * 1024 * 1024)


def layer_normalise(values, norm_gain, axis=-1):
    average = jnp.mean(values, axis=axis, keepdims=True)
    centred = values - average
    variance = jnp.mean(centred * centred, axis=axis, keepdims=True)
    return centred * lax.rsqrt(variance + epsilon) * norm_gain


def apply_projection(values, weight):
    return jnp.einsum("...c,cd->...d", values, weight, precision=precise)


def sigmoid(values):
    return 1.0 / (1.0 + jnp.exp(-values))


def split(values):
    high = values.astype(jnp.bfloat16)
    return high, (values - high.astype(jnp.float32)).astype(jnp.bfloat16)


def multiply(left, right, across=False):
    numbers = (((1,), (1 if across else 0,)), ((), ()))

    def one(a, b):
        return lax.dot_general(a, b, numbers, preferred_element_type=jnp.float32)

    (lh, ll), (rh, rl) = split(left), split(right)
    return one(lh, rh) + (one(lh, rl) + one(ll, rh))


def swap_lane_groups(arrays):
    n, arrays = len(arrays), list(arrays)
    width = lanes // n
    wide = arrays[0].shape[-1]
    lane = lax.broadcasted_iota(jnp.int32, arrays[0].shape, arrays[0].ndim - 1)
    group = lax.rem(lane, lanes) // width
    axis = arrays[0].ndim - 1
    step = 1
    while step < n:
        upper = (group // step) % 2 == 1
        for low in range(n):
            if low & step:
                continue
            a, b = arrays[low], arrays[low + step]
            arrays[low] = jnp.where(upper, pltpu.roll(b, step * width, axis), a)
            arrays[low + step] = jnp.where(
                upper, b, pltpu.roll(a, wide - step * width, axis)
            )
        step *= 2
    return arrays


def head_masks(shape, heads):
    column = lax.broadcasted_iota(jnp.int32, shape, 1)
    return [column // (shape[1] // heads) == h for h in range(heads)]


def attend(query, key, value, bias, heads, allowed=None):
    count, inner = query.shape
    masks = head_masks((count, inner), heads)
    spread = jnp.concatenate([jnp.where(m, query, 0.0) for m in masks], axis=0)
    scores = multiply(spread, key, across=True) * (1.0 / math.sqrt(inner // heads))
    if bias is not None:
        scores = scores + bias
    if allowed is not None:
        scores = jnp.where(allowed, scores, -1e30)
    weights = jnp.exp(scores - jnp.max(scores, axis=-1, keepdims=True))
    weights = weights / jnp.sum(weights, axis=-1, keepdims=True)
    mixed = multiply(weights, value)
    result = jnp.where(masks[0], mixed[:count], 0.0)
    for h in range(1, heads):
        result = result + jnp.where(masks[h], mixed[h * count : (h + 1) * count], 0.0)
    return result


def start_copies(pairs, sems):
    copies = [pltpu.make_async_copy(a, b, sems.at[n]) for n, (a, b) in enumerate(pairs)]
    for copy in copies:
        copy.start()
    return copies


def wait_all(copies):
    for copy in copies:
        copy.wait()


def column_index():
    return lax.axis_index("branch") * lax.axis_size("gj") + lax.axis_index("gj")


def cost(kernel):
    name = getattr(kernel, "func", kernel).__name__
    work = {
        "bias_kernel": 2.0,
        "bias_part_kernel": 6.0,
        "row_kernel": 4.5,
        "pair_blocks_kernel": 8.0,
        "column_kernel": 4.5,
        "msa_blocks_kernel": 0.5,
        "pair_kernel": 4.0,
        "triangle_kernel": 2.0,
        "gather_pair_kernel": 1.0,
        "final_kernel": 1.3,
    }.get(name, 1.0)
    return pl.CostEstimate(
        flops=int(work * 1.1e9), bytes_accessed=int(work * 3.6e6), transcendentals=0
    )


def call(kernel, outs, *operands, scratch=(), sems=()):
    def bare(item):
        return item[0] if isinstance(item, list) else item

    n_in, n_out = len(operands), len(outs)
    near_in = [n for n, item in enumerate(operands) if not isinstance(item, list)]
    near_out = [n for n, item in enumerate(outs) if not isinstance(item, list)]
    shapes = [operands[n].shape for n in near_in] + [outs[n] for n in near_out]

    def body(*refs):
        inputs, results = list(refs[:n_in]), list(refs[n_in : n_in + n_out])
        local = refs[n_in + n_out : n_in + n_out + len(shapes)]
        rest, own_sems = refs[n_in + n_out + len(shapes) : -1], refs[-1]
        pairs = list(zip([inputs[n] for n in near_in], local))
        back = list(zip(local[len(near_in) :], [results[n] for n in near_out]))
        for n, ref in zip(near_in, local):
            inputs[n] = ref
        for n, ref in zip(near_out, local[len(near_in) :]):
            results[n] = ref
        copies = start_copies(pairs, own_sems)
        kernel(lambda: wait_all(copies), *inputs, *results, *rest)
        wait_all(start_copies(back, own_sems))

    return pl.pallas_call(
        body,
        out_shape=[jax.ShapeDtypeStruct(bare(out), jnp.float32) for out in outs],
        in_specs=[far] * n_in,
        out_specs=[far] * n_out,
        scratch_shapes=[pltpu.VMEM(shape, jnp.float32) for shape in shapes + list(scratch)]
        + [pltpu.SemaphoreType.DMA((n,)) for n in sems]
        + [pltpu.SemaphoreType.DMA((max(len(near_in), len(near_out), 1),))],
        cost_estimate=cost(kernel),
    )(*[bare(operand) for operand in operands])


def call_near(kernel, outs, *operands, scratch=()):
    return pl.pallas_call(
        lambda *refs: kernel(lambda: None, *refs),
        out_shape=[jax.ShapeDtypeStruct(out, jnp.float32) for out in outs],
        in_specs=[vmem] * len(operands),
        out_specs=[vmem] * len(outs),
        scratch_shapes=[pltpu.VMEM(shape, jnp.float32) for shape in scratch],
        compiler_params=params,
        cost_estimate=cost(kernel),
    )(*operands)


def spread(me, refs, slots):
    for k, ref in enumerate(refs):
        slots[me ^ k] = ref[...]


def spread_rows(me, refs, slots):
    for k, ref in enumerate(refs):
        count = ref.shape[0]
        slots[pl.ds(pl.multiple_of((me ^ k) * count, 8), count), :] = ref[...]


def bias_kernel(
    ready, msa_far, pair_far, gains_far, matrix_far, copies_far, out_ref, msa_ref, pair_ref,
    gains_ref, matrix_ref, sems, out_sems
):
    rows = msa_far.shape[0]
    repeats = copies_far.shape[0] // rows
    copies = start_copies(
        [(msa_far, msa_ref), (gains_far, gains_ref), (matrix_far, matrix_ref), (pair_far, pair_ref)],
        sems,
    )
    residues, pair_cols, _ = pair_ref.shape
    heads = matrix_ref.shape[0]
    per = lanes // pair_cols
    ready()
    wait_all(copies)
    copies = start_copies(
        [(msa_ref, copies_far.at[pl.ds(n * rows, rows)]) for n in range(repeats)], out_sems
    )
    normal = layer_normalise(pair_ref[...], gains_ref[0:1, :][None])
    for i in range(residues):
        here = multiply(matrix_ref[...], normal[i], across=True)
        for h in range(heads):
            out_ref[h // per, i : i + 1, pl.ds(h % per * pair_cols, pair_cols)] = here[h : h + 1]
    wait_all(copies)


def pair_blocks_kernel(few, residues, ready, pair_ref, *rest):
    chunks, slots = rest[:-1], rest[-1]
    n_cols = len(chunks)
    block = chunks[0].shape[0]
    groups = block // (residues * few)
    me = column_index()
    ready()
    for c in range(n_cols):
        for o in range(groups):
            for f in range(few):
                source = pl.ds((o * n_cols + c) * few + f, residues, stride=groups * n_cols * few)
                target = pl.ds(c * block + f * groups + o, residues, stride=few * groups)
                slots[target, :] = pair_ref[source, :]
    for k in range(n_cols):
        start = pl.multiple_of((me ^ k) * block, 8)
        chunks[k][...] = slots[pl.ds(start, block), :]


def bias_part_kernel(per_part, ready, *rest):
    blocks, (out_ref,) = rest[:per_part], rest[per_part:]
    ready()
    spread(lax.rem(lax.axis_index("gi"), per_part), blocks, out_ref)


def row_kernel(n_branch, n_gj, per_part, few, ready, msa_ref, *rest):
    n_cols = n_branch * n_gj
    bias_refs, (gains_ref, qkvg_ref, final_ref, out_ref, slots) = rest[:n_cols], rest[n_cols:]
    half = lax.div(lax.axis_index("gi"), per_part)
    ready()
    _, residues, width = msa_ref.shape
    blocks = slots.shape[2]
    n_gi = lax.axis_size("gi")
    length = n_gi * residues
    per = lanes * n_cols // length
    heads = blocks * per
    rows = msa_ref.shape[0] // n_gi
    inner = final_ref.shape[0]
    queries = per_part * residues
    tokens = jnp.concatenate(
        [msa_ref[g * rows + r] for r in range(rows) for g in range(n_gi)], axis=0
    )
    first = half * (per_part * rows)
    asking = msa_ref[pl.ds(first, per_part * rows)]
    asking = jnp.concatenate(
        [asking[g * rows + r] for r in range(rows) for g in range(per_part)], axis=0
    )
    tokens = layer_normalise(tokens, 1.0)
    normal = layer_normalise(asking, 1.0)
    gain = gains_ref[0:1, :]
    key_value = multiply(tokens * gain, qkvg_ref[:, inner : 3 * inner])
    normal = normal * gain
    query = multiply(normal, qkvg_ref[:, :inner])
    gate = multiply(normal, qkvg_ref[:, 3 * inner :])
    spread(column_index(), bias_refs, slots)
    pieces = [[] for _ in range(heads)]
    for block in range(blocks):
        for g in range(per_part):
            tiles = [[] for _ in range(per)]
            for tile in range(n_cols // per):
                group = [slots[c, g, block] for c in range(tile * per, (tile + 1) * per)]
                for k, piece in enumerate(swap_lane_groups(group)):
                    tiles[k].append(piece)
            for k in range(per):
                pieces[block * per + k].append(jnp.concatenate(tiles[k], axis=1))
    bias = jnp.concatenate([piece for head in pieces for piece in head], axis=0)
    attended = []
    for r in range(rows):
        keys = key_value[r * length : (r + 1) * length, :inner]
        values = key_value[r * length : (r + 1) * length, inner:]
        attended.append(
            attend(query[r * queries : (r + 1) * queries], keys, values, bias, heads)
        )
    attended = jnp.concatenate(attended, axis=0)
    result = asking + multiply(sigmoid(gate) * attended, final_ref[...])
    for b in range(n_branch):
        for g in range(per_part):
            for j in range(n_gj):
                start = g * residues + (b * n_gj + j) * few
                out_ref[(b * per_part + g) * n_gj + j] = jnp.concatenate(
                    [result[r * queries + start : r * queries + start + few] for r in range(rows)],
                    axis=0,
                )


def column_kernel(
    few, heads, ready, msa_ref, gains_ref, qkvg_ref, joined_ref, expand_ref, shrink_ref, left_ref,
    right_ref, out_ref
):
    ready()
    count, width = msa_ref.shape
    inner = qkvg_ref.shape[1] // 4
    half = (joined_ref.shape[0] - inner) // 2
    first = msa_ref[...]
    projected = multiply(layer_normalise(first, gains_ref[1:2, :]), qkvg_ref[...])
    query, key, value, gate = (projected[:, k * inner : (k + 1) * inner] for k in range(4))
    allowed = None
    if few > 1:
        shape = (heads * count, count)
        asks = lax.broadcasted_iota(jnp.int32, shape, 0)
        holds = lax.broadcasted_iota(jnp.int32, shape, 1)
        allowed = lax.rem(asks, few) == lax.rem(holds, few)
    attended = attend(query, key, value, None, heads, allowed)
    second = first + multiply(sigmoid(gate) * attended, joined_ref[:inner])
    expanded = multiply(layer_normalise(second, gains_ref[2:3, :]), expand_ref[...])
    third = second + multiply(jnp.maximum(expanded, 0.0), shrink_ref[...])
    out_ref[...] = third
    factors = multiply(joined_ref[inner:], layer_normalise(third, gains_ref[3:4, :]), across=True)
    left_ref[...] = factors[:half]
    for g in range(right_ref.shape[0]):
        right_ref[g] = factors[half:]


def msa_blocks_kernel(n_branch, n_gj, ready, msa_ref, *rest):
    chunks, slots = rest[:-1], rest[-1]
    per_part, each = slots.shape[1:3]
    ready()
    for b in range(n_branch):
        for g in range(per_part):
            for j in range(n_gj):
                start = ((b * per_part + g) * n_gj + j) * each
                slots[b * n_gj + j, g] = msa_ref[start : start + each]
    for k, chunk in enumerate(chunks):
        chunk[...] = slots[column_index() ^ k]


def gather_msa(few, me, blocks, out_ref, slots):
    n_cols = len(blocks)
    spread(me, blocks, slots)
    for r in range(out_ref.shape[0]):
        out_ref[r] = jnp.concatenate(
            [slots[c, r * few : (r + 1) * few] for c in range(n_cols)], axis=0
        )


def gather_msa_kernel(few, n_cols, ready, *rest):
    ready()
    gather_msa(few, column_index(), rest[:n_cols], *rest[n_cols:])


def gather_pair_kernel(few, n_cols, residues, ready, gains_ref, matrix_ref, *rest):
    blocks, (first_ref, gate_ref, slots) = rest[:n_cols], rest[n_cols:]
    ready()
    spread_rows(column_index(), blocks, slots)
    block = blocks[0].shape[0]
    count = residues * few
    groups = block // count
    for c in range(n_cols):
        for o in range(groups):
            first_ref[pl.ds(o * n_cols + c, count, stride=groups * n_cols), :] = slots[
                pl.ds(c * block + o * count, count), :
            ]
    width = first_ref.shape[1]
    normal = layer_normalise(first_ref[...], gains_ref[1:2, :])
    gate_ref[...] = sigmoid(multiply(normal, matrix_ref[:, 4 * width :]))


def triangle_kernel(few, n_branch, n_gj, ready, tri_ref, *rest):
    n_cols = n_branch * n_gj
    blocks, (out_ref, msa_out, product_ref, slots) = rest[:n_cols], rest[n_cols:]
    ready()
    gather_msa(few, column_index(), blocks, msa_out, slots)
    n_all, rows, _ = out_ref.shape
    n_gi = n_all // n_cols
    share = few
    tiles = rows // few
    each = 2 * share
    wide = lanes // few
    group = lax.broadcasted_iota(jnp.int32, (n_gi * tiles, lanes), 1) // wide
    products = []
    for q in range(share):
        left, right = [], []
        for c in range(n_cols):
            base = (c // n_gj * n_all // n_branch + c % n_gj) * tiles * each
            step = n_gj * tiles * each
            here = jnp.concatenate(
                [
                    tri_ref[pl.ds(base + t * each + q, n_gi, stride=step), :]
                    for t in range(tiles)
                ],
                axis=0,
            )
            left.append(
                jnp.concatenate(
                    [jnp.where(group == i, here, 0.0) for i in range(few)], axis=0
                )
            )
            here = jnp.concatenate(
                [
                    tri_ref[pl.ds(base + g * step + share + q, tiles, stride=each), :]
                    for g in range(n_gi)
                ],
                axis=0,
            )
            rolled = [here] + [pltpu.roll(here, k * wide, 1) for k in range(1, few)]
            copies = []
            for j in range(few):
                copy = rolled[0]
                for k in range(1, few):
                    copy = jnp.where(group == (j + k) % few, rolled[k], copy)
                copies.append(copy)
            step = n_gi * tiles // n_cols
            right.append(
                jnp.concatenate(
                    [copy[k * step : (k + 1) * step] for k in range(n_cols) for copy in copies],
                    axis=0,
                )
            )
        products.append(
            multiply(
                jnp.concatenate(left, axis=1), jnp.concatenate(right, axis=1), across=True
            )
        )
    for c, product in enumerate(swap_lane_groups(products)):
        product_ref[...] = product
        for g in range(n_gi):
            out_ref[(c // n_gj * n_gi + g) * n_gj + c % n_gj] = product_ref[pl.ds(g, rows, stride=n_gi), :]


def pair_kernel(
    few, n_gi, n_cols, ready, *rest
):
    left_refs, pair_refs = rest[:n_cols], rest[n_cols : 2 * n_cols]
    right_ref, gain_ref, matrix_ref, triangle_ref, tri_ref = rest[2 * n_cols : 2 * n_cols + 5]
    chunks = rest[2 * n_cols + 5 : 3 * n_cols + 5]
    rest = rest[3 * n_cols + 5 :]
    left_ref, slots, pair_ref, first_ref = rest
    me = column_index()
    groups_j = n_gi // n_cols
    block = pair_refs[0].shape[0]
    ready()
    spread(me, left_refs, left_ref)
    spread_rows(me, pair_refs, slots)
    _, wide, count = left_ref.shape
    half = block // groups_j
    all_rows = count // few
    residues = n_cols * few
    pair_cols = n_gi * few
    per = lanes // pair_cols
    groups = residues // per
    width = pair_ref.shape[1]
    owner = lax.rem(lax.broadcasted_iota(jnp.int32, (1, count), 1), few)
    left = []
    for c in range(n_cols):
        here = left_ref[c]
        for f in range(few):
            own = jnp.where(owner == f, here, 0.0)
            total = own
            for other in range(few):
                if other != f:
                    total = total + pltpu.roll(own, (other - f) % count, 1)
            left.append(total)
    left = jnp.concatenate(left, axis=0) * (1.0 / all_rows)
    right = []
    for d in range(wide):
        here = right_ref[pl.ds(d, n_gi, stride=wide), :]
        right += [jnp.where(owner == f, here, 0.0) for f in range(few)]
    right = jnp.concatenate(right, axis=0)
    outer = multiply(left, right, across=True)
    outputs = []
    for g in range(groups):
        swapped = swap_lane_groups(
            [outer[(g * per + i) * wide : (g * per + i + 1) * wide] for i in range(per)]
        )
        stacked = [
            s[:, t * lanes : (t + 1) * lanes] for s in swapped for t in range(wide // per)
        ]
        outputs.append(jnp.concatenate(stacked, axis=0))
    for c in range(n_cols):
        for o in range(groups_j):
            pair_ref[pl.ds(c * groups_j + o, half, stride=n_gi), :] = slots[
                pl.ds(c * block + o, half, stride=groups_j), :
            ]
    update = multiply(matrix_ref[...], jnp.concatenate(outputs, axis=1))
    first = pair_ref[...].T + update
    projected = multiply(
        triangle_ref[pl.ds(0, 4 * width), :], layer_normalise(first, gain_ref[...], axis=0)
    )
    tri = sigmoid(projected[2 * width : 4 * width]) * projected[: 2 * width]
    slot_count, _, each, _ = tri_ref.shape
    for g in range(groups):
        tri_ref[:, g] = tri[:, g * lanes : (g + 1) * lanes].reshape(slot_count, each, lanes)
    first_ref[...] = first.T
    for k in range(n_cols):
        for o in range(groups_j):
            rows = pl.ds((me ^ k) * groups_j + o, half, stride=n_gi)
            chunks[k][pl.ds(o * half, half), :] = first_ref[rows, :]


def final_kernel(
    few, residues, packed, ready, product_ref, first_ref, gate_ref, gains_ref, matrix_ref, out_ref,
    channels_ref
):
    positions = out_ref.shape[0]
    ready()
    if packed:
        tiles = residues // few
        tall = product_ref.shape[0] // residues
        product = []
        for t in range(tiles):
            here = [
                product_ref[pl.ds(i * tiles + t, tall, stride=residues), :] for i in range(few)
            ]
            for q, piece in enumerate(swap_lane_groups(here)):
                channels_ref[pl.ds(q, tall, stride=few), :] = piece
            product.append(channels_ref[...])
        product = jnp.concatenate(product, axis=1)
    else:
        product = product_ref[...]
    normal = layer_normalise(product, 1.0, axis=0).T * gains_ref[2:3, :]
    result = first_ref[...] + gate_ref[...] * multiply(normal, matrix_ref[...])
    count = positions // (residues * few)
    for i in range(residues):
        for f in range(few):
            start = (i * few + f) * count
            out_ref[pl.ds(i * few * count + f, count, stride=few), :] = result[
                start : start + count
            ]


def per_device(
    homolog_embedding,
    pair_input_tensor,
    layernorm_scales,
    pair_norm_gains,
    pair_bias_matrix,
    horizontal_qkvg_kernel,
    horizontal_final_kernel,
    vertical_qkvg_kernel,
    vertical_final_kernel,
    feedforward_expand_kernel,
    feedforward_shrink_kernel,
    dyadic_sides_kernel,
    outer_output_matrix,
    triangle_input_matrix,
    triangle_output_matrix,
):
    rows, residues, width = homolog_embedding.shape
    pair_cols, pair_width = pair_input_tensor.shape[1:]
    heads = pair_bias_matrix.shape[1]
    outer_width = dyadic_sides_kernel.shape[1] // 2
    n_branch, n_gi, n_gj = (lax.axis_size(name) for name in everyone)
    n_cols = n_branch * n_gj
    n_all = n_cols * n_gi
    length = residues * n_gi
    few = residues // n_cols
    groups = n_gi // n_cols
    parts = 2
    per_part = n_gi // parts
    own_rows = rows // per_part

    def trade(blocks, axes):
        n = lax.axis_size(axes)
        return [blocks[0]] + [
            lax.ppermute(blocks[k], axes, [(t ^ k, t) for t in range(n) if t ^ k < n])
            for k in range(1, len(blocks))
        ]

    halves = [
        [
            (b * n_gi + part * per_part + g) * n_gj + j
            for b in range(n_branch)
            for g in range(per_part)
            for j in range(n_gj)
        ]
        for part in range(parts)
    ]
    n_half = n_cols * per_part
    positions = residues * pair_cols
    each = own_rows * few

    per = lanes // pair_cols
    bias_block = (heads // per, residues, lanes)
    msa, bias = call(
        bias_kernel,
        [[(parts * rows, residues, width)], bias_block],
        [homolog_embedding],
        [pair_input_tensor],
        [pair_norm_gains],
        [pair_bias_matrix.T],
        scratch=[
            homolog_embedding.shape,
            pair_input_tensor.shape,
            pair_norm_gains.shape,
            (heads, pair_width),
        ],
        sems=[4, parts],
    )
    msa = lax.all_to_all(msa, "gi", 0, 0, tiled=True)
    (bias,) = call_near(
        functools.partial(bias_part_kernel, per_part),
        [(per_part,) + bias_block],
        *trade([bias] * per_part, "gi"),
    )
    bias = trade([bias] * n_cols, columns)
    (msa_first,) = call_near(
        functools.partial(row_kernel, n_branch, n_gj, per_part, few),
        [(n_half, each, width)],
        msa,
        *bias,
        layernorm_scales,
        horizontal_qkvg_kernel,
        horizontal_final_kernel,
        scratch=[(n_cols, per_part) + bias_block],
    )
    pair, msa_first = lax.optimization_barrier((pair_input_tensor, msa_first))

    msa_first = lax.all_to_all(msa_first, everyone, 0, 0, tiled=True, axis_index_groups=halves)
    count = n_half * each
    weights = (
        layernorm_scales,
        vertical_qkvg_kernel,
        jnp.concatenate([vertical_final_kernel, dyadic_sides_kernel.T], axis=0),
        feedforward_expand_kernel,
        feedforward_shrink_kernel,
    )
    left, right, alignment = call_near(
        functools.partial(column_kernel, few, heads),
        [(outer_width, count), (n_gi, outer_width, count), (count, width)],
        msa_first.reshape(count, width),
        *weights,
    )
    alignment = call_near(
        functools.partial(msa_blocks_kernel, n_branch, n_gj),
        [(per_part, each, width)] * n_cols,
        alignment,
        scratch=[(n_cols, per_part, each, width)],
    )
    pair = call_near(
        functools.partial(pair_blocks_kernel, few, residues),
        [(positions // n_cols, pair_width)] * n_cols,
        pair.reshape(positions, pair_width),
        scratch=[(positions, pair_width)],
    )
    pair = trade(pair, columns)
    right = lax.all_to_all(right, "gi", 0, 0, tiled=True)
    right, *alignment = lax.optimization_barrier((right, *alignment))
    left = trade([left] * n_cols, columns)
    alignment = [block.reshape(-1, width) for block in trade(alignment, columns)]
    share = max(pair_width // n_all, 1)
    slots = pair_width // share
    triangle = triangle_input_matrix.T.reshape(5, slots, share, pair_width)
    sides = jnp.stack([triangle[0], triangle[2]], axis=1)
    gates = jnp.stack([triangle[1], triangle[3]], axis=1)
    triangle = jnp.concatenate(
        [side.reshape(2 * pair_width, pair_width) for side in (sides, gates)]
        + [triangle[4].reshape(pair_width, pair_width)],
        axis=0,
    )
    matrix = outer_output_matrix.reshape(outer_width, outer_width // per, per, pair_width)
    matrix = jnp.transpose(matrix, (3, 2, 1, 0)).reshape(pair_width, -1)
    tri, *first = call_near(
        functools.partial(pair_kernel, few, n_gi, n_cols),
        [(slots, positions // lanes, 2 * share, lanes)]
        + [(positions // n_cols, pair_width)] * n_cols,
        *left,
        *pair,
        right.reshape(n_gi * outer_width, count),
        pair_norm_gains[1][:, None],
        matrix,
        triangle,
        scratch=[
            (n_cols, outer_width, count),
            (positions, pair_width),
            (positions, pair_width),
            (positions, pair_width),
        ],
    )

    first, gate = call_near(
        functools.partial(gather_pair_kernel, few, n_cols, residues),
        [(positions, pair_width)] * 2,
        pair_norm_gains,
        triangle_input_matrix,
        *trade(first, columns),
        scratch=[(positions, pair_width)],
    )
    tile = (rows, residues, width)
    scratch = [(n_cols, rows * few, width)]
    packed = share * n_all == pair_width and share == few and few == per
    if packed:
        tri = lax.all_to_all(tri, everyone, 0, 0, tiled=True)
        product, alignment_output = call_near(
            functools.partial(triangle_kernel, few, n_branch, n_gj),
            [(n_all, residues, lanes), tile],
            tri.reshape(-1, lanes),
            *alignment,
            scratch=[(lanes, lanes)] + scratch,
        )
        product = lax.all_to_all(product, everyone, 0, 0, tiled=True)
        product = product.reshape(n_all * residues, lanes)
    else:
        (alignment_output,) = call_near(
            functools.partial(gather_msa_kernel, few, n_cols),
            [tile],
            *alignment,
            scratch=scratch,
        )
        tri = jnp.transpose(tri.reshape(slots, -1, 2, share, lanes), (2, 1, 4, 0, 3))
        tri = tri.reshape(2, residues, pair_cols, pair_width)
        right_columns = lax.all_gather(tri[1], "gi", axis=0, tiled=True)
        product = lax.psum_scatter(
            jnp.einsum("jkc,ikc->jic", right_columns, tri[0], precision=precise),
            columns,
            scatter_dimension=0,
            tiled=True,
        ).reshape(groups, n_cols, few, residues, pair_width)
        product = jnp.transpose(product, (4, 3, 2, 0, 1)).reshape(pair_width, positions)
    (pair_output_tensor,) = call_near(
        functools.partial(final_kernel, few, residues, packed),
        [(positions, pair_width)],
        product,
        first,
        gate,
        pair_norm_gains,
        triangle_output_matrix,
        scratch=[(pair_width, lanes)],
    )
    return (
        alignment_output,
        pair_output_tensor.reshape(residues, pair_cols, pair_width),
    )


def solution(mesh):
    tile, grid = P(("branch", "gj"), "gi", None), P("gi", ("branch", "gj"), None)
    return jax.shard_map(
        per_device,
        mesh=mesh,
        in_specs=(tile, grid) + (P(),) * 13,
        out_specs=(tile, grid),
        check_vma=False,
    )
```

```python
import functools
import math

import jax
import jax.numpy as jnp
from jax import lax
from jax.experimental import pallas as pl
from jax.experimental.pallas import tpu as pltpu
from jax.sharding import PartitionSpec as P

epsilon = 1e-05
precise = lax.Precision.HIGH
everyone = ("branch", "gi", "gj")
columns = ("branch", "gj")
lanes = 128
far = pl.BlockSpec(memory_space=pl.ANY)
vmem = pl.BlockSpec(memory_space=pltpu.VMEM)
params = pltpu.CompilerParams(vmem_limit_bytes=16 * 1024 * 1024)


def layer_normalise(values, norm_gain, axis=-1):
    average = jnp.mean(values, axis=axis, keepdims=True)
    centred = values - average
    variance = jnp.mean(centred * centred, axis=axis, keepdims=True)
    return centred * lax.rsqrt(variance + epsilon) * norm_gain


def apply_projection(values, weight):
    return jnp.einsum("...c,cd->...d", values, weight, precision=precise)


def sigmoid(values):
    return 1.0 / (1.0 + jnp.exp(-values))


def split(values):
    high = values.astype(jnp.bfloat16)
    return high, (values - high.astype(jnp.float32)).astype(jnp.bfloat16)


def multiply(left, right, across=False):
    numbers = (((1,), (1 if across else 0,)), ((), ()))

    def one(a, b):
        return lax.dot_general(a, b, numbers, preferred_element_type=jnp.float32)

    (lh, ll), (rh, rl) = split(left), split(right)
    return one(lh, rh) + (one(lh, rl) + one(ll, rh))


def swap_lane_groups(arrays):
    n, arrays = len(arrays), list(arrays)
    width = lanes // n
    wide = arrays[0].shape[-1]
    lane = lax.broadcasted_iota(jnp.int32, arrays[0].shape, arrays[0].ndim - 1)
    group = lax.rem(lane, lanes) // width
    axis = arrays[0].ndim - 1
    step = 1
    while step < n:
        upper = (group // step) % 2 == 1
        for low in range(n):
            if low & step:
                continue
            a, b = arrays[low], arrays[low + step]
            arrays[low] = jnp.where(upper, pltpu.roll(b, step * width, axis), a)
            arrays[low + step] = jnp.where(
                upper, b, pltpu.roll(a, wide - step * width, axis)
            )
        step *= 2
    return arrays


def head_masks(shape, heads):
    column = lax.broadcasted_iota(jnp.int32, shape, 1)
    return [column // (shape[1] // heads) == h for h in range(heads)]


def attend(query, key, value, bias, heads, allowed=None):
    count, inner = query.shape
    masks = head_masks((count, inner), heads)
    spread = jnp.concatenate([jnp.where(m, query, 0.0) for m in masks], axis=0)
    scores = multiply(spread, key, across=True) * (1.0 / math.sqrt(inner // heads))
    if bias is not None:
        scores = scores + bias
    if allowed is not None:
        scores = jnp.where(allowed, scores, -1e30)
    weights = jnp.exp(scores - jnp.max(scores, axis=-1, keepdims=True))
    weights = weights / jnp.sum(weights, axis=-1, keepdims=True)
    mixed = multiply(weights, value)
    result = jnp.where(masks[0], mixed[:count], 0.0)
    for h in range(1, heads):
        result = result + jnp.where(masks[h], mixed[h * count : (h + 1) * count], 0.0)
    return result


def start_copies(pairs, sems):
    copies = [pltpu.make_async_copy(a, b, sems.at[n]) for n, (a, b) in enumerate(pairs)]
    for copy in copies:
        copy.start()
    return copies


def wait_all(copies):
    for copy in copies:
        copy.wait()


def column_index():
    return lax.axis_index("branch") * lax.axis_size("gj") + lax.axis_index("gj")


def cost(kernel):
    name = getattr(kernel, "func", kernel).__name__
    work = {
        "bias_kernel": 2.0,
        "bias_part_kernel": 6.0,
        "row_kernel": 12.0,
        "pair_blocks_kernel": 14.0,
        "column_kernel": 4.5,
        "msa_blocks_kernel": 0.5,
        "pair_kernel": 4.0,
        "triangle_kernel": 2.0,
        "gather_pair_kernel": 1.0,
        "final_kernel": 1.3,
    }.get(name, 1.0)
    return pl.CostEstimate(
        flops=int(work * 1.1e9), bytes_accessed=int(work * 3.6e6), transcendentals=0
    )


def call(kernel, outs, *operands, scratch=(), sems=()):
    def bare(item):
        return item[0] if isinstance(item, list) else item

    n_in, n_out = len(operands), len(outs)
    near_in = [n for n, item in enumerate(operands) if not isinstance(item, list)]
    near_out = [n for n, item in enumerate(outs) if not isinstance(item, list)]
    shapes = [operands[n].shape for n in near_in] + [outs[n] for n in near_out]

    def body(*refs):
        inputs, results = list(refs[:n_in]), list(refs[n_in : n_in + n_out])
        local = refs[n_in + n_out : n_in + n_out + len(shapes)]
        rest, own_sems = refs[n_in + n_out + len(shapes) : -1], refs[-1]
        pairs = list(zip([inputs[n] for n in near_in], local))
        back = list(zip(local[len(near_in) :], [results[n] for n in near_out]))
        for n, ref in zip(near_in, local):
            inputs[n] = ref
        for n, ref in zip(near_out, local[len(near_in) :]):
            results[n] = ref
        copies = start_copies(pairs, own_sems)
        kernel(lambda: wait_all(copies), *inputs, *results, *rest)
        wait_all(start_copies(back, own_sems))

    return pl.pallas_call(
        body,
        out_shape=[jax.ShapeDtypeStruct(bare(out), jnp.float32) for out in outs],
        in_specs=[far] * n_in,
        out_specs=[far] * n_out,
        scratch_shapes=[pltpu.VMEM(shape, jnp.float32) for shape in shapes + list(scratch)]
        + [pltpu.SemaphoreType.DMA((n,)) for n in sems]
        + [pltpu.SemaphoreType.DMA((max(len(near_in), len(near_out), 1),))],
        cost_estimate=cost(kernel),
    )(*[bare(operand) for operand in operands])


def call_near(kernel, outs, *operands, scratch=()):
    return pl.pallas_call(
        lambda *refs: kernel(lambda: None, *refs),
        out_shape=[jax.ShapeDtypeStruct(out, jnp.float32) for out in outs],
        in_specs=[vmem] * len(operands),
        out_specs=[vmem] * len(outs),
        scratch_shapes=[pltpu.VMEM(shape, jnp.float32) for shape in scratch],
        compiler_params=params,
        cost_estimate=cost(kernel),
    )(*operands)


def spread(me, refs, slots):
    for k, ref in enumerate(refs):
        slots[me ^ k] = ref[...]


def spread_rows(me, refs, slots):
    for k, ref in enumerate(refs):
        count = ref.shape[0]
        slots[pl.ds(pl.multiple_of((me ^ k) * count, 8), count), :] = ref[...]


def bias_kernel(
    ready, msa_far, pair_far, gains_far, matrix_far, copies_far, out_ref, msa_ref, pair_ref,
    gains_ref, matrix_ref, sems, out_sems
):
    rows = msa_far.shape[0]
    repeats = copies_far.shape[0] // rows
    copies = start_copies(
        [(msa_far, msa_ref), (gains_far, gains_ref), (matrix_far, matrix_ref), (pair_far, pair_ref)],
        sems,
    )
    residues, pair_cols, _ = pair_ref.shape
    heads = matrix_ref.shape[0]
    per = lanes // pair_cols
    ready()
    wait_all(copies)
    copies = start_copies(
        [(msa_ref, copies_far.at[pl.ds(n * rows, rows)]) for n in range(repeats)], out_sems
    )
    normal = layer_normalise(pair_ref[...], gains_ref[0:1, :][None])
    for i in range(residues):
        here = multiply(matrix_ref[...], normal[i], across=True)
        for h in range(heads):
            out_ref[h // per, i : i + 1, pl.ds(h % per * pair_cols, pair_cols)] = here[h : h + 1]
    wait_all(copies)


def pair_blocks_kernel(few, residues, ready, pair_ref, *rest):
    chunks, slots = rest[:-1], rest[-1]
    n_cols = len(chunks)
    block = chunks[0].shape[0]
    groups = block // (residues * few)
    me = column_index()
    ready()
    for c in range(n_cols):
        for o in range(groups):
            for f in range(few):
                source = pl.ds((o * n_cols + c) * few + f, residues, stride=groups * n_cols * few)
                target = pl.ds(c * block + f * groups + o, residues, stride=few * groups)
                slots[target, :] = pair_ref[source, :]
    for k in range(n_cols):
        start = pl.multiple_of((me ^ k) * block, 8)
        chunks[k][...] = slots[pl.ds(start, block), :]


def bias_part_kernel(per_part, ready, *rest):
    blocks, (out_ref,) = rest[:per_part], rest[per_part:]
    ready()
    spread(lax.rem(lax.axis_index("gi"), per_part), blocks, out_ref)


def row_kernel(n_branch, n_gj, per_part, few, ready, msa_ref, *rest):
    n_cols = n_branch * n_gj
    bias_refs, (gains_ref, qkvg_ref, final_ref, out_ref, slots) = rest[:n_cols], rest[n_cols:]
    half = lax.div(lax.axis_index("gi"), per_part)
    ready()
    _, residues, width = msa_ref.shape
    blocks = slots.shape[2]
    n_gi = lax.axis_size("gi")
    length = n_gi * residues
    per = lanes * n_cols // length
    heads = blocks * per
    rows = msa_ref.shape[0] // n_gi
    inner = final_ref.shape[0]
    queries = per_part * residues
    tokens = jnp.concatenate(
        [msa_ref[g * rows + r] for r in range(rows) for g in range(n_gi)], axis=0
    )
    first = half * (per_part * rows)
    asking = msa_ref[pl.ds(first, per_part * rows)]
    asking = jnp.concatenate(
        [asking[g * rows + r] for r in range(rows) for g in range(per_part)], axis=0
    )
    tokens = layer_normalise(tokens, 1.0)
    normal = layer_normalise(asking, 1.0)
    gain = gains_ref[0:1, :]
    key_value = multiply(tokens * gain, qkvg_ref[:, inner : 3 * inner])
    normal = normal * gain
    query = multiply(normal, qkvg_ref[:, :inner])
    gate = multiply(normal, qkvg_ref[:, 3 * inner :])
    spread(column_index(), bias_refs, slots)
    pieces = [[] for _ in range(heads)]
    for block in range(blocks):
        for g in range(per_part):
            tiles = [[] for _ in range(per)]
            for tile in range(n_cols // per):
                group = [slots[c, g, block] for c in range(tile * per, (tile + 1) * per)]
                for k, piece in enumerate(swap_lane_groups(group)):
                    tiles[k].append(piece)
            for k in range(per):
                pieces[block * per + k].append(jnp.concatenate(tiles[k], axis=1))
    bias = jnp.concatenate([piece for head in pieces for piece in head], axis=0)
    attended = []
    for r in range(rows):
        keys = key_value[r * length : (r + 1) * length, :inner]
        values = key_value[r * length : (r + 1) * length, inner:]
        attended.append(
            attend(query[r * queries : (r + 1) * queries], keys, values, bias, heads)
        )
    attended = jnp.concatenate(attended, axis=0)
    result = asking + multiply(sigmoid(gate) * attended, final_ref[...])
    for b in range(n_branch):
        for g in range(per_part):
            for j in range(n_gj):
                start = g * residues + (b * n_gj + j) * few
                out_ref[(b * per_part + g) * n_gj + j] = jnp.concatenate(
                    [result[r * queries + start : r * queries + start + few] for r in range(rows)],
                    axis=0,
                )


def column_kernel(
    few, heads, ready, msa_ref, gains_ref, qkvg_ref, final_ref, expand_ref, shrink_ref, sides_ref,
    left_ref, right_ref, out_ref
):
    ready()
    count, width = msa_ref.shape
    inner = final_ref.shape[0]
    half = sides_ref.shape[0] // 2
    first = msa_ref[...]
    projected = multiply(layer_normalise(first, gains_ref[1:2, :]), qkvg_ref[...])
    query, key, value, gate = (projected[:, k * inner : (k + 1) * inner] for k in range(4))
    allowed = None
    if few > 1:
        shape = (heads * count, count)
        asks = lax.broadcasted_iota(jnp.int32, shape, 0)
        holds = lax.broadcasted_iota(jnp.int32, shape, 1)
        allowed = lax.rem(asks, few) == lax.rem(holds, few)
    attended = attend(query, key, value, None, heads, allowed)
    second = first + multiply(sigmoid(gate) * attended, final_ref[...])
    expanded = multiply(layer_normalise(second, gains_ref[2:3, :]), expand_ref[...])
    third = second + multiply(jnp.maximum(expanded, 0.0), shrink_ref[...])
    out_ref[...] = third
    factors = multiply(sides_ref[...], layer_normalise(third, gains_ref[3:4, :]), across=True)
    left_ref[...] = factors[:half]
    for g in range(right_ref.shape[0]):
        right_ref[g] = factors[half:]


def msa_blocks_kernel(n_branch, n_gj, ready, msa_ref, *rest):
    chunks, slots = rest[:-1], rest[-1]
    per_part, each = slots.shape[1:3]
    ready()
    for b in range(n_branch):
        for g in range(per_part):
            for j in range(n_gj):
                start = ((b * per_part + g) * n_gj + j) * each
                slots[b * n_gj + j, g] = msa_ref[start : start + each]
    for k, chunk in enumerate(chunks):
        chunk[...] = slots[column_index() ^ k]


def gather_msa(few, me, blocks, out_ref, slots):
    n_cols = len(blocks)
    spread(me, blocks, slots)
    for r in range(out_ref.shape[0]):
        out_ref[r] = jnp.concatenate(
            [slots[c, r * few : (r + 1) * few] for c in range(n_cols)], axis=0
        )


def gather_msa_kernel(few, n_cols, ready, *rest):
    ready()
    gather_msa(few, column_index(), rest[:n_cols], *rest[n_cols:])


def gather_pair_kernel(few, n_cols, residues, ready, gains_ref, matrix_ref, *rest):
    blocks, (first_ref, gate_ref, slots) = rest[:n_cols], rest[n_cols:]
    ready()
    spread_rows(column_index(), blocks, slots)
    block = blocks[0].shape[0]
    count = residues * few
    groups = block // count
    for c in range(n_cols):
        for o in range(groups):
            first_ref[pl.ds(o * n_cols + c, count, stride=groups * n_cols), :] = slots[
                pl.ds(c * block + o * count, count), :
            ]
    width = first_ref.shape[1]
    normal = layer_normalise(first_ref[...], gains_ref[1:2, :])
    gate_ref[...] = sigmoid(multiply(normal, matrix_ref[:, 4 * width :]))


def triangle_kernel(few, n_branch, n_gj, ready, tri_ref, *rest):
    n_cols = n_branch * n_gj
    blocks, (out_ref, msa_out, product_ref, slots) = rest[:n_cols], rest[n_cols:]
    ready()
    gather_msa(few, column_index(), blocks, msa_out, slots)
    n_all, rows, _ = out_ref.shape
    n_gi = n_all // n_cols
    share = few
    tiles = rows // few
    each = 2 * share
    wide = lanes // few
    group = lax.broadcasted_iota(jnp.int32, (n_gi * tiles, lanes), 1) // wide
    products = []
    for q in range(share):
        left, right = [], []
        for c in range(n_cols):
            base = (c // n_gj * n_all // n_branch + c % n_gj) * tiles * each
            step = n_gj * tiles * each
            here = jnp.concatenate(
                [
                    tri_ref[pl.ds(base + t * each + q, n_gi, stride=step), :]
                    for t in range(tiles)
                ],
                axis=0,
            )
            left.append(
                jnp.concatenate(
                    [jnp.where(group == i, here, 0.0) for i in range(few)], axis=0
                )
            )
            here = jnp.concatenate(
                [
                    tri_ref[pl.ds(base + g * step + share + q, tiles, stride=each), :]
                    for g in range(n_gi)
                ],
                axis=0,
            )
            rolled = [here] + [pltpu.roll(here, k * wide, 1) for k in range(1, few)]
            copies = []
            for j in range(few):
                copy = rolled[0]
                for k in range(1, few):
                    copy = jnp.where(group == (j + k) % few, rolled[k], copy)
                copies.append(copy)
            step = n_gi * tiles // n_cols
            right.append(
                jnp.concatenate(
                    [copy[k * step : (k + 1) * step] for k in range(n_cols) for copy in copies],
                    axis=0,
                )
            )
        products.append(
            multiply(
                jnp.concatenate(left, axis=1), jnp.concatenate(right, axis=1), across=True
            )
        )
    for c, product in enumerate(swap_lane_groups(products)):
        product_ref[...] = product
        for g in range(n_gi):
            out_ref[(c // n_gj * n_gi + g) * n_gj + c % n_gj] = product_ref[pl.ds(g, rows, stride=n_gi), :]


def pair_kernel(
    few, n_gi, n_cols, ready, *rest
):
    left_refs, pair_refs = rest[:n_cols], rest[n_cols : 2 * n_cols]
    right_ref, gain_ref, matrix_ref, triangle_ref, tri_ref = rest[2 * n_cols : 2 * n_cols + 5]
    chunks = rest[2 * n_cols + 5 : 3 * n_cols + 5]
    rest = rest[3 * n_cols + 5 :]
    left_ref, slots, pair_ref, first_ref = rest
    me = column_index()
    groups_j = n_gi // n_cols
    block = pair_refs[0].shape[0]
    ready()
    spread(me, left_refs, left_ref)
    spread_rows(me, pair_refs, slots)
    _, wide, count = left_ref.shape
    half = block // groups_j
    all_rows = count // few
    residues = n_cols * few
    pair_cols = n_gi * few
    per = lanes // pair_cols
    groups = residues // per
    width = pair_ref.shape[1]
    owner = lax.rem(lax.broadcasted_iota(jnp.int32, (1, count), 1), few)
    left = []
    for c in range(n_cols):
        here = left_ref[c]
        for f in range(few):
            own = jnp.where(owner == f, here, 0.0)
            total = own
            for other in range(few):
                if other != f:
                    total = total + pltpu.roll(own, (other - f) % count, 1)
            left.append(total)
    left = jnp.concatenate(left, axis=0) * (1.0 / all_rows)
    right = []
    for d in range(wide):
        here = right_ref[pl.ds(d, n_gi, stride=wide), :]
        right += [jnp.where(owner == f, here, 0.0) for f in range(few)]
    right = jnp.concatenate(right, axis=0)
    outer = multiply(left, right, across=True)
    outputs = []
    for g in range(groups):
        swapped = swap_lane_groups(
            [outer[(g * per + i) * wide : (g * per + i + 1) * wide] for i in range(per)]
        )
        stacked = [
            s[:, t * lanes : (t + 1) * lanes] for s in swapped for t in range(wide // per)
        ]
        outputs.append(jnp.concatenate(stacked, axis=0))
    for c in range(n_cols):
        for o in range(groups_j):
            pair_ref[pl.ds(c * groups_j + o, half, stride=n_gi), :] = slots[
                pl.ds(c * block + o, half, stride=groups_j), :
            ]
    update = multiply(matrix_ref[...], jnp.concatenate(outputs, axis=1))
    first = pair_ref[...].T + update
    projected = multiply(
        triangle_ref[pl.ds(0, 4 * width), :], layer_normalise(first, gain_ref[...], axis=0)
    )
    tri = sigmoid(projected[2 * width : 4 * width]) * projected[: 2 * width]
    slot_count, _, each, _ = tri_ref.shape
    for g in range(groups):
        tri_ref[:, g] = tri[:, g * lanes : (g + 1) * lanes].reshape(slot_count, each, lanes)
    first_ref[...] = first.T
    for k in range(n_cols):
        for o in range(groups_j):
            rows = pl.ds((me ^ k) * groups_j + o, half, stride=n_gi)
            chunks[k][pl.ds(o * half, half), :] = first_ref[rows, :]


def final_kernel(
    few, residues, packed, ready, product_ref, first_ref, gate_ref, gains_ref, matrix_ref, out_ref,
    channels_ref
):
    positions = out_ref.shape[0]
    ready()
    if packed:
        tiles = residues // few
        tall = product_ref.shape[0] // residues
        product = []
        for t in range(tiles):
            here = [
                product_ref[pl.ds(i * tiles + t, tall, stride=residues), :] for i in range(few)
            ]
            for q, piece in enumerate(swap_lane_groups(here)):
                channels_ref[pl.ds(q, tall, stride=few), :] = piece
            product.append(channels_ref[...])
        product = jnp.concatenate(product, axis=1)
    else:
        product = product_ref[...]
    normal = layer_normalise(product, 1.0, axis=0).T * gains_ref[2:3, :]
    result = first_ref[...] + gate_ref[...] * multiply(normal, matrix_ref[...])
    count = positions // (residues * few)
    for i in range(residues):
        for f in range(few):
            start = (i * few + f) * count
            out_ref[pl.ds(i * few * count + f, count, stride=few), :] = result[
                start : start + count
            ]


def per_device(
    homolog_embedding,
    pair_input_tensor,
    layernorm_scales,
    pair_norm_gains,
    pair_bias_matrix,
    horizontal_qkvg_kernel,
    horizontal_final_kernel,
    vertical_qkvg_kernel,
    vertical_final_kernel,
    feedforward_expand_kernel,
    feedforward_shrink_kernel,
    dyadic_sides_kernel,
    outer_output_matrix,
    triangle_input_matrix,
    triangle_output_matrix,
):
    rows, residues, width = homolog_embedding.shape
    pair_cols, pair_width = pair_input_tensor.shape[1:]
    heads = pair_bias_matrix.shape[1]
    outer_width = dyadic_sides_kernel.shape[1] // 2
    n_branch, n_gi, n_gj = (lax.axis_size(name) for name in everyone)
    n_cols = n_branch * n_gj
    n_all = n_cols * n_gi
    length = residues * n_gi
    few = residues // n_cols
    groups = n_gi // n_cols
    parts = 2
    per_part = n_gi // parts
    own_rows = rows // per_part

    def trade(blocks, axes):
        n = lax.axis_size(axes)
        return [blocks[0]] + [
            lax.ppermute(blocks[k], axes, [(t ^ k, t) for t in range(n) if t ^ k < n])
            for k in range(1, len(blocks))
        ]

    halves = [
        [
            (b * n_gi + part * per_part + g) * n_gj + j
            for b in range(n_branch)
            for g in range(per_part)
            for j in range(n_gj)
        ]
        for part in range(parts)
    ]
    n_half = n_cols * per_part
    positions = residues * pair_cols
    each = own_rows * few

    per = lanes // pair_cols
    bias_block = (heads // per, residues, lanes)
    msa, bias = call(
        bias_kernel,
        [[(parts * rows, residues, width)], bias_block],
        [homolog_embedding],
        [pair_input_tensor],
        [pair_norm_gains],
        [pair_bias_matrix.T],
        scratch=[
            homolog_embedding.shape,
            pair_input_tensor.shape,
            pair_norm_gains.shape,
            (heads, pair_width),
        ],
        sems=[4, parts],
    )
    msa = lax.all_to_all(msa, "gi", 0, 0, tiled=True)
    (bias,) = call_near(
        functools.partial(bias_part_kernel, per_part),
        [(per_part,) + bias_block],
        *trade([bias] * per_part, "gi"),
    )
    bias = trade([bias] * n_cols, columns)
    (msa_first,) = call_near(
        functools.partial(row_kernel, n_branch, n_gj, per_part, few),
        [(n_half, each, width)],
        msa,
        *bias,
        layernorm_scales,
        horizontal_qkvg_kernel,
        horizontal_final_kernel,
        scratch=[(n_cols, per_part) + bias_block],
    )
    pair, msa_first = lax.optimization_barrier((pair_input_tensor, msa_first))

    msa_first = lax.all_to_all(msa_first, everyone, 0, 0, tiled=True, axis_index_groups=halves)
    count = n_half * each
    weights = (
        layernorm_scales,
        vertical_qkvg_kernel,
        vertical_final_kernel,
        feedforward_expand_kernel,
        feedforward_shrink_kernel,
        dyadic_sides_kernel.T,
    )
    left, right, alignment = call_near(
        functools.partial(column_kernel, few, heads),
        [(outer_width, count), (n_gi, outer_width, count), (count, width)],
        msa_first.reshape(count, width),
        *weights,
    )
    alignment = call_near(
        functools.partial(msa_blocks_kernel, n_branch, n_gj),
        [(per_part, each, width)] * n_cols,
        alignment,
        scratch=[(n_cols, per_part, each, width)],
    )
    pair = call_near(
        functools.partial(pair_blocks_kernel, few, residues),
        [(positions // n_cols, pair_width)] * n_cols,
        pair.reshape(positions, pair_width),
        scratch=[(positions, pair_width)],
    )
    pair = trade(pair, columns)
    right = lax.all_to_all(right, "gi", 0, 0, tiled=True)
    right, *alignment = lax.optimization_barrier((right, *alignment))
    left = trade([left] * n_cols, columns)
    alignment = [block.reshape(-1, width) for block in trade(alignment, columns)]
    share = max(pair_width // n_all, 1)
    slots = pair_width // share
    triangle = triangle_input_matrix.T.reshape(5, slots, share, pair_width)
    sides = jnp.stack([triangle[0], triangle[2]], axis=1)
    gates = jnp.stack([triangle[1], triangle[3]], axis=1)
    triangle = jnp.concatenate(
        [side.reshape(2 * pair_width, pair_width) for side in (sides, gates)]
        + [triangle[4].reshape(pair_width, pair_width)],
        axis=0,
    )
    matrix = outer_output_matrix.reshape(outer_width, outer_width // per, per, pair_width)
    matrix = jnp.transpose(matrix, (3, 2, 1, 0)).reshape(pair_width, -1)
    tri, *first = call_near(
        functools.partial(pair_kernel, few, n_gi, n_cols),
        [(slots, positions // lanes, 2 * share, lanes)]
        + [(positions // n_cols, pair_width)] * n_cols,
        *left,
        *pair,
        right.reshape(n_gi * outer_width, count),
        pair_norm_gains[1][:, None],
        matrix,
        triangle,
        scratch=[
            (n_cols, outer_width, count),
            (positions, pair_width),
            (positions, pair_width),
            (positions, pair_width),
        ],
    )

    first, gate = call_near(
        functools.partial(gather_pair_kernel, few, n_cols, residues),
        [(positions, pair_width)] * 2,
        pair_norm_gains,
        triangle_input_matrix,
        *trade(first, columns),
        scratch=[(positions, pair_width)],
    )
    tile = (rows, residues, width)
    scratch = [(n_cols, rows * few, width)]
    packed = share * n_all == pair_width and share == few and few == per
    if packed:
        tri = lax.all_to_all(tri, everyone, 0, 0, tiled=True)
        product, alignment_output = call_near(
            functools.partial(triangle_kernel, few, n_branch, n_gj),
            [(n_all, residues, lanes), tile],
            tri.reshape(-1, lanes),
            *alignment,
            scratch=[(lanes, lanes)] + scratch,
        )
        product = lax.all_to_all(product, everyone, 0, 0, tiled=True)
        product = product.reshape(n_all * residues, lanes)
    else:
        (alignment_output,) = call_near(
            functools.partial(gather_msa_kernel, few, n_cols),
            [tile],
            *alignment,
            scratch=scratch,
        )
        tri = jnp.transpose(tri.reshape(slots, -1, 2, share, lanes), (2, 1, 4, 0, 3))
        tri = tri.reshape(2, residues, pair_cols, pair_width)
        right_columns = lax.all_gather(tri[1], "gi", axis=0, tiled=True)
        product = lax.psum_scatter(
            jnp.einsum("jkc,ikc->jic", right_columns, tri[0], precision=precise),
            columns,
            scatter_dimension=0,
            tiled=True,
        ).reshape(groups, n_cols, few, residues, pair_width)
        product = jnp.transpose(product, (4, 3, 2, 0, 1)).reshape(pair_width, positions)
    (pair_output_tensor,) = call_near(
        functools.partial(final_kernel, few, residues, packed),
        [(positions, pair_width)],
        product,
        first,
        gate,
        pair_norm_gains,
        triangle_output_matrix,
        scratch=[(pair_width, lanes)],
    )
    return (
        alignment_output,
        pair_output_tensor.reshape(residues, pair_cols, pair_width),
    )


def solution(mesh):
    tile, grid = P(("branch", "gj"), "gi", None), P("gi", ("branch", "gj"), None)
    return jax.shard_map(
        per_device,
        mesh=mesh,
        in_specs=(tile, grid) + (P(),) * 13,
        out_specs=(tile, grid),
        check_vma=False,
    )
```

```python
import functools
import math

import jax
import jax.numpy as jnp
from jax import lax
from jax.experimental import pallas as pl
from jax.experimental.pallas import tpu as pltpu
from jax.sharding import PartitionSpec as P

epsilon = 1e-05
precise = lax.Precision.HIGH
everyone = ("branch", "gi", "gj")
columns = ("branch", "gj")
lanes = 128
far = pl.BlockSpec(memory_space=pl.ANY)
vmem = pl.BlockSpec(memory_space=pltpu.VMEM)
params = pltpu.CompilerParams(vmem_limit_bytes=16 * 1024 * 1024)


def layer_normalise(values, norm_gain, axis=-1):
    average = jnp.mean(values, axis=axis, keepdims=True)
    centred = values - average
    variance = jnp.mean(centred * centred, axis=axis, keepdims=True)
    return centred * lax.rsqrt(variance + epsilon) * norm_gain


def apply_projection(values, weight):
    return jnp.einsum("...c,cd->...d", values, weight, precision=precise)


def sigmoid(values):
    return 1.0 / (1.0 + jnp.exp(-values))


def split(values):
    high = values.astype(jnp.bfloat16)
    return high, (values - high.astype(jnp.float32)).astype(jnp.bfloat16)


def multiply(left, right, across=False):
    numbers = (((1,), (1 if across else 0,)), ((), ()))

    def one(a, b):
        return lax.dot_general(a, b, numbers, preferred_element_type=jnp.float32)

    (lh, ll), (rh, rl) = split(left), split(right)
    return one(lh, rh) + (one(lh, rl) + one(ll, rh))


def swap_lane_groups(arrays):
    n, arrays = len(arrays), list(arrays)
    width = lanes // n
    wide = arrays[0].shape[-1]
    lane = lax.broadcasted_iota(jnp.int32, arrays[0].shape, arrays[0].ndim - 1)
    group = lax.rem(lane, lanes) // width
    axis = arrays[0].ndim - 1
    step = 1
    while step < n:
        upper = (group // step) % 2 == 1
        for low in range(n):
            if low & step:
                continue
            a, b = arrays[low], arrays[low + step]
            arrays[low] = jnp.where(upper, pltpu.roll(b, step * width, axis), a)
            arrays[low + step] = jnp.where(
                upper, b, pltpu.roll(a, wide - step * width, axis)
            )
        step *= 2
    return arrays


def head_masks(shape, heads):
    column = lax.broadcasted_iota(jnp.int32, shape, 1)
    return [column // (shape[1] // heads) == h for h in range(heads)]


def attend(query, key, value, bias, heads, allowed=None):
    count, inner = query.shape
    masks = head_masks((count, inner), heads)
    spread = jnp.concatenate([jnp.where(m, query, 0.0) for m in masks], axis=0)
    scores = multiply(spread, key, across=True) * (1.0 / math.sqrt(inner // heads))
    if bias is not None:
        scores = scores + bias
    if allowed is not None:
        scores = jnp.where(allowed, scores, -1e30)
    weights = jnp.exp(scores - jnp.max(scores, axis=-1, keepdims=True))
    weights = weights / jnp.sum(weights, axis=-1, keepdims=True)
    mixed = multiply(weights, value)
    result = jnp.where(masks[0], mixed[:count], 0.0)
    for h in range(1, heads):
        result = result + jnp.where(masks[h], mixed[h * count : (h + 1) * count], 0.0)
    return result


def start_copies(pairs, sems):
    copies = [pltpu.make_async_copy(a, b, sems.at[n]) for n, (a, b) in enumerate(pairs)]
    for copy in copies:
        copy.start()
    return copies


def wait_all(copies):
    for copy in copies:
        copy.wait()


def column_index():
    return lax.axis_index("branch") * lax.axis_size("gj") + lax.axis_index("gj")


def cost(kernel):
    name = getattr(kernel, "func", kernel).__name__
    work = {
        "bias_kernel": 2.0,
        "bias_part_kernel": 6.0,
        "row_kernel": 4.5,
        "pair_blocks_kernel": 8.0,
        "column_kernel": 4.5,
        "msa_blocks_kernel": 0.5,
        "pair_kernel": 4.0,
        "triangle_kernel": 2.0,
        "gather_pair_kernel": 1.0,
        "final_kernel": 1.3,
    }.get(name, 1.0)
    return pl.CostEstimate(
        flops=int(work * 1.1e9), bytes_accessed=int(work * 3.6e6), transcendentals=0
    )


def call(kernel, outs, *operands, scratch=(), sems=()):
    def bare(item):
        return item[0] if isinstance(item, list) else item

    n_in, n_out = len(operands), len(outs)
    near_in = [n for n, item in enumerate(operands) if not isinstance(item, list)]
    near_out = [n for n, item in enumerate(outs) if not isinstance(item, list)]
    shapes = [operands[n].shape for n in near_in] + [outs[n] for n in near_out]

    def body(*refs):
        inputs, results = list(refs[:n_in]), list(refs[n_in : n_in + n_out])
        local = refs[n_in + n_out : n_in + n_out + len(shapes)]
        rest, own_sems = refs[n_in + n_out + len(shapes) : -1], refs[-1]
        pairs = list(zip([inputs[n] for n in near_in], local))
        back = list(zip(local[len(near_in) :], [results[n] for n in near_out]))
        for n, ref in zip(near_in, local):
            inputs[n] = ref
        for n, ref in zip(near_out, local[len(near_in) :]):
            results[n] = ref
        copies = start_copies(pairs, own_sems)
        kernel(lambda: wait_all(copies), *inputs, *results, *rest)
        wait_all(start_copies(back, own_sems))

    return pl.pallas_call(
        body,
        out_shape=[jax.ShapeDtypeStruct(bare(out), jnp.float32) for out in outs],
        in_specs=[far] * n_in,
        out_specs=[far] * n_out,
        scratch_shapes=[pltpu.VMEM(shape, jnp.float32) for shape in shapes + list(scratch)]
        + [pltpu.SemaphoreType.DMA((n,)) for n in sems]
        + [pltpu.SemaphoreType.DMA((max(len(near_in), len(near_out), 1),))],
        cost_estimate=cost(kernel),
    )(*[bare(operand) for operand in operands])


def call_near(kernel, outs, *operands, scratch=()):
    return pl.pallas_call(
        lambda *refs: kernel(lambda: None, *refs),
        out_shape=[jax.ShapeDtypeStruct(out, jnp.float32) for out in outs],
        in_specs=[vmem] * len(operands),
        out_specs=[vmem] * len(outs),
        scratch_shapes=[pltpu.VMEM(shape, jnp.float32) for shape in scratch],
        compiler_params=params,
        cost_estimate=cost(kernel),
    )(*operands)


def spread(me, refs, slots):
    for k, ref in enumerate(refs):
        slots[me ^ k] = ref[...]


def spread_rows(me, refs, slots):
    for k, ref in enumerate(refs):
        count = ref.shape[0]
        slots[pl.ds(pl.multiple_of((me ^ k) * count, 8), count), :] = ref[...]


def bias_kernel(
    ready, msa_far, pair_far, gains_far, matrix_far, copies_far, out_ref, msa_ref, pair_ref,
    gains_ref, matrix_ref, sems, out_sems
):
    rows = msa_far.shape[0]
    repeats = copies_far.shape[0] // rows
    copies = start_copies(
        [(msa_far, msa_ref), (gains_far, gains_ref), (matrix_far, matrix_ref), (pair_far, pair_ref)],
        sems,
    )
    residues, pair_cols, _ = pair_ref.shape
    heads = matrix_ref.shape[0]
    per = lanes // pair_cols
    ready()
    wait_all(copies)
    copies = start_copies(
        [(msa_ref, copies_far.at[pl.ds(n * rows, rows)]) for n in range(repeats)], out_sems
    )
    normal = layer_normalise(pair_ref[...], gains_ref[0:1, :][None])
    for i in range(residues):
        here = multiply(matrix_ref[...], normal[i], across=True)
        for h in range(heads):
            out_ref[h // per, i : i + 1, pl.ds(h % per * pair_cols, pair_cols)] = here[h : h + 1]
    wait_all(copies)


def pair_blocks_kernel(few, residues, ready, pair_ref, *rest):
    chunks, slots = rest[:-1], rest[-1]
    n_cols = len(chunks)
    block = chunks[0].shape[0]
    groups = block // (residues * few)
    me = column_index()
    ready()
    for c in range(n_cols):
        for o in range(groups):
            for f in range(few):
                source = pl.ds((o * n_cols + c) * few + f, residues, stride=groups * n_cols * few)
                target = pl.ds(c * block + f * groups + o, residues, stride=few * groups)
                slots[target, :] = pair_ref[source, :]
    for k in range(n_cols):
        start = pl.multiple_of((me ^ k) * block, 8)
        chunks[k][...] = slots[pl.ds(start, block), :]


def bias_part_kernel(per_part, ready, *rest):
    blocks, (out_ref,) = rest[:per_part], rest[per_part:]
    ready()
    spread(lax.rem(lax.axis_index("gi"), per_part), blocks, out_ref)


def row_kernel(n_branch, n_gj, per_part, few, ready, msa_ref, *rest):
    n_cols = n_branch * n_gj
    bias_refs, (gains_ref, qkvg_ref, final_ref, out_ref, slots) = rest[:n_cols], rest[n_cols:]
    half = lax.div(lax.axis_index("gi"), per_part)
    ready()
    _, residues, width = msa_ref.shape
    blocks = slots.shape[2]
    n_gi = lax.axis_size("gi")
    length = n_gi * residues
    per = lanes * n_cols // length
    heads = blocks * per
    rows = msa_ref.shape[0] // n_gi
    inner = final_ref.shape[0]
    queries = per_part * residues
    tokens = jnp.concatenate(
        [msa_ref[g * rows + r] for r in range(rows) for g in range(n_gi)], axis=0
    )
    first = half * (per_part * rows)
    asking = msa_ref[pl.ds(first, per_part * rows)]
    asking = jnp.concatenate(
        [asking[g * rows + r] for r in range(rows) for g in range(per_part)], axis=0
    )
    tokens = layer_normalise(tokens, 1.0)
    normal = layer_normalise(asking, 1.0)
    gain = gains_ref[0:1, :]
    key_value = multiply(tokens * gain, qkvg_ref[:, inner : 3 * inner])
    normal = normal * gain
    query = multiply(normal, qkvg_ref[:, :inner])
    gate = multiply(normal, qkvg_ref[:, 3 * inner :])
    spread(column_index(), bias_refs, slots)
    pieces = [[] for _ in range(heads)]
    for block in range(blocks):
        for g in range(per_part):
            tiles = [[] for _ in range(per)]
            for tile in range(n_cols // per):
                group = [slots[c, g, block] for c in range(tile * per, (tile + 1) * per)]
                for k, piece in enumerate(swap_lane_groups(group)):
                    tiles[k].append(piece)
            for k in range(per):
                pieces[block * per + k].append(jnp.concatenate(tiles[k], axis=1))
    bias = jnp.concatenate([piece for head in pieces for piece in head], axis=0)
    attended = []
    for r in range(rows):
        keys = key_value[r * length : (r + 1) * length, :inner]
        values = key_value[r * length : (r + 1) * length, inner:]
        attended.append(
            attend(query[r * queries : (r + 1) * queries], keys, values, bias, heads)
        )
    attended = jnp.concatenate(attended, axis=0)
    result = asking + multiply(sigmoid(gate) * attended, final_ref[...])
    for b in range(n_branch):
        for g in range(per_part):
            for j in range(n_gj):
                start = g * residues + (b * n_gj + j) * few
                out_ref[(b * per_part + g) * n_gj + j] = jnp.concatenate(
                    [result[r * queries + start : r * queries + start + few] for r in range(rows)],
                    axis=0,
                )


def column_kernel(
    few, heads, ready, msa_ref, gains_ref, qkvg_ref, final_ref, expand_ref, shrink_ref, sides_ref,
    left_ref, right_ref, out_ref
):
    ready()
    count, width = msa_ref.shape
    inner = final_ref.shape[0]
    half = sides_ref.shape[0] // 2
    first = msa_ref[...]
    projected = multiply(layer_normalise(first, gains_ref[1:2, :]), qkvg_ref[...])
    query, key, value, gate = (projected[:, k * inner : (k + 1) * inner] for k in range(4))
    allowed = None
    if few > 1:
        shape = (heads * count, count)
        asks = lax.broadcasted_iota(jnp.int32, shape, 0)
        holds = lax.broadcasted_iota(jnp.int32, shape, 1)
        allowed = lax.rem(asks, few) == lax.rem(holds, few)
    attended = attend(query, key, value, None, heads, allowed)
    second = first + multiply(sigmoid(gate) * attended, final_ref[...])
    expanded = multiply(layer_normalise(second, gains_ref[2:3, :]), expand_ref[...])
    third = second + multiply(jnp.maximum(expanded, 0.0), shrink_ref[...])
    out_ref[...] = third
    factors = multiply(sides_ref[...], layer_normalise(third, gains_ref[3:4, :]), across=True)
    left_ref[...] = factors[:half]
    for g in range(right_ref.shape[0]):
        right_ref[g] = factors[half:]


def msa_blocks_kernel(n_branch, n_gj, ready, msa_ref, *rest):
    chunks, slots = rest[:-1], rest[-1]
    per_part, each = slots.shape[1:3]
    ready()
    for b in range(n_branch):
        for g in range(per_part):
            for j in range(n_gj):
                start = ((b * per_part + g) * n_gj + j) * each
                slots[b * n_gj + j, g] = msa_ref[start : start + each]
    for k, chunk in enumerate(chunks):
        chunk[...] = slots[column_index() ^ k]


def gather_msa(few, me, blocks, out_ref, slots):
    n_cols = len(blocks)
    spread(me, blocks, slots)
    for r in range(out_ref.shape[0]):
        out_ref[r] = jnp.concatenate(
            [slots[c, r * few : (r + 1) * few] for c in range(n_cols)], axis=0
        )


def gather_msa_kernel(few, n_cols, ready, *rest):
    ready()
    gather_msa(few, column_index(), rest[:n_cols], *rest[n_cols:])


def gather_pair_kernel(few, n_cols, residues, ready, gains_ref, matrix_ref, *rest):
    blocks, (first_ref, gate_ref, slots) = rest[:n_cols], rest[n_cols:]
    ready()
    spread_rows(column_index(), blocks, slots)
    block = blocks[0].shape[0]
    count = residues * few
    groups = block // count
    for c in range(n_cols):
        for o in range(groups):
            first_ref[pl.ds(o * n_cols + c, count, stride=groups * n_cols), :] = slots[
                pl.ds(c * block + o * count, count), :
            ]
    width = first_ref.shape[1]
    normal = layer_normalise(first_ref[...], gains_ref[1:2, :])
    gate_ref[...] = sigmoid(multiply(normal, matrix_ref[:, 4 * width :]))


def triangle_kernel(few, n_branch, n_gj, ready, tri_ref, *rest):
    n_cols = n_branch * n_gj
    blocks, (out_ref, msa_out, product_ref, slots) = rest[:n_cols], rest[n_cols:]
    ready()
    gather_msa(few, column_index(), blocks, msa_out, slots)
    n_all, rows, _ = out_ref.shape
    n_gi = n_all // n_cols
    share = few
    tiles = rows // few
    each = 2 * share
    wide = lanes // few
    group = lax.broadcasted_iota(jnp.int32, (n_gi * tiles, lanes), 1) // wide
    products = []
    for q in range(share):
        left, right = [], []
        for c in range(n_cols):
            base = (c // n_gj * n_all // n_branch + c % n_gj) * tiles * each
            step = n_gj * tiles * each
            here = jnp.concatenate(
                [
                    tri_ref[pl.ds(base + t * each + q, n_gi, stride=step), :]
                    for t in range(tiles)
                ],
                axis=0,
            )
            left.append(
                jnp.concatenate(
                    [jnp.where(group == i, here, 0.0) for i in range(few)], axis=0
                )
            )
            here = jnp.concatenate(
                [
                    tri_ref[pl.ds(base + g * step + share + q, tiles, stride=each), :]
                    for g in range(n_gi)
                ],
                axis=0,
            )
            rolled = [here] + [pltpu.roll(here, k * wide, 1) for k in range(1, few)]
            copies = []
            for j in range(few):
                copy = rolled[0]
                for k in range(1, few):
                    copy = jnp.where(group == (j + k) % few, rolled[k], copy)
                copies.append(copy)
            step = n_gi * tiles // n_cols
            right.append(
                jnp.concatenate(
                    [copy[k * step : (k + 1) * step] for k in range(n_cols) for copy in copies],
                    axis=0,
                )
            )
        products.append(
            multiply(
                jnp.concatenate(left, axis=1), jnp.concatenate(right, axis=1), across=True
            )
        )
    for c, product in enumerate(swap_lane_groups(products)):
        product_ref[...] = product
        for g in range(n_gi):
            out_ref[(c // n_gj * n_gi + g) * n_gj + c % n_gj] = product_ref[pl.ds(g, rows, stride=n_gi), :]


def pair_kernel(
    few, n_gi, n_cols, ready, *rest
):
    left_refs, pair_refs = rest[:n_cols], rest[n_cols : 2 * n_cols]
    right_ref, gain_ref, matrix_ref, triangle_ref, tri_ref = rest[2 * n_cols : 2 * n_cols + 5]
    chunks = rest[2 * n_cols + 5 : 3 * n_cols + 5]
    rest = rest[3 * n_cols + 5 :]
    left_ref, slots, pair_ref, first_ref = rest
    me = column_index()
    groups_j = n_gi // n_cols
    block = pair_refs[0].shape[0]
    ready()
    spread(me, left_refs, left_ref)
    spread_rows(me, pair_refs, slots)
    _, wide, count = left_ref.shape
    half = block // groups_j
    all_rows = count // few
    residues = n_cols * few
    pair_cols = n_gi * few
    per = lanes // pair_cols
    groups = residues // per
    width = pair_ref.shape[1]
    owner = lax.rem(lax.broadcasted_iota(jnp.int32, (1, count), 1), few)
    left = []
    for c in range(n_cols):
        here = left_ref[c]
        for f in range(few):
            own = jnp.where(owner == f, here, 0.0)
            total = own
            for other in range(few):
                if other != f:
                    total = total + pltpu.roll(own, (other - f) % count, 1)
            left.append(total)
    left = jnp.concatenate(left, axis=0) * (1.0 / all_rows)
    right = []
    for d in range(wide):
        here = right_ref[pl.ds(d, n_gi, stride=wide), :]
        right += [jnp.where(owner == f, here, 0.0) for f in range(few)]
    right = jnp.concatenate(right, axis=0)
    outer = multiply(left, right, across=True)
    outputs = []
    for g in range(groups):
        swapped = swap_lane_groups(
            [outer[(g * per + i) * wide : (g * per + i + 1) * wide] for i in range(per)]
        )
        stacked = [
            s[:, t * lanes : (t + 1) * lanes] for s in swapped for t in range(wide // per)
        ]
        outputs.append(jnp.concatenate(stacked, axis=0))
    for c in range(n_cols):
        for o in range(groups_j):
            pair_ref[pl.ds(c * groups_j + o, half, stride=n_gi), :] = slots[
                pl.ds(c * block + o, half, stride=groups_j), :
            ]
    update = multiply(matrix_ref[...], jnp.concatenate(outputs, axis=1))
    first = pair_ref[...].T + update
    projected = multiply(
        triangle_ref[pl.ds(0, 4 * width), :], layer_normalise(first, gain_ref[...], axis=0)
    )
    tri = sigmoid(projected[2 * width : 4 * width]) * projected[: 2 * width]
    slot_count, _, each, _ = tri_ref.shape
    for g in range(groups):
        tri_ref[:, g] = tri[:, g * lanes : (g + 1) * lanes].reshape(slot_count, each, lanes)
    first_ref[...] = first.T
    for k in range(n_cols):
        for o in range(groups_j):
            rows = pl.ds((me ^ k) * groups_j + o, half, stride=n_gi)
            chunks[k][pl.ds(o * half, half), :] = first_ref[rows, :]


def final_kernel(
    few, residues, packed, ready, product_ref, first_ref, gate_ref, gains_ref, matrix_ref, out_ref,
    channels_ref
):
    positions = out_ref.shape[0]
    ready()
    if packed:
        tiles = residues // few
        tall = product_ref.shape[0] // residues
        product = []
        for t in range(tiles):
            here = [
                product_ref[pl.ds(i * tiles + t, tall, stride=residues), :] for i in range(few)
            ]
            for q, piece in enumerate(swap_lane_groups(here)):
                channels_ref[pl.ds(q, tall, stride=few), :] = piece
            product.append(channels_ref[...])
        product = jnp.concatenate(product, axis=1)
    else:
        product = product_ref[...]
    normal = layer_normalise(product, 1.0, axis=0).T * gains_ref[2:3, :]
    result = first_ref[...] + gate_ref[...] * multiply(normal, matrix_ref[...])
    count = positions // (residues * few)
    for i in range(residues):
        for f in range(few):
            start = (i * few + f) * count
            out_ref[pl.ds(i * few * count + f, count, stride=few), :] = result[
                start : start + count
            ]


def per_device(
    homolog_embedding,
    pair_input_tensor,
    layernorm_scales,
    pair_norm_gains,
    pair_bias_matrix,
    horizontal_qkvg_kernel,
    horizontal_final_kernel,
    vertical_qkvg_kernel,
    vertical_final_kernel,
    feedforward_expand_kernel,
    feedforward_shrink_kernel,
    dyadic_sides_kernel,
    outer_output_matrix,
    triangle_input_matrix,
    triangle_output_matrix,
):
    rows, residues, width = homolog_embedding.shape
    pair_cols, pair_width = pair_input_tensor.shape[1:]
    heads = pair_bias_matrix.shape[1]
    outer_width = dyadic_sides_kernel.shape[1] // 2
    n_branch, n_gi, n_gj = (lax.axis_size(name) for name in everyone)
    n_cols = n_branch * n_gj
    n_all = n_cols * n_gi
    length = residues * n_gi
    few = residues // n_cols
    groups = n_gi // n_cols
    parts = 2
    per_part = n_gi // parts
    own_rows = rows // per_part

    def trade(blocks, axes):
        n = lax.axis_size(axes)
        return [blocks[0]] + [
            lax.ppermute(blocks[k], axes, [(t ^ k, t) for t in range(n) if t ^ k < n])
            for k in range(1, len(blocks))
        ]

    halves = [
        [
            (b * n_gi + part * per_part + g) * n_gj + j
            for b in range(n_branch)
            for g in range(per_part)
            for j in range(n_gj)
        ]
        for part in range(parts)
    ]
    n_half = n_cols * per_part
    positions = residues * pair_cols
    each = own_rows * few

    per = lanes // pair_cols
    bias_block = (heads // per, residues, lanes)
    msa, bias = call(
        bias_kernel,
        [[(parts * rows, residues, width)], bias_block],
        [homolog_embedding],
        [pair_input_tensor],
        [pair_norm_gains],
        [pair_bias_matrix.T],
        scratch=[
            homolog_embedding.shape,
            pair_input_tensor.shape,
            pair_norm_gains.shape,
            (heads, pair_width),
        ],
        sems=[4, parts],
    )
    msa = lax.all_to_all(msa, "gi", 0, 0, tiled=True)
    (bias,) = call_near(
        functools.partial(bias_part_kernel, per_part),
        [(per_part,) + bias_block],
        *trade([bias] * per_part, "gi"),
    )
    bias = trade([bias] * n_cols, columns)
    (msa_first,) = call_near(
        functools.partial(row_kernel, n_branch, n_gj, per_part, few),
        [(n_half, each, width)],
        msa,
        *bias,
        layernorm_scales,
        horizontal_qkvg_kernel,
        horizontal_final_kernel,
        scratch=[(n_cols, per_part) + bias_block],
    )
    pair, msa_first = lax.optimization_barrier((pair_input_tensor, msa_first))

    msa_first = lax.all_to_all(msa_first, everyone, 0, 0, tiled=True, axis_index_groups=halves)
    count = n_half * each
    weights = (
        layernorm_scales,
        vertical_qkvg_kernel,
        vertical_final_kernel,
        feedforward_expand_kernel,
        feedforward_shrink_kernel,
        dyadic_sides_kernel.T,
    )
    pair = call_near(
        functools.partial(pair_blocks_kernel, few, residues),
        [(positions // n_cols, pair_width)] * n_cols,
        pair.reshape(positions, pair_width),
        scratch=[(positions, pair_width)],
    )
    msa_first, _ = lax.optimization_barrier((msa_first, pair[0]))
    pair = trade(pair, columns)
    left, right, alignment = call_near(
        functools.partial(column_kernel, few, heads),
        [(outer_width, count), (n_gi, outer_width, count), (count, width)],
        msa_first.reshape(count, width),
        *weights,
    )
    alignment = call_near(
        functools.partial(msa_blocks_kernel, n_branch, n_gj),
        [(per_part, each, width)] * n_cols,
        alignment,
        scratch=[(n_cols, per_part, each, width)],
    )
    right = lax.all_to_all(right, "gi", 0, 0, tiled=True)
    right, _ = lax.optimization_barrier((right, alignment[0]))
    left = trade([left] * n_cols, columns)
    alignment = [block.reshape(-1, width) for block in trade(alignment, columns)]
    share = max(pair_width // n_all, 1)
    slots = pair_width // share
    triangle = triangle_input_matrix.T.reshape(5, slots, share, pair_width)
    sides = jnp.stack([triangle[0], triangle[2]], axis=1)
    gates = jnp.stack([triangle[1], triangle[3]], axis=1)
    triangle = jnp.concatenate(
        [side.reshape(2 * pair_width, pair_width) for side in (sides, gates)]
        + [triangle[4].reshape(pair_width, pair_width)],
        axis=0,
    )
    matrix = outer_output_matrix.reshape(outer_width, outer_width // per, per, pair_width)
    matrix = jnp.transpose(matrix, (3, 2, 1, 0)).reshape(pair_width, -1)
    tri, *first = call_near(
        functools.partial(pair_kernel, few, n_gi, n_cols),
        [(slots, positions // lanes, 2 * share, lanes)]
        + [(positions // n_cols, pair_width)] * n_cols,
        *left,
        *pair,
        right.reshape(n_gi * outer_width, count),
        pair_norm_gains[1][:, None],
        matrix,
        triangle,
        scratch=[
            (n_cols, outer_width, count),
            (positions, pair_width),
            (positions, pair_width),
            (positions, pair_width),
        ],
    )

    first, gate = call_near(
        functools.partial(gather_pair_kernel, few, n_cols, residues),
        [(positions, pair_width)] * 2,
        pair_norm_gains,
        triangle_input_matrix,
        *trade(first, columns),
        scratch=[(positions, pair_width)],
    )
    tile = (rows, residues, width)
    scratch = [(n_cols, rows * few, width)]
    packed = share * n_all == pair_width and share == few and few == per
    if packed:
        tri = lax.all_to_all(tri, everyone, 0, 0, tiled=True)
        product, alignment_output = call_near(
            functools.partial(triangle_kernel, few, n_branch, n_gj),
            [(n_all, residues, lanes), tile],
            tri.reshape(-1, lanes),
            *alignment,
            scratch=[(lanes, lanes)] + scratch,
        )
        product = lax.all_to_all(product, everyone, 0, 0, tiled=True)
        product = product.reshape(n_all * residues, lanes)
    else:
        (alignment_output,) = call_near(
            functools.partial(gather_msa_kernel, few, n_cols),
            [tile],
            *alignment,
            scratch=scratch,
        )
        tri = jnp.transpose(tri.reshape(slots, -1, 2, share, lanes), (2, 1, 4, 0, 3))
        tri = tri.reshape(2, residues, pair_cols, pair_width)
        right_columns = lax.all_gather(tri[1], "gi", axis=0, tiled=True)
        product = lax.psum_scatter(
            jnp.einsum("jkc,ikc->jic", right_columns, tri[0], precision=precise),
            columns,
            scatter_dimension=0,
            tiled=True,
        ).reshape(groups, n_cols, few, residues, pair_width)
        product = jnp.transpose(product, (4, 3, 2, 0, 1)).reshape(pair_width, positions)
    (pair_output_tensor,) = call_near(
        functools.partial(final_kernel, few, residues, packed),
        [(positions, pair_width)],
        product,
        first,
        gate,
        pair_norm_gains,
        triangle_output_matrix,
        scratch=[(pair_width, lanes)],
    )
    return (
        alignment_output,
        pair_output_tensor.reshape(residues, pair_cols, pair_width),
    )


def solution(mesh):
    tile, grid = P(("branch", "gj"), "gi", None), P("gi", ("branch", "gj"), None)
    return jax.shard_map(
        per_device,
        mesh=mesh,
        in_specs=(tile, grid) + (P(),) * 13,
        out_specs=(tile, grid),
        check_vma=False,
    )
```

```python
import functools
import math

import jax
import jax.numpy as jnp
from jax import lax
from jax.experimental import pallas as pl
from jax.experimental.pallas import tpu as pltpu
from jax.sharding import PartitionSpec as P

epsilon = 1e-05
precise = lax.Precision.HIGH
everyone = ("branch", "gi", "gj")
columns = ("branch", "gj")
lanes = 128
far = pl.BlockSpec(memory_space=pl.ANY)
vmem = pl.BlockSpec(memory_space=pltpu.VMEM)
params = pltpu.CompilerParams(vmem_limit_bytes=16 * 1024 * 1024)


def layer_normalise(values, norm_gain, axis=-1):
    average = jnp.mean(values, axis=axis, keepdims=True)
    centred = values - average
    variance = jnp.mean(centred * centred, axis=axis, keepdims=True)
    return centred * lax.rsqrt(variance + epsilon) * norm_gain


def apply_projection(values, weight):
    return jnp.einsum("...c,cd->...d", values, weight, precision=precise)


def sigmoid(values):
    return 1.0 / (1.0 + jnp.exp(-values))


def split(values):
    high = values.astype(jnp.bfloat16)
    return high, (values - high.astype(jnp.float32)).astype(jnp.bfloat16)


def multiply(left, right, across=False):
    numbers = (((1,), (1 if across else 0,)), ((), ()))

    def one(a, b):
        return lax.dot_general(a, b, numbers, preferred_element_type=jnp.float32)

    (lh, ll), (rh, rl) = split(left), split(right)
    return one(lh, rh) + (one(lh, rl) + one(ll, rh))


def swap_lane_groups(arrays):
    n, arrays = len(arrays), list(arrays)
    width = lanes // n
    wide = arrays[0].shape[-1]
    lane = lax.broadcasted_iota(jnp.int32, arrays[0].shape, arrays[0].ndim - 1)
    group = lax.rem(lane, lanes) // width
    axis = arrays[0].ndim - 1
    step = 1
    while step < n:
        upper = (group // step) % 2 == 1
        for low in range(n):
            if low & step:
                continue
            a, b = arrays[low], arrays[low + step]
            arrays[low] = jnp.where(upper, pltpu.roll(b, step * width, axis), a)
            arrays[low + step] = jnp.where(
                upper, b, pltpu.roll(a, wide - step * width, axis)
            )
        step *= 2
    return arrays


def head_masks(shape, heads):
    column = lax.broadcasted_iota(jnp.int32, shape, 1)
    return [column // (shape[1] // heads) == h for h in range(heads)]


def attend(query, key, value, bias, heads, allowed=None):
    count, inner = query.shape
    masks = head_masks((count, inner), heads)
    spread = jnp.concatenate([jnp.where(m, query, 0.0) for m in masks], axis=0)
    scores = multiply(spread, key, across=True) * (1.0 / math.sqrt(inner // heads))
    if bias is not None:
        scores = scores + bias
    if allowed is not None:
        scores = jnp.where(allowed, scores, -1e30)
    weights = jnp.exp(scores - jnp.max(scores, axis=-1, keepdims=True))
    weights = weights / jnp.sum(weights, axis=-1, keepdims=True)
    mixed = multiply(weights, value)
    result = jnp.where(masks[0], mixed[:count], 0.0)
    for h in range(1, heads):
        result = result + jnp.where(masks[h], mixed[h * count : (h + 1) * count], 0.0)
    return result


def start_copies(pairs, sems):
    copies = [pltpu.make_async_copy(a, b, sems.at[n]) for n, (a, b) in enumerate(pairs)]
    for copy in copies:
        copy.start()
    return copies


def wait_all(copies):
    for copy in copies:
        copy.wait()


def column_index():
    return lax.axis_index("branch") * lax.axis_size("gj") + lax.axis_index("gj")


def cost(kernel):
    name = getattr(kernel, "func", kernel).__name__
    work = {
        "bias_kernel": 2.0,
        "bias_part_kernel": 6.0,
        "row_kernel": 4.5,
        "pair_blocks_kernel": 8.0,
        "column_kernel": 6.0,
        "transition_kernel": 3.0,
        "msa_blocks_kernel": 0.5,
        "pair_kernel": 4.0,
        "triangle_kernel": 2.0,
        "gather_pair_kernel": 1.0,
        "final_kernel": 1.3,
    }.get(name, 1.0)
    return pl.CostEstimate(
        flops=int(work * 1.1e9), bytes_accessed=int(work * 3.6e6), transcendentals=0
    )


def call(kernel, outs, *operands, scratch=(), sems=()):
    def bare(item):
        return item[0] if isinstance(item, list) else item

    n_in, n_out = len(operands), len(outs)
    near_in = [n for n, item in enumerate(operands) if not isinstance(item, list)]
    near_out = [n for n, item in enumerate(outs) if not isinstance(item, list)]
    shapes = [operands[n].shape for n in near_in] + [outs[n] for n in near_out]

    def body(*refs):
        inputs, results = list(refs[:n_in]), list(refs[n_in : n_in + n_out])
        local = refs[n_in + n_out : n_in + n_out + len(shapes)]
        rest, own_sems = refs[n_in + n_out + len(shapes) : -1], refs[-1]
        pairs = list(zip([inputs[n] for n in near_in], local))
        back = list(zip(local[len(near_in) :], [results[n] for n in near_out]))
        for n, ref in zip(near_in, local):
            inputs[n] = ref
        for n, ref in zip(near_out, local[len(near_in) :]):
            results[n] = ref
        copies = start_copies(pairs, own_sems)
        kernel(lambda: wait_all(copies), *inputs, *results, *rest)
        wait_all(start_copies(back, own_sems))

    return pl.pallas_call(
        body,
        out_shape=[jax.ShapeDtypeStruct(bare(out), jnp.float32) for out in outs],
        in_specs=[far] * n_in,
        out_specs=[far] * n_out,
        scratch_shapes=[pltpu.VMEM(shape, jnp.float32) for shape in shapes + list(scratch)]
        + [pltpu.SemaphoreType.DMA((n,)) for n in sems]
        + [pltpu.SemaphoreType.DMA((max(len(near_in), len(near_out), 1),))],
        cost_estimate=cost(kernel),
    )(*[bare(operand) for operand in operands])


def call_near(kernel, outs, *operands, scratch=(), sems=()):
    return pl.pallas_call(
        lambda *refs: kernel(lambda: None, *refs),
        out_shape=[
            jax.ShapeDtypeStruct(out[0] if isinstance(out, list) else out, jnp.float32)
            for out in outs
        ],
        in_specs=[vmem] * len(operands),
        out_specs=[far if isinstance(out, list) else vmem for out in outs],
        scratch_shapes=[pltpu.VMEM(shape, jnp.float32) for shape in scratch]
        + [pltpu.SemaphoreType.DMA((n,)) for n in sems],
        compiler_params=params,
        cost_estimate=cost(kernel),
    )(*operands)


def spread(me, refs, slots):
    for k, ref in enumerate(refs):
        slots[me ^ k] = ref[...]


def spread_rows(me, refs, slots):
    for k, ref in enumerate(refs):
        count = ref.shape[0]
        slots[pl.ds(pl.multiple_of((me ^ k) * count, 8), count), :] = ref[...]


def bias_kernel(
    ready, msa_far, pair_far, gains_far, matrix_far, copies_far, out_ref, msa_ref, pair_ref,
    gains_ref, matrix_ref, sems, out_sems
):
    rows = msa_far.shape[0]
    repeats = copies_far.shape[0] // rows
    copies = start_copies(
        [(msa_far, msa_ref), (gains_far, gains_ref), (matrix_far, matrix_ref), (pair_far, pair_ref)],
        sems,
    )
    residues, pair_cols, _ = pair_ref.shape
    heads = matrix_ref.shape[0]
    per = lanes // pair_cols
    ready()
    wait_all(copies)
    copies = start_copies(
        [(msa_ref, copies_far.at[pl.ds(n * rows, rows)]) for n in range(repeats)], out_sems
    )
    normal = layer_normalise(pair_ref[...], gains_ref[0:1, :][None])
    for i in range(residues):
        here = multiply(matrix_ref[...], normal[i], across=True)
        for h in range(heads):
            out_ref[h // per, i : i + 1, pl.ds(h % per * pair_cols, pair_cols)] = here[h : h + 1]
    wait_all(copies)


def pair_blocks_kernel(few, residues, ready, pair_ref, *rest):
    chunks, slots = rest[:-1], rest[-1]
    n_cols = len(chunks)
    block = chunks[0].shape[0]
    groups = block // (residues * few)
    me = column_index()
    ready()
    for c in range(n_cols):
        for o in range(groups):
            for f in range(few):
                source = pl.ds((o * n_cols + c) * few + f, residues, stride=groups * n_cols * few)
                target = pl.ds(c * block + f * groups + o, residues, stride=few * groups)
                slots[target, :] = pair_ref[source, :]
    for k in range(n_cols):
        start = pl.multiple_of((me ^ k) * block, 8)
        chunks[k][...] = slots[pl.ds(start, block), :]


def bias_part_kernel(per_part, ready, *rest):
    blocks, (out_ref,) = rest[:per_part], rest[per_part:]
    ready()
    spread(lax.rem(lax.axis_index("gi"), per_part), blocks, out_ref)


def row_kernel(n_branch, n_gj, per_part, few, ready, msa_ref, *rest):
    n_cols = n_branch * n_gj
    bias_refs, (gains_ref, qkvg_ref, final_ref, out_ref, slots) = rest[:n_cols], rest[n_cols:]
    half = lax.div(lax.axis_index("gi"), per_part)
    ready()
    _, residues, width = msa_ref.shape
    blocks = slots.shape[2]
    n_gi = lax.axis_size("gi")
    length = n_gi * residues
    per = lanes * n_cols // length
    heads = blocks * per
    rows = msa_ref.shape[0] // n_gi
    inner = final_ref.shape[0]
    queries = per_part * residues
    tokens = jnp.concatenate(
        [msa_ref[g * rows + r] for r in range(rows) for g in range(n_gi)], axis=0
    )
    first = half * (per_part * rows)
    asking = msa_ref[pl.ds(first, per_part * rows)]
    asking = jnp.concatenate(
        [asking[g * rows + r] for r in range(rows) for g in range(per_part)], axis=0
    )
    tokens = layer_normalise(tokens, 1.0)
    normal = layer_normalise(asking, 1.0)
    gain = gains_ref[0:1, :]
    key_value = multiply(tokens * gain, qkvg_ref[:, inner : 3 * inner])
    normal = normal * gain
    query = multiply(normal, qkvg_ref[:, :inner])
    gate = multiply(normal, qkvg_ref[:, 3 * inner :])
    spread(column_index(), bias_refs, slots)
    pieces = [[] for _ in range(heads)]
    for block in range(blocks):
        for g in range(per_part):
            tiles = [[] for _ in range(per)]
            for tile in range(n_cols // per):
                group = [slots[c, g, block] for c in range(tile * per, (tile + 1) * per)]
                for k, piece in enumerate(swap_lane_groups(group)):
                    tiles[k].append(piece)
            for k in range(per):
                pieces[block * per + k].append(jnp.concatenate(tiles[k], axis=1))
    bias = jnp.concatenate([piece for head in pieces for piece in head], axis=0)
    attended = []
    for r in range(rows):
        keys = key_value[r * length : (r + 1) * length, :inner]
        values = key_value[r * length : (r + 1) * length, inner:]
        attended.append(
            attend(query[r * queries : (r + 1) * queries], keys, values, bias, heads)
        )
    attended = jnp.concatenate(attended, axis=0)
    result = asking + multiply(sigmoid(gate) * attended, final_ref[...])
    for b in range(n_branch):
        for g in range(per_part):
            for j in range(n_gj):
                start = g * residues + (b * n_gj + j) * few
                out_ref[(b * per_part + g) * n_gj + j] = jnp.concatenate(
                    [result[r * queries + start : r * queries + start + few] for r in range(rows)],
                    axis=0,
                )


def column_kernel(few, heads, ready, msa_ref, gains_ref, qkvg_ref, final_ref, out_ref):
    ready()
    count, width = msa_ref.shape
    inner = final_ref.shape[0]
    first = msa_ref[...]
    projected = multiply(layer_normalise(first, gains_ref[1:2, :]), qkvg_ref[...])
    query, key, value, gate = (projected[:, k * inner : (k + 1) * inner] for k in range(4))
    allowed = None
    if few > 1:
        shape = (heads * count, count)
        asks = lax.broadcasted_iota(jnp.int32, shape, 0)
        holds = lax.broadcasted_iota(jnp.int32, shape, 1)
        allowed = lax.rem(asks, few) == lax.rem(holds, few)
    attended = attend(query, key, value, None, heads, allowed)
    out_ref[...] = first + multiply(sigmoid(gate) * attended, final_ref[...])


def transition_kernel(
    ready, msa_ref, gains_ref, expand_ref, shrink_ref, sides_ref, left_ref, right_ref, out_ref
):
    ready()
    half = sides_ref.shape[0] // 2
    second = msa_ref[...]
    expanded = multiply(layer_normalise(second, gains_ref[2:3, :]), expand_ref[...])
    third = second + multiply(jnp.maximum(expanded, 0.0), shrink_ref[...])
    out_ref[...] = third
    factors = multiply(sides_ref[...], layer_normalise(third, gains_ref[3:4, :]), across=True)
    left_ref[...] = factors[:half]
    for g in range(right_ref.shape[0]):
        right_ref[g] = factors[half:]


def msa_blocks_kernel(n_branch, n_gj, ready, msa_ref, *rest):
    chunks, slots = rest[:-1], rest[-1]
    per_part, each = slots.shape[1:3]
    ready()
    for b in range(n_branch):
        for g in range(per_part):
            for j in range(n_gj):
                start = ((b * per_part + g) * n_gj + j) * each
                slots[b * n_gj + j, g] = msa_ref[start : start + each]
    for k, chunk in enumerate(chunks):
        chunk[...] = slots[column_index() ^ k]


def gather_msa(few, me, blocks, out_ref, slots):
    n_cols = len(blocks)
    spread(me, blocks, slots)
    for r in range(out_ref.shape[0]):
        out_ref[r] = jnp.concatenate(
            [slots[c, r * few : (r + 1) * few] for c in range(n_cols)], axis=0
        )


def gather_msa_kernel(few, n_cols, ready, *rest):
    ready()
    gather_msa(few, column_index(), rest[:n_cols], *rest[n_cols:])


def gather_pair_kernel(few, n_cols, residues, ready, gains_ref, matrix_ref, *rest):
    blocks, (first_ref, gate_ref, slots) = rest[:n_cols], rest[n_cols:]
    ready()
    spread_rows(column_index(), blocks, slots)
    block = blocks[0].shape[0]
    count = residues * few
    groups = block // count
    for c in range(n_cols):
        for o in range(groups):
            first_ref[pl.ds(o * n_cols + c, count, stride=groups * n_cols), :] = slots[
                pl.ds(c * block + o * count, count), :
            ]
    width = first_ref.shape[1]
    normal = layer_normalise(first_ref[...], gains_ref[1:2, :])
    gate_ref[...] = sigmoid(multiply(normal, matrix_ref[:, 4 * width :]))


def triangle_kernel(few, n_branch, n_gj, ready, tri_ref, *rest):
    n_cols = n_branch * n_gj
    blocks, (out_ref, msa_out, product_ref, slots) = rest[:n_cols], rest[n_cols:]
    ready()
    gather_msa(few, column_index(), blocks, msa_out, slots)
    n_all, rows, _ = out_ref.shape
    n_gi = n_all // n_cols
    share = few
    tiles = rows // few
    each = 2 * share
    wide = lanes // few
    group = lax.broadcasted_iota(jnp.int32, (n_gi * tiles, lanes), 1) // wide
    products = []
    for q in range(share):
        left, right = [], []
        for c in range(n_cols):
            base = (c // n_gj * n_all // n_branch + c % n_gj) * tiles * each
            step = n_gj * tiles * each
            here = jnp.concatenate(
                [
                    tri_ref[pl.ds(base + t * each + q, n_gi, stride=step), :]
                    for t in range(tiles)
                ],
                axis=0,
            )
            left.append(
                jnp.concatenate(
                    [jnp.where(group == i, here, 0.0) for i in range(few)], axis=0
                )
            )
            here = jnp.concatenate(
                [
                    tri_ref[pl.ds(base + g * step + share + q, tiles, stride=each), :]
                    for g in range(n_gi)
                ],
                axis=0,
            )
            rolled = [here] + [pltpu.roll(here, k * wide, 1) for k in range(1, few)]
            copies = []
            for j in range(few):
                copy = rolled[0]
                for k in range(1, few):
                    copy = jnp.where(group == (j + k) % few, rolled[k], copy)
                copies.append(copy)
            step = n_gi * tiles // n_cols
            right.append(
                jnp.concatenate(
                    [copy[k * step : (k + 1) * step] for k in range(n_cols) for copy in copies],
                    axis=0,
                )
            )
        products.append(
            multiply(
                jnp.concatenate(left, axis=1), jnp.concatenate(right, axis=1), across=True
            )
        )
    for c, product in enumerate(swap_lane_groups(products)):
        product_ref[...] = product
        for g in range(n_gi):
            out_ref[(c // n_gj * n_gi + g) * n_gj + c % n_gj] = product_ref[pl.ds(g, rows, stride=n_gi), :]


def pair_kernel(
    few, n_gi, n_cols, ready, *rest
):
    left_refs, pair_refs = rest[:n_cols], rest[n_cols : 2 * n_cols]
    right_ref, gain_ref, matrix_ref, triangle_ref, tri_far = rest[2 * n_cols : 2 * n_cols + 5]
    chunks = rest[2 * n_cols + 5 : 3 * n_cols + 5]
    rest = rest[3 * n_cols + 5 :]
    left_ref, slots, pair_ref, first_ref, tri_ref, sems = rest
    me = column_index()
    groups_j = n_gi // n_cols
    block = pair_refs[0].shape[0]
    ready()
    spread(me, left_refs, left_ref)
    spread_rows(me, pair_refs, slots)
    _, wide, count = left_ref.shape
    half = block // groups_j
    all_rows = count // few
    residues = n_cols * few
    pair_cols = n_gi * few
    per = lanes // pair_cols
    groups = residues // per
    width = pair_ref.shape[1]
    owner = lax.rem(lax.broadcasted_iota(jnp.int32, (1, count), 1), few)
    left = []
    for c in range(n_cols):
        here = left_ref[c]
        for f in range(few):
            own = jnp.where(owner == f, here, 0.0)
            total = own
            for other in range(few):
                if other != f:
                    total = total + pltpu.roll(own, (other - f) % count, 1)
            left.append(total)
    left = jnp.concatenate(left, axis=0) * (1.0 / all_rows)
    right = []
    for d in range(wide):
        here = right_ref[pl.ds(d, n_gi, stride=wide), :]
        right += [jnp.where(owner == f, here, 0.0) for f in range(few)]
    right = jnp.concatenate(right, axis=0)
    outer = multiply(left, right, across=True)
    outputs = []
    for g in range(groups):
        swapped = swap_lane_groups(
            [outer[(g * per + i) * wide : (g * per + i + 1) * wide] for i in range(per)]
        )
        stacked = [
            s[:, t * lanes : (t + 1) * lanes] for s in swapped for t in range(wide // per)
        ]
        outputs.append(jnp.concatenate(stacked, axis=0))
    for c in range(n_cols):
        for o in range(groups_j):
            pair_ref[pl.ds(c * groups_j + o, half, stride=n_gi), :] = slots[
                pl.ds(c * block + o, half, stride=groups_j), :
            ]
    update = multiply(matrix_ref[...], jnp.concatenate(outputs, axis=1))
    first = pair_ref[...].T + update
    projected = multiply(
        triangle_ref[pl.ds(0, 4 * width), :], layer_normalise(first, gain_ref[...], axis=0)
    )
    slot_count, _, each, _ = tri_far.shape
    copies = []
    for g in range(groups):
        here = slice(g * lanes, (g + 1) * lanes)
        tri = sigmoid(projected[2 * width : 4 * width, here]) * projected[: 2 * width, here]
        tri_ref[g] = tri.reshape(slot_count, each, lanes)
        copies.append(pltpu.make_async_copy(tri_ref.at[g], tri_far.at[:, g], sems.at[g]))
        copies[-1].start()
    first_ref[...] = first.T
    for k in range(n_cols):
        for o in range(groups_j):
            rows = pl.ds((me ^ k) * groups_j + o, half, stride=n_gi)
            chunks[k][pl.ds(o * half, half), :] = first_ref[rows, :]
    wait_all(copies)


def final_kernel(
    few, residues, packed, ready, product_ref, first_ref, gate_ref, gains_ref, matrix_ref, out_ref,
    channels_ref
):
    positions = out_ref.shape[0]
    ready()
    if packed:
        tiles = residues // few
        tall = product_ref.shape[0] // residues
        product = []
        for t in range(tiles):
            here = [
                product_ref[pl.ds(i * tiles + t, tall, stride=residues), :] for i in range(few)
            ]
            for q, piece in enumerate(swap_lane_groups(here)):
                channels_ref[pl.ds(q, tall, stride=few), :] = piece
            product.append(channels_ref[...])
        product = jnp.concatenate(product, axis=1)
    else:
        product = product_ref[...]
    normal = layer_normalise(product, 1.0, axis=0).T * gains_ref[2:3, :]
    result = first_ref[...] + gate_ref[...] * multiply(normal, matrix_ref[...])
    count = positions // (residues * few)
    for i in range(residues):
        for f in range(few):
            start = (i * few + f) * count
            out_ref[pl.ds(i * few * count + f, count, stride=few), :] = result[
                start : start + count
            ]


def per_device(
    homolog_embedding,
    pair_input_tensor,
    layernorm_scales,
    pair_norm_gains,
    pair_bias_matrix,
    horizontal_qkvg_kernel,
    horizontal_final_kernel,
    vertical_qkvg_kernel,
    vertical_final_kernel,
    feedforward_expand_kernel,
    feedforward_shrink_kernel,
    dyadic_sides_kernel,
    outer_output_matrix,
    triangle_input_matrix,
    triangle_output_matrix,
):
    rows, residues, width = homolog_embedding.shape
    pair_cols, pair_width = pair_input_tensor.shape[1:]
    heads = pair_bias_matrix.shape[1]
    outer_width = dyadic_sides_kernel.shape[1] // 2
    n_branch, n_gi, n_gj = (lax.axis_size(name) for name in everyone)
    n_cols = n_branch * n_gj
    n_all = n_cols * n_gi
    length = residues * n_gi
    few = residues // n_cols
    groups = n_gi // n_cols
    parts = 2
    per_part = n_gi // parts
    own_rows = rows // per_part

    def trade(blocks, axes):
        n = lax.axis_size(axes)
        return [blocks[0]] + [
            lax.ppermute(blocks[k], axes, [(t ^ k, t) for t in range(n) if t ^ k < n])
            for k in range(1, len(blocks))
        ]

    halves = [
        [
            (b * n_gi + part * per_part + g) * n_gj + j
            for b in range(n_branch)
            for g in range(per_part)
            for j in range(n_gj)
        ]
        for part in range(parts)
    ]
    n_half = n_cols * per_part
    positions = residues * pair_cols
    each = own_rows * few

    per = lanes // pair_cols
    bias_block = (heads // per, residues, lanes)
    msa, bias = call(
        bias_kernel,
        [[(parts * rows, residues, width)], bias_block],
        [homolog_embedding],
        [pair_input_tensor],
        [pair_norm_gains],
        [pair_bias_matrix.T],
        scratch=[
            homolog_embedding.shape,
            pair_input_tensor.shape,
            pair_norm_gains.shape,
            (heads, pair_width),
        ],
        sems=[4, parts],
    )
    msa = lax.all_to_all(msa, "gi", 0, 0, tiled=True)
    (bias,) = call_near(
        functools.partial(bias_part_kernel, per_part),
        [(per_part,) + bias_block],
        *trade([bias] * per_part, "gi"),
    )
    bias = trade([bias] * n_cols, columns)
    (msa_first,) = call_near(
        functools.partial(row_kernel, n_branch, n_gj, per_part, few),
        [(n_half, each, width)],
        msa,
        *bias,
        layernorm_scales,
        horizontal_qkvg_kernel,
        horizontal_final_kernel,
        scratch=[(n_cols, per_part) + bias_block],
    )
    pair, msa_first = lax.optimization_barrier((pair_input_tensor, msa_first))

    msa_first = lax.all_to_all(msa_first, everyone, 0, 0, tiled=True, axis_index_groups=halves)
    count = n_half * each
    (msa_second,) = call_near(
        functools.partial(column_kernel, few, heads),
        [(count, width)],
        msa_first.reshape(count, width),
        layernorm_scales,
        vertical_qkvg_kernel,
        vertical_final_kernel,
    )
    left, right, alignment = call_near(
        transition_kernel,
        [(outer_width, count), (n_gi, outer_width, count), (count, width)],
        msa_second,
        layernorm_scales,
        feedforward_expand_kernel,
        feedforward_shrink_kernel,
        dyadic_sides_kernel.T,
    )
    alignment = call_near(
        functools.partial(msa_blocks_kernel, n_branch, n_gj),
        [(per_part, each, width)] * n_cols,
        alignment,
        scratch=[(n_cols, per_part, each, width)],
    )
    pair = call_near(
        functools.partial(pair_blocks_kernel, few, residues),
        [(positions // n_cols, pair_width)] * n_cols,
        pair.reshape(positions, pair_width),
        scratch=[(positions, pair_width)],
    )
    pair = trade(pair, columns)
    right = lax.all_to_all(right, "gi", 0, 0, tiled=True)
    left = trade([left] * n_cols, columns)
    alignment = [block.reshape(-1, width) for block in trade(alignment, columns)]
    share = max(pair_width // n_all, 1)
    slots = pair_width // share
    triangle = triangle_input_matrix.T.reshape(5, slots, share, pair_width)
    sides = jnp.stack([triangle[0], triangle[2]], axis=1)
    gates = jnp.stack([triangle[1], triangle[3]], axis=1)
    triangle = jnp.concatenate(
        [side.reshape(2 * pair_width, pair_width) for side in (sides, gates)]
        + [triangle[4].reshape(pair_width, pair_width)],
        axis=0,
    )
    matrix = outer_output_matrix.reshape(outer_width, outer_width // per, per, pair_width)
    matrix = jnp.transpose(matrix, (3, 2, 1, 0)).reshape(pair_width, -1)
    tri, *first = call_near(
        functools.partial(pair_kernel, few, n_gi, n_cols),
        [[(slots, positions // lanes, 2 * share, lanes)]]
        + [(positions // n_cols, pair_width)] * n_cols,
        *left,
        *pair,
        right.reshape(n_gi * outer_width, count),
        pair_norm_gains[1][:, None],
        matrix,
        triangle,
        scratch=[
            (n_cols, outer_width, count),
            (positions, pair_width),
            (positions, pair_width),
            (positions, pair_width),
            (positions // lanes, slots, 2 * share, lanes),
        ],
        sems=[positions // lanes],
    )

    first, gate = call_near(
        functools.partial(gather_pair_kernel, few, n_cols, residues),
        [(positions, pair_width)] * 2,
        pair_norm_gains,
        triangle_input_matrix,
        *trade(first, columns),
        scratch=[(positions, pair_width)],
    )
    tile = (rows, residues, width)
    scratch = [(n_cols, rows * few, width)]
    packed = share * n_all == pair_width and share == few and few == per
    if packed:
        tri = lax.all_to_all(tri, everyone, 0, 0, tiled=True)
        product, alignment_output = call_near(
            functools.partial(triangle_kernel, few, n_branch, n_gj),
            [(n_all, residues, lanes), tile],
            tri.reshape(-1, lanes),
            *alignment,
            scratch=[(lanes, lanes)] + scratch,
        )
        product = lax.all_to_all(product, everyone, 0, 0, tiled=True)
        product = product.reshape(n_all * residues, lanes)
    else:
        (alignment_output,) = call_near(
            functools.partial(gather_msa_kernel, few, n_cols),
            [tile],
            *alignment,
            scratch=scratch,
        )
        tri = jnp.transpose(tri.reshape(slots, -1, 2, share, lanes), (2, 1, 4, 0, 3))
        tri = tri.reshape(2, residues, pair_cols, pair_width)
        right_columns = lax.all_gather(tri[1], "gi", axis=0, tiled=True)
        product = lax.psum_scatter(
            jnp.einsum("jkc,ikc->jic", right_columns, tri[0], precision=precise),
            columns,
            scatter_dimension=0,
            tiled=True,
        ).reshape(groups, n_cols, few, residues, pair_width)
        product = jnp.transpose(product, (4, 3, 2, 0, 1)).reshape(pair_width, positions)
    (pair_output_tensor,) = call_near(
        functools.partial(final_kernel, few, residues, packed),
        [(positions, pair_width)],
        product,
        first,
        gate,
        pair_norm_gains,
        triangle_output_matrix,
        scratch=[(pair_width, lanes)],
    )
    return (
        alignment_output,
        pair_output_tensor.reshape(residues, pair_cols, pair_width),
    )


def solution(mesh):
    tile, grid = P(("branch", "gj"), "gi", None), P("gi", ("branch", "gj"), None)
    return jax.shard_map(
        per_device,
        mesh=mesh,
        in_specs=(tile, grid) + (P(),) * 13,
        out_specs=(tile, grid),
        check_vma=False,
    )
```

```python
import functools
import math

import jax
import jax.numpy as jnp
from jax import lax
from jax.experimental import pallas as pl
from jax.experimental.pallas import tpu as pltpu
from jax.sharding import PartitionSpec as P

epsilon = 1e-05
precise = lax.Precision.HIGH
everyone = ("branch", "gi", "gj")
columns = ("branch", "gj")
lanes = 128
far = pl.BlockSpec(memory_space=pl.ANY)
vmem = pl.BlockSpec(memory_space=pltpu.VMEM)
params = pltpu.CompilerParams(vmem_limit_bytes=16 * 1024 * 1024)


def layer_normalise(values, norm_gain, axis=-1):
    average = jnp.mean(values, axis=axis, keepdims=True)
    centred = values - average
    variance = jnp.mean(centred * centred, axis=axis, keepdims=True)
    return centred * lax.rsqrt(variance + epsilon) * norm_gain


def apply_projection(values, weight):
    return jnp.einsum("...c,cd->...d", values, weight, precision=precise)


def sigmoid(values):
    return 1.0 / (1.0 + jnp.exp(-values))


def split(values):
    high = values.astype(jnp.bfloat16)
    return high, (values - high.astype(jnp.float32)).astype(jnp.bfloat16)


def multiply(left, right, across=False):
    numbers = (((1,), (1 if across else 0,)), ((), ()))

    def one(a, b):
        return lax.dot_general(a, b, numbers, preferred_element_type=jnp.float32)

    (lh, ll), (rh, rl) = split(left), split(right)
    depth_axis = 1 if across else 0
    if left.shape[1] == lanes:
        both = one(
            jnp.concatenate([lh, ll], axis=1), jnp.concatenate([rh, rh], axis=depth_axis)
        )
        return both + one(lh, rl)
    if right.shape[1 - depth_axis] == lanes:
        both = one(lh, jnp.concatenate([rh, rl], axis=1 - depth_axis))
        return both[:, :lanes] + (both[:, lanes:] + one(ll, rh))
    return one(lh, rh) + (one(lh, rl) + one(ll, rh))


def swap_lane_groups(arrays):
    n, arrays = len(arrays), list(arrays)
    width = lanes // n
    wide = arrays[0].shape[-1]
    lane = lax.broadcasted_iota(jnp.int32, arrays[0].shape, arrays[0].ndim - 1)
    group = lax.rem(lane, lanes) // width
    axis = arrays[0].ndim - 1
    step = 1
    while step < n:
        upper = (group // step) % 2 == 1
        for low in range(n):
            if low & step:
                continue
            a, b = arrays[low], arrays[low + step]
            arrays[low] = jnp.where(upper, pltpu.roll(b, step * width, axis), a)
            arrays[low + step] = jnp.where(
                upper, b, pltpu.roll(a, wide - step * width, axis)
            )
        step *= 2
    return arrays


def head_masks(shape, heads):
    column = lax.broadcasted_iota(jnp.int32, shape, 1)
    return [column // (shape[1] // heads) == h for h in range(heads)]


def attend(query, key, value, bias, heads, allowed=None):
    count, inner = query.shape
    masks = head_masks((count, inner), heads)
    spread = jnp.concatenate([jnp.where(m, query, 0.0) for m in masks], axis=0)
    scores = multiply(spread, key, across=True) * (1.0 / math.sqrt(inner // heads))
    if bias is not None:
        scores = scores + bias
    if allowed is not None:
        scores = jnp.where(allowed, scores, -1e30)
    weights = jnp.exp(scores - jnp.max(scores, axis=-1, keepdims=True))
    weights = weights / jnp.sum(weights, axis=-1, keepdims=True)
    mixed = multiply(weights, value)
    result = jnp.where(masks[0], mixed[:count], 0.0)
    for h in range(1, heads):
        result = result + jnp.where(masks[h], mixed[h * count : (h + 1) * count], 0.0)
    return result


def start_copies(pairs, sems):
    copies = [pltpu.make_async_copy(a, b, sems.at[n]) for n, (a, b) in enumerate(pairs)]
    for copy in copies:
        copy.start()
    return copies


def wait_all(copies):
    for copy in copies:
        copy.wait()


def column_index():
    return lax.axis_index("branch") * lax.axis_size("gj") + lax.axis_index("gj")


def cost(kernel):
    name = getattr(kernel, "func", kernel).__name__
    work = {
        "bias_kernel": 2.0,
        "bias_part_kernel": 6.0,
        "row_kernel": 4.5,
        "pair_blocks_kernel": 8.0,
        "column_kernel": 6.0,
        "transition_kernel": 3.0,
        "msa_blocks_kernel": 0.5,
        "pair_kernel": 4.0,
        "triangle_kernel": 2.0,
        "gather_pair_kernel": 1.0,
        "final_kernel": 1.3,
    }.get(name, 1.0)
    return pl.CostEstimate(
        flops=int(work * 1.1e9), bytes_accessed=int(work * 3.6e6), transcendentals=0
    )


def call(kernel, outs, *operands, scratch=(), sems=()):
    def bare(item):
        return item[0] if isinstance(item, list) else item

    n_in, n_out = len(operands), len(outs)
    near_in = [n for n, item in enumerate(operands) if not isinstance(item, list)]
    near_out = [n for n, item in enumerate(outs) if not isinstance(item, list)]
    shapes = [operands[n].shape for n in near_in] + [outs[n] for n in near_out]

    def body(*refs):
        inputs, results = list(refs[:n_in]), list(refs[n_in : n_in + n_out])
        local = refs[n_in + n_out : n_in + n_out + len(shapes)]
        rest, own_sems = refs[n_in + n_out + len(shapes) : -1], refs[-1]
        pairs = list(zip([inputs[n] for n in near_in], local))
        back = list(zip(local[len(near_in) :], [results[n] for n in near_out]))
        for n, ref in zip(near_in, local):
            inputs[n] = ref
        for n, ref in zip(near_out, local[len(near_in) :]):
            results[n] = ref
        copies = start_copies(pairs, own_sems)
        kernel(lambda: wait_all(copies), *inputs, *results, *rest)
        wait_all(start_copies(back, own_sems))

    return pl.pallas_call(
        body,
        out_shape=[jax.ShapeDtypeStruct(bare(out), jnp.float32) for out in outs],
        in_specs=[far] * n_in,
        out_specs=[far] * n_out,
        scratch_shapes=[pltpu.VMEM(shape, jnp.float32) for shape in shapes + list(scratch)]
        + [pltpu.SemaphoreType.DMA((n,)) for n in sems]
        + [pltpu.SemaphoreType.DMA((max(len(near_in), len(near_out), 1),))],
        cost_estimate=cost(kernel),
    )(*[bare(operand) for operand in operands])


def call_near(kernel, outs, *operands, scratch=(), sems=()):
    return pl.pallas_call(
        lambda *refs: kernel(lambda: None, *refs),
        out_shape=[
            jax.ShapeDtypeStruct(out[0] if isinstance(out, list) else out, jnp.float32)
            for out in outs
        ],
        in_specs=[vmem] * len(operands),
        out_specs=[far if isinstance(out, list) else vmem for out in outs],
        scratch_shapes=[pltpu.VMEM(shape, jnp.float32) for shape in scratch]
        + [pltpu.SemaphoreType.DMA((n,)) for n in sems],
        compiler_params=params,
        cost_estimate=cost(kernel),
    )(*operands)


def spread(me, refs, slots):
    for k, ref in enumerate(refs):
        slots[me ^ k] = ref[...]


def spread_rows(me, refs, slots):
    for k, ref in enumerate(refs):
        count = ref.shape[0]
        slots[pl.ds(pl.multiple_of((me ^ k) * count, 8), count), :] = ref[...]


def bias_kernel(
    ready, msa_far, pair_far, gains_far, matrix_far, copies_far, out_ref, msa_ref, pair_ref,
    gains_ref, matrix_ref, sems, out_sems
):
    rows = msa_far.shape[0]
    repeats = copies_far.shape[0] // rows
    copies = start_copies(
        [(msa_far, msa_ref), (gains_far, gains_ref), (matrix_far, matrix_ref), (pair_far, pair_ref)],
        sems,
    )
    residues, pair_cols, _ = pair_ref.shape
    heads = matrix_ref.shape[0]
    per = lanes // pair_cols
    ready()
    wait_all(copies)
    copies = start_copies(
        [(msa_ref, copies_far.at[pl.ds(n * rows, rows)]) for n in range(repeats)], out_sems
    )
    normal = layer_normalise(pair_ref[...], gains_ref[0:1, :][None])
    for i in range(residues):
        here = multiply(matrix_ref[...], normal[i], across=True)
        for h in range(heads):
            out_ref[h // per, i : i + 1, pl.ds(h % per * pair_cols, pair_cols)] = here[h : h + 1]
    wait_all(copies)


def pair_blocks_kernel(few, residues, ready, pair_ref, *rest):
    chunks, slots = rest[:-1], rest[-1]
    n_cols = len(chunks)
    block = chunks[0].shape[0]
    groups = block // (residues * few)
    me = column_index()
    ready()
    for c in range(n_cols):
        for o in range(groups):
            for f in range(few):
                source = pl.ds((o * n_cols + c) * few + f, residues, stride=groups * n_cols * few)
                target = pl.ds(c * block + f * groups + o, residues, stride=few * groups)
                slots[target, :] = pair_ref[source, :]
    for k in range(n_cols):
        start = pl.multiple_of((me ^ k) * block, 8)
        chunks[k][...] = slots[pl.ds(start, block), :]


def bias_part_kernel(per_part, ready, *rest):
    blocks, (out_ref,) = rest[:per_part], rest[per_part:]
    ready()
    spread(lax.rem(lax.axis_index("gi"), per_part), blocks, out_ref)


def row_kernel(n_branch, n_gj, per_part, few, ready, msa_ref, *rest):
    n_cols = n_branch * n_gj
    bias_refs, (gains_ref, qkvg_ref, final_ref, out_ref, slots) = rest[:n_cols], rest[n_cols:]
    half = lax.div(lax.axis_index("gi"), per_part)
    ready()
    _, residues, width = msa_ref.shape
    blocks = slots.shape[2]
    n_gi = lax.axis_size("gi")
    length = n_gi * residues
    per = lanes * n_cols // length
    heads = blocks * per
    rows = msa_ref.shape[0] // n_gi
    inner = final_ref.shape[0]
    queries = per_part * residues
    tokens = jnp.concatenate(
        [msa_ref[g * rows + r] for r in range(rows) for g in range(n_gi)], axis=0
    )
    first = half * (per_part * rows)
    asking = msa_ref[pl.ds(first, per_part * rows)]
    asking = jnp.concatenate(
        [asking[g * rows + r] for r in range(rows) for g in range(per_part)], axis=0
    )
    tokens = layer_normalise(tokens, 1.0)
    normal = layer_normalise(asking, 1.0)
    gain = gains_ref[0:1, :]
    key_value = multiply(tokens * gain, qkvg_ref[:, inner : 3 * inner])
    normal = normal * gain
    query = multiply(normal, qkvg_ref[:, :inner])
    gate = multiply(normal, qkvg_ref[:, 3 * inner :])
    spread(column_index(), bias_refs, slots)
    pieces = [[] for _ in range(heads)]
    for block in range(blocks):
        for g in range(per_part):
            tiles = [[] for _ in range(per)]
            for tile in range(n_cols // per):
                group = [slots[c, g, block] for c in range(tile * per, (tile + 1) * per)]
                for k, piece in enumerate(swap_lane_groups(group)):
                    tiles[k].append(piece)
            for k in range(per):
                pieces[block * per + k].append(jnp.concatenate(tiles[k], axis=1))
    bias = jnp.concatenate([piece for head in pieces for piece in head], axis=0)
    attended = []
    for r in range(rows):
        keys = key_value[r * length : (r + 1) * length, :inner]
        values = key_value[r * length : (r + 1) * length, inner:]
        attended.append(
            attend(query[r * queries : (r + 1) * queries], keys, values, bias, heads)
        )
    attended = jnp.concatenate(attended, axis=0)
    result = asking + multiply(sigmoid(gate) * attended, final_ref[...])
    for b in range(n_branch):
        for g in range(per_part):
            for j in range(n_gj):
                start = g * residues + (b * n_gj + j) * few
                out_ref[(b * per_part + g) * n_gj + j] = jnp.concatenate(
                    [result[r * queries + start : r * queries + start + few] for r in range(rows)],
                    axis=0,
                )


def column_kernel(few, heads, ready, msa_ref, gains_ref, qkvg_ref, final_ref, out_ref):
    ready()
    count, width = msa_ref.shape
    inner = final_ref.shape[0]
    first = msa_ref[...]
    projected = multiply(layer_normalise(first, gains_ref[1:2, :]), qkvg_ref[...])
    query, key, value, gate = (projected[:, k * inner : (k + 1) * inner] for k in range(4))
    allowed = None
    if few > 1:
        shape = (heads * count, count)
        asks = lax.broadcasted_iota(jnp.int32, shape, 0)
        holds = lax.broadcasted_iota(jnp.int32, shape, 1)
        allowed = lax.rem(asks, few) == lax.rem(holds, few)
    attended = attend(query, key, value, None, heads, allowed)
    out_ref[...] = first + multiply(sigmoid(gate) * attended, final_ref[...])


def transition_kernel(
    ready, msa_ref, gains_ref, expand_ref, shrink_ref, sides_ref, left_ref, right_ref, out_ref
):
    ready()
    half = sides_ref.shape[0] // 2
    second = msa_ref[...]
    expanded = multiply(layer_normalise(second, gains_ref[2:3, :]), expand_ref[...])
    third = second + multiply(jnp.maximum(expanded, 0.0), shrink_ref[...])
    out_ref[...] = third
    factors = multiply(sides_ref[...], layer_normalise(third, gains_ref[3:4, :]), across=True)
    left_ref[...] = factors[:half]
    for g in range(right_ref.shape[0]):
        right_ref[g] = factors[half:]


def msa_blocks_kernel(n_branch, n_gj, ready, msa_ref, *rest):
    chunks, slots = rest[:-1], rest[-1]
    per_part, each = slots.shape[1:3]
    ready()
    for b in range(n_branch):
        for g in range(per_part):
            for j in range(n_gj):
                start = ((b * per_part + g) * n_gj + j) * each
                slots[b * n_gj + j, g] = msa_ref[start : start + each]
    for k, chunk in enumerate(chunks):
        chunk[...] = slots[column_index() ^ k]


def gather_msa(few, me, blocks, out_ref, slots):
    n_cols = len(blocks)
    spread(me, blocks, slots)
    for r in range(out_ref.shape[0]):
        out_ref[r] = jnp.concatenate(
            [slots[c, r * few : (r + 1) * few] for c in range(n_cols)], axis=0
        )


def gather_msa_kernel(few, n_cols, ready, *rest):
    ready()
    gather_msa(few, column_index(), rest[:n_cols], *rest[n_cols:])


def gather_pair_kernel(few, n_cols, residues, ready, gains_ref, matrix_ref, *rest):
    blocks, (first_ref, gate_ref, slots) = rest[:n_cols], rest[n_cols:]
    ready()
    spread_rows(column_index(), blocks, slots)
    block = blocks[0].shape[0]
    count = residues * few
    groups = block // count
    for c in range(n_cols):
        for o in range(groups):
            first_ref[pl.ds(o * n_cols + c, count, stride=groups * n_cols), :] = slots[
                pl.ds(c * block + o * count, count), :
            ]
    width = first_ref.shape[1]
    normal = layer_normalise(first_ref[...], gains_ref[1:2, :])
    gate_ref[...] = sigmoid(multiply(normal, matrix_ref[:, 4 * width :]))


def triangle_kernel(few, n_branch, n_gj, ready, tri_ref, *rest):
    n_cols = n_branch * n_gj
    blocks, (out_ref, msa_out, product_ref, slots) = rest[:n_cols], rest[n_cols:]
    ready()
    gather_msa(few, column_index(), blocks, msa_out, slots)
    n_all, rows, _ = out_ref.shape
    n_gi = n_all // n_cols
    share = few
    tiles = rows // few
    each = 2 * share
    wide = lanes // few
    group = lax.broadcasted_iota(jnp.int32, (n_gi * tiles, lanes), 1) // wide
    products = []
    for q in range(share):
        left, right = [], []
        for c in range(n_cols):
            base = (c // n_gj * n_all // n_branch + c % n_gj) * tiles * each
            step = n_gj * tiles * each
            here = jnp.concatenate(
                [
                    tri_ref[pl.ds(base + t * each + q, n_gi, stride=step), :]
                    for t in range(tiles)
                ],
                axis=0,
            )
            left.append(
                jnp.concatenate(
                    [jnp.where(group == i, here, 0.0) for i in range(few)], axis=0
                )
            )
            here = jnp.concatenate(
                [
                    tri_ref[pl.ds(base + g * step + share + q, tiles, stride=each), :]
                    for g in range(n_gi)
                ],
                axis=0,
            )
            rolled = [here] + [pltpu.roll(here, k * wide, 1) for k in range(1, few)]
            copies = []
            for j in range(few):
                copy = rolled[0]
                for k in range(1, few):
                    copy = jnp.where(group == (j + k) % few, rolled[k], copy)
                copies.append(copy)
            step = n_gi * tiles // n_cols
            right.append(
                jnp.concatenate(
                    [copy[k * step : (k + 1) * step] for k in range(n_cols) for copy in copies],
                    axis=0,
                )
            )
        products.append(
            multiply(
                jnp.concatenate(left, axis=1), jnp.concatenate(right, axis=1), across=True
            )
        )
    for c, product in enumerate(swap_lane_groups(products)):
        product_ref[...] = product
        for g in range(n_gi):
            out_ref[(c // n_gj * n_gi + g) * n_gj + c % n_gj] = product_ref[pl.ds(g, rows, stride=n_gi), :]


def pair_kernel(
    few, n_gi, n_cols, ready, *rest
):
    left_refs, pair_refs = rest[:n_cols], rest[n_cols : 2 * n_cols]
    right_ref, gain_ref, matrix_ref, triangle_ref, tri_far = rest[2 * n_cols : 2 * n_cols + 5]
    chunks = rest[2 * n_cols + 5 : 3 * n_cols + 5]
    rest = rest[3 * n_cols + 5 :]
    left_ref, slots, pair_ref, first_ref, tri_ref, sems = rest
    me = column_index()
    groups_j = n_gi // n_cols
    block = pair_refs[0].shape[0]
    ready()
    spread(me, left_refs, left_ref)
    spread_rows(me, pair_refs, slots)
    _, wide, count = left_ref.shape
    half = block // groups_j
    all_rows = count // few
    residues = n_cols * few
    pair_cols = n_gi * few
    per = lanes // pair_cols
    groups = residues // per
    width = pair_ref.shape[1]
    owner = lax.rem(lax.broadcasted_iota(jnp.int32, (1, count), 1), few)
    left = []
    for c in range(n_cols):
        here = left_ref[c]
        for f in range(few):
            own = jnp.where(owner == f, here, 0.0)
            total = own
            for other in range(few):
                if other != f:
                    total = total + pltpu.roll(own, (other - f) % count, 1)
            left.append(total)
    left = jnp.concatenate(left, axis=0) * (1.0 / all_rows)
    right = []
    for d in range(wide):
        here = right_ref[pl.ds(d, n_gi, stride=wide), :]
        right += [jnp.where(owner == f, here, 0.0) for f in range(few)]
    right = jnp.concatenate(right, axis=0)
    outer = multiply(left, right, across=True)
    outputs = []
    for g in range(groups):
        swapped = swap_lane_groups(
            [outer[(g * per + i) * wide : (g * per + i + 1) * wide] for i in range(per)]
        )
        stacked = [
            s[:, t * lanes : (t + 1) * lanes] for s in swapped for t in range(wide // per)
        ]
        outputs.append(jnp.concatenate(stacked, axis=0))
    for c in range(n_cols):
        for o in range(groups_j):
            pair_ref[pl.ds(c * groups_j + o, half, stride=n_gi), :] = slots[
                pl.ds(c * block + o, half, stride=groups_j), :
            ]
    update = multiply(matrix_ref[...], jnp.concatenate(outputs, axis=1))
    first = pair_ref[...].T + update
    projected = multiply(
        triangle_ref[pl.ds(0, 4 * width), :], layer_normalise(first, gain_ref[...], axis=0)
    )
    slot_count, _, each, _ = tri_far.shape
    copies = []
    for g in range(groups):
        here = slice(g * lanes, (g + 1) * lanes)
        tri = sigmoid(projected[2 * width : 4 * width, here]) * projected[: 2 * width, here]
        tri_ref[g] = tri.reshape(slot_count, each, lanes)
        copies.append(pltpu.make_async_copy(tri_ref.at[g], tri_far.at[:, g], sems.at[g]))
        copies[-1].start()
    first_ref[...] = first.T
    for k in range(n_cols):
        for o in range(groups_j):
            rows = pl.ds((me ^ k) * groups_j + o, half, stride=n_gi)
            chunks[k][pl.ds(o * half, half), :] = first_ref[rows, :]
    wait_all(copies)


def final_kernel(
    few, residues, packed, ready, product_ref, first_ref, gate_ref, gains_ref, matrix_ref, out_ref,
    channels_ref
):
    positions = out_ref.shape[0]
    ready()
    if packed:
        tiles = residues // few
        tall = product_ref.shape[0] // residues
        product = []
        for t in range(tiles):
            here = [
                product_ref[pl.ds(i * tiles + t, tall, stride=residues), :] for i in range(few)
            ]
            for q, piece in enumerate(swap_lane_groups(here)):
                channels_ref[pl.ds(q, tall, stride=few), :] = piece
            product.append(channels_ref[...])
        product = jnp.concatenate(product, axis=1)
    else:
        product = product_ref[...]
    normal = layer_normalise(product, 1.0, axis=0).T * gains_ref[2:3, :]
    result = first_ref[...] + gate_ref[...] * multiply(normal, matrix_ref[...])
    count = positions // (residues * few)
    for i in range(residues):
        for f in range(few):
            start = (i * few + f) * count
            out_ref[pl.ds(i * few * count + f, count, stride=few), :] = result[
                start : start + count
            ]


def per_device(
    homolog_embedding,
    pair_input_tensor,
    layernorm_scales,
    pair_norm_gains,
    pair_bias_matrix,
    horizontal_qkvg_kernel,
    horizontal_final_kernel,
    vertical_qkvg_kernel,
    vertical_final_kernel,
    feedforward_expand_kernel,
    feedforward_shrink_kernel,
    dyadic_sides_kernel,
    outer_output_matrix,
    triangle_input_matrix,
    triangle_output_matrix,
):
    rows, residues, width = homolog_embedding.shape
    pair_cols, pair_width = pair_input_tensor.shape[1:]
    heads = pair_bias_matrix.shape[1]
    outer_width = dyadic_sides_kernel.shape[1] // 2
    n_branch, n_gi, n_gj = (lax.axis_size(name) for name in everyone)
    n_cols = n_branch * n_gj
    n_all = n_cols * n_gi
    length = residues * n_gi
    few = residues // n_cols
    groups = n_gi // n_cols
    parts = 2
    per_part = n_gi // parts
    own_rows = rows // per_part

    def trade(blocks, axes):
        n = lax.axis_size(axes)
        return [blocks[0]] + [
            lax.ppermute(blocks[k], axes, [(t ^ k, t) for t in range(n) if t ^ k < n])
            for k in range(1, len(blocks))
        ]

    halves = [
        [
            (b * n_gi + part * per_part + g) * n_gj + j
            for b in range(n_branch)
            for g in range(per_part)
            for j in range(n_gj)
        ]
        for part in range(parts)
    ]
    n_half = n_cols * per_part
    positions = residues * pair_cols
    each = own_rows * few

    per = lanes // pair_cols
    bias_block = (heads // per, residues, lanes)
    msa, bias = call(
        bias_kernel,
        [[(parts * rows, residues, width)], bias_block],
        [homolog_embedding],
        [pair_input_tensor],
        [pair_norm_gains],
        [pair_bias_matrix.T],
        scratch=[
            homolog_embedding.shape,
            pair_input_tensor.shape,
            pair_norm_gains.shape,
            (heads, pair_width),
        ],
        sems=[4, parts],
    )
    msa = lax.all_to_all(msa, "gi", 0, 0, tiled=True)
    (bias,) = call_near(
        functools.partial(bias_part_kernel, per_part),
        [(per_part,) + bias_block],
        *trade([bias] * per_part, "gi"),
    )
    bias = trade([bias] * n_cols, columns)
    (msa_first,) = call_near(
        functools.partial(row_kernel, n_branch, n_gj, per_part, few),
        [(n_half, each, width)],
        msa,
        *bias,
        layernorm_scales,
        horizontal_qkvg_kernel,
        horizontal_final_kernel,
        scratch=[(n_cols, per_part) + bias_block],
    )
    pair, msa_first = lax.optimization_barrier((pair_input_tensor, msa_first))

    msa_first = lax.all_to_all(msa_first, everyone, 0, 0, tiled=True, axis_index_groups=halves)
    count = n_half * each
    (msa_second,) = call_near(
        functools.partial(column_kernel, few, heads),
        [(count, width)],
        msa_first.reshape(count, width),
        layernorm_scales,
        vertical_qkvg_kernel,
        vertical_final_kernel,
    )
    left, right, alignment = call_near(
        transition_kernel,
        [(outer_width, count), (n_gi, outer_width, count), (count, width)],
        msa_second,
        layernorm_scales,
        feedforward_expand_kernel,
        feedforward_shrink_kernel,
        dyadic_sides_kernel.T,
    )
    alignment = call_near(
        functools.partial(msa_blocks_kernel, n_branch, n_gj),
        [(per_part, each, width)] * n_cols,
        alignment,
        scratch=[(n_cols, per_part, each, width)],
    )
    pair = call_near(
        functools.partial(pair_blocks_kernel, few, residues),
        [(positions // n_cols, pair_width)] * n_cols,
        pair.reshape(positions, pair_width),
        scratch=[(positions, pair_width)],
    )
    pair = trade(pair, columns)
    right = lax.all_to_all(right, "gi", 0, 0, tiled=True)
    left = trade([left] * n_cols, columns)
    alignment = [block.reshape(-1, width) for block in trade(alignment, columns)]
    share = max(pair_width // n_all, 1)
    slots = pair_width // share
    triangle = triangle_input_matrix.T.reshape(5, slots, share, pair_width)
    sides = jnp.stack([triangle[0], triangle[2]], axis=1)
    gates = jnp.stack([triangle[1], triangle[3]], axis=1)
    triangle = jnp.concatenate(
        [side.reshape(2 * pair_width, pair_width) for side in (sides, gates)]
        + [triangle[4].reshape(pair_width, pair_width)],
        axis=0,
    )
    matrix = outer_output_matrix.reshape(outer_width, outer_width // per, per, pair_width)
    matrix = jnp.transpose(matrix, (3, 2, 1, 0)).reshape(pair_width, -1)
    tri, *first = call_near(
        functools.partial(pair_kernel, few, n_gi, n_cols),
        [[(slots, positions // lanes, 2 * share, lanes)]]
        + [(positions // n_cols, pair_width)] * n_cols,
        *left,
        *pair,
        right.reshape(n_gi * outer_width, count),
        pair_norm_gains[1][:, None],
        matrix,
        triangle,
        scratch=[
            (n_cols, outer_width, count),
            (positions, pair_width),
            (positions, pair_width),
            (positions, pair_width),
            (positions // lanes, slots, 2 * share, lanes),
        ],
        sems=[positions // lanes],
    )

    first, gate = call_near(
        functools.partial(gather_pair_kernel, few, n_cols, residues),
        [(positions, pair_width)] * 2,
        pair_norm_gains,
        triangle_input_matrix,
        *trade(first, columns),
        scratch=[(positions, pair_width)],
    )
    tile = (rows, residues, width)
    scratch = [(n_cols, rows * few, width)]
    packed = share * n_all == pair_width and share == few and few == per
    if packed:
        tri = lax.all_to_all(tri, everyone, 0, 0, tiled=True)
        product, alignment_output = call_near(
            functools.partial(triangle_kernel, few, n_branch, n_gj),
            [(n_all, residues, lanes), tile],
            tri.reshape(-1, lanes),
            *alignment,
            scratch=[(lanes, lanes)] + scratch,
        )
        product = lax.all_to_all(product, everyone, 0, 0, tiled=True)
        product = product.reshape(n_all * residues, lanes)
    else:
        (alignment_output,) = call_near(
            functools.partial(gather_msa_kernel, few, n_cols),
            [tile],
            *alignment,
            scratch=scratch,
        )
        tri = jnp.transpose(tri.reshape(slots, -1, 2, share, lanes), (2, 1, 4, 0, 3))
        tri = tri.reshape(2, residues, pair_cols, pair_width)
        right_columns = lax.all_gather(tri[1], "gi", axis=0, tiled=True)
        product = lax.psum_scatter(
            jnp.einsum("jkc,ikc->jic", right_columns, tri[0], precision=precise),
            columns,
            scatter_dimension=0,
            tiled=True,
        ).reshape(groups, n_cols, few, residues, pair_width)
        product = jnp.transpose(product, (4, 3, 2, 0, 1)).reshape(pair_width, positions)
    (pair_output_tensor,) = call_near(
        functools.partial(final_kernel, few, residues, packed),
        [(positions, pair_width)],
        product,
        first,
        gate,
        pair_norm_gains,
        triangle_output_matrix,
        scratch=[(pair_width, lanes)],
    )
    return (
        alignment_output,
        pair_output_tensor.reshape(residues, pair_cols, pair_width),
    )


def solution(mesh):
    tile, grid = P(("branch", "gj"), "gi", None), P("gi", ("branch", "gj"), None)
    return jax.shard_map(
        per_device,
        mesh=mesh,
        in_specs=(tile, grid) + (P(),) * 13,
        out_specs=(tile, grid),
        check_vma=False,
    )
```

```python
import functools
import math

import jax
import jax.numpy as jnp
from jax import lax
from jax.experimental import pallas as pl
from jax.experimental.pallas import tpu as pltpu
from jax.sharding import PartitionSpec as P

epsilon = 1e-05
precise = lax.Precision.HIGH
everyone = ("branch", "gi", "gj")
columns = ("branch", "gj")
lanes = 128
far = pl.BlockSpec(memory_space=pl.ANY)
vmem = pl.BlockSpec(memory_space=pltpu.VMEM)
params = pltpu.CompilerParams(vmem_limit_bytes=16 * 1024 * 1024)


def layer_normalise(values, norm_gain, axis=-1):
    average = jnp.mean(values, axis=axis, keepdims=True)
    centred = values - average
    variance = jnp.mean(centred * centred, axis=axis, keepdims=True)
    return centred * lax.rsqrt(variance + epsilon) * norm_gain


def apply_projection(values, weight):
    return jnp.einsum("...c,cd->...d", values, weight, precision=precise)


def sigmoid(values):
    return 1.0 / (1.0 + jnp.exp(-values))


def split(values):
    high = values.astype(jnp.bfloat16)
    return high, (values - high.astype(jnp.float32)).astype(jnp.bfloat16)


def multiply(left, right, across=False):
    numbers = (((1,), (1 if across else 0,)), ((), ()))

    def one(a, b):
        return lax.dot_general(a, b, numbers, preferred_element_type=jnp.float32)

    lh, ll = left if isinstance(left, tuple) else split(left)
    rh, rl = split(right)
    depth_axis = 1 if across else 0
    if lh.shape[1] == lanes:
        both = one(
            jnp.concatenate([lh, ll], axis=1), jnp.concatenate([rh, rh], axis=depth_axis)
        )
        return both + one(lh, rl)
    if right.shape[1 - depth_axis] == lanes:
        both = one(lh, jnp.concatenate([rh, rl], axis=1 - depth_axis))
        return both[:, :lanes] + (both[:, lanes:] + one(ll, rh))
    return one(lh, rh) + (one(lh, rl) + one(ll, rh))


def swap_lane_groups(arrays):
    n, arrays = len(arrays), list(arrays)
    width = lanes // n
    wide = arrays[0].shape[-1]
    lane = lax.broadcasted_iota(jnp.int32, arrays[0].shape, arrays[0].ndim - 1)
    group = lax.rem(lane, lanes) // width
    axis = arrays[0].ndim - 1
    step = 1
    while step < n:
        upper = (group // step) % 2 == 1
        for low in range(n):
            if low & step:
                continue
            a, b = arrays[low], arrays[low + step]
            arrays[low] = jnp.where(upper, pltpu.roll(b, step * width, axis), a)
            arrays[low + step] = jnp.where(
                upper, b, pltpu.roll(a, wide - step * width, axis)
            )
        step *= 2
    return arrays


def head_masks(shape, heads):
    column = lax.broadcasted_iota(jnp.int32, shape, 1)
    return [column // (shape[1] // heads) == h for h in range(heads)]


def attend(query, key, value, bias, heads, allowed=None):
    count, inner = query.shape
    masks = head_masks((count, inner), heads)
    ones = [jnp.where(m, 1.0, 0.0).astype(jnp.bfloat16) for m in masks]
    pair = split(query * (1.0 / math.sqrt(inner // heads)))
    spread = tuple(jnp.concatenate([half * one for one in ones], axis=0) for half in pair)
    scores = multiply(spread, key, across=True)
    if bias is not None:
        scores = scores + bias
    if allowed is not None:
        scores = jnp.where(allowed, scores, -1e30)
    weights = jnp.exp(scores - jnp.max(scores, axis=-1, keepdims=True))
    weights = weights / jnp.sum(weights, axis=-1, keepdims=True)
    mixed = multiply(weights, value)
    result = jnp.where(masks[0], mixed[:count], 0.0)
    for h in range(1, heads):
        result = result + jnp.where(masks[h], mixed[h * count : (h + 1) * count], 0.0)
    return result


def start_copies(pairs, sems):
    copies = [pltpu.make_async_copy(a, b, sems.at[n]) for n, (a, b) in enumerate(pairs)]
    for copy in copies:
        copy.start()
    return copies


def wait_all(copies):
    for copy in copies:
        copy.wait()


def column_index():
    return lax.axis_index("branch") * lax.axis_size("gj") + lax.axis_index("gj")


def cost(kernel):
    name = getattr(kernel, "func", kernel).__name__
    work = {
        "bias_kernel": 2.0,
        "bias_part_kernel": 6.0,
        "row_kernel": 4.5,
        "pair_blocks_kernel": 8.0,
        "column_kernel": 6.0,
        "transition_kernel": 3.0,
        "msa_blocks_kernel": 0.5,
        "pair_kernel": 4.0,
        "triangle_kernel": 2.0,
        "gather_pair_kernel": 1.0,
        "final_kernel": 1.3,
    }.get(name, 1.0)
    return pl.CostEstimate(
        flops=int(work * 1.1e9), bytes_accessed=int(work * 3.6e6), transcendentals=0
    )


def call(kernel, outs, *operands, scratch=(), sems=()):
    def bare(item):
        return item[0] if isinstance(item, list) else item

    n_in, n_out = len(operands), len(outs)
    near_in = [n for n, item in enumerate(operands) if not isinstance(item, list)]
    near_out = [n for n, item in enumerate(outs) if not isinstance(item, list)]
    shapes = [operands[n].shape for n in near_in] + [outs[n] for n in near_out]

    def body(*refs):
        inputs, results = list(refs[:n_in]), list(refs[n_in : n_in + n_out])
        local = refs[n_in + n_out : n_in + n_out + len(shapes)]
        rest, own_sems = refs[n_in + n_out + len(shapes) : -1], refs[-1]
        pairs = list(zip([inputs[n] for n in near_in], local))
        back = list(zip(local[len(near_in) :], [results[n] for n in near_out]))
        for n, ref in zip(near_in, local):
            inputs[n] = ref
        for n, ref in zip(near_out, local[len(near_in) :]):
            results[n] = ref
        copies = start_copies(pairs, own_sems)
        kernel(lambda: wait_all(copies), *inputs, *results, *rest)
        wait_all(start_copies(back, own_sems))

    return pl.pallas_call(
        body,
        out_shape=[jax.ShapeDtypeStruct(bare(out), jnp.float32) for out in outs],
        in_specs=[far] * n_in,
        out_specs=[far] * n_out,
        scratch_shapes=[pltpu.VMEM(shape, jnp.float32) for shape in shapes + list(scratch)]
        + [pltpu.SemaphoreType.DMA((n,)) for n in sems]
        + [pltpu.SemaphoreType.DMA((max(len(near_in), len(near_out), 1),))],
        cost_estimate=cost(kernel),
    )(*[bare(operand) for operand in operands])


def call_near(kernel, outs, *operands, scratch=(), sems=()):
    return pl.pallas_call(
        lambda *refs: kernel(lambda: None, *refs),
        out_shape=[
            jax.ShapeDtypeStruct(out[0] if isinstance(out, list) else out, jnp.float32)
            for out in outs
        ],
        in_specs=[vmem] * len(operands),
        out_specs=[far if isinstance(out, list) else vmem for out in outs],
        scratch_shapes=[pltpu.VMEM(shape, jnp.float32) for shape in scratch]
        + [pltpu.SemaphoreType.DMA((n,)) for n in sems],
        compiler_params=params,
        cost_estimate=cost(kernel),
    )(*operands)


def spread(me, refs, slots):
    for k, ref in enumerate(refs):
        slots[me ^ k] = ref[...]


def spread_rows(me, refs, slots):
    for k, ref in enumerate(refs):
        count = ref.shape[0]
        slots[pl.ds(pl.multiple_of((me ^ k) * count, 8), count), :] = ref[...]


def bias_kernel(
    ready, msa_far, pair_far, gains_far, matrix_far, copies_far, out_ref, msa_ref, pair_ref,
    gains_ref, matrix_ref, sems, out_sems
):
    rows = msa_far.shape[0]
    repeats = copies_far.shape[0] // rows
    step = max(pair_far.shape[0] // 4, 1)
    starts = range(0, pair_far.shape[0], step)
    copies = start_copies(
        [(msa_far, msa_ref), (gains_far, gains_ref), (matrix_far, matrix_ref)]
        + [(pair_far.at[pl.ds(n, step)], pair_ref.at[pl.ds(n, step)]) for n in starts],
        sems,
    )
    residues, pair_cols, _ = pair_ref.shape
    heads = matrix_ref.shape[0]
    per = lanes // pair_cols
    ready()
    wait_all(copies[:1])
    back = start_copies(
        [(msa_ref, copies_far.at[pl.ds(n * rows, rows)]) for n in range(repeats)], out_sems
    )
    wait_all(copies[1:3])
    for i in range(residues):
        if i % step == 0:
            wait_all([copies[3 + i // step]])
            normal = layer_normalise(pair_ref[pl.ds(i, step)], gains_ref[0:1, :][None])
        here = multiply(matrix_ref[...], normal[i % step], across=True)
        for h in range(heads):
            out_ref[h // per, i : i + 1, pl.ds(h % per * pair_cols, pair_cols)] = here[h : h + 1]
    wait_all(back)


def pair_blocks_kernel(few, residues, ready, pair_ref, *rest):
    chunks, slots = rest[:-1], rest[-1]
    n_cols = len(chunks)
    block = chunks[0].shape[0]
    groups = block // (residues * few)
    me = column_index()
    ready()
    for c in range(n_cols):
        for o in range(groups):
            for f in range(few):
                source = pl.ds((o * n_cols + c) * few + f, residues, stride=groups * n_cols * few)
                target = pl.ds(c * block + f * groups + o, residues, stride=few * groups)
                slots[target, :] = pair_ref[source, :]
    for k in range(n_cols):
        start = pl.multiple_of((me ^ k) * block, 8)
        chunks[k][...] = slots[pl.ds(start, block), :]


def bias_part_kernel(per_part, ready, *rest):
    blocks, (out_ref,) = rest[:per_part], rest[per_part:]
    ready()
    spread(lax.rem(lax.axis_index("gi"), per_part), blocks, out_ref)


def row_kernel(n_branch, n_gj, per_part, few, ready, msa_ref, *rest):
    n_cols = n_branch * n_gj
    bias_refs, (gains_ref, qkvg_ref, final_ref, out_ref, slots) = rest[:n_cols], rest[n_cols:]
    half = lax.div(lax.axis_index("gi"), per_part)
    ready()
    _, residues, width = msa_ref.shape
    blocks = slots.shape[2]
    n_gi = lax.axis_size("gi")
    length = n_gi * residues
    per = lanes * n_cols // length
    heads = blocks * per
    rows = msa_ref.shape[0] // n_gi
    inner = final_ref.shape[0]
    queries = per_part * residues
    tokens = jnp.concatenate(
        [msa_ref[g * rows + r] for r in range(rows) for g in range(n_gi)], axis=0
    )
    first = half * (per_part * rows)
    asking = msa_ref[pl.ds(first, per_part * rows)]
    asking = jnp.concatenate(
        [asking[g * rows + r] for r in range(rows) for g in range(per_part)], axis=0
    )
    tokens = layer_normalise(tokens, 1.0)
    normal = layer_normalise(asking, 1.0)
    gain = gains_ref[0:1, :]
    key_value = multiply(tokens * gain, qkvg_ref[:, inner : 3 * inner])
    normal = normal * gain
    query = multiply(normal, qkvg_ref[:, :inner])
    gate = multiply(normal, qkvg_ref[:, 3 * inner :])
    spread(column_index(), bias_refs, slots)
    pieces = [[] for _ in range(heads)]
    for block in range(blocks):
        for g in range(per_part):
            tiles = [[] for _ in range(per)]
            for tile in range(n_cols // per):
                group = [slots[c, g, block] for c in range(tile * per, (tile + 1) * per)]
                for k, piece in enumerate(swap_lane_groups(group)):
                    tiles[k].append(piece)
            for k in range(per):
                pieces[block * per + k].append(jnp.concatenate(tiles[k], axis=1))
    bias = jnp.concatenate([piece for head in pieces for piece in head], axis=0)
    attended = []
    for r in range(rows):
        keys = key_value[r * length : (r + 1) * length, :inner]
        values = key_value[r * length : (r + 1) * length, inner:]
        attended.append(
            attend(query[r * queries : (r + 1) * queries], keys, values, bias, heads)
        )
    attended = jnp.concatenate(attended, axis=0)
    result = asking + multiply(sigmoid(gate) * attended, final_ref[...])
    for b in range(n_branch):
        for g in range(per_part):
            for j in range(n_gj):
                start = g * residues + (b * n_gj + j) * few
                out_ref[(b * per_part + g) * n_gj + j] = jnp.concatenate(
                    [result[r * queries + start : r * queries + start + few] for r in range(rows)],
                    axis=0,
                )


def column_kernel(few, heads, ready, msa_ref, gains_ref, qkvg_ref, final_ref, out_ref):
    ready()
    count, width = msa_ref.shape
    inner = final_ref.shape[0]
    first = msa_ref[...]
    projected = multiply(layer_normalise(first, gains_ref[1:2, :]), qkvg_ref[...])
    query, key, value, gate = (projected[:, k * inner : (k + 1) * inner] for k in range(4))
    allowed = None
    if few > 1:
        shape = (heads * count, count)
        asks = lax.broadcasted_iota(jnp.int32, shape, 0)
        holds = lax.broadcasted_iota(jnp.int32, shape, 1)
        allowed = lax.rem(asks, few) == lax.rem(holds, few)
    attended = attend(query, key, value, None, heads, allowed)
    out_ref[...] = first + multiply(sigmoid(gate) * attended, final_ref[...])


def transition_kernel(
    ready, msa_ref, gains_ref, expand_ref, shrink_ref, sides_ref, left_ref, right_ref, out_ref
):
    ready()
    half = sides_ref.shape[0] // 2
    second = msa_ref[...]
    expanded = multiply(layer_normalise(second, gains_ref[2:3, :]), expand_ref[...])
    third = second + multiply(jnp.maximum(expanded, 0.0), shrink_ref[...])
    out_ref[...] = third
    factors = multiply(sides_ref[...], layer_normalise(third, gains_ref[3:4, :]), across=True)
    left_ref[...] = factors[:half]
    for g in range(right_ref.shape[0]):
        right_ref[g] = factors[half:]


def msa_blocks_kernel(n_branch, n_gj, ready, msa_ref, *rest):
    chunks, slots = rest[:-1], rest[-1]
    per_part, each = slots.shape[1:3]
    ready()
    for b in range(n_branch):
        for g in range(per_part):
            for j in range(n_gj):
                start = ((b * per_part + g) * n_gj + j) * each
                slots[b * n_gj + j, g] = msa_ref[start : start + each]
    for k, chunk in enumerate(chunks):
        chunk[...] = slots[column_index() ^ k]


def gather_msa(few, me, blocks, out_ref, slots):
    n_cols = len(blocks)
    spread(me, blocks, slots)
    for r in range(out_ref.shape[0]):
        out_ref[r] = jnp.concatenate(
            [slots[c, r * few : (r + 1) * few] for c in range(n_cols)], axis=0
        )


def gather_msa_kernel(few, n_cols, ready, *rest):
    ready()
    gather_msa(few, column_index(), rest[:n_cols], *rest[n_cols:])


def gather_pair_kernel(few, n_cols, residues, ready, gains_ref, matrix_ref, *rest):
    blocks, (first_ref, gate_ref, slots) = rest[:n_cols], rest[n_cols:]
    ready()
    spread_rows(column_index(), blocks, slots)
    block = blocks[0].shape[0]
    count = residues * few
    groups = block // count
    for c in range(n_cols):
        for o in range(groups):
            first_ref[pl.ds(o * n_cols + c, count, stride=groups * n_cols), :] = slots[
                pl.ds(c * block + o * count, count), :
            ]
    width = first_ref.shape[1]
    normal = layer_normalise(first_ref[...], gains_ref[1:2, :])
    gate_ref[...] = sigmoid(multiply(normal, matrix_ref[:, 4 * width :]))


def triangle_kernel(few, n_branch, n_gj, ready, tri_ref, *rest):
    n_cols = n_branch * n_gj
    blocks, (out_ref, msa_out, product_ref, slots) = rest[:n_cols], rest[n_cols:]
    ready()
    gather_msa(few, column_index(), blocks, msa_out, slots)
    n_all, rows, _ = out_ref.shape
    n_gi = n_all // n_cols
    share = few
    tiles = rows // few
    each = 2 * share
    wide = lanes // few
    group = lax.broadcasted_iota(jnp.int32, (n_gi * tiles, lanes), 1) // wide
    products = []
    for q in range(share):
        left, right = [], []
        for c in range(n_cols):
            base = (c // n_gj * n_all // n_branch + c % n_gj) * tiles * each
            step = n_gj * tiles * each
            here = jnp.concatenate(
                [
                    tri_ref[pl.ds(base + t * each + q, n_gi, stride=step), :]
                    for t in range(tiles)
                ],
                axis=0,
            )
            left.append(
                jnp.concatenate(
                    [jnp.where(group == i, here, 0.0) for i in range(few)], axis=0
                )
            )
            here = jnp.concatenate(
                [
                    tri_ref[pl.ds(base + g * step + share + q, tiles, stride=each), :]
                    for g in range(n_gi)
                ],
                axis=0,
            )
            rolled = [here] + [pltpu.roll(here, k * wide, 1) for k in range(1, few)]
            copies = []
            for j in range(few):
                copy = rolled[0]
                for k in range(1, few):
                    copy = jnp.where(group == (j + k) % few, rolled[k], copy)
                copies.append(copy)
            step = n_gi * tiles // n_cols
            right.append(
                jnp.concatenate(
                    [copy[k * step : (k + 1) * step] for k in range(n_cols) for copy in copies],
                    axis=0,
                )
            )
        products.append(
            multiply(
                jnp.concatenate(left, axis=1), jnp.concatenate(right, axis=1), across=True
            )
        )
    for c, product in enumerate(swap_lane_groups(products)):
        product_ref[...] = product
        for g in range(n_gi):
            out_ref[(c // n_gj * n_gi + g) * n_gj + c % n_gj] = product_ref[pl.ds(g, rows, stride=n_gi), :]


def pair_kernel(
    few, n_gi, n_cols, ready, *rest
):
    left_refs, pair_refs = rest[:n_cols], rest[n_cols : 2 * n_cols]
    right_ref, gain_ref, matrix_ref, triangle_ref, tri_far = rest[2 * n_cols : 2 * n_cols + 5]
    chunks = rest[2 * n_cols + 5 : 3 * n_cols + 5]
    rest = rest[3 * n_cols + 5 :]
    left_ref, slots, pair_ref, first_ref, tri_ref, sems = rest
    me = column_index()
    groups_j = n_gi // n_cols
    block = pair_refs[0].shape[0]
    ready()
    spread(me, left_refs, left_ref)
    spread_rows(me, pair_refs, slots)
    _, wide, count = left_ref.shape
    half = block // groups_j
    all_rows = count // few
    residues = n_cols * few
    pair_cols = n_gi * few
    per = lanes // pair_cols
    groups = residues // per
    width = pair_ref.shape[1]
    owner = lax.rem(lax.broadcasted_iota(jnp.int32, (1, count), 1), few)
    left = []
    for c in range(n_cols):
        here = left_ref[c]
        for f in range(few):
            own = jnp.where(owner == f, here, 0.0)
            total = own
            for other in range(few):
                if other != f:
                    total = total + pltpu.roll(own, (other - f) % count, 1)
            left.append(total)
    left = jnp.concatenate(left, axis=0) * (1.0 / all_rows)
    right = []
    for d in range(wide):
        here = right_ref[pl.ds(d, n_gi, stride=wide), :]
        right += [jnp.where(owner == f, here, 0.0) for f in range(few)]
    right = jnp.concatenate(right, axis=0)
    outer = multiply(left, right, across=True)
    outputs = []
    for g in range(groups):
        swapped = swap_lane_groups(
            [outer[(g * per + i) * wide : (g * per + i + 1) * wide] for i in range(per)]
        )
        stacked = [
            s[:, t * lanes : (t + 1) * lanes] for s in swapped for t in range(wide // per)
        ]
        outputs.append(jnp.concatenate(stacked, axis=0))
    for c in range(n_cols):
        for o in range(groups_j):
            pair_ref[pl.ds(c * groups_j + o, half, stride=n_gi), :] = slots[
                pl.ds(c * block + o, half, stride=groups_j), :
            ]
    update = multiply(matrix_ref[...], jnp.concatenate(outputs, axis=1))
    first = pair_ref[...].T + update
    projected = multiply(
        triangle_ref[pl.ds(0, 4 * width), :], layer_normalise(first, gain_ref[...], axis=0)
    )
    slot_count, _, each, _ = tri_far.shape
    copies = []
    for g in range(groups):
        here = slice(g * lanes, (g + 1) * lanes)
        tri = sigmoid(projected[2 * width : 4 * width, here]) * projected[: 2 * width, here]
        tri_ref[g] = tri.reshape(slot_count, each, lanes)
        copies.append(pltpu.make_async_copy(tri_ref.at[g], tri_far.at[:, g], sems.at[g]))
        copies[-1].start()
    first_ref[...] = first.T
    for k in range(n_cols):
        for o in range(groups_j):
            rows = pl.ds((me ^ k) * groups_j + o, half, stride=n_gi)
            chunks[k][pl.ds(o * half, half), :] = first_ref[rows, :]
    wait_all(copies)


def final_kernel(
    few, residues, packed, ready, product_ref, first_ref, gate_ref, gains_ref, matrix_ref, out_ref,
    channels_ref
):
    positions = out_ref.shape[0]
    ready()
    if packed:
        tiles = residues // few
        tall = product_ref.shape[0] // residues
        product = []
        for t in range(tiles):
            here = [
                product_ref[pl.ds(i * tiles + t, tall, stride=residues), :] for i in range(few)
            ]
            for q, piece in enumerate(swap_lane_groups(here)):
                channels_ref[pl.ds(q, tall, stride=few), :] = piece
            product.append(channels_ref[...])
        product = jnp.concatenate(product, axis=1)
    else:
        product = product_ref[...]
    normal = layer_normalise(product, 1.0, axis=0).T * gains_ref[2:3, :]
    result = first_ref[...] + gate_ref[...] * multiply(normal, matrix_ref[...])
    count = positions // (residues * few)
    for i in range(residues):
        for f in range(few):
            start = (i * few + f) * count
            out_ref[pl.ds(i * few * count + f, count, stride=few), :] = result[
                start : start + count
            ]


def per_device(
    homolog_embedding,
    pair_input_tensor,
    layernorm_scales,
    pair_norm_gains,
    pair_bias_matrix,
    horizontal_qkvg_kernel,
    horizontal_final_kernel,
    vertical_qkvg_kernel,
    vertical_final_kernel,
    feedforward_expand_kernel,
    feedforward_shrink_kernel,
    dyadic_sides_kernel,
    outer_output_matrix,
    triangle_input_matrix,
    triangle_output_matrix,
):
    rows, residues, width = homolog_embedding.shape
    pair_cols, pair_width = pair_input_tensor.shape[1:]
    heads = pair_bias_matrix.shape[1]
    outer_width = dyadic_sides_kernel.shape[1] // 2
    n_branch, n_gi, n_gj = (lax.axis_size(name) for name in everyone)
    n_cols = n_branch * n_gj
    n_all = n_cols * n_gi
    length = residues * n_gi
    few = residues // n_cols
    groups = n_gi // n_cols
    parts = 2
    per_part = n_gi // parts
    own_rows = rows // per_part

    def trade(blocks, axes):
        n = lax.axis_size(axes)
        return [blocks[0]] + [
            lax.ppermute(blocks[k], axes, [(t ^ k, t) for t in range(n) if t ^ k < n])
            for k in range(1, len(blocks))
        ]

    halves = [
        [
            (b * n_gi + part * per_part + g) * n_gj + j
            for b in range(n_branch)
            for g in range(per_part)
            for j in range(n_gj)
        ]
        for part in range(parts)
    ]
    n_half = n_cols * per_part
    positions = residues * pair_cols
    each = own_rows * few

    per = lanes // pair_cols
    bias_block = (heads // per, residues, lanes)
    msa, bias = call(
        bias_kernel,
        [[(parts * rows, residues, width)], bias_block],
        [homolog_embedding],
        [pair_input_tensor],
        [pair_norm_gains],
        [pair_bias_matrix.T],
        scratch=[
            homolog_embedding.shape,
            pair_input_tensor.shape,
            pair_norm_gains.shape,
            (heads, pair_width),
        ],
        sems=[3 + len(range(0, residues, max(residues // 4, 1))), parts],
    )
    msa = lax.all_to_all(msa, "gi", 0, 0, tiled=True)
    (bias,) = call_near(
        functools.partial(bias_part_kernel, per_part),
        [(per_part,) + bias_block],
        *trade([bias] * per_part, "gi"),
    )
    bias = trade([bias] * n_cols, columns)
    (msa_first,) = call_near(
        functools.partial(row_kernel, n_branch, n_gj, per_part, few),
        [(n_half, each, width)],
        msa,
        *bias,
        layernorm_scales,
        horizontal_qkvg_kernel,
        horizontal_final_kernel,
        scratch=[(n_cols, per_part) + bias_block],
    )
    pair, msa_first = lax.optimization_barrier((pair_input_tensor, msa_first))

    msa_first = lax.all_to_all(msa_first, everyone, 0, 0, tiled=True, axis_index_groups=halves)
    count = n_half * each
    (msa_second,) = call_near(
        functools.partial(column_kernel, few, heads),
        [(count, width)],
        msa_first.reshape(count, width),
        layernorm_scales,
        vertical_qkvg_kernel,
        vertical_final_kernel,
    )
    left, right, alignment = call_near(
        transition_kernel,
        [(outer_width, count), (n_gi, outer_width, count), (count, width)],
        msa_second,
        layernorm_scales,
        feedforward_expand_kernel,
        feedforward_shrink_kernel,
        dyadic_sides_kernel.T,
    )
    alignment = call_near(
        functools.partial(msa_blocks_kernel, n_branch, n_gj),
        [(per_part, each, width)] * n_cols,
        alignment,
        scratch=[(n_cols, per_part, each, width)],
    )
    pair = call_near(
        functools.partial(pair_blocks_kernel, few, residues),
        [(positions // n_cols, pair_width)] * n_cols,
        pair.reshape(positions, pair_width),
        scratch=[(positions, pair_width)],
    )
    pair = trade(pair, columns)
    right = lax.all_to_all(right, "gi", 0, 0, tiled=True)
    left = trade([left] * n_cols, columns)
    alignment = [block.reshape(-1, width) for block in trade(alignment, columns)]
    share = max(pair_width // n_all, 1)
    slots = pair_width // share
    triangle = triangle_input_matrix.T.reshape(5, slots, share, pair_width)
    sides = jnp.stack([triangle[0], triangle[2]], axis=1)
    gates = jnp.stack([triangle[1], triangle[3]], axis=1)
    triangle = jnp.concatenate(
        [side.reshape(2 * pair_width, pair_width) for side in (sides, gates)]
        + [triangle[4].reshape(pair_width, pair_width)],
        axis=0,
    )
    matrix = outer_output_matrix.reshape(outer_width, outer_width // per, per, pair_width)
    matrix = jnp.transpose(matrix, (3, 2, 1, 0)).reshape(pair_width, -1)
    tri, *first = call_near(
        functools.partial(pair_kernel, few, n_gi, n_cols),
        [[(slots, positions // lanes, 2 * share, lanes)]]
        + [(positions // n_cols, pair_width)] * n_cols,
        *left,
        *pair,
        right.reshape(n_gi * outer_width, count),
        pair_norm_gains[1][:, None],
        matrix,
        triangle,
        scratch=[
            (n_cols, outer_width, count),
            (positions, pair_width),
            (positions, pair_width),
            (positions, pair_width),
            (positions // lanes, slots, 2 * share, lanes),
        ],
        sems=[positions // lanes],
    )

    first, gate = call_near(
        functools.partial(gather_pair_kernel, few, n_cols, residues),
        [(positions, pair_width)] * 2,
        pair_norm_gains,
        triangle_input_matrix,
        *trade(first, columns),
        scratch=[(positions, pair_width)],
    )
    tile = (rows, residues, width)
    scratch = [(n_cols, rows * few, width)]
    packed = share * n_all == pair_width and share == few and few == per
    if packed:
        tri = lax.all_to_all(tri, everyone, 0, 0, tiled=True)
        product, alignment_output = call_near(
            functools.partial(triangle_kernel, few, n_branch, n_gj),
            [(n_all, residues, lanes), tile],
            tri.reshape(-1, lanes),
            *alignment,
            scratch=[(lanes, lanes)] + scratch,
        )
        product = lax.all_to_all(product, everyone, 0, 0, tiled=True)
        product = product.reshape(n_all * residues, lanes)
    else:
        (alignment_output,) = call_near(
            functools.partial(gather_msa_kernel, few, n_cols),
            [tile],
            *alignment,
            scratch=scratch,
        )
        tri = jnp.transpose(tri.reshape(slots, -1, 2, share, lanes), (2, 1, 4, 0, 3))
        tri = tri.reshape(2, residues, pair_cols, pair_width)
        right_columns = lax.all_gather(tri[1], "gi", axis=0, tiled=True)
        product = lax.psum_scatter(
            jnp.einsum("jkc,ikc->jic", right_columns, tri[0], precision=precise),
            columns,
            scatter_dimension=0,
            tiled=True,
        ).reshape(groups, n_cols, few, residues, pair_width)
        product = jnp.transpose(product, (4, 3, 2, 0, 1)).reshape(pair_width, positions)
    (pair_output_tensor,) = call_near(
        functools.partial(final_kernel, few, residues, packed),
        [(positions, pair_width)],
        product,
        first,
        gate,
        pair_norm_gains,
        triangle_output_matrix,
        scratch=[(pair_width, lanes)],
    )
    return (
        alignment_output,
        pair_output_tensor.reshape(residues, pair_cols, pair_width),
    )


def solution(mesh):
    tile, grid = P(("branch", "gj"), "gi", None), P("gi", ("branch", "gj"), None)
    return jax.shard_map(
        per_device,
        mesh=mesh,
        in_specs=(tile, grid) + (P(),) * 13,
        out_specs=(tile, grid),
        check_vma=False,
    )
```
